128 devices in a mesh: wide: 16 (over y, z_lo, core), narrow: 8 (over z_hi, x).
Axes of the slice: x: 4, y: 4, z: 4 (z_hi: 2, z_lo: 2; z = z_hi * 2 + z_lo), core: 2. Of those that a mesh axis runs over, the one named last changes fastest.
Arguments:
- gradient: bfloat16 [3584, 18432], P(('wide', 'narrow')), may hold values from -3000 to 3000
Outputs:
- update: bfloat16 [3584, 18432], P(('wide', 'narrow'))
The draws below stay inside these ranges and needn't reach their ends.
All inputs are finite; a program needn't handle non-finite values.
Results may differ from the reference program's by a relative error of at most 0.0055.
Values may be sent and summed in bfloat16 or wider, within the bound.
A program may use at most 64 MiB of HBM per device.

```python
import math
import jax
import jax.numpy as jnp

M = 3584
K = 18432


def draw_gradient(key, part):
    key = jax.random.fold_in(key, 11)
    first, second, third = jax.random.split(key, 3)
    top = 10.0
    positions = jnp.arange(M, dtype=jnp.float32)
    rising = jnp.exp(math.log(3.0) * positions / M)
    row_scale = jnp.exp(jax.random.uniform(first, (M,), jnp.float32, 0.0, math.log(top))) * rising
    col_scale = jnp.exp(jax.random.uniform(second, (K,), jnp.float32, 0.0, math.log(top)))
    values = jnp.clip(jax.random.normal(third, (M, K), jnp.float32), -6.0, 6.0)
    return (values * row_scale[:, None] * col_scale[None, :]).astype(jnp.bfloat16)


def setup_inputs(seed: int = 0) -> dict:
    key_of = jax.random.split(jax.random.key(seed), 2)
    return {
        "gradient": draw_gradient(jax.random.fold_in(key_of[1], 71), 0),
    }


COEFF_A = 3.4445
COEFF_B = -4.775
COEFF_C = 2.0315

def reference(gradient):
    widened = gradient.astype(jnp.float32)
    squares = jnp.sum(widened * widened)
    factor = 0.3 * math.sqrt(M) / (jnp.sqrt(squares) + 1e-07)
    scaled = (widened * factor).astype(jnp.bfloat16)
    gram = jnp.dot(scaled, scaled.T, preferred_element_type=jnp.float32).astype(jnp.bfloat16)
    square = jnp.dot(gram, gram, preferred_element_type=jnp.float32)
    poly = (COEFF_B * gram.astype(jnp.float32) + COEFF_C * square).astype(jnp.bfloat16)
    mixed = COEFF_A * scaled.astype(jnp.float32) + jnp.dot(poly, scaled, preferred_element_type=jnp.float32)
    return (math.sqrt(K) * mixed).astype(jnp.bfloat16)
```

```python
import math

import jax
import jax.numpy as jnp
from jax import lax
from jax.experimental import pallas as pl
from jax.experimental.pallas import tpu as pltpu
from jax.sharding import PartitionSpec as P

M = 3584
K = 18432
COLS = K // 128
PAD = 256

COEFF_A = 3.4445
COEFF_B = -4.775
COEFF_C = 2.0315

MESH = pl.DeviceIdType.MESH
BF = jnp.bfloat16
F32 = jnp.float32

BLK = 256
NB = M // BLK
SLOTS = 54
PART = 9216
CORE_ROWS = 3 * PART
SIZES = (2304, 576, 144)
TOPS = (1152, 288, 80)
BOTS = (1152, 288, 64)
AXES = ((0, 1, 2), (1, 2, 0), (2, 0, 1))


def al(x, m=16):
    return pl.multiple_of(x, m)


def kernel(
    s_ref, st_ref, out_ref,
    sp, t, g, r1, r2, r3, sq, ybf, yf,
    slab_sem, rs_send, rs_recv, ag_send, ag_recv, fw_send, fw_recv, sq_send, sq_recv,
):
    recv_bufs = (r1, r2, r3)
    w, n_ = lax.axis_index("wide"), lax.axis_index("narrow")
    core, z_lo, y = w % 2, (w // 2) % 2, w // 4
    x, z_hi = n_ % 4, n_ // 4
    z = z_hi * 2 + z_lo
    pos = (x, y, z)

    def device(x, y, z, core):
        return ((y * 2 + z % 2) * 2 + core, (z // 2) * 4 + x)

    def shifted(axis, by):
        p = [x, y, z]
        p[axis] = (p[axis] + by) % 4
        return device(*p, core)

    right = [shifted(a, 1) for a in range(3)]
    left = [shifted(a, 3) for a in range(3)]
    partner = device(x, y, z, 1 - core)

    barrier = pltpu.get_barrier_semaphore()
    for d in right + left + [partner]:
        pl.semaphore_signal(barrier, inc=1, device_id=d, device_id_type=MESH)
    pl.semaphore_wait(barrier, 7)

    def remote(src, dst, send, recv, dev):
        return pltpu.make_async_remote_copy(
            src_ref=src, dst_ref=dst, send_sem=send, recv_sem=recv, device_id=dev, device_id_type=MESH
        )

    sent = []

    slab = remote(s_ref, sp, slab_sem.at[0], slab_sem.at[1], partner)
    slab.start()
    slab.wait()

    def gram_block(m, carry):
        n = core * SLOTS + m
        i, d = n % NB, n // NB
        j = (i + d) % NB
        ri = pl.ds(al(i * BLK, BLK), BLK)
        rj = pl.ds(al(j * BLK, BLK), BLK)
        nt = (((1,), (1,)), ((), ()))
        acc = lax.dot_general(s_ref[ri, :], s_ref[rj, :], nt, preferred_element_type=F32)
        acc += lax.dot_general(sp[ri, :], sp[rj, :], nt, preferred_element_type=F32)
        acc = acc.astype(BF)
        t[pl.ds(al(m * 512, 512), 256), :] = acc[:, :128]
        t[pl.ds(al(m * 512 + 256, 256), 256), :] = acc[:, 128:]
        return carry

    lax.fori_loop(0, SLOTS, gram_block, 0)

    def square_rows(k, total):
        rows = pl.ds(al(k * 128, 128), 128)
        for ref in (s_ref, sp):
            v = ref[rows, :].astype(F32)
            v = v * v
            v = v[:, :128] + v[:, 128:]
            total = total + jnp.sum(v.reshape(16, 8, 128), axis=0)
        return total

    sq[0] = lax.fori_loop(0, M // 128, square_rows, jnp.zeros((8, 128), F32))

    def add_rows(dst_off, rows, srcs):
        step = 96 if rows % 96 == 0 else 16

        def body(k, carry):
            o = k * step
            total = t[pl.ds(al(dst_off + o), step), :].astype(F32)
            for src in srcs:
                total = total + src[pl.ds(al(o), step), :].astype(F32)
            t[pl.ds(al(dst_off + o), step), :] = total.astype(BF)
            return carry

        lax.fori_loop(0, rows // step, body, 0)

    base = [p * PART for p in range(3)]
    bases = [list(base)]
    for s in range(3):
        size, top, bot = SIZES[s], TOPS[s], BOTS[s]
        buf = recv_bufs[s]

        def quarter(p, by, s=s, size=size):
            return base[p] + ((pos[AXES[p][s]] + by) % 4) * size

        copies = {}

        def push(p, k, off, rows, s=s, buf=buf, copies=copies):
            a = AXES[p][s]
            c = remote(
                t.at[pl.ds(al(off), rows), :],
                buf.at[p, k, pl.ds(0, rows), :],
                rs_send.at[s, p, k],
                rs_recv.at[s, p, k],
                right[a] if k < 3 else left[a],
            )
            c.start()
            copies[p, k] = c
            sent.append(c)

        for p in range(3):
            push(p, 0, quarter(p, 2), top)
            push(p, 3, quarter(p, 2) + top, bot)
            push(p, 1, quarter(p, 1) + top, bot)
            push(p, 4, quarter(p, 3), top)
        sq_copies = [
            remote(sq.at[4 * s], sq.at[4 * s + 1 + k], sq_send.at[s, k], sq_recv.at[s, k], dev)
            for k, dev in enumerate((right[s], left[s]))
        ]
        for c in sq_copies:
            c.start()
        for p in range(3):
            copies[p, 0].wait_recv()
            add_rows(quarter(p, 1), top, [buf.at[p, 0]])
            push(p, 2, quarter(p, 1), top)
            copies[p, 3].wait_recv()
            add_rows(quarter(p, 3) + top, bot, [buf.at[p, 3]])
            push(p, 5, quarter(p, 3) + top, bot)
        sq_copies[0].wait_recv()
        c = remote(sq.at[4 * s + 1], sq.at[4 * s + 3], sq_send.at[s, 2], sq_recv.at[s, 2], right[s])
        c.start()
        sq_copies[1].wait_recv()
        sq_copies.append(c)
        for p in range(3):
            copies[p, 4].wait_recv()
            copies[p, 2].wait_recv()
            add_rows(quarter(p, 0), top, [buf.at[p, 4], buf.at[p, 2]])
            copies[p, 1].wait_recv()
            copies[p, 5].wait_recv()
            add_rows(quarter(p, 0) + top, bot, [buf.at[p, 1], buf.at[p, 5]])
        c.wait_recv()
        sq[4 * s + 4] = (sq[4 * s] + sq[4 * s + 3]) + (sq[4 * s + 1] + sq[4 * s + 2])
        sent.extend(sq_copies)
        base = [quarter(p, 0) for p in range(3)]
        bases.append(list(base))

    mine = core * CORE_ROWS
    for p in range(3):
        g[pl.ds(al(mine + base[p]), 144), :] = t[pl.ds(al(base[p]), 144), :]

    forwards = []

    def forward(p, k, off, rows):
        here = g.at[pl.ds(al(off), rows), :]
        c = remote(here, here, fw_send.at[p, k], fw_recv.at[p, k], partner)
        c.start()
        forwards.append(c)

    for s in (2, 1, 0):
        size, top, bot = SIZES[s], TOPS[s], BOTS[s]
        base = bases[s]
        last = s == 0

        def quarter(p, by, s=s, size=size, base=base):
            return mine + base[p] + ((pos[AXES[p][s]] + by) % 4) * size

        copies = {}

        def spread(p, k, off, rows, s=s, copies=copies):
            a = AXES[p][s]
            here = g.at[pl.ds(al(off), rows), :]
            c = remote(here, here, ag_send.at[s, p, k], ag_recv.at[s, p, k], right[a] if k % 2 == 0 else left[a])
            c.start()
            copies[p, k] = c
            sent.append(c)

        for p in range(3):
            spread(p, 0, quarter(p, 0), size)
            spread(p, 1, quarter(p, 0), size)
            if last:
                forward(p, 0, quarter(p, 0), size)
        for p in range(3):
            copies[p, 0].wait_recv()
            spread(p, 2, quarter(p, 3), top)
            copies[p, 1].wait_recv()
            spread(p, 3, quarter(p, 1) + top, bot)
            if last:
                forward(p, 1, quarter(p, 3), size)
                forward(p, 2, quarter(p, 1), size)
        for p in range(3):
            copies[p, 2].wait_recv()
            if last:
                forward(p, 3, quarter(p, 2), top)
            copies[p, 3].wait_recv()
            if last:
                forward(p, 4, quarter(p, 2) + top, bot)

    for c in forwards:
        c.wait_recv()

    factor = 0.3 * math.sqrt(M) / (jnp.sqrt(jnp.sum(sq[12], axis=(0, 1), keepdims=True)) + 1e-07)
    factor2 = factor * factor

    def band(a_ref, j):
        def cols(i):
            return a_ref[:, pl.ds(al(i * BLK, BLK), BLK)]

        def block(n):
            o = n * 512
            return jnp.concatenate(
                [g[pl.ds(al(o, 512), 256), :], g[pl.ds(al(o + 256, 256), 256), :]], axis=1
            )

        def straight(i, n):
            return jnp.dot(cols(i), block(n), preferred_element_type=F32)

        def turned(i, n):
            return lax.dot_general(cols(i), block(n), (((1,), (1,)), ((), ())), preferred_element_type=F32)

        acc = straight(j, j)
        for d in range(1, 7):
            i = (j + NB - d) % NB
            acc += straight(i, d * NB + i)
            acc += turned((j + d) % NB, d * NB + j)
        return acc, straight, turned

    def band_all(a_ref, finish):
        def lower(j, carry):
            acc, _, turned = band(a_ref, j)
            finish(j, acc + turned(j + 7, 7 * NB + j))
            return carry

        def upper(j, carry):
            acc, straight, _ = band(a_ref, j)
            finish(j, acc + straight(j - 7, 7 * NB + j - 7))
            return carry

        lax.fori_loop(0, 7, lower, 0)
        lax.fori_loop(7, NB, upper, 0)

    def first(j, acc):
        v = factor2 * acc
        at = pl.ds(al(j * BLK, BLK), BLK)
        yf[:, at] = v
        ybf[:, at] = v.astype(BF)

    def second(j, acc):
        at = pl.ds(al(j * BLK, BLK), BLK)
        scaled = (factor * st_ref[:, at].astype(F32)).astype(BF).astype(F32)
        product = factor * (COEFF_B * yf[:, at] + COEFF_C * (factor2 * acc))
        out_ref[:, at] = (math.sqrt(K) * (COEFF_A * scaled + product)).astype(BF)

    band_all(st_ref, first)
    band_all(ybf, second)

    for c in sent + forwards:
        c.wait_send()


def local(gradient):
    columns = lax.all_to_all(gradient, ("wide", "narrow"), split_axis=1, concat_axis=0, tiled=True)
    padded = jnp.pad(columns, ((0, 0), (0, PAD - COLS)))
    turned = columns.T
    vmem = pl.BlockSpec(memory_space=pltpu.VMEM)
    update = pl.pallas_call(
        kernel,
        out_shape=jax.ShapeDtypeStruct((COLS, M), BF),
        in_specs=[vmem, vmem],
        out_specs=vmem,
        scratch_shapes=[
            pltpu.VMEM((M, PAD), BF),
            pltpu.VMEM((CORE_ROWS, 128), BF),
            pltpu.VMEM((2 * CORE_ROWS, 128), BF),
            pltpu.VMEM((3, 6, 1152, 128), BF),
            pltpu.VMEM((3, 6, 288, 128), BF),
            pltpu.VMEM((3, 6, 80, 128), BF),
            pltpu.VMEM((13, 8, 128), F32),
            pltpu.VMEM((COLS, M), BF),
            pltpu.VMEM((COLS, M), F32),
            pltpu.SemaphoreType.DMA((2,)),
            pltpu.SemaphoreType.DMA((3, 3, 6)),
            pltpu.SemaphoreType.DMA((3, 3, 6)),
            pltpu.SemaphoreType.DMA((3, 3, 4)),
            pltpu.SemaphoreType.DMA((3, 3, 4)),
            pltpu.SemaphoreType.DMA((3, 5)),
            pltpu.SemaphoreType.DMA((3, 5)),
            pltpu.SemaphoreType.DMA((3, 3)),
            pltpu.SemaphoreType.DMA((3, 3)),
        ],
        compiler_params=pltpu.CompilerParams(
            collective_id=0, has_side_effects=True, vmem_limit_bytes=56 * 1024 * 1024
        ),
        cost_estimate=pl.CostEstimate(flops=16 * 10**9, bytes_accessed=5 * 10**6, transcendentals=0),
    )(padded, turned)
    return lax.all_to_all(update.T, ("wide", "narrow"), split_axis=0, concat_axis=1, tiled=True)


def solution(mesh):
    spec = P(("wide", "narrow"), None)
    return jax.shard_map(local, mesh=mesh, in_specs=(spec,), out_specs=spec, check_vma=False)
```

```python
import math

import jax
import jax.numpy as jnp
from jax import lax
from jax.experimental import pallas as pl
from jax.experimental.pallas import tpu as pltpu
from jax.sharding import PartitionSpec as P

M = 3584
K = 18432

COEFF_A = 3.4445
COEFF_B = -4.775
COEFF_C = 2.0315

MESH = pl.DeviceIdType.MESH
BF = jnp.bfloat16
F32 = jnp.float32
NT = (((1,), (1,)), ((), ()))

ROWS = 28
PIECE = 32
THIRD = K // 3
COL1 = THIRD // 4
COL2 = COL1 // 4
COL3 = COL2 // 4
HALF3 = COL3 // 2
OWN = 3 * HALF3
HALF_M = M // 2
AXES = ((0, 1, 2), (1, 2, 0), (2, 0, 1))

BLK = 256
NB = M // BLK
SLOTS = 54
PART = 9216
CORE_ROWS = 3 * PART
SIZES = (2304, 576, 144)
TOPS = (1152, 288, 80)
BOTS = (1152, 288, 64)


def al(x, m=16):
    return pl.multiple_of(x, m)


def kernel(
    in_ref, out_ref,
    x0, x1, x2, x2p, x3, s_all, st,
    ut, y3, y2p, y2, y1, y0,
    t, g, r1, r2, r3, sq, ybf, yf,
    in_send, in_recv, in_copy, core_send, core_recv, out_send, out_recv, out_copy, ut_send, ut_recv,
    rs_send, rs_recv, ag_send, ag_recv, fw_send, fw_recv, sq_send, sq_recv,
):
    recv_bufs = (r1, r2, r3)
    w, n_ = lax.axis_index("wide"), lax.axis_index("narrow")
    core, z_lo, y = w % 2, (w // 2) % 2, w // 4
    x, z_hi = n_ % 4, n_ // 4
    z = z_hi * 2 + z_lo
    pos = (x, y, z)

    def device(x, y, z, core):
        return ((y * 2 + z % 2) * 2 + core, (z // 2) * 4 + x)

    def shifted(axis, by):
        p = [x, y, z]
        p[axis] = (p[axis] + by) % 4
        return device(*p, core)

    right = [shifted(a, 1) for a in range(3)]
    left = [shifted(a, 3) for a in range(3)]
    across = [shifted(a, 2) for a in range(3)]
    partner = device(x, y, z, 1 - core)

    barrier = pltpu.get_barrier_semaphore()
    for d in right + left + across + [partner]:
        pl.semaphore_signal(barrier, inc=1, device_id=d, device_id_type=MESH)

    def load(k, total):
        cols = pl.ds(al(k * 512, 512), 512)
        v = in_ref[:, cols]
        x0[pl.ds(0, ROWS), cols] = v
        x0[pl.ds(ROWS, PIECE - ROWS), cols] = jnp.zeros((PIECE - ROWS, 512), BF)
        return total

    lax.fori_loop(0, K // 512, load, 0)
    pl.semaphore_wait(barrier, 10)

    def remote(src, dst, send, recv, dev):
        return pltpu.make_async_remote_copy(
            src_ref=src, dst_ref=dst, send_sem=send, recv_sem=recv, device_id=dev, device_id_type=MESH
        )

    sent = []

    def exchange(stage, axis_no, src, dst, send, recv, copy):
        arriving = []
        for p in range(3):
            a = AXES[p][axis_no]
            me = pos[a]
            group = []
            for k, dev in ((2, across[a]), (1, right[a]), (3, left[a])):
                c = remote(src(p, (me + k) % 4), dst(p, me), send.at[stage, p, k - 1], recv.at[stage, p, k - 1], dev)
                c.start()
                group.append(c)
                sent.append(c)
            own = pltpu.make_async_copy(src(p, me), dst(p, me), copy.at[stage, p])
            own.start()
            arriving.append((group, own))
        return arriving

    def arrive(item):
        group, own = item
        for c in group:
            c.wait_recv()
        own.wait()

    def lanes(k, size):
        return pl.ds(al(k * size, size), size)

    arriving = exchange(
        0, 0,
        lambda p, q: x0.at[:, pl.ds(al(p * THIRD + q * COL1, COL1), COL1)],
        lambda p, q: x1.at[p, q],
        in_send, in_recv, in_copy,
    )

    def square(k, total):
        v = x0[:, pl.ds(al(k * 512, 512), 512)].astype(F32)
        v = v * v
        v = (v[:, :128] + v[:, 128:256]) + (v[:, 256:384] + v[:, 384:])
        return total + ((v[:8] + v[8:16]) + (v[16:24] + v[24:]))

    sq[13] = lax.fori_loop(0, K // 512, square, jnp.zeros((8, 128), F32))
    sq_core = remote(sq.at[13], sq.at[14], sq_send.at[3, 0], sq_recv.at[3, 0], partner)
    sq_core.start()
    sent.append(sq_core)

    def iota(shape, d):
        return lax.broadcasted_iota(jnp.int32, shape, d)

    def ones_where(cond):
        return jnp.where(cond, 1.0, 0.0).astype(BF)

    def spread_matrix(shape, wide, unit, narrow):
        s, r = iota(shape, wide), iota(shape, 1 - wide)
        return ones_where((s % unit < narrow) & (r == (s // unit) * narrow + s % unit))

    for item in arriving:
        arrive(item)

    plane = lambda buf, p, q: buf.at[p, q] if p == 2 else buf.at[p, :, q]
    arriving = exchange(
        1, 1,
        lambda p, q: x1.at[p, :, :, lanes(q, COL2)],
        lambda p, q: plane(x2, p, q),
        in_send, in_recv, in_copy,
    )
    widen = spread_matrix((COL2, 512), 1, 128, COL3)
    for p in range(3):
        arrive(arriving[p])
        for h in range(2):
            rows = x2[p, pl.ds(2 * h, 2)].reshape(256, COL2)
            x2p[p, pl.ds(2 * h, 2)] = (
                jnp.dot(rows, widen, preferred_element_type=F32).astype(BF).reshape(2, 4, PIECE, 512)
            )

    def cube(buf, p, q, lane):
        if p == 0:
            return buf.at[:, :, q, :, lane]
        if p == 1:
            return buf.at[q, :, :, :, lane]
        return buf.at[:, q, :, :, lane]

    arriving = exchange(
        2, 2,
        lambda p, q: x2p.at[p, :, :, :, lanes(q, 128)],
        lambda p, q: cube(x3.at[core], p, q, pl.ds(128 * p, 128)),
        in_send, in_recv, in_copy,
    )
    crossing = []
    for p in range(3):
        arrive(arriving[p])
        here = x3.at[core, :, :, :, :, pl.ds(128 * p, 128)]
        c = remote(here, here, core_send.at[p], core_recv.at[p], partner)
        c.start()
        crossing.append(c)
        sent.append(c)

    pack = spread_matrix((8 * ROWS, 8 * PIECE), 1, PIECE, ROWS)

    def pack_rows(owner):
        def body(k, carry):
            rows = x3[owner, k // 2, pl.ds((k % 2) * 2, 2)].reshape(8 * PIECE, 384)
            at = pl.ds(al(owner * HALF_M + k * 8 * ROWS), 8 * ROWS)
            s_all[at, :] = jnp.dot(pack, rows, preferred_element_type=F32).astype(BF)
            return carry

        lax.fori_loop(0, 8, body, 0)

    pack_rows(core)
    for c in crossing:
        c.wait_recv()
    pack_rows(1 - core)

    kk, ll = iota((OWN, 384), 0), iota((OWN, 384), 1)
    lane = ll % 128 - core * HALF3
    pick = ones_where((lane >= 0) & (lane < HALF3) & (kk == (ll // 128) * HALF3 + lane))

    def turn(j, carry):
        at = pl.ds(al(j * BLK, BLK), BLK)
        st[:, at] = lax.dot_general(pick, s_all[at, :], NT, preferred_element_type=F32).astype(BF)
        return carry

    lax.fori_loop(0, NB, turn, 0)

    def gram_block(m, carry):
        n = core * SLOTS + m
        i, d = n % NB, n // NB
        j = (i + d) % NB
        ri = pl.ds(al(i * BLK, BLK), BLK)
        rj = pl.ds(al(j * BLK, BLK), BLK)
        acc = lax.dot_general(s_all[ri, :], s_all[rj, :], NT, preferred_element_type=F32).astype(BF)
        t[pl.ds(al(m * 512, 512), 256), :] = acc[:, :128]
        t[pl.ds(al(m * 512 + 256, 256), 256), :] = acc[:, 128:]
        return carry

    lax.fori_loop(0, SLOTS, gram_block, 0)

    sq_core.wait_recv()
    sq[0] = sq[13] + sq[14]

    def add_rows(dst_off, rows, srcs):
        step = 288 if rows % 288 == 0 else 16

        def body(k, carry):
            o = k * step
            total = t[pl.ds(al(dst_off + o), step), :].astype(F32)
            for src in srcs:
                total = total + src[pl.ds(al(o), step), :].astype(F32)
            t[pl.ds(al(dst_off + o), step), :] = total.astype(BF)
            return carry

        lax.fori_loop(0, rows // step, body, 0)

    base = [p * PART for p in range(3)]
    bases = [list(base)]
    for s in range(3):
        size, top, bot = SIZES[s], TOPS[s], BOTS[s]
        buf = recv_bufs[s]

        def quarter(p, by, s=s, size=size):
            return base[p] + ((pos[AXES[p][s]] + by) % 4) * size

        copies = {}

        def push(p, k, off, rows, s=s, buf=buf, copies=copies):
            a = AXES[p][s]
            c = remote(
                t.at[pl.ds(al(off), rows), :],
                buf.at[p, k, pl.ds(0, rows), :],
                rs_send.at[s, p, k],
                rs_recv.at[s, p, k],
                right[a] if k < 3 else left[a],
            )
            c.start()
            copies[p, k] = c
            sent.append(c)

        for p in range(3):
            push(p, 0, quarter(p, 2), top)
            push(p, 3, quarter(p, 2) + top, bot)
            push(p, 1, quarter(p, 1) + top, bot)
            push(p, 4, quarter(p, 3), top)
        sq_copies = [
            remote(sq.at[4 * s], sq.at[4 * s + 1 + k], sq_send.at[s, k], sq_recv.at[s, k], dev)
            for k, dev in enumerate((right[s], left[s]))
        ]
        for c in sq_copies:
            c.start()
        for p in range(3):
            copies[p, 0].wait_recv()
            add_rows(quarter(p, 1), top, [buf.at[p, 0]])
            push(p, 2, quarter(p, 1), top)
            copies[p, 3].wait_recv()
            add_rows(quarter(p, 3) + top, bot, [buf.at[p, 3]])
            push(p, 5, quarter(p, 3) + top, bot)
        sq_copies[0].wait_recv()
        c = remote(sq.at[4 * s + 1], sq.at[4 * s + 3], sq_send.at[s, 2], sq_recv.at[s, 2], right[s])
        c.start()
        sq_copies[1].wait_recv()
        sq_copies.append(c)
        for p in range(3):
            copies[p, 4].wait_recv()
            copies[p, 2].wait_recv()
            add_rows(quarter(p, 0), top, [buf.at[p, 4], buf.at[p, 2]])
            copies[p, 1].wait_recv()
            copies[p, 5].wait_recv()
            add_rows(quarter(p, 0) + top, bot, [buf.at[p, 1], buf.at[p, 5]])
        c.wait_recv()
        sq[4 * s + 4] = (sq[4 * s] + sq[4 * s + 3]) + (sq[4 * s + 1] + sq[4 * s + 2])
        sent.extend(sq_copies)
        base = [quarter(p, 0) for p in range(3)]
        bases.append(list(base))

    mine = core * CORE_ROWS
    for p in range(3):
        g[pl.ds(al(mine + base[p]), 144), :] = t[pl.ds(al(base[p]), 144), :]

    forwards = []

    def forward(p, k, off, rows):
        here = g.at[pl.ds(al(off), rows), :]
        c = remote(here, here, fw_send.at[p, k], fw_recv.at[p, k], partner)
        c.start()
        forwards.append(c)

    for s in (2, 1, 0):
        size, top, bot = SIZES[s], TOPS[s], BOTS[s]
        base = bases[s]
        last = s == 0

        def quarter(p, by, s=s, size=size, base=base):
            return mine + base[p] + ((pos[AXES[p][s]] + by) % 4) * size

        copies = {}

        def spread(p, k, off, rows, s=s, copies=copies):
            a = AXES[p][s]
            here = g.at[pl.ds(al(off), rows), :]
            c = remote(here, here, ag_send.at[s, p, k], ag_recv.at[s, p, k], right[a] if k % 2 == 0 else left[a])
            c.start()
            copies[p, k] = c
            sent.append(c)

        for p in range(3):
            spread(p, 0, quarter(p, 0), size)
            spread(p, 1, quarter(p, 0), size)
            if last:
                forward(p, 0, quarter(p, 0), size)
        for p in range(3):
            copies[p, 0].wait_recv()
            spread(p, 2, quarter(p, 3), top)
            copies[p, 1].wait_recv()
            spread(p, 3, quarter(p, 1) + top, bot)
            if last:
                forward(p, 1, quarter(p, 3), size)
                forward(p, 2, quarter(p, 1), size)
        for p in range(3):
            copies[p, 2].wait_recv()
            if last:
                forward(p, 3, quarter(p, 2), top)
            copies[p, 3].wait_recv()
            if last:
                forward(p, 4, quarter(p, 2) + top, bot)

    for c in forwards:
        c.wait_recv()

    factor = 0.3 * math.sqrt(M) / (jnp.sqrt(jnp.sum(sq[12], axis=(0, 1), keepdims=True)) + 1e-07)
    factor2 = factor * factor

    def band(a_ref, j):
        def cols(i):
            return a_ref[:, pl.ds(al(i * BLK, BLK), BLK)]

        def block(n):
            o = n * 512
            return jnp.concatenate(
                [g[pl.ds(al(o, 512), 256), :], g[pl.ds(al(o + 256, 256), 256), :]], axis=1
            )

        def straight(i, n):
            return jnp.dot(cols(i), block(n), preferred_element_type=F32)

        def turned(i, n):
            return lax.dot_general(cols(i), block(n), NT, preferred_element_type=F32)

        acc = straight(j, j)
        for d in range(1, 7):
            i = (j + NB - d) % NB
            acc += straight(i, d * NB + i)
            acc += turned((j + d) % NB, d * NB + j)
        return acc, straight, turned

    def band_all(a_ref, finish):
        def lower(j, carry):
            acc, _, turned = band(a_ref, j)
            finish(j, acc + turned(j + 7, 7 * NB + j))
            return carry

        def upper(j, carry):
            acc, straight, _ = band(a_ref, j)
            finish(j, acc + straight(j - 7, 7 * NB + j - 7))
            return carry

        lax.fori_loop(0, 7, lower, 0)
        lax.fori_loop(7, NB, upper, 0)

    def first(j, acc):
        v = factor2 * acc
        at = pl.ds(al(j * BLK, BLK), BLK)
        yf[:, at] = v
        ybf[:, at] = v.astype(BF)

    def second(j, acc):
        at = pl.ds(al(j * BLK, BLK), BLK)
        scaled = (factor * st[:, at].astype(F32)).astype(BF).astype(F32)
        product = factor * (COEFF_B * yf[:, at] + COEFF_C * (factor2 * acc))
        u = (math.sqrt(K) * (COEFF_A * scaled + product)).astype(BF)
        for p in range(3):
            ut[pl.ds(al(p * 128 + core * HALF3), HALF3), at] = u[p * HALF3 : (p + 1) * HALF3]

    band_all(st, first)
    for p in range(3):
        ut[pl.ds(p * 128 + COL3, 128 - COL3), :] = jnp.zeros((128 - COL3, M), BF)
    band_all(ybf, second)

    halves = []
    for p in range(3):
        here = ut.at[pl.ds(al(p * 128 + core * HALF3), HALF3), lanes(1 - core, HALF_M)]
        c = remote(here, here, ut_send.at[p], ut_recv.at[p], partner)
        c.start()
        halves.append(c)
        sent.append(c)
    unpack = spread_matrix((8 * PIECE, 8 * ROWS), 0, PIECE, ROWS)
    for c in halves:
        c.wait_recv()
    for m in range(8):
        o = m * 8 * ROWS
        first_lane = o // 128 * 128
        skip = o - first_lane
        width = -(-(skip + 8 * ROWS) // 128) * 128
        v = ut[:, pl.ds(al(core * HALF_M + first_lane, 128), width)][:, skip : skip + 8 * ROWS]
        rows = lax.dot_general(unpack, v, NT, preferred_element_type=F32).astype(BF)
        y3[m // 2, pl.ds((m % 2) * 2, 2)] = rows.reshape(2, 4, PIECE, 384)

    arriving = exchange(
        0, 2,
        lambda p, q: cube(y3, p, q, pl.ds(128 * p, 128)),
        lambda p, q: y2p.at[p, :, :, :, lanes(q, 128)],
        out_send, out_recv, out_copy,
    )
    narrow = spread_matrix((512, COL2), 0, 128, COL3)
    for p in range(3):
        arrive(arriving[p])
        for h in range(2):
            rows = y2p[p, pl.ds(2 * h, 2)].reshape(256, 512)
            y2[p, pl.ds(2 * h, 2)] = (
                jnp.dot(rows, narrow, preferred_element_type=F32).astype(BF).reshape(2, 4, PIECE, COL2)
            )
    arriving = exchange(
        1, 1,
        lambda p, q: plane(y2, p, q),
        lambda p, q: y1.at[p, :, :, lanes(q, COL2)],
        out_send, out_recv, out_copy,
    )
    for item in arriving:
        arrive(item)
    arriving = exchange(
        2, 0,
        lambda p, q: y1.at[p, q],
        lambda p, q: y0.at[:, pl.ds(al(p * THIRD + q * COL1, COL1), COL1)],
        out_send, out_recv, out_copy,
    )
    for p in range(3):
        arrive(arriving[p])

        def store(k, carry, p=p):
            cols = pl.ds(al(p * THIRD + k * 512, 512), 512)
            out_ref[:, cols] = y0[pl.ds(0, PIECE), cols][:ROWS]
            return carry

        lax.fori_loop(0, THIRD // 512, store, 0)

    for c in sent + forwards:
        c.wait_send()


def local(gradient):
    vmem = pl.BlockSpec(memory_space=pltpu.VMEM)
    dma = pltpu.SemaphoreType.DMA
    return pl.pallas_call(
        kernel,
        out_shape=jax.ShapeDtypeStruct((ROWS, K), BF),
        in_specs=[vmem],
        out_specs=vmem,
        scratch_shapes=[
            pltpu.VMEM((PIECE, K), BF),
            pltpu.VMEM((3, 4, PIECE, COL1), BF),
            pltpu.VMEM((3, 4, 4, PIECE, COL2), BF),
            pltpu.VMEM((3, 4, 4, PIECE, 512), BF),
            pltpu.VMEM((2, 4, 4, 4, PIECE, 384), BF),
            pltpu.VMEM((M, 384), BF),
            pltpu.VMEM((OWN, M), BF),
            pltpu.VMEM((384, M), BF),
            pltpu.VMEM((4, 4, 4, PIECE, 384), BF),
            pltpu.VMEM((3, 4, 4, PIECE, 512), BF),
            pltpu.VMEM((3, 4, 4, PIECE, COL2), BF),
            pltpu.VMEM((3, 4, PIECE, COL1), BF),
            pltpu.VMEM((PIECE, K), BF),
            pltpu.VMEM((CORE_ROWS, 128), BF),
            pltpu.VMEM((2 * CORE_ROWS, 128), BF),
            pltpu.VMEM((3, 6, 1152, 128), BF),
            pltpu.VMEM((3, 6, 288, 128), BF),
            pltpu.VMEM((3, 6, 80, 128), BF),
            pltpu.VMEM((15, 8, 128), F32),
            pltpu.VMEM((OWN, M), BF),
            pltpu.VMEM((OWN, M), F32),
            dma((3, 3, 3)),
            dma((3, 3, 3)),
            dma((3, 3)),
            dma((3,)),
            dma((3,)),
            dma((3, 3, 3)),
            dma((3, 3, 3)),
            dma((3, 3)),
            dma((3,)),
            dma((3,)),
            dma((3, 3, 6)),
            dma((3, 3, 6)),
            dma((3, 3, 4)),
            dma((3, 3, 4)),
            dma((3, 5)),
            dma((3, 5)),
            dma((4, 3)),
            dma((4, 3)),
        ],
        compiler_params=pltpu.CompilerParams(
            collective_id=0, has_side_effects=True, vmem_limit_bytes=60 * 1024 * 1024
        ),
        cost_estimate=pl.CostEstimate(flops=16 * 10**9, bytes_accessed=5 * 10**6, transcendentals=0),
    )(gradient)


def solution(mesh):
    spec = P(("wide", "narrow"), None)
    return jax.shard_map(local, mesh=mesh, in_specs=(spec,), out_specs=spec, check_vma=False)
```

```python
import math

import jax
import jax.numpy as jnp
from jax import lax
from jax.experimental import pallas as pl
from jax.experimental.pallas import tpu as pltpu
from jax.sharding import PartitionSpec as P

M = 3584
K = 18432

COEFF_A = 3.4445
COEFF_B = -4.775
COEFF_C = 2.0315

MESH = pl.DeviceIdType.MESH
BF = jnp.bfloat16
F32 = jnp.float32
NT = (((1,), (1,)), ((), ()))

ROWS = 28
PIECE = 32
THIRD = K // 3
COL1 = THIRD // 4
COL2 = COL1 // 4
COL3 = COL2 // 4
HALF3 = COL3 // 2
OWN = 3 * HALF3
HALF_M = M // 2
AXES = ((0, 1, 2), (1, 2, 0), (2, 0, 1))

BLK = 256
NB = M // BLK
SLOTS = 54
PART = 9216
CORE_ROWS = 3 * PART
SIZES = (2304, 576, 144)
TOPS = (1152, 288, 80)
BOTS = (1152, 288, 64)


def al(x, m=16):
    return pl.multiple_of(x, m)


def kernel(
    in_ref, out_ref,
    x0, x1, x2, x2p, x3, s_all, st,
    ut, y3, y2p, y2, y1,
    h1, h2, h3, k1, k2, k3,
    t, g, r1, r2, r3, sq, ybf, yf,
    in_send, in_recv, in_copy, core_send, core_recv, out_send, out_recv, out_copy, ut_send, ut_recv,
    rs_send, rs_recv, ag_send, ag_recv, fw_send, fw_recv, sq_send, sq_recv,
):
    recv_bufs = (r1, r2, r3)
    w, n_ = lax.axis_index("wide"), lax.axis_index("narrow")
    core, z_lo, y = w % 2, (w // 2) % 2, w // 4
    x, z_hi = n_ % 4, n_ // 4
    z = z_hi * 2 + z_lo
    pos = (x, y, z)

    def device(x, y, z, core):
        return ((y * 2 + z % 2) * 2 + core, (z // 2) * 4 + x)

    def shifted(axis, by):
        p = [x, y, z]
        p[axis] = (p[axis] + by) % 4
        return device(*p, core)

    right = [shifted(a, 1) for a in range(3)]
    left = [shifted(a, 3) for a in range(3)]
    partner = device(x, y, z, 1 - core)

    barrier = pltpu.get_barrier_semaphore()
    for d in right + left + [partner]:
        pl.semaphore_signal(barrier, inc=1, device_id=d, device_id_type=MESH)

    def load(k, total):
        cols = pl.ds(al(k * 512, 512), 512)
        v = in_ref[:, cols]
        x0[pl.ds(0, ROWS), cols] = v
        x0[pl.ds(ROWS, PIECE - ROWS), cols] = jnp.zeros((PIECE - ROWS, 512), BF)
        return total

    lax.fori_loop(0, K // 512, load, 0)
    pl.semaphore_wait(barrier, 7)

    def remote(src, dst, send, recv, dev):
        return pltpu.make_async_remote_copy(
            src_ref=src, dst_ref=dst, send_sem=send, recv_sem=recv, device_id=dev, device_id_type=MESH
        )

    sent = []

    class Exchange:
        def __init__(self, stage, axis_no, src, dst, hop, sems):
            self.stage, self.axis_no, self.src, self.dst, self.hop, self.sems = stage, axis_no, src, dst, hop, sems
            self.copies = {}

        def push(self, p, k, src, dst, dev):
            send, recv, _ = self.sems
            c = remote(src, dst, send.at[self.stage, p, k], recv.at[self.stage, p, k], dev)
            c.start()
            self.copies[p, k] = c
            sent.append(c)

        def begin(self, p):
            a = AXES[p][self.axis_no]
            me = pos[a]
            self.push(p, 0, self.src(p, (me + 2) % 4, 0), self.hop.at[p, 0], right[a])
            self.push(p, 1, self.src(p, (me + 2) % 4, 1), self.hop.at[p, 1], left[a])
            self.push(p, 2, self.src(p, (me + 1) % 4, None), self.dst(p, me, None), right[a])
            self.push(p, 3, self.src(p, (me + 3) % 4, None), self.dst(p, me, None), left[a])
            own = pltpu.make_async_copy(self.src(p, me, None), self.dst(p, me, None), self.sems[2].at[self.stage, p])
            own.start()
            self.copies[p, "own"] = own

        def hand_on(self, p):
            a = AXES[p][self.axis_no]
            me = pos[a]
            self.copies[p, 0].wait_recv()
            self.push(p, 4, self.hop.at[p, 0], self.dst(p, (me + 3) % 4, 0), right[a])
            self.copies[p, 1].wait_recv()
            self.push(p, 5, self.hop.at[p, 1], self.dst(p, (me + 1) % 4, 1), left[a])

        def arrive(self, p):
            for k in (2, 3, 4, 5):
                self.copies[p, k].wait_recv()
            self.copies[p, "own"].wait()

    def seg(h, size):
        return pl.ds(0, size) if h is None else pl.ds(h * (size // 2), size // 2)

    def tall(p, q, h):
        o = p * THIRD + q * COL1
        return pl.ds(al(o, 128), COL1) if h is None else pl.ds(al(o + h * (COL1 // 2), 128), COL1 // 2)

    def lanes(k, size):
        return pl.ds(al(k * size, size), size)

    ins = (in_send, in_recv, in_copy)
    outs = (out_send, out_recv, out_copy)

    def plane(buf, p, q, h):
        return buf.at[p, q, seg(h, 4)] if p == 2 else buf.at[p, seg(h, 4), q]

    def cube(buf, p, q, h):
        lane = pl.ds(128 * p, 128)
        if p == 0:
            return buf.at[seg(h, 4), :, q, :, lane]
        if p == 1:
            return buf.at[q, seg(h, 4), :, :, lane]
        return buf.at[seg(h, 4), q, :, :, lane]

    in1 = Exchange(
        0, 0, lambda p, q, h: x0.at[:, tall(p, q, h)], lambda p, q, h: x1.at[p, q, :, seg(h, COL1)], h1, ins
    )
    in2 = Exchange(
        1, 1, lambda p, q, h: x1.at[p, seg(h, 4), :, lanes(q, COL2)], lambda p, q, h: plane(x2, p, q, h), h2, ins
    )
    in3 = Exchange(
        2, 2, lambda p, q, h: x2p.at[p, seg(h, 4), :, :, lanes(q, 128)],
        lambda p, q, h: cube(x3.at[core], p, q, h), h3, ins,
    )
    for p in range(3):
        in1.begin(p)

    def square(k, total):
        v = x0[:, pl.ds(al(k * 512, 512), 512)].astype(F32)
        v = v * v
        v = (v[:, :128] + v[:, 128:256]) + (v[:, 256:384] + v[:, 384:])
        return total + ((v[:8] + v[8:16]) + (v[16:24] + v[24:]))

    sq[13] = lax.fori_loop(0, K // 512, square, jnp.zeros((8, 128), F32))
    sq_core = remote(sq.at[13], sq.at[14], sq_send.at[3, 0], sq_recv.at[3, 0], partner)
    sq_core.start()
    sent.append(sq_core)

    def iota(shape, d):
        return lax.broadcasted_iota(jnp.int32, shape, d)

    def ones_where(cond):
        return jnp.where(cond, 1.0, 0.0).astype(BF)

    def spread_matrix(shape, wide, unit, narrow):
        s, r = iota(shape, wide), iota(shape, 1 - wide)
        return ones_where((s % unit < narrow) & (r == (s // unit) * narrow + s % unit))

    for p in range(3):
        in1.hand_on(p)
    for p in range(3):
        in1.arrive(p)
        in2.begin(p)
    for p in range(3):
        in2.hand_on(p)
    widen = spread_matrix((COL2, 512), 1, 128, COL3)
    for p in range(3):
        in2.arrive(p)
        for h in range(2):
            rows = x2[p, pl.ds(2 * h, 2)].reshape(256, COL2)
            x2p[p, pl.ds(2 * h, 2)] = (
                jnp.dot(rows, widen, preferred_element_type=F32).astype(BF).reshape(2, 4, PIECE, 512)
            )
        in3.begin(p)
    for p in range(3):
        in3.hand_on(p)
    crossing = []
    for p in range(3):
        in3.arrive(p)
        here = x3.at[core, :, :, :, :, pl.ds(128 * p, 128)]
        c = remote(here, here, core_send.at[p], core_recv.at[p], partner)
        c.start()
        crossing.append(c)
        sent.append(c)

    pack = spread_matrix((8 * ROWS, 8 * PIECE), 1, PIECE, ROWS)

    def pack_rows(owner):
        def body(k, carry):
            rows = x3[owner, k // 2, pl.ds((k % 2) * 2, 2)].reshape(8 * PIECE, 384)
            at = pl.ds(al(owner * HALF_M + k * 8 * ROWS), 8 * ROWS)
            s_all[at, :] = jnp.dot(pack, rows, preferred_element_type=F32).astype(BF)
            return carry

        lax.fori_loop(0, 8, body, 0)

    pack_rows(core)
    for c in crossing:
        c.wait_recv()
    pack_rows(1 - core)

    kk, ll = iota((OWN, 384), 0), iota((OWN, 384), 1)
    lane = ll % 128 - core * HALF3
    pick = ones_where((lane >= 0) & (lane < HALF3) & (kk == (ll // 128) * HALF3 + lane))

    def turn(j, carry):
        at = pl.ds(al(j * BLK, BLK), BLK)
        st[:, at] = lax.dot_general(pick, s_all[at, :], NT, preferred_element_type=F32).astype(BF)
        return carry

    lax.fori_loop(0, NB, turn, 0)

    def gram_block(m, carry):
        n = core * SLOTS + m
        i, d = n % NB, n // NB
        j = (i + d) % NB
        ri = pl.ds(al(i * BLK, BLK), BLK)
        rj = pl.ds(al(j * BLK, BLK), BLK)
        acc = lax.dot_general(s_all[ri, :], s_all[rj, :], NT, preferred_element_type=F32).astype(BF)
        t[pl.ds(al(m * 512, 512), 256), :] = acc[:, :128]
        t[pl.ds(al(m * 512 + 256, 256), 256), :] = acc[:, 128:]
        return carry

    lax.fori_loop(0, SLOTS, gram_block, 0)

    sq_core.wait_recv()
    sq[0] = sq[13] + sq[14]

    def add_rows(dst_off, rows, srcs):
        step = 288 if rows % 288 == 0 else 16

        def body(k, carry):
            o = k * step
            total = t[pl.ds(al(dst_off + o), step), :].astype(F32)
            for src in srcs:
                total = total + src[pl.ds(al(o), step), :].astype(F32)
            t[pl.ds(al(dst_off + o), step), :] = total.astype(BF)
            return carry

        lax.fori_loop(0, rows // step, body, 0)

    base = [p * PART for p in range(3)]
    bases = [list(base)]
    for s in range(3):
        size, top, bot = SIZES[s], TOPS[s], BOTS[s]
        buf = recv_bufs[s]

        def quarter(p, by, s=s, size=size):
            return base[p] + ((pos[AXES[p][s]] + by) % 4) * size

        copies = {}

        def push(p, k, off, rows, s=s, buf=buf, copies=copies):
            a = AXES[p][s]
            c = remote(
                t.at[pl.ds(al(off), rows), :],
                buf.at[p, k, pl.ds(0, rows), :],
                rs_send.at[s, p, k],
                rs_recv.at[s, p, k],
                right[a] if k < 3 else left[a],
            )
            c.start()
            copies[p, k] = c
            sent.append(c)

        for p in range(3):
            push(p, 0, quarter(p, 2), top)
            push(p, 3, quarter(p, 2) + top, bot)
            push(p, 1, quarter(p, 1) + top, bot)
            push(p, 4, quarter(p, 3), top)
        sq_copies = [
            remote(sq.at[4 * s], sq.at[4 * s + 1 + k], sq_send.at[s, k], sq_recv.at[s, k], dev)
            for k, dev in enumerate((right[s], left[s]))
        ]
        for c in sq_copies:
            c.start()
        for p in range(3):
            copies[p, 0].wait_recv()
            add_rows(quarter(p, 1), top, [buf.at[p, 0]])
            push(p, 2, quarter(p, 1), top)
            copies[p, 3].wait_recv()
            add_rows(quarter(p, 3) + top, bot, [buf.at[p, 3]])
            push(p, 5, quarter(p, 3) + top, bot)
        sq_copies[0].wait_recv()
        c = remote(sq.at[4 * s + 1], sq.at[4 * s + 3], sq_send.at[s, 2], sq_recv.at[s, 2], right[s])
        c.start()
        sq_copies[1].wait_recv()
        sq_copies.append(c)
        for p in range(3):
            copies[p, 4].wait_recv()
            copies[p, 2].wait_recv()
            add_rows(quarter(p, 0), top, [buf.at[p, 4], buf.at[p, 2]])
            copies[p, 1].wait_recv()
            copies[p, 5].wait_recv()
            add_rows(quarter(p, 0) + top, bot, [buf.at[p, 1], buf.at[p, 5]])
        c.wait_recv()
        sq[4 * s + 4] = (sq[4 * s] + sq[4 * s + 3]) + (sq[4 * s + 1] + sq[4 * s + 2])
        sent.extend(sq_copies)
        base = [quarter(p, 0) for p in range(3)]
        bases.append(list(base))

    mine = core * CORE_ROWS
    for p in range(3):
        g[pl.ds(al(mine + base[p]), 144), :] = t[pl.ds(al(base[p]), 144), :]

    forwards = []

    def forward(p, k, off, rows):
        here = g.at[pl.ds(al(off), rows), :]
        c = remote(here, here, fw_send.at[p, k], fw_recv.at[p, k], partner)
        c.start()
        forwards.append(c)

    for s in (2, 1, 0):
        size, top, bot = SIZES[s], TOPS[s], BOTS[s]
        base = bases[s]
        last = s == 0

        def quarter(p, by, s=s, size=size, base=base):
            return mine + base[p] + ((pos[AXES[p][s]] + by) % 4) * size

        copies = {}

        def spread(p, k, off, rows, s=s, copies=copies):
            a = AXES[p][s]
            here = g.at[pl.ds(al(off), rows), :]
            c = remote(here, here, ag_send.at[s, p, k], ag_recv.at[s, p, k], right[a] if k % 2 == 0 else left[a])
            c.start()
            copies[p, k] = c
            sent.append(c)

        for p in range(3):
            spread(p, 0, quarter(p, 0), size)
            spread(p, 1, quarter(p, 0), size)
            if last:
                forward(p, 0, quarter(p, 0), size)
        for p in range(3):
            copies[p, 0].wait_recv()
            spread(p, 2, quarter(p, 3), top)
            copies[p, 1].wait_recv()
            spread(p, 3, quarter(p, 1) + top, bot)
            if last:
                forward(p, 1, quarter(p, 3), size)
                forward(p, 2, quarter(p, 1), size)
        for p in range(3):
            copies[p, 2].wait_recv()
            if last:
                forward(p, 3, quarter(p, 2), top)
            copies[p, 3].wait_recv()
            if last:
                forward(p, 4, quarter(p, 2) + top, bot)

    for c in forwards:
        c.wait_recv()

    factor = 0.3 * math.sqrt(M) / (jnp.sqrt(jnp.sum(sq[12], axis=(0, 1), keepdims=True)) + 1e-07)
    factor2 = factor * factor

    def band(a_ref, j):
        def cols(i):
            return a_ref[:, pl.ds(al(i * BLK, BLK), BLK)]

        def block(n):
            o = n * 512
            return jnp.concatenate(
                [g[pl.ds(al(o, 512), 256), :], g[pl.ds(al(o + 256, 256), 256), :]], axis=1
            )

        def straight(i, n):
            return jnp.dot(cols(i), block(n), preferred_element_type=F32)

        def turned(i, n):
            return lax.dot_general(cols(i), block(n), NT, preferred_element_type=F32)

        acc = straight(j, j)
        for d in range(1, 7):
            i = (j + NB - d) % NB
            acc += straight(i, d * NB + i)
            acc += turned((j + d) % NB, d * NB + j)
        return acc, straight, turned

    def band_all(a_ref, finish):
        def lower(j, carry):
            acc, _, turned = band(a_ref, j)
            finish(j, acc + turned(j + 7, 7 * NB + j))
            return carry

        def upper(j, carry):
            acc, straight, _ = band(a_ref, j)
            finish(j, acc + straight(j - 7, 7 * NB + j - 7))
            return carry

        lax.fori_loop(0, 7, lower, 0)
        lax.fori_loop(7, NB, upper, 0)

    def first(j, acc):
        v = factor2 * acc
        at = pl.ds(al(j * BLK, BLK), BLK)
        yf[:, at] = v
        ybf[:, at] = v.astype(BF)

    def second(j, acc):
        at = pl.ds(al(j * BLK, BLK), BLK)
        scaled = (factor * st[:, at].astype(F32)).astype(BF).astype(F32)
        product = factor * (COEFF_B * yf[:, at] + COEFF_C * (factor2 * acc))
        u = (math.sqrt(K) * (COEFF_A * scaled + product)).astype(BF)
        for p in range(3):
            ut[pl.ds(al(p * 128 + core * HALF3), HALF3), at] = u[p * HALF3 : (p + 1) * HALF3]

    band_all(st, first)
    for p in range(3):
        ut[pl.ds(p * 128 + COL3, 128 - COL3), :] = jnp.zeros((128 - COL3, M), BF)
    band_all(ybf, second)

    halves = []
    for p in range(3):
        here = ut.at[pl.ds(al(p * 128 + core * HALF3), HALF3), lanes(1 - core, HALF_M)]
        c = remote(here, here, ut_send.at[p], ut_recv.at[p], partner)
        c.start()
        halves.append(c)
        sent.append(c)
    unpack = spread_matrix((8 * PIECE, 8 * ROWS), 0, PIECE, ROWS)
    for c in halves:
        c.wait_recv()
    for m in range(8):
        o = m * 8 * ROWS
        first_lane = o // 128 * 128
        skip = o - first_lane
        width = -(-(skip + 8 * ROWS) // 128) * 128
        v = ut[:, pl.ds(al(core * HALF_M + first_lane, 128), width)][:, skip : skip + 8 * ROWS]
        rows = lax.dot_general(unpack, v, NT, preferred_element_type=F32).astype(BF)
        y3[m // 2, pl.ds((m % 2) * 2, 2)] = rows.reshape(2, 4, PIECE, 384)

    out1 = Exchange(
        0, 2, lambda p, q, h: cube(y3, p, q, h), lambda p, q, h: y2p.at[p, seg(h, 4), :, :, lanes(q, 128)], k1, outs
    )
    out2 = Exchange(
        1, 1, lambda p, q, h: plane(y2, p, q, h), lambda p, q, h: y1.at[p, seg(h, 4), :, lanes(q, COL2)], k2, outs
    )
    out3 = Exchange(
        2, 0, lambda p, q, h: y1.at[p, q, :, seg(h, COL1)], lambda p, q, h: out_ref.at[:, tall(p, q, h)], k3, outs
    )
    for p in range(3):
        out1.begin(p)
    for p in range(3):
        out1.hand_on(p)
    narrow = spread_matrix((512, COL2), 0, 128, COL3)
    for p in range(3):
        out1.arrive(p)
        for h in range(2):
            rows = y2p[p, pl.ds(2 * h, 2)].reshape(256, 512)
            y2[p, pl.ds(2 * h, 2)] = (
                jnp.dot(rows, narrow, preferred_element_type=F32).astype(BF).reshape(2, 4, PIECE, COL2)
            )
        out2.begin(p)
    for p in range(3):
        out2.hand_on(p)
    for p in range(3):
        out2.arrive(p)
        out3.begin(p)
    for p in range(3):
        out3.hand_on(p)
    for p in range(3):
        out3.arrive(p)

    for c in sent + forwards:
        c.wait_send()


def local(gradient):
    vmem = pl.BlockSpec(memory_space=pltpu.VMEM)
    dma = pltpu.SemaphoreType.DMA
    padded = pl.pallas_call(
        kernel,
        out_shape=jax.ShapeDtypeStruct((PIECE, K), BF),
        in_specs=[vmem],
        out_specs=vmem,
        scratch_shapes=[
            pltpu.VMEM((PIECE, K), BF),
            pltpu.VMEM((3, 4, PIECE, COL1), BF),
            pltpu.VMEM((3, 4, 4, PIECE, COL2), BF),
            pltpu.VMEM((3, 4, 4, PIECE, 512), BF),
            pltpu.VMEM((2, 4, 4, 4, PIECE, 384), BF),
            pltpu.VMEM((M, 384), BF),
            pltpu.VMEM((OWN, M), BF),
            pltpu.VMEM((384, M), BF),
            pltpu.VMEM((4, 4, 4, PIECE, 384), BF),
            pltpu.VMEM((3, 4, 4, PIECE, 512), BF),
            pltpu.VMEM((3, 4, 4, PIECE, COL2), BF),
            pltpu.VMEM((3, 4, PIECE, COL1), BF),
            pltpu.VMEM((3, 2, PIECE, COL1 // 2), BF),
            pltpu.VMEM((3, 2, 2, PIECE, COL2), BF),
            pltpu.VMEM((3, 2, 2, 4, PIECE, 128), BF),
            pltpu.VMEM((3, 2, 2, 4, PIECE, 128), BF),
            pltpu.VMEM((3, 2, 2, PIECE, COL2), BF),
            pltpu.VMEM((3, 2, PIECE, COL1 // 2), BF),
            pltpu.VMEM((CORE_ROWS, 128), BF),
            pltpu.VMEM((2 * CORE_ROWS, 128), BF),
            pltpu.VMEM((3, 6, 1152, 128), BF),
            pltpu.VMEM((3, 6, 288, 128), BF),
            pltpu.VMEM((3, 6, 80, 128), BF),
            pltpu.VMEM((15, 8, 128), F32),
            pltpu.VMEM((OWN, M), BF),
            pltpu.VMEM((OWN, M), F32),
            dma((3, 3, 6)),
            dma((3, 3, 6)),
            dma((3, 3)),
            dma((3,)),
            dma((3,)),
            dma((3, 3, 6)),
            dma((3, 3, 6)),
            dma((3, 3)),
            dma((3,)),
            dma((3,)),
            dma((3, 3, 6)),
            dma((3, 3, 6)),
            dma((3, 3, 4)),
            dma((3, 3, 4)),
            dma((3, 5)),
            dma((3, 5)),
            dma((4, 3)),
            dma((4, 3)),
        ],
        compiler_params=pltpu.CompilerParams(
            collective_id=0, has_side_effects=True, vmem_limit_bytes=60 * 1024 * 1024
        ),
        cost_estimate=pl.CostEstimate(flops=16 * 10**9, bytes_accessed=5 * 10**6, transcendentals=0),
    )(gradient)
    return padded[:ROWS]


def solution(mesh):
    spec = P(("wide", "narrow"), None)
    return jax.shard_map(local, mesh=mesh, in_specs=(spec,), out_specs=spec, check_vma=False)
```

```python
import math

import jax
import jax.numpy as jnp
from jax import lax
from jax.experimental import pallas as pl
from jax.experimental.pallas import tpu as pltpu
from jax.sharding import PartitionSpec as P

M = 3584
K = 18432

COEFF_A = 3.4445
COEFF_B = -4.775
COEFF_C = 2.0315

MESH = pl.DeviceIdType.MESH
BF = jnp.bfloat16
F32 = jnp.float32
NT = (((1,), (1,)), ((), ()))

ROWS = 28
PIECE = 32
THIRD = K // 3
COL1 = THIRD // 4
COL2 = COL1 // 4
COL3 = COL2 // 4
HALF3 = COL3 // 2
OWN = 3 * HALF3
HALF_M = M // 2
AXES = ((0, 1, 2), (1, 2, 0), (2, 0, 1))

BLK = 256
NB = M // BLK
SLOTS = 54
PART = 9216
CORE_ROWS = 3 * PART
SIZES = (2304, 576, 144)
TOPS = (1152, 288)
BOTS = (1152, 288)


def al(x, m=16):
    return pl.multiple_of(x, m)


def kernel(
    in_ref, out_ref,
    x0, x1, x2, x2p, x3, s_all, st,
    ut, y3, y2p, y2, y1,
    t, g, r1, r2, r3, sq, ybf, yf, tail,
    in_send, in_recv, in_copy, core_send, core_recv, out_send, out_recv, out_copy, ut_send, ut_recv,
    rs_send, rs_recv, ag_send, ag_recv, fw_send, fw_recv, sq_send, sq_recv,
):
    recv_bufs = (r1, r2, r3)
    w, n_ = lax.axis_index("wide"), lax.axis_index("narrow")
    core, z_lo, y = w % 2, (w // 2) % 2, w // 4
    x, z_hi = n_ % 4, n_ // 4
    z = z_hi * 2 + z_lo
    pos = (x, y, z)

    def device(x, y, z, core):
        return ((y * 2 + z % 2) * 2 + core, (z // 2) * 4 + x)

    def shifted(axis, by):
        p = [x, y, z]
        p[axis] = (p[axis] + by) % 4
        return device(*p, core)

    right = [shifted(a, 1) for a in range(3)]
    left = [shifted(a, 3) for a in range(3)]
    across = [shifted(a, 2) for a in range(3)]
    partner = device(x, y, z, 1 - core)

    barrier = pltpu.get_barrier_semaphore()
    for d in right + left + across + [partner]:
        pl.semaphore_signal(barrier, inc=1, device_id=d, device_id_type=MESH)

    def load(k, total):
        cols = pl.ds(al(k * 512, 512), 512)
        v = in_ref[:, cols]
        x0[pl.ds(0, ROWS), cols] = v
        x0[pl.ds(ROWS, PIECE - ROWS), cols] = jnp.zeros((PIECE - ROWS, 512), BF)
        return total

    lax.fori_loop(0, K // 512, load, 0)
    pl.semaphore_wait(barrier, 10)

    def remote(src, dst, send, recv, dev):
        return pltpu.make_async_remote_copy(
            src_ref=src, dst_ref=dst, send_sem=send, recv_sem=recv, device_id=dev, device_id_type=MESH
        )

    sent = []

    class Exchange:
        def __init__(self, stage, axis_no, src, dst, sems):
            self.stage, self.axis_no, self.src, self.dst, self.sems = stage, axis_no, src, dst, sems
            self.copies = {}

        def begin(self, p):
            a = AXES[p][self.axis_no]
            me = pos[a]
            send, recv, copy = self.sems
            group = []
            for k, dev in ((2, across[a]), (1, right[a]), (3, left[a])):
                c = remote(
                    self.src(p, (me + k) % 4), self.dst(p, me),
                    send.at[self.stage, p, k - 1], recv.at[self.stage, p, k - 1], dev,
                )
                c.start()
                group.append(c)
                sent.append(c)
            own = pltpu.make_async_copy(self.src(p, me), self.dst(p, me), copy.at[self.stage, p])
            own.start()
            self.copies[p] = group, own

        def arrive(self, p):
            group, own = self.copies[p]
            for c in group:
                c.wait_recv()
            own.wait()

    def tall(p, q):
        return pl.ds(al(p * THIRD + q * COL1, COL1), COL1)

    def lanes(k, size):
        return pl.ds(al(k * size, size), size)

    ins = (in_send, in_recv, in_copy)
    outs = (out_send, out_recv, out_copy)

    def plane(buf, p, q):
        return buf.at[p, q] if p == 2 else buf.at[p, :, q]

    def cube(buf, p, q):
        lane = pl.ds(128 * p, 128)
        if p == 0:
            return buf.at[:, :, q, :, lane]
        if p == 1:
            return buf.at[q, :, :, :, lane]
        return buf.at[:, q, :, :, lane]

    in1 = Exchange(0, 0, lambda p, q: x0.at[:, tall(p, q)], lambda p, q: x1.at[p, q], ins)
    in2 = Exchange(1, 1, lambda p, q: x1.at[p, :, :, lanes(q, COL2)], lambda p, q: plane(x2, p, q), ins)
    in3 = Exchange(2, 2, lambda p, q: x2p.at[p, :, :, :, lanes(q, 128)], lambda p, q: cube(x3.at[core], p, q), ins)
    for p in range(3):
        in1.begin(p)

    def square(k, total):
        v = x0[:, pl.ds(al(k * 512, 512), 512)].astype(F32)
        v = v * v
        v = (v[:, :128] + v[:, 128:256]) + (v[:, 256:384] + v[:, 384:])
        return total + ((v[:8] + v[8:16]) + (v[16:24] + v[24:]))

    sq[13] = lax.fori_loop(0, K // 512, square, jnp.zeros((8, 128), F32))
    sq_core = remote(sq.at[13], sq.at[14], sq_send.at[3, 0], sq_recv.at[3, 0], partner)
    sq_core.start()
    sent.append(sq_core)

    def iota(shape, d):
        return lax.broadcasted_iota(jnp.int32, shape, d)

    def ones_where(cond):
        return jnp.where(cond, 1.0, 0.0).astype(BF)

    def spread_matrix(shape, wide, unit, narrow):
        s, r = iota(shape, wide), iota(shape, 1 - wide)
        return ones_where((s % unit < narrow) & (r == (s // unit) * narrow + s % unit))

    for p in range(3):
        in1.arrive(p)
        in2.begin(p)
    widen = spread_matrix((COL2, 512), 1, 128, COL3)
    for p in range(3):
        in2.arrive(p)
        for h in range(2):
            rows = x2[p, pl.ds(2 * h, 2)].reshape(256, COL2)
            x2p[p, pl.ds(2 * h, 2)] = (
                jnp.dot(rows, widen, preferred_element_type=F32).astype(BF).reshape(2, 4, PIECE, 512)
            )
        in3.begin(p)
    crossing = []
    for p in range(3):
        in3.arrive(p)
        here = x3.at[core, :, :, :, :, pl.ds(128 * p, 128)]
        c = remote(here, here, core_send.at[p], core_recv.at[p], partner)
        c.start()
        crossing.append(c)
        sent.append(c)

    pack = spread_matrix((8 * ROWS, 8 * PIECE), 1, PIECE, ROWS)

    def pack_rows(owner):
        def body(k, carry):
            rows = x3[owner, k // 2, pl.ds((k % 2) * 2, 2)].reshape(8 * PIECE, 384)
            at = pl.ds(al(owner * HALF_M + k * 8 * ROWS), 8 * ROWS)
            s_all[at, :] = jnp.dot(pack, rows, preferred_element_type=F32).astype(BF)
            return carry

        lax.fori_loop(0, 8, body, 0)

    pack_rows(core)
    for c in crossing:
        c.wait_recv()
    pack_rows(1 - core)

    def turn_own():
        kk, ll = iota((OWN, 384), 0), iota((OWN, 384), 1)
        lane = ll % 128 - core * HALF3
        pick = ones_where((lane >= 0) & (lane < HALF3) & (kk == (ll // 128) * HALF3 + lane))

        def turn(j, carry):
            at = pl.ds(al(j * BLK, BLK), BLK)
            st[:, at] = lax.dot_general(pick, s_all[at, :], NT, preferred_element_type=F32).astype(BF)
            return carry

        lax.fori_loop(0, NB, turn, 0)

    def gram_block(m, carry):
        n = core * SLOTS + m
        i, d = n % NB, n // NB
        j = (i + d) % NB
        ri = pl.ds(al(i * BLK, BLK), BLK)
        rj = pl.ds(al(j * BLK, BLK), BLK)
        acc = lax.dot_general(s_all[ri, :], s_all[rj, :], NT, preferred_element_type=F32).astype(BF)
        t[pl.ds(al(m * 512, 512), 256), :] = acc[:, :128]
        t[pl.ds(al(m * 512 + 256, 256), 256), :] = acc[:, 128:]
        return carry

    def gram_blocks(start, count):
        lax.fori_loop(0, count, lambda m, carry: gram_block(start + m, carry), 0)

    def add_rows(dst_off, rows, srcs):
        step = 288 if rows % 288 == 0 else 144

        def body(k, carry):
            o = k * step
            total = t[pl.ds(al(dst_off + o), step), :].astype(F32)
            for src in srcs:
                total = total + src[pl.ds(al(o), step), :].astype(F32)
            t[pl.ds(al(dst_off + o), step), :] = total.astype(BF)
            return carry

        lax.fori_loop(0, rows // step, body, 0)

    def square_begin(s):
        group = [
            remote(sq.at[4 * s], sq.at[4 * s + 1 + k], sq_send.at[s, k], sq_recv.at[s, k], dev)
            for k, dev in enumerate((right[s], left[s], across[s]))
        ]
        for c in group:
            c.start()
        sent.extend(group)
        return group

    def square_end(s, group):
        for c in group:
            c.wait_recv()
        sq[4 * s + 4] = (sq[4 * s] + sq[4 * s + 3]) + (sq[4 * s + 1] + sq[4 * s + 2])

    base = [p * PART for p in range(3)]
    bases = [list(base)]
    for s in range(2):
        size, top, bot = SIZES[s], TOPS[s], BOTS[s]
        buf = recv_bufs[s]

        def quarter(p, by, s=s, size=size):
            return base[p] + ((pos[AXES[p][s]] + by) % 4) * size

        copies = {}

        def push(p, k, off, rows, s=s, buf=buf, copies=copies):
            a = AXES[p][s]
            c = remote(
                t.at[pl.ds(al(off), rows), :],
                buf.at[p, k, pl.ds(0, rows), :],
                rs_send.at[s, p, k],
                rs_recv.at[s, p, k],
                right[a] if k < 3 else left[a],
            )
            c.start()
            copies[p, k] = c
            sent.append(c)

        for p in range(3):
            if s == 0:
                gram_blocks(p * 18 + 9 * ((pos[AXES[p][0]] + 2) % 4) // 2, 5)
            push(p, 0, quarter(p, 2), top)
            push(p, 3, quarter(p, 2) + top, bot)
        for p in range(3):
            if s == 0:
                me = pos[AXES[p][0]]
                gram_blocks(p * 18 + 4 + 9 * (me // 2), 1)
                gram_blocks(p * 18 + (9 * ((me + 1) % 4) + 1) // 2, 4)
                gram_blocks(p * 18 + (9 * ((me + 3) % 4) + 1) // 2, 4)
            push(p, 1, quarter(p, 1) + top, bot)
            push(p, 4, quarter(p, 3), top)
        if s == 0:
            for p in range(3):
                gram_blocks(p * 18 + (9 * pos[AXES[p][0]] + 1) // 2, 4)
            sq_core.wait_recv()
            sq[0] = sq[13] + sq[14]
        squares = square_begin(s)
        if s == 0:
            turn_own()
        for p in range(3):
            copies[p, 0].wait_recv()
            add_rows(quarter(p, 1), top, [buf.at[p, 0]])
            push(p, 2, quarter(p, 1), top)
            copies[p, 3].wait_recv()
            add_rows(quarter(p, 3) + top, bot, [buf.at[p, 3]])
            push(p, 5, quarter(p, 3) + top, bot)
        for p in range(3):
            copies[p, 4].wait_recv()
            copies[p, 2].wait_recv()
            add_rows(quarter(p, 0), top, [buf.at[p, 4], buf.at[p, 2]])
            copies[p, 1].wait_recv()
            copies[p, 5].wait_recv()
            add_rows(quarter(p, 0) + top, bot, [buf.at[p, 1], buf.at[p, 5]])
        square_end(s, squares)
        base = [quarter(p, 0) for p in range(3)]
        bases.append(list(base))

    size = SIZES[2]
    squares = square_begin(2)
    direct = {}
    for p in range(3):
        a = AXES[p][2]
        for k, dev in ((2, across[a]), (1, right[a]), (3, left[a])):
            off = base[p] + ((pos[a] + k) % 4) * size
            c = remote(
                t.at[pl.ds(al(off), size), :], r3.at[p, k - 1], rs_send.at[2, p, k - 1], rs_recv.at[2, p, k - 1], dev
            )
            c.start()
            direct[p, k] = c
            sent.append(c)
    for p in range(3):
        for k in (1, 2, 3):
            direct[p, k].wait_recv()
        base[p] = base[p] + pos[AXES[p][2]] * size
        add_rows(base[p], size, [r3.at[p, k] for k in range(3)])
    square_end(2, squares)

    mine = core * CORE_ROWS
    for p in range(3):
        g[pl.ds(al(mine + base[p]), 144), :] = t[pl.ds(al(base[p]), 144), :]

    forwards = []

    def forward(p, k, off, rows):
        here = g.at[pl.ds(al(off), rows), :]
        c = remote(here, here, fw_send.at[p, k], fw_recv.at[p, k], partner)
        c.start()
        forwards.append(c)

    for p in range(3):
        a = AXES[p][2]
        here = g.at[pl.ds(al(mine + base[p]), size), :]
        for k, dev in ((2, across[a]), (1, right[a]), (3, left[a])):
            c = remote(here, here, ag_send.at[2, p, k - 1], ag_recv.at[2, p, k - 1], dev)
            c.start()
            direct[p, k] = c
            sent.append(c)
    for p in range(3):
        for k in (1, 2, 3):
            direct[p, k].wait_recv()
    for s in (1, 0):
        size, top, bot = SIZES[s], TOPS[s], BOTS[s]
        base = bases[s]
        last = s == 0

        def quarter(p, by, s=s, size=size, base=base):
            return mine + base[p] + ((pos[AXES[p][s]] + by) % 4) * size

        copies = {}

        def spread(p, k, off, rows, s=s, copies=copies):
            a = AXES[p][s]
            here = g.at[pl.ds(al(off), rows), :]
            c = remote(here, here, ag_send.at[s, p, k], ag_recv.at[s, p, k], right[a] if k % 2 == 0 else left[a])
            c.start()
            copies[p, k] = c
            sent.append(c)

        for p in range(3):
            spread(p, 0, quarter(p, 0), size)
            spread(p, 1, quarter(p, 0), size)
            if last:
                forward(p, 0, quarter(p, 0), size)
        for p in range(3):
            copies[p, 0].wait_recv()
            spread(p, 2, quarter(p, 3), top)
            copies[p, 1].wait_recv()
            spread(p, 3, quarter(p, 1) + top, bot)
            if last:
                forward(p, 1, quarter(p, 3), size)
                forward(p, 2, quarter(p, 1), size)
        for p in range(3):
            copies[p, 2].wait_recv()
            if last:
                forward(p, 3, quarter(p, 2), top)
            copies[p, 3].wait_recv()
            if last:
                forward(p, 4, quarter(p, 2) + top, bot)

    for c in forwards:
        c.wait_recv()

    factor = 0.3 * math.sqrt(M) / (jnp.sqrt(jnp.sum(sq[12], axis=(0, 1), keepdims=True)) + 1e-07)
    factor2 = factor * factor

    def band(a_ref, j):
        def cols(i):
            return a_ref[:, pl.ds(al(i * BLK, BLK), BLK)]

        def block(n):
            o = n * 512
            return jnp.concatenate(
                [g[pl.ds(al(o, 512), 256), :], g[pl.ds(al(o + 256, 256), 256), :]], axis=1
            )

        def straight(i, n):
            return jnp.dot(cols(i), block(n), preferred_element_type=F32)

        def turned(i, n):
            return lax.dot_general(cols(i), block(n), NT, preferred_element_type=F32)

        acc = straight(j, j)
        for d in range(1, 7):
            i = (j + NB - d) % NB
            acc += straight(i, d * NB + i)
            acc += turned((j + d) % NB, d * NB + j)
        i, n = (j + 7) % NB, 7 * NB + j % 7

        @pl.when(j < 7)
        def _():
            tail[...] = turned(i, n)

        @pl.when(j >= 7)
        def _():
            tail[...] = straight(i, n)

        return acc + tail[...]

    def bands(a_ref, half, finish):
        def body(k, carry):
            j = half * 7 + k
            finish(j, band(a_ref, j))
            return carry

        lax.fori_loop(0, 7, body, 0)

    def first(j, acc):
        v = factor2 * acc
        at = pl.ds(al(j * BLK, BLK), BLK)
        yf[:, at] = v
        ybf[:, at] = v.astype(BF)

    def second(j, acc):
        at = pl.ds(al(j * BLK, BLK), BLK)
        scaled = (factor * st[:, at].astype(F32)).astype(BF).astype(F32)
        product = factor * (COEFF_B * yf[:, at] + COEFF_C * (factor2 * acc))
        u = (math.sqrt(K) * (COEFF_A * scaled + product)).astype(BF)
        for p in range(3):
            ut[pl.ds(al(p * 128 + core * HALF3), HALF3), at] = u[p * HALF3 : (p + 1) * HALF3]

    bands(st, 0, first)
    bands(st, 1, first)
    for p in range(3):
        ut[pl.ds(p * 128 + COL3, 128 - COL3), :] = jnp.zeros((128 - COL3, M), BF)
    bands(ybf, 1 - core, second)
    halves = []
    for p in range(3):
        here = ut.at[pl.ds(al(p * 128 + core * HALF3), HALF3), lanes(1 - core, HALF_M)]
        c = remote(here, here, ut_send.at[p], ut_recv.at[p], partner)
        c.start()
        halves.append(c)
        sent.append(c)
    bands(ybf, core, second)
    unpack = spread_matrix((8 * PIECE, 8 * ROWS), 0, PIECE, ROWS)
    for c in halves:
        c.wait_recv()
    for m in range(8):
        o = m * 8 * ROWS
        first_lane = o // 128 * 128
        skip = o - first_lane
        width = -(-(skip + 8 * ROWS) // 128) * 128
        v = ut[:, pl.ds(al(core * HALF_M + first_lane, 128), width)][:, skip : skip + 8 * ROWS]
        rows = lax.dot_general(unpack, v, NT, preferred_element_type=F32).astype(BF)
        y3[m // 2, pl.ds((m % 2) * 2, 2)] = rows.reshape(2, 4, PIECE, 384)

    out1 = Exchange(0, 2, lambda p, q: cube(y3, p, q), lambda p, q: y2p.at[p, :, :, :, lanes(q, 128)], outs)
    out2 = Exchange(1, 1, lambda p, q: plane(y2, p, q), lambda p, q: y1.at[p, :, :, lanes(q, COL2)], outs)
    out3 = Exchange(2, 0, lambda p, q: y1.at[p, q], lambda p, q: out_ref.at[:, tall(p, q)], outs)
    for p in range(3):
        out1.begin(p)
    narrow = spread_matrix((512, COL2), 0, 128, COL3)
    for p in range(3):
        out1.arrive(p)
        for h in range(2):
            rows = y2p[p, pl.ds(2 * h, 2)].reshape(256, 512)
            y2[p, pl.ds(2 * h, 2)] = (
                jnp.dot(rows, narrow, preferred_element_type=F32).astype(BF).reshape(2, 4, PIECE, COL2)
            )
        out2.begin(p)
    for p in range(3):
        out2.arrive(p)
        out3.begin(p)
    for p in range(3):
        out3.arrive(p)

    for c in sent + forwards:
        c.wait_send()


def local(gradient):
    vmem = pl.BlockSpec(memory_space=pltpu.VMEM)
    dma = pltpu.SemaphoreType.DMA
    padded = pl.pallas_call(
        kernel,
        out_shape=jax.ShapeDtypeStruct((PIECE, K), BF),
        in_specs=[vmem],
        out_specs=vmem,
        scratch_shapes=[
            pltpu.VMEM((PIECE, K), BF),
            pltpu.VMEM((3, 4, PIECE, COL1), BF),
            pltpu.VMEM((3, 4, 4, PIECE, COL2), BF),
            pltpu.VMEM((3, 4, 4, PIECE, 512), BF),
            pltpu.VMEM((2, 4, 4, 4, PIECE, 384), BF),
            pltpu.VMEM((M, 384), BF),
            pltpu.VMEM((OWN, M), BF),
            pltpu.VMEM((384, M), BF),
            pltpu.VMEM((4, 4, 4, PIECE, 384), BF),
            pltpu.VMEM((3, 4, 4, PIECE, 512), BF),
            pltpu.VMEM((3, 4, 4, PIECE, COL2), BF),
            pltpu.VMEM((3, 4, PIECE, COL1), BF),
            pltpu.VMEM((CORE_ROWS, 128), BF),
            pltpu.VMEM((2 * CORE_ROWS, 128), BF),
            pltpu.VMEM((3, 6, 1152, 128), BF),
            pltpu.VMEM((3, 6, 288, 128), BF),
            pltpu.VMEM((3, 3, 144, 128), BF),
            pltpu.VMEM((15, 8, 128), F32),
            pltpu.VMEM((OWN, M), BF),
            pltpu.VMEM((OWN, M), F32),
            pltpu.VMEM((OWN, BLK), F32),
            dma((3, 3, 3)),
            dma((3, 3, 3)),
            dma((3, 3)),
            dma((3,)),
            dma((3,)),
            dma((3, 3, 3)),
            dma((3, 3, 3)),
            dma((3, 3)),
            dma((3,)),
            dma((3,)),
            dma((3, 3, 6)),
            dma((3, 3, 6)),
            dma((3, 3, 4)),
            dma((3, 3, 4)),
            dma((3, 5)),
            dma((3, 5)),
            dma((4, 3)),
            dma((4, 3)),
        ],
        compiler_params=pltpu.CompilerParams(
            collective_id=0, has_side_effects=True, vmem_limit_bytes=60 * 1024 * 1024
        ),
        cost_estimate=pl.CostEstimate(flops=16 * 10**9, bytes_accessed=5 * 10**6, transcendentals=0),
    )(gradient)
    return padded[:ROWS]


def solution(mesh):
    spec = P(("wide", "narrow"), None)
    return jax.shard_map(local, mesh=mesh, in_specs=(spec,), out_specs=spec, check_vma=False)
```

```python
import math

import jax
import jax.numpy as jnp
from jax import lax
from jax.experimental import pallas as pl
from jax.experimental.pallas import tpu as pltpu
from jax.sharding import PartitionSpec as P

M = 3584
K = 18432

COEFF_A = 3.4445
COEFF_B = -4.775
COEFF_C = 2.0315

MESH = pl.DeviceIdType.MESH
BF = jnp.bfloat16
F32 = jnp.float32
NT = (((1,), (1,)), ((), ()))

ROWS = 28
PIECE = 32
THIRD = K // 3
COL1 = THIRD // 4
COL2 = COL1 // 4
COL3 = COL2 // 4
HALF3 = COL3 // 2
OWN = 3 * HALF3
HALF_M = M // 2
AXES = ((0, 1, 2), (1, 2, 0), (2, 0, 1))

BLK = 256
NB = M // BLK
SLOTS = 54
PART = 9216
CORE_ROWS = 3 * PART
SIZES = (2304, 576, 144)
TOPS = (1152, 288)
BOTS = (1152, 288)


def al(x, m=16):
    return pl.multiple_of(x, m)


def kernel(
    in_ref, out_ref,
    x0, x1, x2, x2p, x3, s_all, st,
    ut, y3, y2p, y2, y1,
    t, g, r1, r2, r3, sq, ybf, yf, tail,
    in_send, in_recv, in_copy, core_send, core_recv, out_send, out_recv, out_copy, ut_send, ut_recv,
    rs_send, rs_recv, ag_send, ag_recv, fw_send, fw_recv, sq_send, sq_recv,
):
    recv_bufs = (r1, r2, r3)
    w, n_ = lax.axis_index("wide"), lax.axis_index("narrow")
    core, z_lo, y = w % 2, (w // 2) % 2, w // 4
    x, z_hi = n_ % 4, n_ // 4
    z = z_hi * 2 + z_lo
    pos = (x, y, z)

    def device(x, y, z, core):
        return ((y * 2 + z % 2) * 2 + core, (z // 2) * 4 + x)

    def shifted(axis, by):
        p = [x, y, z]
        p[axis] = (p[axis] + by) % 4
        return device(*p, core)

    right = [shifted(a, 1) for a in range(3)]
    left = [shifted(a, 3) for a in range(3)]
    across = [shifted(a, 2) for a in range(3)]
    partner = device(x, y, z, 1 - core)

    barrier = pltpu.get_barrier_semaphore()
    for d in right + left + across + [partner]:
        pl.semaphore_signal(barrier, inc=1, device_id=d, device_id_type=MESH)

    def load(k, total):
        cols = pl.ds(al(k * 512, 512), 512)
        v = in_ref[:, cols]
        x0[pl.ds(0, ROWS), cols] = v
        x0[pl.ds(ROWS, PIECE - ROWS), cols] = jnp.zeros((PIECE - ROWS, 512), BF)
        return total

    lax.fori_loop(0, K // 512, load, 0)
    pl.semaphore_wait(barrier, 10)

    def remote(src, dst, send, recv, dev):
        return pltpu.make_async_remote_copy(
            src_ref=src, dst_ref=dst, send_sem=send, recv_sem=recv, device_id=dev, device_id_type=MESH
        )

    sent = []

    class Exchange:
        def __init__(self, stage, axis_no, src, dst, sems):
            self.stage, self.axis_no, self.src, self.dst, self.sems = stage, axis_no, src, dst, sems
            self.copies = {}

        def begin(self, p):
            a = AXES[p][self.axis_no]
            me = pos[a]
            send, recv, copy = self.sems
            group = []
            for k, dev in ((2, across[a]), (1, right[a]), (3, left[a])):
                c = remote(
                    self.src(p, (me + k) % 4), self.dst(p, me),
                    send.at[self.stage, p, k - 1], recv.at[self.stage, p, k - 1], dev,
                )
                c.start()
                group.append(c)
                sent.append(c)
            own = pltpu.make_async_copy(self.src(p, me), self.dst(p, me), copy.at[self.stage, p])
            own.start()
            self.copies[p] = group, own

        def arrive(self, p):
            group, own = self.copies[p]
            for c in group:
                c.wait_recv()
            own.wait()

    def tall(p, q):
        return pl.ds(al(p * THIRD + q * COL1, COL1), COL1)

    def lanes(k, size):
        return pl.ds(al(k * size, size), size)

    ins = (in_send, in_recv, in_copy)
    outs = (out_send, out_recv, out_copy)

    def plane(buf, p, q):
        return buf.at[p, q] if p == 2 else buf.at[p, :, q]

    def cube(buf, p, q):
        lane = pl.ds(128 * p, 128)
        if p == 0:
            return buf.at[:, :, q, :, lane]
        if p == 1:
            return buf.at[q, :, :, :, lane]
        return buf.at[:, q, :, :, lane]

    in1 = Exchange(0, 0, lambda p, q: x0.at[:, tall(p, q)], lambda p, q: x1.at[p, q], ins)
    in2 = Exchange(1, 1, lambda p, q: x1.at[p, :, :, lanes(q, COL2)], lambda p, q: plane(x2, p, q), ins)
    in3 = Exchange(2, 2, lambda p, q: x2p.at[p, :, :, :, lanes(q, 128)], lambda p, q: cube(x3.at[core], p, q), ins)
    for p in range(3):
        in1.begin(p)

    def square(k, total):
        v = x0[:, pl.ds(al(k * 512, 512), 512)].astype(F32)
        v = v * v
        v = (v[:, :128] + v[:, 128:256]) + (v[:, 256:384] + v[:, 384:])
        return total + ((v[:8] + v[8:16]) + (v[16:24] + v[24:]))

    sq[13] = lax.fori_loop(0, K // 512, square, jnp.zeros((8, 128), F32))
    sq_core = remote(sq.at[13], sq.at[14], sq_send.at[3, 0], sq_recv.at[3, 0], partner)
    sq_core.start()
    sent.append(sq_core)

    def iota(shape, d):
        return lax.broadcasted_iota(jnp.int32, shape, d)

    def ones_where(cond):
        return jnp.where(cond, 1.0, 0.0).astype(BF)

    def spread_matrix(shape, wide, unit, narrow):
        s, r = iota(shape, wide), iota(shape, 1 - wide)
        return ones_where((s % unit < narrow) & (r == (s // unit) * narrow + s % unit))

    for p in range(3):
        in1.arrive(p)
        in2.begin(p)
    widen = spread_matrix((COL2, 512), 1, 128, COL3)
    for p in range(3):
        in2.arrive(p)
        for h in range(2):
            rows = x2[p, pl.ds(2 * h, 2)].reshape(256, COL2)
            x2p[p, pl.ds(2 * h, 2)] = (
                jnp.dot(rows, widen, preferred_element_type=F32).astype(BF).reshape(2, 4, PIECE, 512)
            )
        in3.begin(p)
    crossing = []
    for p in range(3):
        in3.arrive(p)
        here = x3.at[core, :, :, :, :, pl.ds(128 * p, 128)]
        c = remote(here, here, core_send.at[p], core_recv.at[p], partner)
        c.start()
        crossing.append(c)
        sent.append(c)

    pack = spread_matrix((8 * ROWS, 8 * PIECE), 1, PIECE, ROWS)

    def pack_rows(owner):
        def body(k, carry):
            rows = x3[owner, k // 2, pl.ds((k % 2) * 2, 2)].reshape(8 * PIECE, 384)
            at = pl.ds(al(owner * HALF_M + k * 8 * ROWS), 8 * ROWS)
            s_all[at, :] = jnp.dot(pack, rows, preferred_element_type=F32).astype(BF)
            return carry

        lax.fori_loop(0, 8, body, 0)

    pack_rows(core)
    for c in crossing:
        c.wait_recv()
    pack_rows(1 - core)

    def turn_own():
        kk, ll = iota((OWN, 384), 0), iota((OWN, 384), 1)
        lane = ll % 128 - core * HALF3
        pick = ones_where((lane >= 0) & (lane < HALF3) & (kk == (ll // 128) * HALF3 + lane))

        def turn(j, carry):
            at = pl.ds(al(j * BLK, BLK), BLK)
            st[:, at] = lax.dot_general(pick, s_all[at, :], NT, preferred_element_type=F32).astype(BF)
            return carry

        lax.fori_loop(0, NB, turn, 0)

    def gram_block(m, carry):
        n = core * SLOTS + m
        i, d = n % NB, n // NB
        j = (i + d) % NB
        ri = pl.ds(al(i * BLK, BLK), BLK)
        rj = pl.ds(al(j * BLK, BLK), BLK)
        acc = lax.dot_general(s_all[ri, :], s_all[rj, :], NT, preferred_element_type=F32).astype(BF)
        t[pl.ds(al(m * 512, 512), 256), :] = acc[:, :128]
        t[pl.ds(al(m * 512 + 256, 256), 256), :] = acc[:, 128:]
        return carry

    def gram_blocks(start, count):
        lax.fori_loop(0, count, lambda m, carry: gram_block(start + m, carry), 0)

    def add_rows(dst_off, rows, srcs):
        step = 288 if rows % 288 == 0 else 144

        def body(k, carry):
            o = k * step
            total = t[pl.ds(al(dst_off + o), step), :].astype(F32)
            for src in srcs:
                total = total + src[pl.ds(al(o), step), :].astype(F32)
            t[pl.ds(al(dst_off + o), step), :] = total.astype(BF)
            return carry

        lax.fori_loop(0, rows // step, body, 0)

    def square_begin(s):
        group = [
            remote(sq.at[4 * s], sq.at[4 * s + 1 + k], sq_send.at[s, k], sq_recv.at[s, k], dev)
            for k, dev in enumerate((right[s], left[s], across[s]))
        ]
        for c in group:
            c.start()
        sent.extend(group)
        return group

    def square_end(s, group):
        for c in group:
            c.wait_recv()
        sq[4 * s + 4] = (sq[4 * s] + sq[4 * s + 3]) + (sq[4 * s + 1] + sq[4 * s + 2])

    base = [p * PART for p in range(3)]
    bases = [list(base)]
    for s in range(2):
        size, top, bot = SIZES[s], TOPS[s], BOTS[s]
        buf = recv_bufs[s]

        def quarter(p, by, s=s, size=size):
            return base[p] + ((pos[AXES[p][s]] + by) % 4) * size

        copies = {}

        def push(p, k, off, rows, s=s, buf=buf, copies=copies):
            a = AXES[p][s]
            c = remote(
                t.at[pl.ds(al(off), rows), :],
                buf.at[p, k, pl.ds(0, rows), :],
                rs_send.at[s, p, k],
                rs_recv.at[s, p, k],
                right[a] if k < 3 else left[a],
            )
            c.start()
            copies[p, k] = c
            sent.append(c)

        for p in range(3):
            if s == 0:
                gram_blocks(p * 18 + 9 * ((pos[AXES[p][0]] + 2) % 4) // 2, 5)
            push(p, 0, quarter(p, 2), top)
            push(p, 3, quarter(p, 2) + top, bot)
        for p in range(3):
            if s == 0:
                me = pos[AXES[p][0]]
                gram_blocks(p * 18 + 4 + 9 * (me // 2), 1)
                gram_blocks(p * 18 + (9 * ((me + 1) % 4) + 1) // 2, 4)
                gram_blocks(p * 18 + (9 * ((me + 3) % 4) + 1) // 2, 4)
            push(p, 1, quarter(p, 1) + top, bot)
            push(p, 4, quarter(p, 3), top)
        if s == 0:
            for p in range(3):
                gram_blocks(p * 18 + (9 * pos[AXES[p][0]] + 1) // 2, 4)
            sq_core.wait_recv()
            sq[0] = sq[13] + sq[14]
        squares = square_begin(s)
        if s == 0:
            turn_own()
            yf[...] = jnp.zeros((OWN, M), F32)
        for p in range(3):
            copies[p, 0].wait_recv()
            add_rows(quarter(p, 1), top, [buf.at[p, 0]])
            push(p, 2, quarter(p, 1), top)
            copies[p, 3].wait_recv()
            add_rows(quarter(p, 3) + top, bot, [buf.at[p, 3]])
            push(p, 5, quarter(p, 3) + top, bot)
        for p in range(3):
            copies[p, 4].wait_recv()
            copies[p, 2].wait_recv()
            add_rows(quarter(p, 0), top, [buf.at[p, 4], buf.at[p, 2]])
            copies[p, 1].wait_recv()
            copies[p, 5].wait_recv()
            add_rows(quarter(p, 0) + top, bot, [buf.at[p, 1], buf.at[p, 5]])
        square_end(s, squares)
        base = [quarter(p, 0) for p in range(3)]
        bases.append(list(base))

    size = SIZES[2]
    squares = square_begin(2)
    direct = {}
    for p in range(3):
        a = AXES[p][2]
        for k, dev in ((2, across[a]), (1, right[a]), (3, left[a])):
            off = base[p] + ((pos[a] + k) % 4) * size
            c = remote(
                t.at[pl.ds(al(off), size), :], r3.at[p, k - 1], rs_send.at[2, p, k - 1], rs_recv.at[2, p, k - 1], dev
            )
            c.start()
            direct[p, k] = c
            sent.append(c)
    for p in range(3):
        for k in (1, 2, 3):
            direct[p, k].wait_recv()
        base[p] = base[p] + pos[AXES[p][2]] * size
        add_rows(base[p], size, [r3.at[p, k] for k in range(3)])
    square_end(2, squares)

    mine = core * CORE_ROWS
    for p in range(3):
        g[pl.ds(al(mine + base[p]), 144), :] = t[pl.ds(al(base[p]), 144), :]

    def cols(a_ref, i):
        return a_ref[:, pl.ds(al(i * BLK, BLK), BLK)]

    def block(n):
        o = n * 512
        return jnp.concatenate([g[pl.ds(al(o, 512), 256), :], g[pl.ds(al(o + 256, 256), 256), :]], axis=1)

    def add_block(n):
        i, d = n % NB, n // NB
        j = (i + d) % NB

        @pl.when(d * NB + i < 7 * NB + 7)
        def _():
            b = block(n)
            yf[:, pl.ds(al(j * BLK, BLK), BLK)] += jnp.dot(cols(st, i), b, preferred_element_type=F32)

            @pl.when(d > 0)
            def _():
                yf[:, pl.ds(al(i * BLK, BLK), BLK)] += lax.dot_general(
                    cols(st, j), b, NT, preferred_element_type=F32
                )

    def add_quarter(c, by):
        for p in range(3):
            start = c * SLOTS + p * 18 + (9 * ((pos[AXES[p][0]] + by) % 4) + 1) // 2

            def body(m, carry, start=start):
                add_block(start + m)
                return carry

            lax.fori_loop(0, 4, body, 0)

    forwards = {}

    def forward(p, k, off, rows):
        here = g.at[pl.ds(al(off), rows), :]
        c = remote(here, here, fw_send.at[p, k], fw_recv.at[p, k], partner)
        c.start()
        forwards[p, k] = c
        sent.append(c)

    for p in range(3):
        a = AXES[p][2]
        here = g.at[pl.ds(al(mine + base[p]), size), :]
        for k, dev in ((2, across[a]), (1, right[a]), (3, left[a])):
            c = remote(here, here, ag_send.at[2, p, k - 1], ag_recv.at[2, p, k - 1], dev)
            c.start()
            direct[p, k] = c
            sent.append(c)
    for p in range(3):
        for k in (1, 2, 3):
            direct[p, k].wait_recv()
    for s in (1, 0):
        size, top, bot = SIZES[s], TOPS[s], BOTS[s]
        base = bases[s]
        last = s == 0

        def quarter(p, by, s=s, size=size, base=base):
            return mine + base[p] + ((pos[AXES[p][s]] + by) % 4) * size

        copies = {}

        def spread(p, k, off, rows, s=s, copies=copies):
            a = AXES[p][s]
            here = g.at[pl.ds(al(off), rows), :]
            c = remote(here, here, ag_send.at[s, p, k], ag_recv.at[s, p, k], right[a] if k in (0, 2, 4) else left[a])
            c.start()
            copies[p, k] = c
            sent.append(c)

        for p in range(3):
            spread(p, 0, quarter(p, 0), top)
            spread(p, 1, quarter(p, 0) + top, bot)
        for p in range(3):
            spread(p, 2, quarter(p, 0) + top, bot)
            spread(p, 3, quarter(p, 0), top)
        if last:
            for p in range(3):
                forward(p, 0, quarter(p, 0), size)
            add_quarter(core, 0)
            for p in range(3):
                forwards[p, 0].wait_recv()
            add_quarter(1 - core, 0)
        for p in range(3):
            copies[p, 0].wait_recv()
            spread(p, 4, quarter(p, 3), top)
            copies[p, 1].wait_recv()
            spread(p, 5, quarter(p, 1) + top, bot)
        for p in range(3):
            copies[p, 2].wait_recv()
            copies[p, 3].wait_recv()
            if last:
                forward(p, 3, quarter(p, 3), size)
                forward(p, 1, quarter(p, 1), size)
        if last:
            for c, by in ((core, 3), (core, 1), (1 - core, 3), (1 - core, 1)):
                if c is not core:
                    for p in range(3):
                        forwards[p, by].wait_recv()
                add_quarter(c, by)
        for p in range(3):
            copies[p, 4].wait_recv()
            copies[p, 5].wait_recv()
            if last:
                forward(p, 2, quarter(p, 2), size)
    add_quarter(core, 2)
    for p in range(3):
        for m in (4, 13):
            add_block(core * SLOTS + p * 18 + m)
    for p in range(3):
        forwards[p, 2].wait_recv()
    add_quarter(1 - core, 2)
    for p in range(3):
        for m in (4, 13):
            add_block((1 - core) * SLOTS + p * 18 + m)

    factor = 0.3 * math.sqrt(M) / (jnp.sqrt(jnp.sum(sq[12], axis=(0, 1), keepdims=True)) + 1e-07)
    factor2 = factor * factor

    def band(a_ref, j):
        def straight(i, n):
            return jnp.dot(cols(a_ref, i), block(n), preferred_element_type=F32)

        def turned(i, n):
            return lax.dot_general(cols(a_ref, i), block(n), NT, preferred_element_type=F32)

        acc = straight(j, j)
        for d in range(1, 7):
            i = (j + NB - d) % NB
            acc += straight(i, d * NB + i)
            acc += turned((j + d) % NB, d * NB + j)
        i, n = (j + 7) % NB, 7 * NB + j % 7

        @pl.when(j < 7)
        def _():
            tail[...] = turned(i, n)

        @pl.when(j >= 7)
        def _():
            tail[...] = straight(i, n)

        return acc + tail[...]

    def bands(a_ref, half, finish):
        def body(k, carry):
            j = half * 7 + k
            finish(j, band(a_ref, j))
            return carry

        lax.fori_loop(0, 7, body, 0)

    def first(j, carry):
        at = pl.ds(al(j * BLK, BLK), BLK)
        v = factor2 * yf[:, at]
        yf[:, at] = v
        ybf[:, at] = v.astype(BF)
        return carry

    def second(j, acc):
        at = pl.ds(al(j * BLK, BLK), BLK)
        scaled = (factor * st[:, at].astype(F32)).astype(BF).astype(F32)
        product = factor * (COEFF_B * yf[:, at] + COEFF_C * (factor2 * acc))
        u = (math.sqrt(K) * (COEFF_A * scaled + product)).astype(BF)
        for p in range(3):
            ut[pl.ds(al(p * 128 + core * HALF3), HALF3), at] = u[p * HALF3 : (p + 1) * HALF3]

    lax.fori_loop(0, NB, first, 0)
    for p in range(3):
        ut[pl.ds(p * 128 + COL3, 128 - COL3), :] = jnp.zeros((128 - COL3, M), BF)
    bands(ybf, 1 - core, second)
    halves = []
    for p in range(3):
        here = ut.at[pl.ds(al(p * 128 + core * HALF3), HALF3), lanes(1 - core, HALF_M)]
        c = remote(here, here, ut_send.at[p], ut_recv.at[p], partner)
        c.start()
        halves.append(c)
        sent.append(c)
    bands(ybf, core, second)
    unpack = spread_matrix((8 * PIECE, 8 * ROWS), 0, PIECE, ROWS)
    for c in halves:
        c.wait_recv()
    for m in range(8):
        o = m * 8 * ROWS
        first_lane = o // 128 * 128
        skip = o - first_lane
        width = -(-(skip + 8 * ROWS) // 128) * 128
        v = ut[:, pl.ds(al(core * HALF_M + first_lane, 128), width)][:, skip : skip + 8 * ROWS]
        rows = lax.dot_general(unpack, v, NT, preferred_element_type=F32).astype(BF)
        y3[m // 2, pl.ds((m % 2) * 2, 2)] = rows.reshape(2, 4, PIECE, 384)

    out1 = Exchange(0, 2, lambda p, q: cube(y3, p, q), lambda p, q: y2p.at[p, :, :, :, lanes(q, 128)], outs)
    out2 = Exchange(1, 1, lambda p, q: plane(y2, p, q), lambda p, q: y1.at[p, :, :, lanes(q, COL2)], outs)
    out3 = Exchange(2, 0, lambda p, q: y1.at[p, q], lambda p, q: out_ref.at[:, tall(p, q)], outs)
    for p in range(3):
        out1.begin(p)
    narrow = spread_matrix((512, COL2), 0, 128, COL3)
    for p in range(3):
        out1.arrive(p)
        for h in range(2):
            rows = y2p[p, pl.ds(2 * h, 2)].reshape(256, 512)
            y2[p, pl.ds(2 * h, 2)] = (
                jnp.dot(rows, narrow, preferred_element_type=F32).astype(BF).reshape(2, 4, PIECE, COL2)
            )
        out2.begin(p)
    for p in range(3):
        out2.arrive(p)
        out3.begin(p)
    for p in range(3):
        out3.arrive(p)

    for c in sent:
        c.wait_send()


def local(gradient):
    vmem = pl.BlockSpec(memory_space=pltpu.VMEM)
    dma = pltpu.SemaphoreType.DMA
    padded = pl.pallas_call(
        kernel,
        out_shape=jax.ShapeDtypeStruct((PIECE, K), BF),
        in_specs=[vmem],
        out_specs=vmem,
        scratch_shapes=[
            pltpu.VMEM((PIECE, K), BF),
            pltpu.VMEM((3, 4, PIECE, COL1), BF),
            pltpu.VMEM((3, 4, 4, PIECE, COL2), BF),
            pltpu.VMEM((3, 4, 4, PIECE, 512), BF),
            pltpu.VMEM((2, 4, 4, 4, PIECE, 384), BF),
            pltpu.VMEM((M, 384), BF),
            pltpu.VMEM((OWN, M), BF),
            pltpu.VMEM((384, M), BF),
            pltpu.VMEM((4, 4, 4, PIECE, 384), BF),
            pltpu.VMEM((3, 4, 4, PIECE, 512), BF),
            pltpu.VMEM((3, 4, 4, PIECE, COL2), BF),
            pltpu.VMEM((3, 4, PIECE, COL1), BF),
            pltpu.VMEM((CORE_ROWS, 128), BF),
            pltpu.VMEM((2 * CORE_ROWS, 128), BF),
            pltpu.VMEM((3, 6, 1152, 128), BF),
            pltpu.VMEM((3, 6, 288, 128), BF),
            pltpu.VMEM((3, 3, 144, 128), BF),
            pltpu.VMEM((15, 8, 128), F32),
            pltpu.VMEM((OWN, M), BF),
            pltpu.VMEM((OWN, M), F32),
            pltpu.VMEM((OWN, BLK), F32),
            dma((3, 3, 3)),
            dma((3, 3, 3)),
            dma((3, 3)),
            dma((3,)),
            dma((3,)),
            dma((3, 3, 3)),
            dma((3, 3, 3)),
            dma((3, 3)),
            dma((3,)),
            dma((3,)),
            dma((3, 3, 6)),
            dma((3, 3, 6)),
            dma((3, 3, 6)),
            dma((3, 3, 6)),
            dma((3, 4)),
            dma((3, 4)),
            dma((4, 3)),
            dma((4, 3)),
        ],
        compiler_params=pltpu.CompilerParams(
            collective_id=0, has_side_effects=True, vmem_limit_bytes=60 * 1024 * 1024
        ),
        cost_estimate=pl.CostEstimate(flops=16 * 10**9, bytes_accessed=5 * 10**6, transcendentals=0),
    )(gradient)
    return padded[:ROWS]


def solution(mesh):
    spec = P(("wide", "narrow"), None)
    return jax.shard_map(local, mesh=mesh, in_specs=(spec,), out_specs=spec, check_vma=False)
```

```python
import math

import jax
import jax.numpy as jnp
from jax import lax
from jax.experimental import pallas as pl
from jax.experimental.pallas import tpu as pltpu
from jax.sharding import PartitionSpec as P

M = 3584
K = 18432

COEFF_A = 3.4445
COEFF_B = -4.775
COEFF_C = 2.0315

MESH = pl.DeviceIdType.MESH
BF = jnp.bfloat16
F32 = jnp.float32
NT = (((1,), (1,)), ((), ()))

ROWS = 28
PIECE = 32
THIRD = K // 3
COL1 = THIRD // 4
COL2 = COL1 // 4
COL3 = COL2 // 4
HALF3 = COL3 // 2
OWN = 3 * HALF3
HALF_M = M // 2
AXES = ((0, 1, 2), (1, 2, 0), (2, 0, 1))

BLK = 256
NB = M // BLK
PER_PART = (10, 8)
ROW0 = (0, 2 * 3 * 10 * 512)
SIZES = ((1280, 320, 80), (1024, 256, 64))
G_ROWS = 108 * 512


def al(x, m=16):
    return pl.multiple_of(x, m)


def kernel(
    in_ref, out_ref,
    x0, x1, x2, x2p, x3, s_all, st,
    ut, y3, y2p, y2, y1,
    ta, tb, g, r1a, r2a, r3a, r1b, r2b, r3b, sq, ybf, yf, tail,
    in_send, in_recv, in_copy, core_send, core_recv, out_send, out_recv, out_copy, ut_send, ut_recv,
    rsa_send, rsa_recv, aga_send, aga_recv, fwa_send, fwa_recv,
    rsb_send, rsb_recv, agb_send, agb_recv, fwb_send, fwb_recv, sq_send, sq_recv,
):
    w, n_ = lax.axis_index("wide"), lax.axis_index("narrow")
    core, z_lo, y = w % 2, (w // 2) % 2, w // 4
    x, z_hi = n_ % 4, n_ // 4
    z = z_hi * 2 + z_lo
    pos = (x, y, z)

    def device(x, y, z, core):
        return ((y * 2 + z % 2) * 2 + core, (z // 2) * 4 + x)

    def shifted(axis, by):
        p = [x, y, z]
        p[axis] = (p[axis] + by) % 4
        return device(*p, core)

    right = [shifted(a, 1) for a in range(3)]
    left = [shifted(a, 3) for a in range(3)]
    across = [shifted(a, 2) for a in range(3)]
    partner = device(x, y, z, 1 - core)

    barrier = pltpu.get_barrier_semaphore()
    for d in right + left + across + [partner]:
        pl.semaphore_signal(barrier, inc=1, device_id=d, device_id_type=MESH)

    def load(k, total):
        cols = pl.ds(al(k * 512, 512), 512)
        v = in_ref[:, cols]
        x0[pl.ds(0, ROWS), cols] = v
        x0[pl.ds(ROWS, PIECE - ROWS), cols] = jnp.zeros((PIECE - ROWS, 512), BF)
        return total

    lax.fori_loop(0, K // 512, load, 0)
    pl.semaphore_wait(barrier, 10)

    def remote(src, dst, send, recv, dev):
        return pltpu.make_async_remote_copy(
            src_ref=src, dst_ref=dst, send_sem=send, recv_sem=recv, device_id=dev, device_id_type=MESH
        )

    sent = []

    class Exchange:
        def __init__(self, stage, axis_no, src, dst, sems):
            self.stage, self.axis_no, self.src, self.dst, self.sems = stage, axis_no, src, dst, sems
            self.copies = {}

        def begin(self, p):
            a = AXES[p][self.axis_no]
            me = pos[a]
            send, recv, copy = self.sems
            group = []
            for k, dev in ((2, across[a]), (1, right[a]), (3, left[a])):
                c = remote(
                    self.src(p, (me + k) % 4), self.dst(p, me),
                    send.at[self.stage, p, k - 1], recv.at[self.stage, p, k - 1], dev,
                )
                c.start()
                group.append(c)
                sent.append(c)
            own = pltpu.make_async_copy(self.src(p, me), self.dst(p, me), copy.at[self.stage, p])
            own.start()
            self.copies[p] = group, own

        def arrive(self, p):
            group, own = self.copies[p]
            for c in group:
                c.wait_recv()
            own.wait()

    def tall(p, q):
        return pl.ds(al(p * THIRD + q * COL1, COL1), COL1)

    def lanes(k, size):
        return pl.ds(al(k * size, size), size)

    ins = (in_send, in_recv, in_copy)
    outs = (out_send, out_recv, out_copy)

    def plane(buf, p, q):
        return buf.at[p, q] if p == 2 else buf.at[p, :, q]

    def cube(buf, p, q):
        lane = pl.ds(128 * p, 128)
        if p == 0:
            return buf.at[:, :, q, :, lane]
        if p == 1:
            return buf.at[q, :, :, :, lane]
        return buf.at[:, q, :, :, lane]

    in1 = Exchange(0, 0, lambda p, q: x0.at[:, tall(p, q)], lambda p, q: x1.at[p, q], ins)
    in2 = Exchange(1, 1, lambda p, q: x1.at[p, :, :, lanes(q, COL2)], lambda p, q: plane(x2, p, q), ins)
    in3 = Exchange(2, 2, lambda p, q: x2p.at[p, :, :, :, lanes(q, 128)], lambda p, q: cube(x3.at[core], p, q), ins)
    for p in range(3):
        in1.begin(p)

    def square(k, total):
        v = x0[:, pl.ds(al(k * 512, 512), 512)].astype(F32)
        v = v * v
        v = (v[:, :128] + v[:, 128:256]) + (v[:, 256:384] + v[:, 384:])
        return total + ((v[:8] + v[8:16]) + (v[16:24] + v[24:]))

    sq[13] = lax.fori_loop(0, K // 512, square, jnp.zeros((8, 128), F32))
    sq_core = remote(sq.at[13], sq.at[14], sq_send.at[3, 0], sq_recv.at[3, 0], partner)
    sq_core.start()
    sent.append(sq_core)

    def iota(shape, d):
        return lax.broadcasted_iota(jnp.int32, shape, d)

    def ones_where(cond):
        return jnp.where(cond, 1.0, 0.0).astype(BF)

    def spread_matrix(shape, wide, unit, narrow):
        s, r = iota(shape, wide), iota(shape, 1 - wide)
        return ones_where((s % unit < narrow) & (r == (s // unit) * narrow + s % unit))

    for p in range(3):
        in1.arrive(p)
        in2.begin(p)
    widen = spread_matrix((COL2, 512), 1, 128, COL3)
    for p in range(3):
        in2.arrive(p)
        for h in range(2):
            rows = x2[p, pl.ds(2 * h, 2)].reshape(256, COL2)
            x2p[p, pl.ds(2 * h, 2)] = (
                jnp.dot(rows, widen, preferred_element_type=F32).astype(BF).reshape(2, 4, PIECE, 512)
            )
        in3.begin(p)
    crossing = []
    for p in range(3):
        in3.arrive(p)
        here = x3.at[core, :, :, :, :, pl.ds(128 * p, 128)]
        c = remote(here, here, core_send.at[p], core_recv.at[p], partner)
        c.start()
        crossing.append(c)
        sent.append(c)

    pack = spread_matrix((8 * ROWS, 8 * PIECE), 1, PIECE, ROWS)

    def pack_rows(owner):
        def body(k, carry):
            rows = x3[owner, k // 2, pl.ds((k % 2) * 2, 2)].reshape(8 * PIECE, 384)
            at = pl.ds(al(owner * HALF_M + k * 8 * ROWS), 8 * ROWS)
            s_all[at, :] = jnp.dot(pack, rows, preferred_element_type=F32).astype(BF)
            return carry

        lax.fori_loop(0, 8, body, 0)

    pack_rows(core)
    for c in crossing:
        c.wait_recv()
    pack_rows(1 - core)

    def turn_own():
        kk, ll = iota((OWN, 384), 0), iota((OWN, 384), 1)
        lane = ll % 128 - core * HALF3
        pick = ones_where((lane >= 0) & (lane < HALF3) & (kk == (ll // 128) * HALF3 + lane))

        def turn(j, carry):
            at = pl.ds(al(j * BLK, BLK), BLK)
            st[:, at] = lax.dot_general(pick, s_all[at, :], NT, preferred_element_type=F32).astype(BF)
            return carry

        lax.fori_loop(0, NB, turn, 0)

    def gram_block(chunk, m, t):
        slot = core * 3 * PER_PART[chunk] + m
        n = slot + 56 if chunk else jnp.where(slot < 56, slot, 104)
        i, d = n % NB, n // NB
        j = (i + d) % NB
        ri = pl.ds(al(i * BLK, BLK), BLK)
        rj = pl.ds(al(j * BLK, BLK), BLK)
        acc = lax.dot_general(s_all[ri, :], s_all[rj, :], NT, preferred_element_type=F32).astype(BF)
        t[pl.ds(al(m * 512, 512), 256), :] = acc[:, :128]
        t[pl.ds(al(m * 512 + 256, 256), 256), :] = acc[:, 128:]

    def square_begin(s):
        group = [
            remote(sq.at[4 * s], sq.at[4 * s + 1 + k], sq_send.at[s, k], sq_recv.at[s, k], dev)
            for k, dev in enumerate((right[s], left[s], across[s]))
        ]
        for c in group:
            c.start()
        sent.extend(group)
        return group

    def square_end(s, group):
        for c in group:
            c.wait_recv()
        sq[4 * s + 4] = (sq[4 * s] + sq[4 * s + 3]) + (sq[4 * s + 1] + sq[4 * s + 2])

    class Chunk:
        def __init__(self, no, t, bufs, rs, ag, fw):
            self.no, self.t, self.bufs, self.rs, self.ag, self.fw = no, t, bufs, rs, ag, fw
            self.blocks = PER_PART[no]
            self.sizes = SIZES[no]
            base = [p * self.blocks * 512 for p in range(3)]
            self.bases = [base]
            for k in range(3):
                base = [base[p] + pos[AXES[p][k]] * self.sizes[k] for p in range(3)]
                self.bases.append(base)
            self.mine = ROW0[no] + core * 3 * self.blocks * 512
            self.copies = {}

        def quarter(self, k, p, by):
            return self.bases[k][p] + ((pos[AXES[p][k]] + by) % 4) * self.sizes[k]

        def gram(self, p, start, count):
            def body(m, carry):
                gram_block(self.no, p * self.blocks + start + m, self.t)
                return carry

            lax.fori_loop(0, count, body, 0)

        def gram_far(self):
            for p in range(3):
                q = (pos[AXES[p][0]] + 2) % 4
                self.gram(p, self.blocks * q // 4, 2 + self.blocks % 4 // 2)

        def gram_near(self):
            for p in range(3):
                me = pos[AXES[p][0]]
                if self.blocks % 4:
                    self.gram(p, self.blocks // 4 + self.blocks // 2 * (me // 2), 1)
                for by in (1, 3):
                    self.gram(p, (self.blocks * ((me + by) % 4) + 2) // 4, 2)

        def gram_own(self):
            for p in range(3):
                self.gram(p, (self.blocks * pos[AXES[p][0]] + 2) // 4, 2)

        def push(self, k, p, no, off, rows):
            a = AXES[p][k]
            c = remote(
                self.t.at[pl.ds(al(off), rows), :],
                self.bufs[k].at[p, no],
                self.rs[0].at[k, p, no],
                self.rs[1].at[k, p, no],
                right[a] if no < 3 else left[a],
            )
            c.start()
            self.copies[k, p, no] = c
            sent.append(c)

        def add_rows(self, off, rows, srcs):
            step = 160 if rows % 160 == 0 else 128 if rows % 128 == 0 else rows
            t = self.t

            def body(m, carry):
                at = pl.ds(al(off + m * step), step)
                total = t[at, :].astype(F32)
                for src in srcs:
                    total = total + src[pl.ds(al(m * step), step), :].astype(F32)
                t[at, :] = total.astype(BF)
                return carry

            lax.fori_loop(0, rows // step, body, 0)

        def scatter_far(self, k):
            half = self.sizes[k] // 2
            for p in range(3):
                self.push(k, p, 0, self.quarter(k, p, 2), half)
                self.push(k, p, 3, self.quarter(k, p, 2) + half, half)

        def scatter_near(self, k):
            half = self.sizes[k] // 2
            for p in range(3):
                self.push(k, p, 1, self.quarter(k, p, 1) + half, half)
                self.push(k, p, 4, self.quarter(k, p, 3), half)

        def scatter_mid(self, k):
            half = self.sizes[k] // 2
            for p in range(3):
                self.copies[k, p, 0].wait_recv()
                self.add_rows(self.quarter(k, p, 1), half, [self.bufs[k].at[p, 0]])
                self.push(k, p, 2, self.quarter(k, p, 1), half)
                self.copies[k, p, 3].wait_recv()
                self.add_rows(self.quarter(k, p, 3) + half, half, [self.bufs[k].at[p, 3]])
                self.push(k, p, 5, self.quarter(k, p, 3) + half, half)

        def scatter_end(self, k):
            half = self.sizes[k] // 2
            for p in range(3):
                for h, one, two in ((0, 4, 2), (1, 1, 5)):
                    self.copies[k, p, one].wait_recv()
                    self.copies[k, p, two].wait_recv()
                    self.add_rows(
                        self.quarter(k, p, 0) + h * half, half, [self.bufs[k].at[p, one], self.bufs[k].at[p, two]]
                    )

        def last_begin(self):
            size = self.sizes[2]
            for p in range(3):
                a = AXES[p][2]
                for k, dev in ((2, across[a]), (1, right[a]), (3, left[a])):
                    c = remote(
                        self.t.at[pl.ds(al(self.quarter(2, p, k)), size), :],
                        self.bufs[2].at[p, k - 1],
                        self.rs[0].at[2, p, k - 1],
                        self.rs[1].at[2, p, k - 1],
                        dev,
                    )
                    c.start()
                    self.copies[2, p, k] = c
                    sent.append(c)

        def last_end(self):
            size = self.sizes[2]
            for p in range(3):
                for k in (1, 2, 3):
                    self.copies[2, p, k].wait_recv()
                off = self.bases[3][p]
                self.add_rows(off, size, [self.bufs[2].at[p, k] for k in range(3)])
                here = pl.ds(al(self.mine + off), size)
                g[here, :] = self.t[pl.ds(al(off), size), :]
                a = AXES[p][2]
                for k, dev in ((2, across[a]), (1, right[a]), (3, left[a])):
                    self.spread(2, p, k - 1, off, size, dev)

        def spread(self, k, p, no, off, rows, dev):
            here = g.at[pl.ds(al(self.mine + off), rows), :]
            c = remote(here, here, self.ag[0].at[k, p, no], self.ag[1].at[k, p, no], dev)
            c.start()
            self.copies["g", k, p, no] = c
            sent.append(c)

        def forward(self, p, no, off, rows):
            here = g.at[pl.ds(al(self.mine + off), rows), :]
            c = remote(here, here, self.fw[0].at[p, no], self.fw[1].at[p, no], partner)
            c.start()
            self.copies["f", p, no] = c
            sent.append(c)

        def got(self, k, p, *nos):
            for no in nos:
                self.copies["g", k, p, no].wait_recv()

        def gather_first_end(self):
            for p in range(3):
                self.got(2, p, 0, 1, 2)

        def gather_begin(self, k):
            half = self.sizes[k] // 2
            for p in range(3):
                own = self.quarter(k, p, 0)
                a = AXES[p][k]
                self.spread(k, p, 0, own, half, right[a])
                self.spread(k, p, 1, own + half, half, left[a])
            for p in range(3):
                own = self.quarter(k, p, 0)
                a = AXES[p][k]
                self.spread(k, p, 2, own + half, half, right[a])
                self.spread(k, p, 3, own, half, left[a])
            if k == 0:
                for p in range(3):
                    self.forward(p, 0, self.quarter(k, p, 0), 2 * half)

        def gather_mid(self, k):
            half = self.sizes[k] // 2
            for p in range(3):
                a = AXES[p][k]
                self.got(k, p, 0)
                self.spread(k, p, 4, self.quarter(k, p, 3), half, right[a])
                self.got(k, p, 1)
                self.spread(k, p, 5, self.quarter(k, p, 1) + half, half, left[a])

        def gather_end(self, k):
            size = self.sizes[k]
            for p in range(3):
                self.got(k, p, 2, 3)
                if k == 0:
                    self.forward(p, 3, self.quarter(k, p, 3), size)
                    self.forward(p, 1, self.quarter(k, p, 1), size)
            for p in range(3):
                self.got(k, p, 4, 5)
                if k == 0:
                    self.forward(p, 2, self.quarter(k, p, 2), size)

        def gather_all(self):
            for p in range(3):
                for no in range(4):
                    self.copies["f", p, no].wait_recv()

    one = Chunk(0, ta, (r1a, r2a, r3a), (rsa_send, rsa_recv), (aga_send, aga_recv), (fwa_send, fwa_recv))
    two = Chunk(1, tb, (r1b, r2b, r3b), (rsb_send, rsb_recv), (agb_send, agb_recv), (fwb_send, fwb_recv))

    one.gram_far()
    one.scatter_far(0)
    one.gram_near()
    one.scatter_near(0)
    two.gram_far()
    one.gram_own()
    one.scatter_mid(0)
    two.scatter_far(0)
    two.gram_near()
    two.scatter_near(0)
    two.gram_own()
    sq_core.wait_recv()
    sq[0] = sq[13] + sq[14]
    squares = square_begin(0)
    turn_own()
    one.scatter_end(0)
    one.scatter_far(1)
    one.scatter_near(1)
    square_end(0, squares)
    squares = square_begin(1)
    two.scatter_mid(0)
    one.scatter_mid(1)
    one.scatter_end(1)
    one.last_begin()
    two.scatter_end(0)
    two.scatter_far(1)
    two.scatter_near(1)
    one.last_end()
    square_end(1, squares)
    squares = square_begin(2)
    two.scatter_mid(1)
    one.gather_first_end()
    one.gather_begin(1)
    two.scatter_end(1)
    two.last_begin()
    one.gather_mid(1)
    one.gather_end(1)
    one.gather_begin(0)
    two.last_end()
    square_end(2, squares)
    one.gather_mid(0)
    two.gather_first_end()
    two.gather_begin(1)
    two.gather_mid(1)
    two.gather_end(1)
    two.gather_begin(0)
    one.gather_end(0)
    one.gather_all()

    factor = 0.3 * math.sqrt(M) / (jnp.sqrt(jnp.sum(sq[12], axis=(0, 1), keepdims=True)) + 1e-07)
    factor2 = factor * factor

    def cols(a_ref, i):
        return a_ref[:, pl.ds(al(i * BLK, BLK), BLK)]

    def block(slot):
        o = slot * 512
        return jnp.concatenate([g[pl.ds(al(o, 512), 256), :], g[pl.ds(al(o + 256, 256), 256), :]], axis=1)

    def slot_of(d, i):
        return d * NB + i + (4 if d >= 4 else 0)

    def band(a_ref, j, ds):
        up = [((j + NB - d) % NB, d) for d in ds]
        acc = jnp.dot(
            jnp.concatenate([cols(a_ref, i) for i, d in up], axis=1),
            jnp.concatenate([block(slot_of(d, i)) for i, d in up], axis=0),
            preferred_element_type=F32,
        )
        down = [((j + d) % NB, d) for d in ds if d > 0]
        return acc + lax.dot_general(
            jnp.concatenate([cols(a_ref, i) for i, d in down], axis=1),
            jnp.concatenate([block(slot_of(d, j)) for i, d in down], axis=1),
            NT,
            preferred_element_type=F32,
        )

    def seventh(a_ref, j):
        i = (j + 7) % NB
        slot = jnp.where(j % 7 == 6, 56, 102 + j % 7)

        @pl.when(j < 7)
        def _():
            tail[...] = lax.dot_general(cols(a_ref, i), block(slot), NT, preferred_element_type=F32)

        @pl.when(j >= 7)
        def _():
            tail[...] = jnp.dot(cols(a_ref, i), block(slot), preferred_element_type=F32)

        return tail[...]

    def bands(first_j, finish):
        def body(k, carry):
            finish(first_j + k)
            return carry

        lax.fori_loop(0, 7, body, 0)

    def first_part(j):
        yf[:, pl.ds(al(j * BLK, BLK), BLK)] = band(st, j, (0, 1, 2, 3))

    def first_rest(j):
        at = pl.ds(al(j * BLK, BLK), BLK)
        v = factor2 * (yf[:, at] + (band(st, j, (4, 5, 6)) + seventh(st, j)))
        yf[:, at] = v
        ybf[:, at] = v.astype(BF)

    def second(j):
        at = pl.ds(al(j * BLK, BLK), BLK)
        acc = (band(ybf, j, (0, 1, 2, 3)) + band(ybf, j, (4, 5, 6))) + seventh(ybf, j)
        scaled = (factor * st[:, at].astype(F32)).astype(BF).astype(F32)
        product = factor * (COEFF_B * yf[:, at] + COEFF_C * (factor2 * acc))
        u = (math.sqrt(K) * (COEFF_A * scaled + product)).astype(BF)
        for p in range(3):
            ut[pl.ds(al(p * 128 + core * HALF3), HALF3), at] = u[p * HALF3 : (p + 1) * HALF3]

    bands(0, first_part)
    two.gather_mid(0)
    bands(7, first_part)
    two.gather_end(0)
    two.gather_all()
    bands(0, first_rest)
    bands(7, first_rest)
    for p in range(3):
        ut[pl.ds(p * 128 + COL3, 128 - COL3), :] = jnp.zeros((128 - COL3, M), BF)
    bands((1 - core) * 7, second)
    halves = []
    for p in range(3):
        here = ut.at[pl.ds(al(p * 128 + core * HALF3), HALF3), lanes(1 - core, HALF_M)]
        c = remote(here, here, ut_send.at[p], ut_recv.at[p], partner)
        c.start()
        halves.append(c)
        sent.append(c)
    bands(core * 7, second)
    unpack = spread_matrix((8 * PIECE, 8 * ROWS), 0, PIECE, ROWS)
    for c in halves:
        c.wait_recv()
    for m in range(8):
        o = m * 8 * ROWS
        first_lane = o // 128 * 128
        skip = o - first_lane
        width = -(-(skip + 8 * ROWS) // 128) * 128
        v = ut[:, pl.ds(al(core * HALF_M + first_lane, 128), width)][:, skip : skip + 8 * ROWS]
        rows = lax.dot_general(unpack, v, NT, preferred_element_type=F32).astype(BF)
        y3[m // 2, pl.ds((m % 2) * 2, 2)] = rows.reshape(2, 4, PIECE, 384)

    out1 = Exchange(0, 2, lambda p, q: cube(y3, p, q), lambda p, q: y2p.at[p, :, :, :, lanes(q, 128)], outs)
    out2 = Exchange(1, 1, lambda p, q: plane(y2, p, q), lambda p, q: y1.at[p, :, :, lanes(q, COL2)], outs)
    out3 = Exchange(2, 0, lambda p, q: y1.at[p, q], lambda p, q: out_ref.at[:, tall(p, q)], outs)
    for p in range(3):
        out1.begin(p)
    narrow = spread_matrix((512, COL2), 0, 128, COL3)
    for p in range(3):
        out1.arrive(p)
        for h in range(2):
            rows = y2p[p, pl.ds(2 * h, 2)].reshape(256, 512)
            y2[p, pl.ds(2 * h, 2)] = (
                jnp.dot(rows, narrow, preferred_element_type=F32).astype(BF).reshape(2, 4, PIECE, COL2)
            )
        out2.begin(p)
    for p in range(3):
        out2.arrive(p)
        out3.begin(p)
    for p in range(3):
        out3.arrive(p)

    for c in sent:
        c.wait_send()


def local(gradient):
    vmem = pl.BlockSpec(memory_space=pltpu.VMEM)
    dma = pltpu.SemaphoreType.DMA
    padded = pl.pallas_call(
        kernel,
        out_shape=jax.ShapeDtypeStruct((PIECE, K), BF),
        in_specs=[vmem],
        out_specs=vmem,
        scratch_shapes=[
            pltpu.VMEM((PIECE, K), BF),
            pltpu.VMEM((3, 4, PIECE, COL1), BF),
            pltpu.VMEM((3, 4, 4, PIECE, COL2), BF),
            pltpu.VMEM((3, 4, 4, PIECE, 512), BF),
            pltpu.VMEM((2, 4, 4, 4, PIECE, 384), BF),
            pltpu.VMEM((M, 384), BF),
            pltpu.VMEM((OWN, M), BF),
            pltpu.VMEM((384, M), BF),
            pltpu.VMEM((4, 4, 4, PIECE, 384), BF),
            pltpu.VMEM((3, 4, 4, PIECE, 512), BF),
            pltpu.VMEM((3, 4, 4, PIECE, COL2), BF),
            pltpu.VMEM((3, 4, PIECE, COL1), BF),
            pltpu.VMEM((3 * 10 * 512, 128), BF),
            pltpu.VMEM((3 * 8 * 512, 128), BF),
            pltpu.VMEM((G_ROWS, 128), BF),
            pltpu.VMEM((3, 6, 640, 128), BF),
            pltpu.VMEM((3, 6, 160, 128), BF),
            pltpu.VMEM((3, 3, 80, 128), BF),
            pltpu.VMEM((3, 6, 512, 128), BF),
            pltpu.VMEM((3, 6, 128, 128), BF),
            pltpu.VMEM((3, 3, 64, 128), BF),
            pltpu.VMEM((15, 8, 128), F32),
            pltpu.VMEM((OWN, M), BF),
            pltpu.VMEM((OWN, M), F32),
            pltpu.VMEM((OWN, BLK), F32),
            dma((3, 3, 3)),
            dma((3, 3, 3)),
            dma((3, 3)),
            dma((3,)),
            dma((3,)),
            dma((3, 3, 3)),
            dma((3, 3, 3)),
            dma((3, 3)),
            dma((3,)),
            dma((3,)),
            dma((3, 3, 6)),
            dma((3, 3, 6)),
            dma((3, 3, 6)),
            dma((3, 3, 6)),
            dma((3, 4)),
            dma((3, 4)),
            dma((3, 3, 6)),
            dma((3, 3, 6)),
            dma((3, 3, 6)),
            dma((3, 3, 6)),
            dma((3, 4)),
            dma((3, 4)),
            dma((4, 3)),
            dma((4, 3)),
        ],
        compiler_params=pltpu.CompilerParams(
            collective_id=0, has_side_effects=True, vmem_limit_bytes=60 * 1024 * 1024
        ),
        cost_estimate=pl.CostEstimate(flops=16 * 10**9, bytes_accessed=5 * 10**6, transcendentals=0),
    )(gradient)
    return padded[:ROWS]


def solution(mesh):
    spec = P(("wide", "narrow"), None)
    return jax.shard_map(local, mesh=mesh, in_specs=(spec,), out_specs=spec, check_vma=False)
```

```python
import math

import jax
import jax.numpy as jnp
from jax import lax
from jax.experimental import pallas as pl
from jax.experimental.pallas import tpu as pltpu
from jax.sharding import PartitionSpec as P

M = 3584
K = 18432

COEFF_A = 3.4445
COEFF_B = -4.775
COEFF_C = 2.0315

MESH = pl.DeviceIdType.MESH
BF = jnp.bfloat16
F32 = jnp.float32
NT = (((1,), (1,)), ((), ()))

ROWS = 28
PIECE = 32
THIRD = K // 3
COL1 = THIRD // 4
COL2 = COL1 // 4
COL3 = COL2 // 4
CHIP = 3 * COL3
HALF_M = M // 2
AXES = ((0, 1, 2), (1, 2, 0), (2, 0, 1))

BLK = 256
NB = M // BLK
PER_PART = (10, 8)
SECOND = 3 * PER_PART[0]
SLOTS = 3 * sum(PER_PART)
SIZES = ((1280, 320, 80), (1024, 256, 64))


def al(x, m=16):
    return pl.multiple_of(x, m)


def kernel(
    in_ref, out_ref,
    x0, x1, x2, x2p, x3, s_all, st,
    ut, y3, y2p, y2, y1,
    ta, tb, g, r1a, r2a, r3a, r1b, r2b, r3b, sq, yf, ybf, yp, yr, zf, zp, zr,
    in_send, in_recv, in_copy, core_send, core_recv, out_send, out_recv, out_copy, part_send, part_recv,
    rsa_send, rsa_recv, aga_send, aga_recv, rsb_send, rsb_recv, agb_send, agb_recv, sq_send, sq_recv,
):
    w, n_ = lax.axis_index("wide"), lax.axis_index("narrow")
    core, z_lo, y = w % 2, (w // 2) % 2, w // 4
    x, z_hi = n_ % 4, n_ // 4
    z = z_hi * 2 + z_lo
    pos = (x, y, z)

    def device(x, y, z, core):
        return ((y * 2 + z % 2) * 2 + core, (z // 2) * 4 + x)

    def shifted(axis, by):
        p = [x, y, z]
        p[axis] = (p[axis] + by) % 4
        return device(*p, core)

    right = [shifted(a, 1) for a in range(3)]
    left = [shifted(a, 3) for a in range(3)]
    across = [shifted(a, 2) for a in range(3)]
    partner = device(x, y, z, 1 - core)

    barrier = pltpu.get_barrier_semaphore()
    for d in right + left + across + [partner]:
        pl.semaphore_signal(barrier, inc=1, device_id=d, device_id_type=MESH)

    def load(k, total):
        cols = pl.ds(al(k * 512, 512), 512)
        v = in_ref[:, cols]
        x0[pl.ds(0, ROWS), cols] = v
        x0[pl.ds(ROWS, PIECE - ROWS), cols] = jnp.zeros((PIECE - ROWS, 512), BF)
        return total

    lax.fori_loop(0, K // 512, load, 0)
    pl.semaphore_wait(barrier, 10)

    def remote(src, dst, send, recv, dev):
        return pltpu.make_async_remote_copy(
            src_ref=src, dst_ref=dst, send_sem=send, recv_sem=recv, device_id=dev, device_id_type=MESH
        )

    sent = []

    class Exchange:
        def __init__(self, stage, axis_no, src, dst, sems):
            self.stage, self.axis_no, self.src, self.dst, self.sems = stage, axis_no, src, dst, sems
            self.copies = {}

        def begin(self, p):
            a = AXES[p][self.axis_no]
            me = pos[a]
            send, recv, copy = self.sems
            group = []
            for k, dev in ((2, across[a]), (1, right[a]), (3, left[a])):
                c = remote(
                    self.src(p, (me + k) % 4), self.dst(p, me),
                    send.at[self.stage, p, k - 1], recv.at[self.stage, p, k - 1], dev,
                )
                c.start()
                group.append(c)
                sent.append(c)
            own = pltpu.make_async_copy(self.src(p, me), self.dst(p, me), copy.at[self.stage, p])
            own.start()
            self.copies[p] = group, own

        def arrive(self, p):
            group, own = self.copies[p]
            for c in group:
                c.wait_recv()
            own.wait()

    def tall(p, q):
        return pl.ds(al(p * THIRD + q * COL1, COL1), COL1)

    def lanes(k, size):
        return pl.ds(al(k * size, size), size)

    ins = (in_send, in_recv, in_copy)
    outs = (out_send, out_recv, out_copy)

    def plane(buf, p, q):
        return buf.at[p, q] if p == 2 else buf.at[p, :, q]

    def cube(buf, p, q):
        lane = pl.ds(128 * p, 128)
        if p == 0:
            return buf.at[:, :, q, :, lane]
        if p == 1:
            return buf.at[q, :, :, :, lane]
        return buf.at[:, q, :, :, lane]

    in1 = Exchange(0, 0, lambda p, q: x0.at[:, tall(p, q)], lambda p, q: x1.at[p, q], ins)
    in2 = Exchange(1, 1, lambda p, q: x1.at[p, :, :, lanes(q, COL2)], lambda p, q: plane(x2, p, q), ins)
    in3 = Exchange(2, 2, lambda p, q: x2p.at[p, :, :, :, lanes(q, 128)], lambda p, q: cube(x3.at[core], p, q), ins)
    for p in range(3):
        in1.begin(p)

    def square(k, total):
        v = x0[:, pl.ds(al(k * 512, 512), 512)].astype(F32)
        v = v * v
        v = (v[:, :128] + v[:, 128:256]) + (v[:, 256:384] + v[:, 384:])
        return total + ((v[:8] + v[8:16]) + (v[16:24] + v[24:]))

    sq[13] = lax.fori_loop(0, K // 512, square, jnp.zeros((8, 128), F32))
    sq_core = remote(sq.at[13], sq.at[14], sq_send.at[3, 0], sq_recv.at[3, 0], partner)
    sq_core.start()
    sent.append(sq_core)

    def iota(shape, d):
        return lax.broadcasted_iota(jnp.int32, shape, d)

    def ones_where(cond):
        return jnp.where(cond, 1.0, 0.0).astype(BF)

    def spread_matrix(shape, wide, unit, narrow):
        s, r = iota(shape, wide), iota(shape, 1 - wide)
        return ones_where((s % unit < narrow) & (r == (s // unit) * narrow + s % unit))

    for p in range(3):
        in1.arrive(p)
        in2.begin(p)
    widen = spread_matrix((COL2, 512), 1, 128, COL3)
    for p in range(3):
        in2.arrive(p)
        for h in range(2):
            rows = x2[p, pl.ds(2 * h, 2)].reshape(256, COL2)
            x2p[p, pl.ds(2 * h, 2)] = (
                jnp.dot(rows, widen, preferred_element_type=F32).astype(BF).reshape(2, 4, PIECE, 512)
            )
        in3.begin(p)
    crossing = []
    for p in range(3):
        in3.arrive(p)
        here = x3.at[core, :, :, :, :, pl.ds(128 * p, 128)]
        c = remote(here, here, core_send.at[p], core_recv.at[p], partner)
        c.start()
        crossing.append(c)
        sent.append(c)

    pack = spread_matrix((8 * ROWS, 8 * PIECE), 1, PIECE, ROWS)

    def pack_rows(owner):
        def body(k, carry):
            rows = x3[owner, k // 2, pl.ds((k % 2) * 2, 2)].reshape(8 * PIECE, 384)
            at = pl.ds(al(owner * HALF_M + k * 8 * ROWS), 8 * ROWS)
            s_all[at, :] = jnp.dot(pack, rows, preferred_element_type=F32).astype(BF)
            return carry

        lax.fori_loop(0, 8, body, 0)

    pack_rows(core)
    for c in crossing:
        c.wait_recv()
    pack_rows(1 - core)

    def turn_all():
        kk, ll = iota((CHIP, 384), 0), iota((CHIP, 384), 1)
        pick = ones_where((ll % 128 < COL3) & (kk == (ll // 128) * COL3 + ll % 128))

        def turn(j, carry):
            at = pl.ds(al(j * BLK, BLK), BLK)
            st[:, at] = lax.dot_general(pick, s_all[at, :], NT, preferred_element_type=F32).astype(BF)
            return carry

        lax.fori_loop(0, NB, turn, 0)

    def block_of(chunk, m):
        if chunk == 0:
            i = jnp.where(m < 28, m % NB, 4 * core + m - 28)
            d = jnp.where(m < 28, 2 * core + m // NB, 7)
            return i, d, jnp.where(d == 0, 0.5, 1.0)
        i = jnp.where(m < 14, m, jnp.where(m < 21, 7 * core + m - 14, (4 * core + m - 19) % NB))
        d = jnp.where(m < 14, 4 + 2 * core, jnp.where(m < 21, 5, 7))
        return i, d, jnp.where((d == 7) & ((i >= 7) | (m == 23)), 0.0, 1.0)

    def gram_block(chunk, m, t):
        i, d, scale = block_of(chunk, m)
        j = (i + d) % NB
        ri = pl.ds(al(i * BLK, BLK), BLK)
        rj = pl.ds(al(j * BLK, BLK), BLK)
        acc = lax.dot_general(s_all[ri, :], s_all[rj, :], NT, preferred_element_type=F32)
        acc = (scale * acc).astype(BF)
        t[pl.ds(al(m * 512, 512), 256), :] = acc[:, :128]
        t[pl.ds(al(m * 512 + 256, 256), 256), :] = acc[:, 128:]

    def square_begin(s):
        group = [
            remote(sq.at[4 * s], sq.at[4 * s + 1 + k], sq_send.at[s, k], sq_recv.at[s, k], dev)
            for k, dev in enumerate((right[s], left[s], across[s]))
        ]
        for c in group:
            c.start()
        sent.extend(group)
        return group

    def square_end(s, group):
        for c in group:
            c.wait_recv()
        sq[4 * s + 4] = (sq[4 * s] + sq[4 * s + 3]) + (sq[4 * s + 1] + sq[4 * s + 2])

    class Chunk:
        def __init__(self, no, t, bufs, rs, ag):
            self.no, self.t, self.bufs, self.rs, self.ag = no, t, bufs, rs, ag
            self.blocks = PER_PART[no]
            self.sizes = SIZES[no]
            base = [p * self.blocks * 512 for p in range(3)]
            self.bases = [base]
            for k in range(3):
                base = [base[p] + pos[AXES[p][k]] * self.sizes[k] for p in range(3)]
                self.bases.append(base)
            self.mine = no * SECOND * 512
            self.copies = {}

        def quarter(self, k, p, by):
            return self.bases[k][p] + ((pos[AXES[p][k]] + by) % 4) * self.sizes[k]

        def gram(self, p, start, count):
            def body(m, carry):
                gram_block(self.no, p * self.blocks + start + m, self.t)
                return carry

            lax.fori_loop(0, count, body, 0)

        def gram_far(self):
            for p in range(3):
                q = (pos[AXES[p][0]] + 2) % 4
                self.gram(p, self.blocks * q // 4, 2 + self.blocks % 4 // 2)

        def gram_near(self):
            for p in range(3):
                me = pos[AXES[p][0]]
                if self.blocks % 4:
                    self.gram(p, self.blocks // 4 + self.blocks // 2 * (me // 2), 1)
                for by in (1, 3):
                    self.gram(p, (self.blocks * ((me + by) % 4) + 2) // 4, 2)

        def gram_own(self):
            for p in range(3):
                self.gram(p, (self.blocks * pos[AXES[p][0]] + 2) // 4, 2)

        def push(self, k, p, no, off, rows):
            a = AXES[p][k]
            c = remote(
                self.t.at[pl.ds(al(off), rows), :],
                self.bufs[k].at[p, no],
                self.rs[0].at[k, p, no],
                self.rs[1].at[k, p, no],
                right[a] if no < 3 else left[a],
            )
            c.start()
            self.copies[k, p, no] = c
            sent.append(c)

        def add_rows(self, off, rows, srcs):
            step = 160 if rows % 160 == 0 else 128 if rows % 128 == 0 else rows
            t = self.t

            def body(m, carry):
                at = pl.ds(al(off + m * step), step)
                total = t[at, :].astype(F32)
                for src in srcs:
                    total = total + src[pl.ds(al(m * step), step), :].astype(F32)
                t[at, :] = total.astype(BF)
                return carry

            lax.fori_loop(0, rows // step, body, 0)

        def scatter_far(self, k):
            half = self.sizes[k] // 2
            for p in range(3):
                self.push(k, p, 0, self.quarter(k, p, 2), half)
                self.push(k, p, 3, self.quarter(k, p, 2) + half, half)

        def scatter_near(self, k):
            half = self.sizes[k] // 2
            for p in range(3):
                self.push(k, p, 1, self.quarter(k, p, 1) + half, half)
                self.push(k, p, 4, self.quarter(k, p, 3), half)

        def scatter_mid(self, k):
            half = self.sizes[k] // 2
            for p in range(3):
                self.copies[k, p, 0].wait_recv()
                self.add_rows(self.quarter(k, p, 1), half, [self.bufs[k].at[p, 0]])
                self.push(k, p, 2, self.quarter(k, p, 1), half)
                self.copies[k, p, 3].wait_recv()
                self.add_rows(self.quarter(k, p, 3) + half, half, [self.bufs[k].at[p, 3]])
                self.push(k, p, 5, self.quarter(k, p, 3) + half, half)

        def scatter_end(self, k):
            half = self.sizes[k] // 2
            for p in range(3):
                for h, one, two in ((0, 4, 2), (1, 1, 5)):
                    self.copies[k, p, one].wait_recv()
                    self.copies[k, p, two].wait_recv()
                    self.add_rows(
                        self.quarter(k, p, 0) + h * half, half, [self.bufs[k].at[p, one], self.bufs[k].at[p, two]]
                    )

        def last_begin(self):
            size = self.sizes[2]
            for p in range(3):
                a = AXES[p][2]
                for k, dev in ((2, across[a]), (1, right[a]), (3, left[a])):
                    c = remote(
                        self.t.at[pl.ds(al(self.quarter(2, p, k)), size), :],
                        self.bufs[2].at[p, k - 1],
                        self.rs[0].at[2, p, k - 1],
                        self.rs[1].at[2, p, k - 1],
                        dev,
                    )
                    c.start()
                    self.copies[2, p, k] = c
                    sent.append(c)

        def last_end(self):
            size = self.sizes[2]
            for p in range(3):
                for k in (1, 2, 3):
                    self.copies[2, p, k].wait_recv()
                off = self.bases[3][p]
                self.add_rows(off, size, [self.bufs[2].at[p, k] for k in range(3)])
                here = pl.ds(al(self.mine + off), size)
                g[here, :] = self.t[pl.ds(al(off), size), :]
                a = AXES[p][2]
                for k, dev in ((2, across[a]), (1, right[a]), (3, left[a])):
                    self.spread(2, p, k - 1, off, size, dev)

        def spread(self, k, p, no, off, rows, dev):
            here = g.at[pl.ds(al(self.mine + off), rows), :]
            c = remote(here, here, self.ag[0].at[k, p, no], self.ag[1].at[k, p, no], dev)
            c.start()
            self.copies["g", k, p, no] = c
            sent.append(c)

        def got(self, k, p, *nos):
            for no in nos:
                self.copies["g", k, p, no].wait_recv()

        def gather_first_end(self):
            for p in range(3):
                self.got(2, p, 0, 1, 2)

        def gather_begin(self, k):
            half = self.sizes[k] // 2
            for p in range(3):
                own = self.quarter(k, p, 0)
                a = AXES[p][k]
                self.spread(k, p, 0, own, half, right[a])
                self.spread(k, p, 1, own + half, half, left[a])
            for p in range(3):
                own = self.quarter(k, p, 0)
                a = AXES[p][k]
                self.spread(k, p, 2, own + half, half, right[a])
                self.spread(k, p, 3, own, half, left[a])

        def gather_mid(self, k):
            half = self.sizes[k] // 2
            for p in range(3):
                a = AXES[p][k]
                self.got(k, p, 0)
                self.spread(k, p, 4, self.quarter(k, p, 3), half, right[a])
                self.got(k, p, 1)
                self.spread(k, p, 5, self.quarter(k, p, 1) + half, half, left[a])

        def gather_end(self, k):
            for p in range(3):
                self.got(k, p, 2, 3, 4, 5)

    one = Chunk(0, ta, (r1a, r2a, r3a), (rsa_send, rsa_recv), (aga_send, aga_recv))
    two = Chunk(1, tb, (r1b, r2b, r3b), (rsb_send, rsb_recv), (agb_send, agb_recv))

    one.gram_far()
    one.scatter_far(0)
    one.gram_near()
    one.scatter_near(0)
    two.gram_far()
    one.gram_own()
    one.scatter_mid(0)
    two.scatter_far(0)
    two.gram_near()
    two.scatter_near(0)
    two.gram_own()
    sq_core.wait_recv()
    sq[0] = sq[13] + sq[14]
    squares = square_begin(0)
    turn_all()
    one.scatter_end(0)
    one.scatter_far(1)
    one.scatter_near(1)
    square_end(0, squares)
    squares = square_begin(1)
    two.scatter_mid(0)
    one.scatter_mid(1)
    one.scatter_end(1)
    one.last_begin()
    two.scatter_end(0)
    two.scatter_far(1)
    two.scatter_near(1)
    one.last_end()
    square_end(1, squares)
    squares = square_begin(2)
    two.scatter_mid(1)
    one.gather_first_end()
    one.gather_begin(1)
    two.scatter_end(1)
    two.last_begin()
    one.gather_mid(1)
    one.gather_end(1)
    one.gather_begin(0)
    two.last_end()
    square_end(2, squares)
    one.gather_mid(0)
    two.gather_first_end()
    two.gather_begin(1)
    two.gather_mid(1)
    two.gather_end(1)
    two.gather_begin(0)
    one.gather_end(0)

    factor = 0.3 * math.sqrt(M) / (jnp.sqrt(jnp.sum(sq[12], axis=(0, 1), keepdims=True)) + 1e-07)
    factor2 = factor * factor

    def cols(a_ref, i):
        return a_ref[:, pl.ds(al(i * BLK, BLK), BLK)]

    def block(slot):
        o = slot * 512
        return jnp.concatenate([g[pl.ds(al(o, 512), 256), :], g[pl.ds(al(o + 256, 256), 256), :]], axis=1)

    def band(a_ref, j, ds):
        def straight(d, first):
            i = (j + NB - d) % NB
            return cols(a_ref, i), block(first + i)

        def turned(d, first):
            return cols(a_ref, (j + d) % NB), block(first + j)

        a, b = zip(*[straight(*e) for e in ds])
        acc = jnp.dot(jnp.concatenate(a, axis=1), jnp.concatenate(b, axis=0), preferred_element_type=F32)
        a, b = zip(*[turned(*e) for e in ds])
        return acc + lax.dot_general(
            jnp.concatenate(a, axis=1), jnp.concatenate(b, axis=1), NT, preferred_element_type=F32
        )

    whole_one = ((2 * core, 0), (2 * core + 1, NB))
    whole_two = ((2 * core + 4, SECOND),)

    def single(acc_ref, a_ref, chunk, m):
        i, d, _ = block_of(chunk, m)
        j = (i + d) % NB
        b = block(chunk * SECOND + m)
        acc_ref[:, pl.ds(al(j * BLK, BLK), BLK)] += jnp.dot(cols(a_ref, i), b, preferred_element_type=F32)
        acc_ref[:, pl.ds(al(i * BLK, BLK), BLK)] += lax.dot_general(
            cols(a_ref, j), b, NT, preferred_element_type=F32
        )

    def loop(first_k, last_k, f):
        def body(k, carry):
            f(k)
            return carry

        lax.fori_loop(first_k, last_k, body, 0)

    def band_at(j):
        return pl.ds(al(j * BLK, BLK), BLK)

    def to_partner(no, src, dst):
        c = remote(src, dst, part_send.at[no], part_recv.at[no], partner)
        c.start()
        sent.append(c)
        return c

    def y_one(j):
        yf[:, band_at(j)] = band(st, j, whole_one)

    loop(0, 7, y_one)
    two.gather_mid(0)
    loop(7, NB, y_one)
    loop(28, 30, lambda m: single(yf, st, 0, m))
    two.gather_end(0)
    loop(14, 23, lambda m: single(yf, st, 1, m))

    def y_two(j):
        v = yf[:, band_at(j)] + band(st, j, whole_two)
        yf[:, band_at(j)] = v
        yp[:, band_at(j)] = v.astype(BF)

    shares = []
    for h in range(2):
        loop(h * 7, h * 7 + 7, y_two)
        here = pl.ds(h * HALF_M, HALF_M)
        shares.append(to_partner(h, yp.at[:, here], yr.at[:, here]))

    factor = 0.3 * math.sqrt(M) / (jnp.sqrt(jnp.sum(sq[12], axis=(0, 1), keepdims=True)) + 1e-07)
    factor2 = factor * factor
    zf[...] = jnp.zeros((CHIP, M), F32)

    def y_sum(j):
        v = factor2 * (yf[:, band_at(j)] + yr[:, band_at(j)].astype(F32))
        yf[:, band_at(j)] = v
        ybf[:, band_at(j)] = v.astype(BF)

    for h in range(2):
        shares[h].wait_recv()
        loop(h * 7, h * 7 + 7, y_sum)

    loop(28, 30, lambda m: single(zf, ybf, 0, m))
    loop(14, 23, lambda m: single(zf, ybf, 1, m))

    def z_band(j):
        return factor2 * (zf[:, band_at(j)] + band(ybf, j, whole_one + whole_two))

    def z_theirs(k):
        zp[:, band_at(k)] = z_band((1 - core) * 7 + k).astype(BF)

    loop(0, 7, z_theirs)
    share = to_partner(2, zp, zr)

    def z_mine(k):
        zf[:, band_at(core * 7 + k)] = z_band(core * 7 + k)

    loop(0, 7, z_mine)
    share.wait_recv()
    for p in range(3):
        ut[pl.ds(p * 128 + COL3, 128 - COL3), :] = jnp.zeros((128 - COL3, HALF_M), BF)

    def finish(k):
        at = band_at(core * 7 + k)
        scaled = (factor * st[:, at].astype(F32)).astype(BF).astype(F32)
        product = factor * (COEFF_B * yf[:, at] + COEFF_C * (zf[:, at] + zr[:, band_at(k)].astype(F32)))
        u = (math.sqrt(K) * (COEFF_A * scaled + product)).astype(BF)
        for p in range(3):
            ut[pl.ds(p * 128, COL3), band_at(k)] = u[p * COL3 : (p + 1) * COL3]

    loop(0, 7, finish)

    unpack = spread_matrix((8 * PIECE, 8 * ROWS), 0, PIECE, ROWS)
    for m in range(8):
        o = m * 8 * ROWS
        first_lane = o // 128 * 128
        skip = o - first_lane
        width = -(-(skip + 8 * ROWS) // 128) * 128
        v = ut[:, pl.ds(first_lane, width)][:, skip : skip + 8 * ROWS]
        rows = lax.dot_general(unpack, v, NT, preferred_element_type=F32).astype(BF)
        y3[m // 2, pl.ds((m % 2) * 2, 2)] = rows.reshape(2, 4, PIECE, 384)

    out1 = Exchange(0, 2, lambda p, q: cube(y3, p, q), lambda p, q: y2p.at[p, :, :, :, lanes(q, 128)], outs)
    out2 = Exchange(1, 1, lambda p, q: plane(y2, p, q), lambda p, q: y1.at[p, :, :, lanes(q, COL2)], outs)
    out3 = Exchange(2, 0, lambda p, q: y1.at[p, q], lambda p, q: out_ref.at[:, tall(p, q)], outs)
    for p in range(3):
        out1.begin(p)
    narrow = spread_matrix((512, COL2), 0, 128, COL3)
    for p in range(3):
        out1.arrive(p)
        for h in range(2):
            rows = y2p[p, pl.ds(2 * h, 2)].reshape(256, 512)
            y2[p, pl.ds(2 * h, 2)] = (
                jnp.dot(rows, narrow, preferred_element_type=F32).astype(BF).reshape(2, 4, PIECE, COL2)
            )
        out2.begin(p)
    for p in range(3):
        out2.arrive(p)
        out3.begin(p)
    for p in range(3):
        out3.arrive(p)

    for c in sent:
        c.wait_send()


def local(gradient):
    vmem = pl.BlockSpec(memory_space=pltpu.VMEM)
    dma = pltpu.SemaphoreType.DMA
    padded = pl.pallas_call(
        kernel,
        out_shape=jax.ShapeDtypeStruct((PIECE, K), BF),
        in_specs=[vmem],
        out_specs=vmem,
        scratch_shapes=[
            pltpu.VMEM((PIECE, K), BF),
            pltpu.VMEM((3, 4, PIECE, COL1), BF),
            pltpu.VMEM((3, 4, 4, PIECE, COL2), BF),
            pltpu.VMEM((3, 4, 4, PIECE, 512), BF),
            pltpu.VMEM((2, 4, 4, 4, PIECE, 384), BF),
            pltpu.VMEM((M, 384), BF),
            pltpu.VMEM((CHIP, M), BF),
            pltpu.VMEM((384, HALF_M), BF),
            pltpu.VMEM((4, 4, 4, PIECE, 384), BF),
            pltpu.VMEM((3, 4, 4, PIECE, 512), BF),
            pltpu.VMEM((3, 4, 4, PIECE, COL2), BF),
            pltpu.VMEM((3, 4, PIECE, COL1), BF),
            pltpu.VMEM((3 * 10 * 512, 128), BF),
            pltpu.VMEM((3 * 8 * 512, 128), BF),
            pltpu.VMEM((SLOTS * 512, 128), BF),
            pltpu.VMEM((3, 6, 640, 128), BF),
            pltpu.VMEM((3, 6, 160, 128), BF),
            pltpu.VMEM((3, 3, 80, 128), BF),
            pltpu.VMEM((3, 6, 512, 128), BF),
            pltpu.VMEM((3, 6, 128, 128), BF),
            pltpu.VMEM((3, 3, 64, 128), BF),
            pltpu.VMEM((15, 8, 128), F32),
            pltpu.VMEM((CHIP, M), F32),
            pltpu.VMEM((CHIP, M), BF),
            pltpu.VMEM((CHIP, M), BF),
            pltpu.VMEM((CHIP, M), BF),
            pltpu.VMEM((CHIP, M), F32),
            pltpu.VMEM((CHIP, HALF_M), BF),
            pltpu.VMEM((CHIP, HALF_M), BF),
            dma((3, 3, 3)),
            dma((3, 3, 3)),
            dma((3, 3)),
            dma((3,)),
            dma((3,)),
            dma((3, 3, 3)),
            dma((3, 3, 3)),
            dma((3, 3)),
            dma((3,)),
            dma((3,)),
            dma((3, 3, 6)),
            dma((3, 3, 6)),
            dma((3, 3, 6)),
            dma((3, 3, 6)),
            dma((3, 3, 6)),
            dma((3, 3, 6)),
            dma((3, 3, 6)),
            dma((3, 3, 6)),
            dma((4, 3)),
            dma((4, 3)),
        ],
        compiler_params=pltpu.CompilerParams(
            collective_id=0, has_side_effects=True, vmem_limit_bytes=60 * 1024 * 1024
        ),
        cost_estimate=pl.CostEstimate(flops=16 * 10**9, bytes_accessed=5 * 10**6, transcendentals=0),
    )(gradient)
    return padded[:ROWS]


def solution(mesh):
    spec = P(("wide", "narrow"), None)
    return jax.shard_map(local, mesh=mesh, in_specs=(spec,), out_specs=spec, check_vma=False)
```

```python
import math

import jax
import jax.numpy as jnp
from jax import lax
from jax.experimental import pallas as pl
from jax.experimental.pallas import tpu as pltpu
from jax.sharding import PartitionSpec as P

M = 3584
K = 18432

COEFF_A = 3.4445
COEFF_B = -4.775
COEFF_C = 2.0315

MESH = pl.DeviceIdType.MESH
BF = jnp.bfloat16
F32 = jnp.float32
NT = (((1,), (1,)), ((), ()))

ROWS = 28
PIECE = 32
THIRD = K // 3
COL1 = THIRD // 4
COL2 = COL1 // 4
COL3 = COL2 // 4
CHIP = 3 * COL3
HALF_M = M // 2
AXES = ((0, 1, 2), (1, 2, 0), (2, 0, 1))

BLK = 256
NB = M // BLK
PER_PART = (10, 8)
SECOND = 3 * PER_PART[0]
SLOTS = 3 * sum(PER_PART)
QUARTER = (1280, 1024)
SHARD = (80, 64)


def al(x, m=16):
    return pl.multiple_of(x, m)


def kernel(
    in_ref, out_ref,
    x0, x1, x1q, x2, x2p, x3, s_all, st,
    ut, y2p, y1, y0,
    ta, tb, g, r1a, r2a, r1b, r2b, sq, yf, ybf, yp, yr, zf, zp, zr,
    in_send, in_recv, in_copy, core_send, core_recv, out_send, out_recv, out_copy, part_send, part_recv,
    rsa_send, rsa_recv, rsa_plane_send, rsa_plane_recv, aga_send, aga_recv, aga_plane_send, aga_plane_recv,
    rsb_send, rsb_recv, rsb_plane_send, rsb_plane_recv, agb_send, agb_recv, agb_plane_send, agb_plane_recv,
    sq_send, sq_recv,
):
    w, n_ = lax.axis_index("wide"), lax.axis_index("narrow")
    core, z_lo, y = w % 2, (w // 2) % 2, w // 4
    x, z_hi = n_ % 4, n_ // 4
    z = z_hi * 2 + z_lo
    pos = (x, y, z)

    def device(x, y, z, core):
        return ((y * 2 + z % 2) * 2 + core, (z // 2) * 4 + x)

    def shifted(axis, by):
        p = [x, y, z]
        p[axis] = (p[axis] + by) % 4
        return device(*p, core)

    right = [shifted(a, 1) for a in range(3)]
    left = [shifted(a, 3) for a in range(3)]
    across = [shifted(a, 2) for a in range(3)]
    partner = device(x, y, z, 1 - core)

    def in_plane(a, b, by, bz):
        p = [x, y, z]
        p[a] = (p[a] + by) % 4
        p[b] = (p[b] + bz) % 4
        return device(*p, core)

    diagonal = [
        in_plane(a, b, by, bz) for a, b in ((0, 1), (1, 2), (2, 0)) for by in (1, 2, 3) for bz in (1, 2, 3)
    ]

    barrier = pltpu.get_barrier_semaphore()
    for d in right + left + across + diagonal + [partner]:
        pl.semaphore_signal(barrier, inc=1, device_id=d, device_id_type=MESH)

    def load(k, carry):
        p, q, c = k // 12, k // 3 % 4, k % 3
        cols = pl.ds(al(c * 512, 512), 512)
        x0[p, q, pl.ds(0, ROWS), cols] = in_ref[:, pl.ds(al(k * 512, 512), 512)]
        x0[p, q, pl.ds(ROWS, PIECE - ROWS), cols] = jnp.zeros((PIECE - ROWS, 512), BF)
        return carry

    lax.fori_loop(0, K // 512, load, 0)
    pl.semaphore_wait(barrier, 37)

    def remote(src, dst, send, recv, dev):
        return pltpu.make_async_remote_copy(
            src_ref=src, dst_ref=dst, send_sem=send, recv_sem=recv, device_id=dev, device_id_type=MESH
        )

    sent = []

    class Exchange:
        def __init__(self, stage, axis_no, src, dst, sems):
            self.stage, self.axis_no, self.src, self.dst, self.sems = stage, axis_no, src, dst, sems
            self.copies = {}

        def begin(self, p):
            a = AXES[p][self.axis_no]
            me = pos[a]
            send, recv, copy = self.sems
            group = []
            for k, dev in ((2, across[a]), (1, right[a]), (3, left[a])):
                c = remote(
                    self.src(p, (me + k) % 4), self.dst(p, me),
                    send.at[self.stage, p, k - 1], recv.at[self.stage, p, k - 1], dev,
                )
                c.start()
                group.append(c)
                sent.append(c)
            own = pltpu.make_async_copy(self.src(p, me), self.dst(p, me), copy.at[self.stage, p])
            own.start()
            self.copies[p] = group, own

        def arrive(self, p):
            group, own = self.copies[p]
            for c in group:
                c.wait_recv()
            own.wait()

    ins = (in_send, in_recv, in_copy)
    outs = (out_send, out_recv, out_copy)

    def plane(p, k):
        return (k, slice(None)) if p == 2 else (slice(None), k)

    in1 = Exchange(0, 0, lambda p, q: x0.at[p, q], lambda p, q: x1.at[p, q], ins)
    in2 = Exchange(1, 1, lambda p, q: x1q.at[p, q], lambda p, q: x2.at[p, q], ins)
    in3 = Exchange(2, 2, lambda p, q: x2p.at[p, q], lambda p, q: x3.at[core, p, q], ins)
    for p in range(3):
        in1.begin(p)

    def square(k, total):
        v = x0[k // 12, k // 3 % 4, :, pl.ds(al(k % 3 * 512, 512), 512)].astype(F32)
        v = v * v
        v = (v[:, :128] + v[:, 128:256]) + (v[:, 256:384] + v[:, 384:])
        return total + ((v[:8] + v[8:16]) + (v[16:24] + v[24:]))

    sq[13] = lax.fori_loop(0, K // 512, square, jnp.zeros((8, 128), F32))
    sq_core = remote(sq.at[13], sq.at[14], sq_send.at[3, 0], sq_recv.at[3, 0], partner)
    sq_core.start()
    sent.append(sq_core)

    def iota(shape, d):
        return lax.broadcasted_iota(jnp.int32, shape, d)

    def ones_where(cond):
        return jnp.where(cond, 1.0, 0.0).astype(BF)

    def spread_matrix(shape, wide, unit, narrow):
        s, r = iota(shape, wide), iota(shape, 1 - wide)
        return ones_where((s % unit < narrow) & (r == (s // unit) * narrow + s % unit))

    for p in range(3):
        in1.arrive(p)
        for a in range(4):
            for q in range(4):
                x1q[p, q, a] = x1[p, a, :, q * COL2 : (q + 1) * COL2]
        in2.begin(p)
    widen = spread_matrix((COL2, 512), 1, 128, COL3)
    for p in range(3):
        in2.arrive(p)
        for a in range(4):
            rows = jnp.dot(x2[p, a].reshape(4 * PIECE, COL2), widen, preferred_element_type=F32).astype(BF)
            for q in range(4):
                x2p[(p, q) + plane(p, a)] = rows[:, q * 128 : (q + 1) * 128].reshape(4, PIECE, 128)
        in3.begin(p)
    crossing = []
    for p in range(3):
        in3.arrive(p)
        here = x3.at[core, p]
        c = remote(here, here, core_send.at[p], core_recv.at[p], partner)
        c.start()
        crossing.append(c)
        sent.append(c)

    pack = spread_matrix((8 * ROWS, 8 * PIECE), 1, PIECE, ROWS)

    def pack_rows(owner):
        def body(k, carry):
            x, y0, group = k // 2, k % 2 * 2, [[], [], []]
            for y in (y0, y0 + 1):
                for z in range(4):
                    group[0].append(x3[owner, 0, z, x, y])
                    group[1].append(x3[owner, 1, x, y, z])
                    group[2].append(x3[owner, 2, y, x, z])
            rows = jnp.concatenate([jnp.concatenate(e, axis=0) for e in group], axis=1)
            at = pl.ds(al(owner * HALF_M + k * 8 * ROWS), 8 * ROWS)
            s_all[at, :] = jnp.dot(pack, rows, preferred_element_type=F32).astype(BF)
            return carry

        lax.fori_loop(0, 8, body, 0)

    pack_rows(core)
    for c in crossing:
        c.wait_recv()
    pack_rows(1 - core)

    def turn_all():
        kk, ll = iota((CHIP, 384), 0), iota((CHIP, 384), 1)
        pick = ones_where((ll % 128 < COL3) & (kk == (ll // 128) * COL3 + ll % 128))

        def turn(j, carry):
            at = pl.ds(al(j * BLK, BLK), BLK)
            st[:, at] = lax.dot_general(pick, s_all[at, :], NT, preferred_element_type=F32).astype(BF)
            return carry

        lax.fori_loop(0, NB, turn, 0)

    def block_of(chunk, m):
        if chunk == 0:
            i = jnp.where(m < 28, m % NB, 4 * core + m - 28)
            d = jnp.where(m < 28, 2 * core + m // NB, 7)
            return i, d, jnp.where(d == 0, 0.5, 1.0)
        i = jnp.where(m < 14, m, jnp.where(m < 21, 7 * core + m - 14, (4 * core + m - 19) % NB))
        d = jnp.where(m < 14, 4 + 2 * core, jnp.where(m < 21, 5, 7))
        return i, d, jnp.where((d == 7) & ((i >= 7) | (m == 23)), 0.0, 1.0)

    def gram_block(chunk, m, t):
        i, d, scale = block_of(chunk, m)
        j = (i + d) % NB
        ri = pl.ds(al(i * BLK, BLK), BLK)
        rj = pl.ds(al(j * BLK, BLK), BLK)
        acc = lax.dot_general(s_all[ri, :], s_all[rj, :], NT, preferred_element_type=F32)
        acc = (scale * acc).astype(BF)
        t[pl.ds(al(m * 512, 512), 256), :] = acc[:, :128]
        t[pl.ds(al(m * 512 + 256, 256), 256), :] = acc[:, 128:]

    def square_begin(s):
        group = [
            remote(sq.at[4 * s], sq.at[4 * s + 1 + k], sq_send.at[s, k], sq_recv.at[s, k], dev)
            for k, dev in enumerate((right[s], left[s], across[s]))
        ]
        for c in group:
            c.start()
        sent.extend(group)
        return group

    def square_end(s, group):
        for c in group:
            c.wait_recv()
        sq[4 * s + 4] = (sq[4 * s] + sq[4 * s + 3]) + (sq[4 * s + 1] + sq[4 * s + 2])

    class Chunk:
        def __init__(self, no, t, bufs, rs, ag):
            self.no, self.t, self.bufs, self.rs, self.ag = no, t, bufs, rs, ag
            self.blocks = PER_PART[no]
            self.size, self.shard = QUARTER[no], SHARD[no]
            self.base = [p * self.blocks * 512 for p in range(3)]
            self.own = [self.quarter(p, 0) + self.place(p, 0) for p in range(3)]
            self.mine = no * SECOND * 512
            self.copies = {}

        def quarter(self, p, by):
            return self.base[p] + ((pos[AXES[p][0]] + by) % 4) * self.size

        def place(self, p, k):
            _, a, b = AXES[p]
            return ((pos[a] + k // 4) % 4 * 4 + (pos[b] + k % 4) % 4) * self.shard

        def gram(self, p, start, count):
            def body(m, carry):
                gram_block(self.no, p * self.blocks + start + m, self.t)
                return carry

            lax.fori_loop(0, count, body, 0)

        def gram_far(self):
            for p in range(3):
                q = (pos[AXES[p][0]] + 2) % 4
                self.gram(p, self.blocks * q // 4, 2 + self.blocks % 4 // 2)

        def gram_near(self):
            for p in range(3):
                me = pos[AXES[p][0]]
                if self.blocks % 4:
                    self.gram(p, self.blocks // 4 + self.blocks // 2 * (me // 2), 1)
                for by in (1, 3):
                    self.gram(p, (self.blocks * ((me + by) % 4) + 2) // 4, 2)

        def gram_own(self):
            for p in range(3):
                self.gram(p, (self.blocks * pos[AXES[p][0]] + 2) // 4, 2)

        def push(self, p, no, off, rows):
            a = AXES[p][0]
            c = remote(
                self.t.at[pl.ds(al(off), rows), :],
                self.bufs[0].at[p, no],
                self.rs[0].at[p, no],
                self.rs[1].at[p, no],
                right[a] if no < 3 else left[a],
            )
            c.start()
            self.copies[p, no] = c
            sent.append(c)

        def add_rows(self, off, rows, srcs):
            step = 160 if rows % 160 == 0 else 128 if rows % 128 == 0 else rows
            t = self.t

            def body(m, carry):
                at = pl.ds(al(off + m * step), step)
                total = t[at, :].astype(F32)
                for src in srcs:
                    total = total + src[pl.ds(al(m * step), step), :].astype(F32)
                t[at, :] = total.astype(BF)
                return carry

            lax.fori_loop(0, rows // step, body, 0)

        def scatter_far(self):
            half = self.size // 2
            for p in range(3):
                self.push(p, 0, self.quarter(p, 2), half)
                self.push(p, 3, self.quarter(p, 2) + half, half)

        def scatter_near(self):
            half = self.size // 2
            for p in range(3):
                self.push(p, 1, self.quarter(p, 1) + half, half)
                self.push(p, 4, self.quarter(p, 3), half)

        def scatter_mid(self):
            half = self.size // 2
            for p in range(3):
                self.copies[p, 0].wait_recv()
                self.add_rows(self.quarter(p, 1), half, [self.bufs[0].at[p, 0]])
                self.push(p, 2, self.quarter(p, 1), half)
                self.copies[p, 3].wait_recv()
                self.add_rows(self.quarter(p, 3) + half, half, [self.bufs[0].at[p, 3]])
                self.push(p, 5, self.quarter(p, 3) + half, half)

        def scatter_end(self):
            half = self.size // 2
            for p in range(3):
                for h, one, two in ((0, 4, 2), (1, 1, 5)):
                    self.copies[p, one].wait_recv()
                    self.copies[p, two].wait_recv()
                    self.add_rows(
                        self.quarter(p, 0) + h * half, half, [self.bufs[0].at[p, one], self.bufs[0].at[p, two]]
                    )

        def to_plane(self, p, k):
            _, a, b = AXES[p]
            return remote(
                self.t.at[pl.ds(al(self.quarter(p, 0) + self.place(p, k)), self.shard), :],
                self.bufs[1].at[p, k - 1],
                self.rs[2].at[p, k - 1],
                self.rs[3].at[p, k - 1],
                in_plane(a, b, k // 4, k % 4),
            )

        def from_plane(self, p, k):
            _, a, b = AXES[p]
            here = g.at[pl.ds(al(self.mine + self.own[p]), self.shard), :]
            return remote(here, here, self.ag[2].at[p, k - 1], self.ag[3].at[p, k - 1], in_plane(a, b, k // 4, k % 4))

        def over_plane(self, p, f):
            def body(k, carry):
                f(p, k)
                return carry

            lax.fori_loop(1, 16, body, 0)

        def plane_begin(self):
            for p in range(3):
                self.over_plane(p, lambda p, k: self.to_plane(p, k).start())

        def plane_end(self):
            for p in range(3):
                self.over_plane(p, lambda p, k: self.to_plane(p, k).wait_recv())
                self.add_rows(self.own[p], self.shard, [self.bufs[1].at[p, k] for k in range(15)])
                here = pl.ds(al(self.mine + self.own[p]), self.shard)
                g[here, :] = self.t[pl.ds(al(self.own[p]), self.shard), :]
                self.over_plane(p, lambda p, k: self.from_plane(p, k).start())

        def plane_gathered(self):
            for p in range(3):
                self.over_plane(p, lambda p, k: self.from_plane(p, k).wait_recv())

        def plane_sent(self):
            for p in range(3):
                self.over_plane(p, lambda p, k: self.to_plane(p, k).wait_send())
                self.over_plane(p, lambda p, k: self.from_plane(p, k).wait_send())

        def spread(self, p, no, off, rows, dev):
            here = g.at[pl.ds(al(self.mine + off), rows), :]
            c = remote(here, here, self.ag[0].at[p, no], self.ag[1].at[p, no], dev)
            c.start()
            self.copies["g", p, no] = c
            sent.append(c)

        def got(self, p, *nos):
            for no in nos:
                self.copies["g", p, no].wait_recv()

        def gather_begin(self):
            half = self.size // 2
            for p in range(3):
                own = self.quarter(p, 0)
                a = AXES[p][0]
                self.spread(p, 0, own, half, right[a])
                self.spread(p, 1, own + half, half, left[a])
            for p in range(3):
                own = self.quarter(p, 0)
                a = AXES[p][0]
                self.spread(p, 2, own + half, half, right[a])
                self.spread(p, 3, own, half, left[a])

        def gather_mid(self):
            half = self.size // 2
            for p in range(3):
                a = AXES[p][0]
                self.got(p, 0)
                self.spread(p, 4, self.quarter(p, 3), half, right[a])
                self.got(p, 1)
                self.spread(p, 5, self.quarter(p, 1) + half, half, left[a])

        def gather_end(self):
            for p in range(3):
                self.got(p, 2, 3, 4, 5)

    one = Chunk(
        0, ta, (r1a, r2a), (rsa_send, rsa_recv, rsa_plane_send, rsa_plane_recv),
        (aga_send, aga_recv, aga_plane_send, aga_plane_recv),
    )
    two = Chunk(
        1, tb, (r1b, r2b), (rsb_send, rsb_recv, rsb_plane_send, rsb_plane_recv),
        (agb_send, agb_recv, agb_plane_send, agb_plane_recv),
    )

    one.gram_far()
    one.scatter_far()
    one.gram_near()
    one.scatter_near()
    two.gram_far()
    one.gram_own()
    one.scatter_mid()
    two.scatter_far()
    two.gram_near()
    two.scatter_near()
    two.gram_own()
    sq_core.wait_recv()
    sq[0] = sq[13] + sq[14]
    squares = square_begin(0)
    turn_all()
    one.scatter_end()
    one.plane_begin()
    square_end(0, squares)
    squares = square_begin(1)
    two.scatter_mid()
    one.plane_end()
    square_end(1, squares)
    squares = square_begin(2)
    two.scatter_end()
    two.plane_begin()
    one.plane_gathered()
    one.gather_begin()
    two.plane_end()
    square_end(2, squares)
    one.gather_mid()
    two.plane_gathered()
    two.gather_begin()
    one.gather_end()

    def cols(a_ref, i):
        return a_ref[:, pl.ds(al(i * BLK, BLK), BLK)]

    def block(slot):
        o = slot * 512
        return jnp.concatenate([g[pl.ds(al(o, 512), 256), :], g[pl.ds(al(o + 256, 256), 256), :]], axis=1)

    def band(a_ref, j, ds):
        def straight(d, first):
            i = (j + NB - d) % NB
            return cols(a_ref, i), block(first + i)

        def turned(d, first):
            return cols(a_ref, (j + d) % NB), block(first + j)

        a, b = zip(*[straight(*e) for e in ds])
        acc = jnp.dot(jnp.concatenate(a, axis=1), jnp.concatenate(b, axis=0), preferred_element_type=F32)
        a, b = zip(*[turned(*e) for e in ds])
        return acc + lax.dot_general(
            jnp.concatenate(a, axis=1), jnp.concatenate(b, axis=1), NT, preferred_element_type=F32
        )

    whole_one = ((2 * core, 0), (2 * core + 1, NB))
    whole_two = ((2 * core + 4, SECOND),)

    def single(acc_ref, a_ref, chunk, m):
        i, d, _ = block_of(chunk, m)
        j = (i + d) % NB
        b = block(chunk * SECOND + m)
        acc_ref[:, pl.ds(al(j * BLK, BLK), BLK)] += jnp.dot(cols(a_ref, i), b, preferred_element_type=F32)
        acc_ref[:, pl.ds(al(i * BLK, BLK), BLK)] += lax.dot_general(
            cols(a_ref, j), b, NT, preferred_element_type=F32
        )

    def loop(first_k, last_k, f):
        def body(k, carry):
            f(k)
            return carry

        lax.fori_loop(first_k, last_k, body, 0)

    def band_at(j):
        return pl.ds(al(j * BLK, BLK), BLK)

    def to_partner(no, src, dst):
        c = remote(src, dst, part_send.at[no], part_recv.at[no], partner)
        c.start()
        sent.append(c)
        return c

    def y_one(j):
        yf[:, band_at(j)] = band(st, j, whole_one)

    loop(0, 7, y_one)
    two.gather_mid()
    loop(7, NB, y_one)
    loop(28, 30, lambda m: single(yf, st, 0, m))
    two.gather_end()
    loop(14, 23, lambda m: single(yf, st, 1, m))

    def y_two(j):
        v = yf[:, band_at(j)] + band(st, j, whole_two)
        yf[:, band_at(j)] = v
        yp[:, band_at(j)] = v.astype(BF)

    shares = []
    for h in range(2):
        loop(h * 7, h * 7 + 7, y_two)
        here = pl.ds(h * HALF_M, HALF_M)
        shares.append(to_partner(h, yp.at[:, here], yr.at[:, here]))

    factor = 0.3 * math.sqrt(M) / (jnp.sqrt(jnp.sum(sq[12], axis=(0, 1), keepdims=True)) + 1e-07)
    factor2 = factor * factor
    zf[...] = jnp.zeros((CHIP, M), F32)

    def y_sum(j):
        v = factor2 * (yf[:, band_at(j)] + yr[:, band_at(j)].astype(F32))
        yf[:, band_at(j)] = v
        ybf[:, band_at(j)] = v.astype(BF)

    for h in range(2):
        shares[h].wait_recv()
        loop(h * 7, h * 7 + 7, y_sum)

    loop(28, 30, lambda m: single(zf, ybf, 0, m))
    loop(14, 23, lambda m: single(zf, ybf, 1, m))

    def z_band(j):
        return factor2 * (zf[:, band_at(j)] + band(ybf, j, whole_one + whole_two))

    def z_theirs(k):
        zp[:, band_at(k)] = z_band((1 - core) * 7 + k).astype(BF)

    loop(0, 7, z_theirs)
    share = to_partner(2, zp, zr)

    def z_mine(k):
        zf[:, band_at(core * 7 + k)] = z_band(core * 7 + k)

    loop(0, 7, z_mine)
    share.wait_recv()
    for p in range(3):
        ut[pl.ds(p * 128 + COL3, 128 - COL3), :] = jnp.zeros((128 - COL3, HALF_M), BF)

    def finish(k):
        at = band_at(core * 7 + k)
        scaled = (factor * st[:, at].astype(F32)).astype(BF).astype(F32)
        product = factor * (COEFF_B * yf[:, at] + COEFF_C * (zf[:, at] + zr[:, band_at(k)].astype(F32)))
        u = (math.sqrt(K) * (COEFF_A * scaled + product)).astype(BF)
        for p in range(3):
            ut[pl.ds(p * 128, COL3), band_at(k)] = u[p * COL3 : (p + 1) * COL3]

    loop(0, 7, finish)

    for c in sent:
        c.wait_send()
    sent.clear()
    one.plane_sent()
    two.plane_sent()
    y3, y2, y1q = x2p, x1q, x0
    unpack = spread_matrix((8 * PIECE, 8 * ROWS), 0, PIECE, ROWS)
    for m in range(8):
        o = m * 8 * ROWS
        first_lane = o // 128 * 128
        skip = o - first_lane
        width = -(-(skip + 8 * ROWS) // 128) * 128
        v = ut[:, pl.ds(first_lane, width)][:, skip : skip + 8 * ROWS]
        rows = lax.dot_general(unpack, v, NT, preferred_element_type=F32).astype(BF)
        for r in range(8):
            x, y, z = m // 2, m % 2 * 2 + r // 4, r % 4
            for p, at in enumerate(((z, x, y), (x, y, z), (y, x, z))):
                y3[(p,) + at] = rows[r * PIECE : (r + 1) * PIECE, p * 128 : (p + 1) * 128]

    out1 = Exchange(0, 2, lambda p, q: y3.at[p, q], lambda p, q: y2p.at[p, q], outs)
    out2 = Exchange(1, 1, lambda p, q: y2.at[p, q], lambda p, q: y1.at[p, q], outs)
    out3 = Exchange(2, 0, lambda p, q: y1q.at[p, q], lambda p, q: y0.at[p, q], outs)
    for p in range(3):
        out1.begin(p)
    narrow = spread_matrix((512, COL2), 0, 128, COL3)
    for p in range(3):
        out1.arrive(p)
        for a in range(4):
            rows = [y2p[(p, q) + plane(p, a)].reshape(4 * PIECE, 128) for q in range(4)]
            rows = jnp.dot(jnp.concatenate(rows, axis=1), narrow, preferred_element_type=F32)
            y2[p, a] = rows.astype(BF).reshape(4, PIECE, COL2)
        out2.begin(p)
    for p in range(3):
        out2.arrive(p)
        for a in range(4):
            for q in range(4):
                y1q[p, a, :, q * COL2 : (q + 1) * COL2] = y1[p, q, a]
        out3.begin(p)
    for p in range(3):
        out3.arrive(p)
        for q in range(4):
            o = p * THIRD + q * COL1
            out_ref[:, o : o + COL1] = y0[p, q][:ROWS]

    for c in sent:
        c.wait_send()


def local(gradient):
    vmem = pl.BlockSpec(memory_space=pltpu.VMEM)
    dma = pltpu.SemaphoreType.DMA
    return pl.pallas_call(
        kernel,
        out_shape=jax.ShapeDtypeStruct((ROWS, K), BF),
        in_specs=[vmem],
        out_specs=vmem,
        scratch_shapes=[
            pltpu.VMEM((3, 4, PIECE, COL1), BF),
            pltpu.VMEM((3, 4, PIECE, COL1), BF),
            pltpu.VMEM((3, 4, 4, PIECE, COL2), BF),
            pltpu.VMEM((3, 4, 4, PIECE, COL2), BF),
            pltpu.VMEM((3, 4, 4, 4, PIECE, 128), BF),
            pltpu.VMEM((2, 3, 4, 4, 4, PIECE, 128), BF),
            pltpu.VMEM((M, 384), BF),
            pltpu.VMEM((CHIP, M), BF),
            pltpu.VMEM((384, HALF_M), BF),
            pltpu.VMEM((3, 4, 4, 4, PIECE, 128), BF),
            pltpu.VMEM((3, 4, 4, PIECE, COL2), BF),
            pltpu.VMEM((3, 4, PIECE, COL1), BF),
            pltpu.VMEM((3 * 10 * 512, 128), BF),
            pltpu.VMEM((3 * 8 * 512, 128), BF),
            pltpu.VMEM((SLOTS * 512, 128), BF),
            pltpu.VMEM((3, 6, 640, 128), BF),
            pltpu.VMEM((3, 15, 80, 128), BF),
            pltpu.VMEM((3, 6, 512, 128), BF),
            pltpu.VMEM((3, 15, 64, 128), BF),
            pltpu.VMEM((15, 8, 128), F32),
            pltpu.VMEM((CHIP, M), F32),
            pltpu.VMEM((CHIP, M), BF),
            pltpu.VMEM((CHIP, M), BF),
            pltpu.VMEM((CHIP, M), BF),
            pltpu.VMEM((CHIP, M), F32),
            pltpu.VMEM((CHIP, HALF_M), BF),
            pltpu.VMEM((CHIP, HALF_M), BF),
            dma((3, 3, 3)),
            dma((3, 3, 3)),
            dma((3, 3)),
            dma((3,)),
            dma((3,)),
            dma((3, 3, 3)),
            dma((3, 3, 3)),
            dma((3, 3)),
            dma((3,)),
            dma((3,)),
            dma((3, 6)),
            dma((3, 6)),
            dma((3, 15)),
            dma((3, 15)),
            dma((3, 6)),
            dma((3, 6)),
            dma((3, 15)),
            dma((3, 15)),
            dma((3, 6)),
            dma((3, 6)),
            dma((3, 15)),
            dma((3, 15)),
            dma((3, 6)),
            dma((3, 6)),
            dma((3, 15)),
            dma((3, 15)),
            dma((4, 3)),
            dma((4, 3)),
        ],
        compiler_params=pltpu.CompilerParams(
            collective_id=0, has_side_effects=True, vmem_limit_bytes=60 * 1024 * 1024
        ),
        cost_estimate=pl.CostEstimate(flops=16 * 10**9, bytes_accessed=5 * 10**6, transcendentals=0),
    )(gradient)


def solution(mesh):
    spec = P(("wide", "narrow"), None)
    return jax.shard_map(local, mesh=mesh, in_specs=(spec,), out_specs=spec, check_vma=False)
```

```python
import math

import jax
import jax.numpy as jnp
from jax import lax
from jax.experimental import pallas as pl
from jax.experimental.pallas import tpu as pltpu
from jax.sharding import PartitionSpec as P

M = 3584
K = 18432

COEFF_A = 3.4445
COEFF_B = -4.775
COEFF_C = 2.0315

MESH = pl.DeviceIdType.MESH
BF = jnp.bfloat16
F32 = jnp.float32
NT = (((1,), (1,)), ((), ()))

ROWS = 28
PIECE = 32
THIRD = K // 3
COL1 = THIRD // 4
COL2 = COL1 // 4
COL3 = COL2 // 4
CHIP = 3 * COL3
HALF_M = M // 2

BLK = 256
NB = M // BLK
PER_PART = (10, 8)
SECOND = 3 * PER_PART[0]
SLOTS = 3 * sum(PER_PART)
SIZES = ((1280, 320, 80), (1024, 256, 64))


def al(x, m=16):
    return pl.multiple_of(x, m)


def rem(a, b):
    return lax.rem(a, jnp.int32(b))


def div(a, b):
    return lax.div(a, jnp.int32(b))


def each(n, f):
    def body(k, carry):
        f(k)
        return carry

    lax.fori_loop(0, n, body, 0)


def kernel(
    in_ref, out_ref,
    x0, x1, x1q, x2, x2p, x3, s_all, st, ut, y2p, y1, y0,
    t, g, r1a, r2a, r3a, r1b, r2b, r3b, sq, yf, ybf, yp, yr, zf, zp, zr,
    in_send, in_recv, in_copy, core_send, core_recv, out_send, out_recv, out_copy, part_send, part_recv,
    rsa_send, rsa_recv, aga_send, aga_recv, rsb_send, rsb_recv, agb_send, agb_recv, sq_send, sq_recv,
):
    w, n_ = lax.axis_index("wide"), lax.axis_index("narrow")
    core, z_lo, y = rem(w, 2), rem(div(w, 2), 2), div(w, 4)
    x, z_hi = rem(n_, 4), div(n_, 4)
    z = z_hi * 2 + z_lo

    def device(x, y, z, core):
        return ((y * 2 + rem(z, 2)) * 2 + core, div(z, 2) * 4 + x)

    def axis(p, k):
        return rem(p + k, 3)

    def place(a):
        return jnp.where(a == 0, x, jnp.where(a == 1, y, z))

    def along(a, by):
        return device(*[jnp.where(a == e, rem(v + by, 4), v) for e, v in enumerate((x, y, z))], core)

    partner = device(x, y, z, 1 - core)

    barrier = pltpu.get_barrier_semaphore()

    def greet(k):
        pl.semaphore_signal(barrier, inc=1, device_id=along(div(k, 3), rem(k, 3) + 1), device_id_type=MESH)

    each(9, greet)
    pl.semaphore_signal(barrier, inc=1, device_id=partner, device_id_type=MESH)

    def load(k):
        p, q, c = div(k, 12), rem(div(k, 3), 4), rem(k, 3)
        cols = pl.ds(al(c * 512, 512), 512)
        x0[p, q, pl.ds(0, ROWS), cols] = in_ref[:, pl.ds(al(k * 512, 512), 512)]
        x0[p, q, pl.ds(ROWS, PIECE - ROWS), cols] = jnp.zeros((PIECE - ROWS, 512), BF)

    each(K // 512, load)
    pl.semaphore_wait(barrier, 10)

    def remote(src, dst, send, recv, dev):
        return pltpu.make_async_remote_copy(
            src_ref=src, dst_ref=dst, send_sem=send, recv_sem=recv, device_id=dev, device_id_type=MESH
        )

    class Exchange:
        def __init__(self, stage, axis_no, src, dst, sems):
            self.stage, self.axis_no, self.src, self.dst, self.sems = stage, axis_no, src, dst, sems

        def far(self, p):
            a = axis(p, self.axis_no)
            me = place(a)
            send, recv, _ = self.sems
            return [
                remote(
                    self.src.at[p, rem(me + k, 4)], self.dst.at[p, me],
                    send.at[self.stage, p, k - 1], recv.at[self.stage, p, k - 1], along(a, k),
                )
                for k in (2, 1, 3)
            ]

        def own(self, p):
            me = place(axis(p, self.axis_no))
            return pltpu.make_async_copy(self.src.at[p, me], self.dst.at[p, me], self.sems[2].at[self.stage, p])

        def begin(self, p):
            for c in self.far(p):
                c.start()
            self.own(p).start()

        def arrive(self, p):
            for c in self.far(p):
                c.wait_recv()
            self.own(p).wait()

        def left(self, p):
            for c in self.far(p):
                c.wait_send()

    ins = (in_send, in_recv, in_copy)
    outs = (out_send, out_recv, out_copy)
    in1 = Exchange(0, 0, x0, x1, ins)
    in2 = Exchange(1, 1, x1q, x2, ins)
    in3 = Exchange(2, 2, x2p, x3.at[core], ins)
    each(3, in1.begin)

    def square(k, total):
        v = x0[div(k, 12), rem(div(k, 3), 4), :, pl.ds(al(rem(k, 3) * 512, 512), 512)].astype(F32)
        v = v * v
        v = (v[:, :128] + v[:, 128:256]) + (v[:, 256:384] + v[:, 384:])
        return total + ((v[:8] + v[8:16]) + (v[16:24] + v[24:]))

    sq[13] = lax.fori_loop(0, K // 512, square, jnp.zeros((8, 128), F32))
    sq_core = remote(sq.at[13], sq.at[14], sq_send.at[3, 0], sq_recv.at[3, 0], partner)
    sq_core.start()

    def iota(shape, d):
        return lax.broadcasted_iota(jnp.int32, shape, d)

    def ones_where(cond):
        return jnp.where(cond, 1.0, 0.0).astype(BF)

    def spread_matrix(shape, wide, unit, narrow):
        s, r = iota(shape, wide), iota(shape, 1 - wide)
        return ones_where((s % unit < narrow) & (r == (s // unit) * narrow + s % unit))

    def in_plane(p, a, b):
        return jnp.where(p == 2, b, a), jnp.where(p == 2, a, b)

    def in_first(p):
        in1.arrive(p)

        def body(a):
            for q in range(4):
                x1q[p, q, a] = x1[p, a, :, q * COL2 : (q + 1) * COL2]

        each(4, body)
        in2.begin(p)

    each(3, in_first)
    widen = spread_matrix((COL2, 512), 1, 128, COL3)

    def in_second(p):
        in2.arrive(p)

        def body(b):
            rows = jnp.dot(x2[p, b].reshape(4 * PIECE, COL2), widen, preferred_element_type=F32).astype(BF)
            for a in range(4):
                u, v = in_plane(p, a, b)
                for q in range(4):
                    x2p[p, q, u, v] = rows[a * PIECE : (a + 1) * PIECE, q * 128 : (q + 1) * 128]

        each(4, body)
        in3.begin(p)

    each(3, in_second)

    def crossing(p):
        here = x3.at[core, p]
        return remote(here, here, core_send.at[p], core_recv.at[p], partner)

    def in_third(p):
        in3.arrive(p)
        crossing(p).start()

    each(3, in_third)

    pack = spread_matrix((8 * ROWS, 8 * PIECE), 1, PIECE, ROWS)

    def pack_rows(k):
        @pl.when(k == 8)
        def _():
            each(3, lambda p: crossing(p).wait_recv())

        owner = jnp.where(k < 8, core, 1 - core)
        m = rem(k, 8)
        x, y0_, group = div(m, 2), rem(m, 2) * 2, [[], [], []]
        for y in (y0_, y0_ + 1):
            for z in range(4):
                group[0].append(x3[owner, 0, z, x, y])
                group[1].append(x3[owner, 1, x, y, z])
                group[2].append(x3[owner, 2, y, x, z])
        rows = jnp.concatenate([jnp.concatenate(e, axis=0) for e in group], axis=1)
        at = pl.ds(al(owner * HALF_M + m * 8 * ROWS), 8 * ROWS)
        s_all[at, :] = jnp.dot(pack, rows, preferred_element_type=F32).astype(BF)

    each(16, pack_rows)

    def block_of(s):
        shared = (s >= 44) & (s < 51)
        whole = (s < 28) | ((s >= 30) & (s < 44))
        i = jnp.where(s < 28, rem(s, NB), jnp.where(s < 30, 4 * core + s - 28, s - 30))
        i = jnp.where(shared, 7 * core + s - 44, jnp.where(s >= 51, rem(4 * core + s - 49, NB), i))
        d = jnp.where(whole, jnp.where(s < 28, 2 * core + div(s, NB), 4 + 2 * core), jnp.where(shared, 5, 7))
        unused = (s == 53) | ((d == 7) & (i >= 7))
        return i, d, jnp.where(unused, 0.0, jnp.where(d == 0, 0.5, 1.0))

    def band_at(j):
        return pl.ds(al(j * BLK, BLK), BLK)

    def gram_block(s):
        i, d, scale = block_of(s)
        j = rem(i + d, NB)
        acc = lax.dot_general(s_all[band_at(i), :], s_all[band_at(j), :], NT, preferred_element_type=F32)
        acc = (scale * acc).astype(BF)
        t[pl.ds(al(s * 512, 512), 256), :] = acc[:, :128]
        t[pl.ds(al(s * 512 + 256, 256), 256), :] = acc[:, 128:]

    def slot_at(k):
        def first(p, m, by):
            q = rem(place(p) + by, 4)
            return p * 10 + div(10 * q + 2, 4) + m

        def second(p, m, by):
            return SECOND + p * 8 + 2 * rem(place(p) + by, 4) + m

        far1 = div(k, 3) * 10 + div(5 * rem(place(div(k, 3)) + 2, 4), 2) + rem(k, 3)
        e = k - 9
        p, m = div(e, 5), rem(e, 5)
        near1 = jnp.where(
            m == 0, p * 10 + 2 + 5 * div(place(p), 2), jnp.where(m < 3, first(p, m - 1, 1), first(p, m - 3, 3))
        )
        far2 = second(div(k - 24, 2), rem(k - 24, 2), 2)
        own1 = first(div(k - 30, 2), rem(k - 30, 2), 0)
        e = k - 36
        near2 = second(div(e, 4), rem(e, 2), jnp.where(rem(e, 4) < 2, 1, 3))
        own2 = second(div(k - 48, 2), rem(k - 48, 2), 0)
        late = jnp.where(k < 36, own1, jnp.where(k < 48, near2, own2))
        return jnp.where(k < 9, far1, jnp.where(k < 24, near1, jnp.where(k < 30, far2, late)))

    def square_copies(s):
        return [
            remote(sq.at[4 * s], sq.at[4 * s + k], sq_send.at[s, k - 1], sq_recv.at[s, k - 1], along(s, k))
            for k in (1, 2, 3)
        ]

    def square_begin(s):
        for c in square_copies(s):
            c.start()

    def square_end(s):
        for c in square_copies(s):
            c.wait_recv()
        sq[4 * s + 4] = (sq[4 * s] + sq[4 * s + 2]) + (sq[4 * s + 1] + sq[4 * s + 3])

    class Chunk:
        def __init__(self, no, bufs, rs, ag):
            self.bufs, self.rs, self.ag = bufs, rs, ag
            self.rows = PER_PART[no] * 512
            self.row0 = no * SECOND * 512
            self.sizes = SIZES[no]

        def base(self, k, p):
            b = self.row0 + p * self.rows
            for e in range(k):
                b = b + place(axis(p, e)) * self.sizes[e]
            return b

        def quarter(self, k, p, by):
            return self.base(k, p) + rem(place(axis(p, k)) + by, 4) * self.sizes[k]

        def hop(self, k, p, no):
            half = self.sizes[k] // 2
            by, low = ((2, 0), (1, 1), (1, 0), (2, 1), (3, 0), (3, 1))[no]
            return remote(
                t.at[pl.ds(al(self.quarter(k, p, by) + low * half), half), :],
                self.bufs[k].at[p, no],
                self.rs[0].at[k, p, no],
                self.rs[1].at[k, p, no],
                along(axis(p, k), 1 if no < 3 else 3),
            )

        def last(self, p, k):
            return remote(
                t.at[pl.ds(al(self.quarter(2, p, k)), self.sizes[2]), :],
                self.bufs[2].at[p, k - 1],
                self.rs[0].at[2, p, k - 1],
                self.rs[1].at[2, p, k - 1],
                along(axis(p, 2), k),
            )

        def add_rows(self, off, rows, srcs):
            step = self.sizes[2]

            def body(m):
                at = pl.ds(al(off + m * step), step)
                total = t[at, :].astype(F32)
                for src in srcs:
                    total = total + src[pl.ds(al(m * step), step), :].astype(F32)
                t[at, :] = total.astype(BF)

            each(rows // step, body)

        def scatter(self, k, *nos):
            def body(p):
                for no in nos:
                    self.hop(k, p, no).start()

            each(3, body)

        def scatter_far(self, k):
            self.scatter(k, 0, 3)

        def scatter_near(self, k):
            self.scatter(k, 1, 4)

        def scatter_mid(self, k):
            half = self.sizes[k] // 2

            def body(p):
                self.hop(k, p, 0).wait_recv()
                self.add_rows(self.quarter(k, p, 1), half, [self.bufs[k].at[p, 0]])
                self.hop(k, p, 2).start()
                self.hop(k, p, 3).wait_recv()
                self.add_rows(self.quarter(k, p, 3) + half, half, [self.bufs[k].at[p, 3]])
                self.hop(k, p, 5).start()

            each(3, body)

        def scatter_end(self, k):
            half = self.sizes[k] // 2

            def body(p):
                for h, one, two in ((0, 4, 2), (1, 1, 5)):
                    self.hop(k, p, one).wait_recv()
                    self.hop(k, p, two).wait_recv()
                    self.add_rows(
                        self.quarter(k, p, 0) + h * half, half, [self.bufs[k].at[p, one], self.bufs[k].at[p, two]]
                    )

            each(3, body)

        def last_begin(self):
            def body(p):
                for k in (2, 1, 3):
                    self.last(p, k).start()

            each(3, body)

        def last_end(self):
            def body(p):
                for k in (1, 2, 3):
                    self.last(p, k).wait_recv()
                here = pl.ds(al(self.base(3, p)), self.sizes[2])
                total = t[here, :].astype(F32)
                for k in range(3):
                    total = total + self.bufs[2][p, k].astype(F32)
                g[here, :] = total.astype(BF)
                for k in (2, 1, 3):
                    self.first(p, k).start()

            each(3, body)

        def spread(self, k, p, no, off, rows, by):
            here = g.at[pl.ds(al(off), rows), :]
            return remote(here, here, self.ag[0].at[k, p, no], self.ag[1].at[k, p, no], along(axis(p, k), by))

        def first(self, p, k):
            return self.spread(2, p, k - 1, self.base(3, p), self.sizes[2], k)

        def send(self, k, p, no):
            half = self.sizes[k] // 2
            by, low, to = ((0, 0, 1), (0, 1, 3), (0, 1, 1), (0, 0, 3), (3, 0, 1), (1, 1, 3))[no]
            return self.spread(k, p, no, self.quarter(k, p, by) + low * half, half, to)

        def gather_first_end(self):
            def body(p):
                for k in (1, 2, 3):
                    self.first(p, k).wait_recv()

            each(3, body)

        def gather_begin(self, k):
            def body(p):
                self.send(k, p, 0).start()
                self.send(k, p, 1).start()

            each(3, body)

            def body(p):
                self.send(k, p, 2).start()
                self.send(k, p, 3).start()

            each(3, body)

        def gather_mid(self, k):
            def body(p):
                self.send(k, p, 0).wait_recv()
                self.send(k, p, 4).start()
                self.send(k, p, 1).wait_recv()
                self.send(k, p, 5).start()

            each(3, body)

        def gather_end(self, k):
            def body(p):
                for no in (2, 3, 4, 5):
                    self.send(k, p, no).wait_recv()

            each(3, body)

        def all_sent(self):
            def body(p):
                for k in range(2):
                    for no in range(6):
                        self.hop(k, p, no).wait_send()
                        self.send(k, p, no).wait_send()
                for k in (1, 2, 3):
                    self.last(p, k).wait_send()
                    self.first(p, k).wait_send()

            each(3, body)

    one = Chunk(0, (r1a, r2a, r3a), (rsa_send, rsa_recv), (aga_send, aga_recv))
    two = Chunk(1, (r1b, r2b, r3b), (rsb_send, rsb_recv), (agb_send, agb_recv))

    def gram(k):
        @pl.when(k == 9)
        def _():
            one.scatter_far(0)

        @pl.when(k == 24)
        def _():
            one.scatter_near(0)

        @pl.when(k == 36)
        def _():
            one.scatter_mid(0)
            two.scatter_far(0)

        @pl.when(k == 48)
        def _():
            two.scatter_near(0)

        gram_block(slot_at(k))

    each(SLOTS, gram)
    sq_core.wait_recv()
    sq[0] = sq[13] + sq[14]
    square_begin(0)

    kk, ll = iota((CHIP, 384), 0), iota((CHIP, 384), 1)
    pick = ones_where((ll % 128 < COL3) & (kk == (ll // 128) * COL3 + ll % 128))

    def turn(j):
        st[:, band_at(j)] = lax.dot_general(pick, s_all[band_at(j), :], NT, preferred_element_type=F32).astype(BF)

    each(NB, turn)

    one.scatter_end(0)
    one.scatter_far(1)
    one.scatter_near(1)
    square_end(0)
    square_begin(1)
    two.scatter_mid(0)
    one.scatter_mid(1)
    one.scatter_end(1)
    one.last_begin()
    two.scatter_end(0)
    two.scatter_far(1)
    two.scatter_near(1)
    one.last_end()
    square_end(1)
    square_begin(2)
    two.scatter_mid(1)
    one.gather_first_end()
    one.gather_begin(1)
    two.scatter_end(1)
    two.last_begin()
    one.gather_mid(1)
    one.gather_end(1)
    one.gather_begin(0)
    two.last_end()
    square_end(2)
    one.gather_mid(0)
    two.gather_first_end()
    two.gather_begin(1)
    two.gather_mid(1)
    two.gather_end(1)
    two.gather_begin(0)
    one.gather_end(0)

    def cols(a_ref, i):
        return a_ref[:, band_at(i)]

    def block(slot):
        o = slot * 512
        return jnp.concatenate([g[pl.ds(al(o, 512), 256), :], g[pl.ds(al(o + 256, 256), 256), :]], axis=1)

    def band(a_ref, j, ds):
        def straight(d, first):
            i = rem(j + NB - d, NB)
            return cols(a_ref, i), block(first + i)

        def turned(d, first):
            return cols(a_ref, rem(j + d, NB)), block(first + j)

        a, b = zip(*[straight(*e) for e in ds])
        acc = jnp.dot(jnp.concatenate(a, axis=1), jnp.concatenate(b, axis=0), preferred_element_type=F32)
        a, b = zip(*[turned(*e) for e in ds])
        return acc + lax.dot_general(
            jnp.concatenate(a, axis=1), jnp.concatenate(b, axis=1), NT, preferred_element_type=F32
        )

    whole_one = ((2 * core, 0), (2 * core + 1, NB))
    whole_two = ((2 * core + 4, SECOND),)

    def singles(acc_ref, a_ref):
        def body(k):
            s = jnp.where(k < 2, 28 + k, 42 + k)
            i, d, _ = block_of(s)
            j = rem(i + d, NB)
            b = block(s)
            acc_ref[:, band_at(j)] += jnp.dot(cols(a_ref, i), b, preferred_element_type=F32)
            acc_ref[:, band_at(i)] += lax.dot_general(cols(a_ref, j), b, NT, preferred_element_type=F32)

        each(11, body)

    def share(no):
        if no == 2:
            return remote(zp, zr, part_send.at[no], part_recv.at[no], partner)
        here = pl.ds(no * HALF_M, HALF_M)
        return remote(yp.at[:, here], yr.at[:, here], part_send.at[no], part_recv.at[no], partner)

    def y_one(j):
        @pl.when(j == 7)
        def _():
            two.gather_mid(0)

        yf[:, band_at(j)] = band(st, j, whole_one)

    each(NB, y_one)
    two.gather_end(0)
    singles(yf, st)

    def y_two(j):
        v = yf[:, band_at(j)] + band(st, j, whole_two)
        yf[:, band_at(j)] = v
        yp[:, band_at(j)] = v.astype(BF)

        @pl.when(j == 6)
        def _():
            share(0).start()

    each(NB, y_two)
    share(1).start()

    factor = 0.3 * math.sqrt(M) / (jnp.sqrt(jnp.sum(sq[12], axis=(0, 1), keepdims=True)) + 1e-07)
    factor2 = factor * factor

    def y_sum(j):
        @pl.when(j == 0)
        def _():
            share(0).wait_recv()

        @pl.when(j == 7)
        def _():
            share(1).wait_recv()

        v = factor2 * (yf[:, band_at(j)] + yr[:, band_at(j)].astype(F32))
        yf[:, band_at(j)] = v
        ybf[:, band_at(j)] = v.astype(BF)
        zf[:, band_at(j)] = jnp.zeros((CHIP, BLK), F32)

    each(NB, y_sum)

    singles(zf, ybf)

    def z_band(k):
        j = rem(k + (1 - core) * 7, NB)
        v = factor2 * (zf[:, band_at(j)] + band(ybf, j, whole_one + whole_two))
        zf[:, band_at(j)] = v

        @pl.when(k < 7)
        def _():
            zp[:, band_at(rem(k, 7))] = v.astype(BF)

        @pl.when(k == 6)
        def _():
            share(2).start()

    each(NB, z_band)
    for p in range(3):
        ut[pl.ds(p * 128 + COL3, 128 - COL3), :] = jnp.zeros((128 - COL3, HALF_M), BF)
    share(2).wait_recv()

    def finish(k):
        at = band_at(core * 7 + k)
        scaled = (factor * st[:, at].astype(F32)).astype(BF).astype(F32)
        product = factor * (COEFF_B * yf[:, at] + COEFF_C * (zf[:, at] + zr[:, band_at(k)].astype(F32)))
        u = (math.sqrt(K) * (COEFF_A * scaled + product)).astype(BF)
        for p in range(3):
            ut[pl.ds(p * 128, COL3), band_at(k)] = u[p * COL3 : (p + 1) * COL3]

    each(7, finish)

    for e in (in1, in2, in3):
        each(3, e.left)
    y3, y2, y1q = x2p, x1q, x0
    unpack = spread_matrix((8 * PIECE, 8 * ROWS), 0, PIECE, ROWS)

    def spread_rows(e):
        for m in range(4):
            o = m * 8 * ROWS
            first_lane = o // 128 * 128
            skip = o - first_lane
            width = -(-(skip + 8 * ROWS) // 128) * 128
            v = ut[:, pl.ds(al(e * (HALF_M // 2) + first_lane, 128), width)][:, skip : skip + 8 * ROWS]
            rows = lax.dot_general(unpack, v, NT, preferred_element_type=F32).astype(BF)
            for r in range(8):
                x, y, z = e * 2 + m // 2, m % 2 * 2 + r // 4, r % 4
                for p, at in enumerate(((z, x, y), (x, y, z), (y, x, z))):
                    y3[(p,) + at] = rows[r * PIECE : (r + 1) * PIECE, p * 128 : (p + 1) * 128]

    each(2, spread_rows)

    out1 = Exchange(0, 2, y3, y2p, outs)
    out2 = Exchange(1, 1, y2, y1, outs)
    out3 = Exchange(2, 0, y1q, y0, outs)
    each(3, out1.begin)
    narrow = spread_matrix((512, COL2), 0, 128, COL3)

    def out_first(p):
        out1.arrive(p)

        def body(b):
            lanes = []
            for q in range(4):
                lanes.append(jnp.concatenate([y2p[(p, q) + in_plane(p, a, b)] for a in range(4)], axis=0))
            rows = jnp.dot(jnp.concatenate(lanes, axis=1), narrow, preferred_element_type=F32)
            y2[p, b] = rows.astype(BF).reshape(4, PIECE, COL2)

        each(4, body)
        out2.begin(p)

    each(3, out_first)

    def out_second(p):
        out2.arrive(p)

        def body(a):
            for q in range(4):
                y1q[p, a, :, q * COL2 : (q + 1) * COL2] = y1[p, q, a]

        each(4, body)
        out3.begin(p)

    each(3, out_second)

    def out_third(p):
        out3.arrive(p)

        def body(q):
            out_ref[:, pl.ds(al(p * THIRD + q * COL1, COL1), COL1)] = y0[p, q][:ROWS]

        each(4, body)

    each(3, out_third)

    for e in (out1, out2, out3):
        each(3, e.left)
    one.all_sent()
    two.all_sent()
    each(3, lambda p: crossing(p).wait_send())
    for s in range(3):
        for c in square_copies(s):
            c.wait_send()
    sq_core.wait_send()
    for no in range(3):
        share(no).wait_send()


def local(gradient):
    vmem = pl.BlockSpec(memory_space=pltpu.VMEM)
    dma = pltpu.SemaphoreType.DMA
    return pl.pallas_call(
        kernel,
        out_shape=jax.ShapeDtypeStruct((ROWS, K), BF),
        in_specs=[vmem],
        out_specs=vmem,
        scratch_shapes=[
            pltpu.VMEM((3, 4, PIECE, COL1), BF),
            pltpu.VMEM((3, 4, PIECE, COL1), BF),
            pltpu.VMEM((3, 4, 4, PIECE, COL2), BF),
            pltpu.VMEM((3, 4, 4, PIECE, COL2), BF),
            pltpu.VMEM((3, 4, 4, 4, PIECE, 128), BF),
            pltpu.VMEM((2, 3, 4, 4, 4, PIECE, 128), BF),
            pltpu.VMEM((M, 384), BF),
            pltpu.VMEM((CHIP, M), BF),
            pltpu.VMEM((384, HALF_M), BF),
            pltpu.VMEM((3, 4, 4, 4, PIECE, 128), BF),
            pltpu.VMEM((3, 4, 4, PIECE, COL2), BF),
            pltpu.VMEM((3, 4, PIECE, COL1), BF),
            pltpu.VMEM((SLOTS * 512, 128), BF),
            pltpu.VMEM((SLOTS * 512, 128), BF),
            pltpu.VMEM((3, 6, 640, 128), BF),
            pltpu.VMEM((3, 6, 160, 128), BF),
            pltpu.VMEM((3, 3, 80, 128), BF),
            pltpu.VMEM((3, 6, 512, 128), BF),
            pltpu.VMEM((3, 6, 128, 128), BF),
            pltpu.VMEM((3, 3, 64, 128), BF),
            pltpu.VMEM((15, 8, 128), F32),
            pltpu.VMEM((CHIP, M), F32),
            pltpu.VMEM((CHIP, M), BF),
            pltpu.VMEM((CHIP, M), BF),
            pltpu.VMEM((CHIP, M), BF),
            pltpu.VMEM((CHIP, M), F32),
            pltpu.VMEM((CHIP, HALF_M), BF),
            pltpu.VMEM((CHIP, HALF_M), BF),
            dma((3, 3, 3)),
            dma((3, 3, 3)),
            dma((3, 3)),
            dma((3,)),
            dma((3,)),
            dma((3, 3, 3)),
            dma((3, 3, 3)),
            dma((3, 3)),
            dma((3,)),
            dma((3,)),
            dma((3, 3, 6)),
            dma((3, 3, 6)),
            dma((3, 3, 6)),
            dma((3, 3, 6)),
            dma((3, 3, 6)),
            dma((3, 3, 6)),
            dma((3, 3, 6)),
            dma((3, 3, 6)),
            dma((4, 3)),
            dma((4, 3)),
        ],
        compiler_params=pltpu.CompilerParams(
            collective_id=0, has_side_effects=True, vmem_limit_bytes=60 * 1024 * 1024
        ),
        cost_estimate=pl.CostEstimate(flops=16 * 10**9, bytes_accessed=5 * 10**6, transcendentals=0),
    )(gradient)


def solution(mesh):
    spec = P(("wide", "narrow"), None)
    return jax.shard_map(local, mesh=mesh, in_specs=(spec,), out_specs=spec, check_vma=False)
```

```python
import math

import jax
import jax.numpy as jnp
from jax import lax
from jax.experimental import pallas as pl
from jax.experimental.pallas import tpu as pltpu
from jax.sharding import PartitionSpec as P

M = 3584
K = 18432

COEFF_A = 3.4445
COEFF_B = -4.775
COEFF_C = 2.0315

MESH = pl.DeviceIdType.MESH
BF = jnp.bfloat16
F32 = jnp.float32
NT = (((1,), (1,)), ((), ()))

ROWS = 28
PIECE = 32
THIRD = K // 3
COL1 = THIRD // 4
COL2 = COL1 // 4
COL3 = COL2 // 4
CHIP = 3 * COL3
HALF_M = M // 2
AXES = ((0, 1, 2), (1, 2, 0), (2, 0, 1))

BLK = 256
NB = M // BLK
PER_PART = (10, 8)
SECOND = 3 * PER_PART[0]
SLOTS = 3 * sum(PER_PART)
SIZES = ((1280, 320, 80), (1024, 256, 64))


def al(x, m=16):
    return pl.multiple_of(x, m)


def kernel(
    in_ref, out_ref,
    x0, x1, x1q, x2, x2p, x3, s_all, st,
    ut, y2p, y1, y0,
    ta, tb, g, r1a, r2a, r3a, r1b, r2b, r3b, sq, yf, ybf, yp, yr, zf, zp, zr,
    in_send, in_recv, core_send, core_recv, out_send, out_recv, part_send, part_recv,
    rsa_send, rsa_recv, aga_send, aga_recv, rsb_send, rsb_recv, agb_send, agb_recv, sq_send, sq_recv,
):
    w, n_ = lax.axis_index("wide"), lax.axis_index("narrow")
    core, z_lo, y = w % 2, (w // 2) % 2, w // 4
    x, z_hi = n_ % 4, n_ // 4
    z = z_hi * 2 + z_lo
    pos = (x, y, z)

    def device(x, y, z, core):
        return ((y * 2 + z % 2) * 2 + core, (z // 2) * 4 + x)

    def shifted(axis, by):
        p = [x, y, z]
        p[axis] = (p[axis] + by) % 4
        return device(*p, core)

    right = [shifted(a, 1) for a in range(3)]
    left = [shifted(a, 3) for a in range(3)]
    across = [shifted(a, 2) for a in range(3)]
    partner = device(x, y, z, 1 - core)

    barrier = pltpu.get_barrier_semaphore()
    for d in right + left + across + [partner]:
        pl.semaphore_signal(barrier, inc=1, device_id=d, device_id_type=MESH)

    def load(k, carry):
        p, q = k // 4, k % 4
        v = in_ref[:, pl.ds(al(k * COL1, COL1), COL1)]
        x0[p, q, pl.ds(0, ROWS), :] = v
        x0[p, q, pl.ds(ROWS, PIECE - ROWS), :] = jnp.zeros((PIECE - ROWS, COL1), BF)
        return carry

    lax.fori_loop(0, 12, load, 0)
    pl.semaphore_wait(barrier, 10)

    def remote(src, dst, send, recv, dev):
        return pltpu.make_async_remote_copy(
            src_ref=src, dst_ref=dst, send_sem=send, recv_sem=recv, device_id=dev, device_id_type=MESH
        )

    sent = []

    def flush(group):
        for c in group:
            c.wait_send()
        group.clear()

    class Exchange:
        def __init__(self, stage, axis_no, src, dst, sems):
            self.stage, self.axis_no, self.src, self.dst, self.sems = stage, axis_no, src, dst, sems
            self.copies = {}

        def begin(self, p):
            a = AXES[p][self.axis_no]
            me = pos[a]
            send, recv = self.sems
            group = []
            for k, dev in ((2, across[a]), (1, right[a]), (3, left[a])):
                c = remote(
                    self.src(p, (me + k) % 4), self.dst(p, me),
                    send.at[self.stage, p, k - 1], recv.at[self.stage, p, k - 1], dev,
                )
                c.start()
                group.append(c)
                sent.append(c)
            self.copies[p] = group

        def keep(self, p):
            me = pos[AXES[p][self.axis_no]]
            src, dst = self.src(p, me), self.dst(p, me)
            dst[...] = src[...]

        def arrive(self, p):
            for c in self.copies[p]:
                c.wait_recv()

    ins = (in_send, in_recv)
    outs = (out_send, out_recv)

    def plane(p, k):
        return (k, slice(None)) if p == 2 else (slice(None), k)

    in1 = Exchange(0, 0, lambda p, q: x0.at[p, q], lambda p, q: x1.at[p, q], ins)
    in2 = Exchange(1, 1, lambda p, q: x1q.at[p, q], lambda p, q: x2.at[p, q], ins)
    in3 = Exchange(2, 2, lambda p, q: x2p.at[p, q], lambda p, q: x3.at[core, p, q], ins)
    for p in range(3):
        in1.begin(p)

    def square(k, total):
        v = x0[k // 12, k // 3 % 4, :, pl.ds(al(k % 3 * 512, 512), 512)].astype(F32)
        v = v * v
        v = (v[:, :128] + v[:, 128:256]) + (v[:, 256:384] + v[:, 384:])
        return total + ((v[:8] + v[8:16]) + (v[16:24] + v[24:]))

    for p in range(3):
        in1.keep(p)
    sq[13] = lax.fori_loop(0, K // 512, square, jnp.zeros((8, 128), F32))
    sq_core = remote(sq.at[13], sq.at[14], sq_send.at[3, 0], sq_recv.at[3, 0], partner)
    sq_core.start()
    sent.append(sq_core)

    def iota(shape, d):
        return lax.broadcasted_iota(jnp.int32, shape, d)

    def ones_where(cond):
        return jnp.where(cond, 1.0, 0.0).astype(BF)

    def spread_matrix(shape, wide, unit, narrow):
        s, r = iota(shape, wide), iota(shape, 1 - wide)
        return ones_where((s % unit < narrow) & (r == (s // unit) * narrow + s % unit))

    for p in range(3):
        in1.arrive(p)
        for a in range(4):
            for q in range(4):
                x1q[p, q, a] = x1[p, a, :, q * COL2 : (q + 1) * COL2]
        in2.begin(p)
    for p in range(3):
        in2.keep(p)
    widen = spread_matrix((COL2, 512), 1, 128, COL3)
    for p in range(3):
        in2.arrive(p)
        for a in range(4):
            rows = jnp.dot(x2[p, a].reshape(4 * PIECE, COL2), widen, preferred_element_type=F32).astype(BF)
            for q in range(4):
                x2p[(p, q) + plane(p, a)] = rows[:, q * 128 : (q + 1) * 128].reshape(4, PIECE, 128)
        in3.begin(p)
    for p in range(3):
        in3.keep(p)
    crossing = []
    for p in range(3):
        in3.arrive(p)
        here = x3.at[core, p]
        c = remote(here, here, core_send.at[p], core_recv.at[p], partner)
        c.start()
        crossing.append(c)
        sent.append(c)

    pack = spread_matrix((8 * ROWS, 8 * PIECE), 1, PIECE, ROWS)

    def pack_rows(owner):
        def body(k, carry):
            x, y0, group = k // 2, k % 2 * 2, [[], [], []]
            for y in (y0, y0 + 1):
                for z in range(4):
                    group[0].append(x3[owner, 0, z, x, y])
                    group[1].append(x3[owner, 1, x, y, z])
                    group[2].append(x3[owner, 2, y, x, z])
            rows = jnp.concatenate([jnp.concatenate(e, axis=0) for e in group], axis=1)
            at = pl.ds(al(owner * HALF_M + k * 8 * ROWS), 8 * ROWS)
            s_all[at, :] = jnp.dot(pack, rows, preferred_element_type=F32).astype(BF)
            return carry

        lax.fori_loop(0, 4, lambda k, carry: body(2 * k + 1, body(2 * k, carry)), 0)

    pack_rows(core)
    for c in crossing:
        c.wait_recv()
    pack_rows(1 - core)

    def turn_all():
        kk, ll = iota((CHIP, 384), 0), iota((CHIP, 384), 1)
        pick = ones_where((ll % 128 < COL3) & (kk == (ll // 128) * COL3 + ll % 128))

        def turn(j, carry):
            at = pl.ds(al(j * BLK, BLK), BLK)
            st[:, at] = lax.dot_general(pick, s_all[at, :], NT, preferred_element_type=F32).astype(BF)
            return carry

        lax.fori_loop(0, NB // 2, lambda k, carry: turn(2 * k + 1, turn(2 * k, carry)), 0)

    def block_of(chunk, m):
        if chunk == 0:
            i = jnp.where(m < 28, m % NB, 4 * core + m - 28)
            d = jnp.where(m < 28, 2 * core + m // NB, 7)
            return i, d, jnp.where(d == 0, 0.5, 1.0)
        i = jnp.where(m < 14, m, jnp.where(m < 21, 7 * core + m - 14, (4 * core + m - 19) % NB))
        d = jnp.where(m < 14, 4 + 2 * core, jnp.where(m < 21, 5, 7))
        return i, d, jnp.where((d == 7) & ((i >= 7) | (m == 23)), 0.0, 1.0)

    def gram_block(chunk, m, t):
        i, d, scale = block_of(chunk, m)
        j = (i + d) % NB
        ri = pl.ds(al(i * BLK, BLK), BLK)
        rj = pl.ds(al(j * BLK, BLK), BLK)
        acc = lax.dot_general(s_all[ri, :], s_all[rj, :], NT, preferred_element_type=F32)
        acc = (scale * acc).astype(BF)
        t[pl.ds(al(m * 512, 512), 256), :] = acc[:, :128]
        t[pl.ds(al(m * 512 + 256, 256), 256), :] = acc[:, 128:]

    def square_begin(s):
        group = [
            remote(sq.at[4 * s], sq.at[4 * s + 1 + k], sq_send.at[s, k], sq_recv.at[s, k], dev)
            for k, dev in enumerate((right[s], left[s], across[s]))
        ]
        for c in group:
            c.start()
        sent.extend(group)
        return group

    def square_end(s, group):
        for c in group:
            c.wait_recv()
        sq[4 * s + 4] = (sq[4 * s] + sq[4 * s + 3]) + (sq[4 * s + 1] + sq[4 * s + 2])

    class Chunk:
        def __init__(self, no, t, bufs, rs, ag):
            self.no, self.t, self.bufs, self.rs, self.ag = no, t, bufs, rs, ag
            self.blocks = PER_PART[no]
            self.sizes = SIZES[no]
            base = [p * self.blocks * 512 for p in range(3)]
            self.bases = [base]
            for k in range(3):
                base = [base[p] + pos[AXES[p][k]] * self.sizes[k] for p in range(3)]
                self.bases.append(base)
            self.mine = no * SECOND * 512
            self.copies = {}

        def quarter(self, k, p, by):
            return self.bases[k][p] + ((pos[AXES[p][k]] + by) % 4) * self.sizes[k]

        def gram(self, p, start, count):
            for m in range(count):
                gram_block(self.no, p * self.blocks + start + m, self.t)

        def gram_far(self):
            for p in range(3):
                q = (pos[AXES[p][0]] + 2) % 4
                self.gram(p, self.blocks * q // 4, 2 + self.blocks % 4 // 2)

        def gram_near(self):
            for p in range(3):
                me = pos[AXES[p][0]]
                if self.blocks % 4:
                    self.gram(p, self.blocks // 4 + self.blocks // 2 * (me // 2), 1)
                for by in (1, 3):
                    self.gram(p, (self.blocks * ((me + by) % 4) + 2) // 4, 2)

        def gram_own(self):
            for p in range(3):
                self.gram(p, (self.blocks * pos[AXES[p][0]] + 2) // 4, 2)

        def push(self, k, p, no, off, rows):
            a = AXES[p][k]
            c = remote(
                self.t.at[pl.ds(al(off), rows), :],
                self.bufs[k].at[p, no],
                self.rs[0].at[k, p, no],
                self.rs[1].at[k, p, no],
                right[a] if no < 3 else left[a],
            )
            c.start()
            self.copies[k, p, no] = c
            sent.append(c)

        def add_rows(self, off, rows, srcs):
            step = 160 if rows % 160 == 0 else 128 if rows % 128 == 0 else rows
            t = self.t

            def body(m, carry):
                at = pl.ds(al(off + m * step), step)
                total = t[at, :].astype(F32)
                for src in srcs:
                    total = total + src[pl.ds(al(m * step), step), :].astype(F32)
                t[at, :] = total.astype(BF)
                return carry

            lax.fori_loop(0, rows // step, body, 0)

        def scatter_far(self, k):
            half = self.sizes[k] // 2
            for p in range(3):
                self.push(k, p, 0, self.quarter(k, p, 2), half)
                self.push(k, p, 3, self.quarter(k, p, 2) + half, half)

        def scatter_near(self, k):
            half = self.sizes[k] // 2
            for p in range(3):
                self.push(k, p, 1, self.quarter(k, p, 1) + half, half)
                self.push(k, p, 4, self.quarter(k, p, 3), half)

        def scatter_mid(self, k):
            half = self.sizes[k] // 2
            for p in range(3):
                self.copies[k, p, 0].wait_recv()
                self.add_rows(self.quarter(k, p, 1), half, [self.bufs[k].at[p, 0]])
                self.push(k, p, 2, self.quarter(k, p, 1), half)
                self.copies[k, p, 3].wait_recv()
                self.add_rows(self.quarter(k, p, 3) + half, half, [self.bufs[k].at[p, 3]])
                self.push(k, p, 5, self.quarter(k, p, 3) + half, half)

        def scatter_end(self, k):
            half = self.sizes[k] // 2
            for p in range(3):
                for h, one, two in ((0, 4, 2), (1, 1, 5)):
                    self.copies[k, p, one].wait_recv()
                    self.copies[k, p, two].wait_recv()
                    self.add_rows(
                        self.quarter(k, p, 0) + h * half, half, [self.bufs[k].at[p, one], self.bufs[k].at[p, two]]
                    )

        def last_begin(self):
            size = self.sizes[2]
            for p in range(3):
                a = AXES[p][2]
                for k, dev in ((2, across[a]), (1, right[a]), (3, left[a])):
                    c = remote(
                        self.t.at[pl.ds(al(self.quarter(2, p, k)), size), :],
                        self.bufs[2].at[p, k - 1],
                        self.rs[0].at[2, p, k - 1],
                        self.rs[1].at[2, p, k - 1],
                        dev,
                    )
                    c.start()
                    self.copies[2, p, k] = c
                    sent.append(c)

        def last_end(self):
            size = self.sizes[2]
            for p in range(3):
                for k in (1, 2, 3):
                    self.copies[2, p, k].wait_recv()
                off = self.bases[3][p]
                self.add_rows(off, size, [self.bufs[2].at[p, k] for k in range(3)])
                here = pl.ds(al(self.mine + off), size)
                g[here, :] = self.t[pl.ds(al(off), size), :]
                a = AXES[p][2]
                for k, dev in ((2, across[a]), (1, right[a]), (3, left[a])):
                    self.spread(2, p, k - 1, off, size, dev)

        def spread(self, k, p, no, off, rows, dev):
            here = g.at[pl.ds(al(self.mine + off), rows), :]
            c = remote(here, here, self.ag[0].at[k, p, no], self.ag[1].at[k, p, no], dev)
            c.start()
            self.copies["g", k, p, no] = c
            sent.append(c)

        def got(self, k, p, *nos):
            for no in nos:
                self.copies["g", k, p, no].wait_recv()

        def gather_first_end(self):
            for p in range(3):
                self.got(2, p, 0, 1, 2)

        def gather_begin(self, k):
            half = self.sizes[k] // 2
            for p in range(3):
                own = self.quarter(k, p, 0)
                a = AXES[p][k]
                self.spread(k, p, 0, own, half, right[a])
                self.spread(k, p, 1, own + half, half, left[a])
            for p in range(3):
                own = self.quarter(k, p, 0)
                a = AXES[p][k]
                self.spread(k, p, 2, own + half, half, right[a])
                self.spread(k, p, 3, own, half, left[a])

        def gather_mid(self, k):
            half = self.sizes[k] // 2
            for p in range(3):
                a = AXES[p][k]
                self.got(k, p, 0)
                self.spread(k, p, 4, self.quarter(k, p, 3), half, right[a])
                self.got(k, p, 1)
                self.spread(k, p, 5, self.quarter(k, p, 1) + half, half, left[a])

        def gather_end(self, k):
            for p in range(3):
                self.got(k, p, 2, 3, 4, 5)

    one = Chunk(0, ta, (r1a, r2a, r3a), (rsa_send, rsa_recv), (aga_send, aga_recv))
    two = Chunk(1, tb, (r1b, r2b, r3b), (rsb_send, rsb_recv), (agb_send, agb_recv))

    early = list(sent)
    sent.clear()
    one.gram_far()
    one.scatter_far(0)
    one.gram_near()
    one.scatter_near(0)
    two.gram_far()
    one.gram_own()
    one.scatter_mid(0)
    two.scatter_far(0)
    two.gram_near()
    two.scatter_near(0)
    two.gram_own()
    sq_core.wait_recv()
    sq[0] = sq[13] + sq[14]
    squares = square_begin(0)
    turn_all()
    flush(early)
    one.scatter_end(0)
    one.scatter_far(1)
    one.scatter_near(1)
    square_end(0, squares)
    squares = square_begin(1)
    two.scatter_mid(0)
    one.scatter_mid(1)
    one.scatter_end(1)
    one.last_begin()
    two.scatter_end(0)
    two.scatter_far(1)
    two.scatter_near(1)
    one.last_end()
    square_end(1, squares)
    squares = square_begin(2)
    two.scatter_mid(1)
    one.gather_first_end()
    one.gather_begin(1)
    two.scatter_end(1)
    two.last_begin()
    one.gather_mid(1)
    one.gather_end(1)
    early.extend(sent)
    sent.clear()
    one.gather_begin(0)
    two.last_end()
    square_end(2, squares)
    one.gather_mid(0)
    two.gather_first_end()
    two.gather_begin(1)
    two.gather_mid(1)
    two.gather_end(1)
    two.gather_begin(0)
    flush(early)
    one.gather_end(0)

    factor = 0.3 * math.sqrt(M) / (jnp.sqrt(jnp.sum(sq[12], axis=(0, 1), keepdims=True)) + 1e-07)
    factor2 = factor * factor

    def cols(a_ref, i):
        return a_ref[:, pl.ds(al(i * BLK, BLK), BLK)]

    def block(slot):
        o = slot * 512
        return jnp.concatenate([g[pl.ds(al(o, 512), 256), :], g[pl.ds(al(o + 256, 256), 256), :]], axis=1)

    def band(a_ref, j, ds):
        def straight(d, first):
            i = (j + NB - d) % NB
            return cols(a_ref, i), block(first + i)

        def turned(d, first):
            return cols(a_ref, (j + d) % NB), block(first + j)

        a, b = zip(*[straight(*e) for e in ds])
        acc = jnp.dot(jnp.concatenate(a, axis=1), jnp.concatenate(b, axis=0), preferred_element_type=F32)
        a, b = zip(*[turned(*e) for e in ds])
        return acc + lax.dot_general(
            jnp.concatenate(a, axis=1), jnp.concatenate(b, axis=1), NT, preferred_element_type=F32
        )

    whole_one = ((2 * core, 0), (2 * core + 1, NB))
    whole_two = ((2 * core + 4, SECOND),)

    def single(acc_ref, a_ref, chunk, m):
        i, d, _ = block_of(chunk, m)
        j = (i + d) % NB
        b = block(chunk * SECOND + m)
        acc_ref[:, pl.ds(al(j * BLK, BLK), BLK)] += jnp.dot(cols(a_ref, i), b, preferred_element_type=F32)
        acc_ref[:, pl.ds(al(i * BLK, BLK), BLK)] += lax.dot_general(
            cols(a_ref, j), b, NT, preferred_element_type=F32
        )

    def loop(first_k, last_k, f):
        def body(k, carry):
            f(first_k + 2 * k)
            f(first_k + 2 * k + 1)
            return carry

        lax.fori_loop(0, (last_k - first_k) // 2, body, 0)
        if (last_k - first_k) % 2:
            f(last_k - 1)

    def band_at(j):
        return pl.ds(al(j * BLK, BLK), BLK)

    def to_partner(no, src, dst):
        c = remote(src, dst, part_send.at[no], part_recv.at[no], partner)
        c.start()
        sent.append(c)
        return c

    def y_one(j):
        yf[:, band_at(j)] = band(st, j, whole_one)

    loop(0, 6, y_one)
    two.gather_mid(0)
    loop(6, NB, y_one)
    zf[...] = jnp.zeros((CHIP, M), F32)
    for m in (28, 29):
        single(yf, st, 0, m)
    two.gather_end(0)
    def shared(k, a_ref=st, acc_ref=yf):
        single(acc_ref, a_ref, 1, 14 + k)

    loop(0, 9, shared)

    def y_two(j):
        v = yf[:, band_at(j)] + band(st, j, whole_two)
        yf[:, band_at(j)] = v
        yp[:, band_at(j)] = v.astype(BF)

    shares = []
    for h in range(2):
        loop(h * 7, h * 7 + 7, y_two)
        here = pl.ds(h * HALF_M, HALF_M)
        shares.append(to_partner(h, yp.at[:, here], yr.at[:, here]))

    factor = 0.3 * math.sqrt(M) / (jnp.sqrt(jnp.sum(sq[12], axis=(0, 1), keepdims=True)) + 1e-07)
    factor2 = factor * factor

    def y_sum(j):
        v = factor2 * (yf[:, band_at(j)] + yr[:, band_at(j)].astype(F32))
        yf[:, band_at(j)] = v
        ybf[:, band_at(j)] = v.astype(BF)

    for h in range(2):
        shares[h].wait_recv()
        loop(h * 7, h * 7 + 7, y_sum)

    for m in (28, 29):
        single(zf, ybf, 0, m)
    def shared(k, a_ref=ybf, acc_ref=zf):
        single(acc_ref, a_ref, 1, 14 + k)

    loop(0, 9, shared)

    def z_band(j):
        return factor2 * (zf[:, band_at(j)] + band(ybf, j, whole_one + whole_two))

    def z_theirs(k):
        zp[:, band_at(k)] = z_band((1 - core) * 7 + k).astype(BF)

    loop(0, 7, z_theirs)
    share = to_partner(2, zp, zr)

    def z_mine(k):
        zf[:, band_at(core * 7 + k)] = z_band(core * 7 + k)

    loop(0, 7, z_mine)
    share.wait_recv()
    for p in range(3):
        ut[pl.ds(p * 128 + COL3, 128 - COL3), :] = jnp.zeros((128 - COL3, HALF_M), BF)

    def finish(k):
        at = band_at(core * 7 + k)
        scaled = (factor * st[:, at].astype(F32)).astype(BF).astype(F32)
        product = factor * (COEFF_B * yf[:, at] + COEFF_C * (zf[:, at] + zr[:, band_at(k)].astype(F32)))
        u = (math.sqrt(K) * (COEFF_A * scaled + product)).astype(BF)
        for p in range(3):
            ut[pl.ds(p * 128, COL3), band_at(k)] = u[p * COL3 : (p + 1) * COL3]

    loop(0, 7, finish)

    early.extend(sent)
    sent.clear()
    y3, y2, y1q = x2p, x1q, x0
    unpack = spread_matrix((8 * PIECE, 8 * ROWS), 0, PIECE, ROWS)
    for m in range(8):
        o = m * 8 * ROWS
        first_lane = o // 128 * 128
        skip = o - first_lane
        width = -(-(skip + 8 * ROWS) // 128) * 128
        v = ut[:, pl.ds(first_lane, width)][:, skip : skip + 8 * ROWS]
        rows = lax.dot_general(unpack, v, NT, preferred_element_type=F32).astype(BF)
        for r in range(8):
            x, y, z = m // 2, m % 2 * 2 + r // 4, r % 4
            for p, at in enumerate(((z, x, y), (x, y, z), (y, x, z))):
                y3[(p,) + at] = rows[r * PIECE : (r + 1) * PIECE, p * 128 : (p + 1) * 128]

    out1 = Exchange(0, 2, lambda p, q: y3.at[p, q], lambda p, q: y2p.at[p, q], outs)
    out2 = Exchange(1, 1, lambda p, q: y2.at[p, q], lambda p, q: y1.at[p, q], outs)
    out3 = Exchange(2, 0, lambda p, q: y1q.at[p, q], lambda p, q: y0.at[p, q], outs)
    for p in range(3):
        out1.begin(p)
    for p in range(3):
        out1.keep(p)
    flush(early)
    early.extend(sent)
    sent.clear()
    narrow = spread_matrix((512, COL2), 0, 128, COL3)
    for p in range(3):
        out1.arrive(p)
        for a in range(4):
            rows = [y2p[(p, q) + plane(p, a)].reshape(4 * PIECE, 128) for q in range(4)]
            rows = jnp.dot(jnp.concatenate(rows, axis=1), narrow, preferred_element_type=F32)
            y2[p, a] = rows.astype(BF).reshape(4, PIECE, COL2)
        out2.begin(p)
    for p in range(3):
        out2.keep(p)
    flush(early)
    early.extend(sent)
    sent.clear()
    for p in range(3):
        out2.arrive(p)
        for a in range(4):
            for q in range(4):
                y1q[p, a, :, q * COL2 : (q + 1) * COL2] = y1[p, q, a]
        out3.begin(p)
    for p in range(3):
        out3.keep(p)
    flush(early)
    for p in range(3):
        out3.arrive(p)
        for q in range(4):
            o = p * THIRD + q * COL1
            out_ref[:, o : o + COL1] = y0[p, q][:ROWS]

    flush(sent)


def local(gradient):
    vmem = pl.BlockSpec(memory_space=pltpu.VMEM)
    dma = pltpu.SemaphoreType.DMA
    return pl.pallas_call(
        kernel,
        out_shape=jax.ShapeDtypeStruct((ROWS, K), BF),
        in_specs=[vmem],
        out_specs=vmem,
        scratch_shapes=[
            pltpu.VMEM((3, 4, PIECE, COL1), BF),
            pltpu.VMEM((3, 4, PIECE, COL1), BF),
            pltpu.VMEM((3, 4, 4, PIECE, COL2), BF),
            pltpu.VMEM((3, 4, 4, PIECE, COL2), BF),
            pltpu.VMEM((3, 4, 4, 4, PIECE, 128), BF),
            pltpu.VMEM((2, 3, 4, 4, 4, PIECE, 128), BF),
            pltpu.VMEM((M, 384), BF),
            pltpu.VMEM((CHIP, M), BF),
            pltpu.VMEM((384, HALF_M), BF),
            pltpu.VMEM((3, 4, 4, 4, PIECE, 128), BF),
            pltpu.VMEM((3, 4, 4, PIECE, COL2), BF),
            pltpu.VMEM((3, 4, PIECE, COL1), BF),
            pltpu.VMEM((3 * 10 * 512, 128), BF),
            pltpu.VMEM((3 * 8 * 512, 128), BF),
            pltpu.VMEM((SLOTS * 512, 128), BF),
            pltpu.VMEM((3, 6, 640, 128), BF),
            pltpu.VMEM((3, 6, 160, 128), BF),
            pltpu.VMEM((3, 3, 80, 128), BF),
            pltpu.VMEM((3, 6, 512, 128), BF),
            pltpu.VMEM((3, 6, 128, 128), BF),
            pltpu.VMEM((3, 3, 64, 128), BF),
            pltpu.VMEM((15, 8, 128), F32),
            pltpu.VMEM((CHIP, M), F32),
            pltpu.VMEM((CHIP, M), BF),
            pltpu.VMEM((CHIP, M), BF),
            pltpu.VMEM((CHIP, M), BF),
            pltpu.VMEM((CHIP, M), F32),
            pltpu.VMEM((CHIP, HALF_M), BF),
            pltpu.VMEM((CHIP, HALF_M), BF),
            dma((3, 3, 3)),
            dma((3, 3, 3)),
            dma((3,)),
            dma((3,)),
            dma((3, 3, 3)),
            dma((3, 3, 3)),
            dma((3,)),
            dma((3,)),
            dma((3, 3, 6)),
            dma((3, 3, 6)),
            dma((3, 3, 6)),
            dma((3, 3, 6)),
            dma((3, 3, 6)),
            dma((3, 3, 6)),
            dma((3, 3, 6)),
            dma((3, 3, 6)),
            dma((4, 3)),
            dma((4, 3)),
        ],
        compiler_params=pltpu.CompilerParams(
            collective_id=0, has_side_effects=True, vmem_limit_bytes=60 * 1024 * 1024
        ),
        cost_estimate=pl.CostEstimate(flops=16 * 10**9, bytes_accessed=5 * 10**6, transcendentals=0),
    )(gradient)


def solution(mesh):
    spec = P(("wide", "narrow"), None)
    return jax.shard_map(local, mesh=mesh, in_specs=(spec,), out_specs=spec, check_vma=False)
```

```python
import math

import jax
import jax.numpy as jnp
from jax import lax
from jax.experimental import pallas as pl
from jax.experimental.pallas import tpu as pltpu
from jax.sharding import PartitionSpec as P

M = 3584
K = 18432

COEFF_A = 3.4445
COEFF_B = -4.775
COEFF_C = 2.0315

MESH = pl.DeviceIdType.MESH
BF = jnp.bfloat16
F32 = jnp.float32
NT = (((1,), (1,)), ((), ()))

ROWS = 28
PIECE = 32
THIRD = K // 3
COL1 = THIRD // 4
COL2 = COL1 // 4
COL3 = COL2 // 4
CHIP = 3 * COL3
HALF_M = M // 2
AXES = ((0, 1, 2), (1, 2, 0), (2, 0, 1))

BLK = 256
NB = M // BLK
PER_PART = (10, 8)
SECOND = 3 * PER_PART[0]
SLOTS = 3 * sum(PER_PART)
SIZES = ((1280, 320, 80), (1024, 256, 64))


def al(x, m=16):
    return pl.multiple_of(x, m)


def kernel(
    in_ref, out_ref,
    x0, x1, x1q, x2, x2p, x3, s_all, st,
    ut, y2p, y1, y0,
    ta, tb, g, r1a, r2a, r3a, r1b, r2b, r3b, sq, yf, ybf, yp, yr, zf, zp, zr,
    in_send, in_recv, core_send, core_recv, out_send, out_recv, part_send, part_recv,
    rsa_send, rsa_recv, aga_send, aga_recv, rsb_send, rsb_recv, agb_send, agb_recv, sq_send, sq_recv,
):
    w, n_ = lax.axis_index("wide"), lax.axis_index("narrow")
    core, z_lo, y = w % 2, (w // 2) % 2, w // 4
    x, z_hi = n_ % 4, n_ // 4
    z = z_hi * 2 + z_lo
    pos = (x, y, z)

    def device(x, y, z, core):
        return ((y * 2 + z % 2) * 2 + core, (z // 2) * 4 + x)

    def shifted(axis, by):
        p = [x, y, z]
        p[axis] = (p[axis] + by) % 4
        return device(*p, core)

    right = [shifted(a, 1) for a in range(3)]
    left = [shifted(a, 3) for a in range(3)]
    across = [shifted(a, 2) for a in range(3)]
    partner = device(x, y, z, 1 - core)

    barrier = pltpu.get_barrier_semaphore()
    for d in right + left + across + [partner]:
        pl.semaphore_signal(barrier, inc=1, device_id=d, device_id_type=MESH)

    def load(k, carry):
        p, q = k // 4, k % 4
        v = in_ref[:, pl.ds(al(k * COL1, COL1), COL1)]
        x0[p, q, pl.ds(0, ROWS), :] = v
        x0[p, q, pl.ds(ROWS, PIECE - ROWS), :] = jnp.zeros((PIECE - ROWS, COL1), BF)
        return carry

    lax.fori_loop(0, 12, load, 0)
    pl.semaphore_wait(barrier, 10)

    def remote(src, dst, send, recv, dev):
        return pltpu.make_async_remote_copy(
            src_ref=src, dst_ref=dst, send_sem=send, recv_sem=recv, device_id=dev, device_id_type=MESH
        )

    sent = []

    def flush(group):
        for c in group:
            c.wait_send()
        group.clear()

    class Exchange:
        def __init__(self, stage, axis_no, src, dst, sems):
            self.stage, self.axis_no, self.src, self.dst, self.sems = stage, axis_no, src, dst, sems
            self.copies = {}

        def begin(self, p):
            a = AXES[p][self.axis_no]
            me = pos[a]
            send, recv = self.sems
            group = []
            for k, dev in ((2, across[a]), (1, right[a]), (3, left[a])):
                c = remote(
                    self.src(p, (me + k) % 4), self.dst(p, me),
                    send.at[self.stage, p, k - 1], recv.at[self.stage, p, k - 1], dev,
                )
                c.start()
                group.append(c)
                sent.append(c)
            self.copies[p] = group

        def keep(self, p):
            me = pos[AXES[p][self.axis_no]]
            src, dst = self.src(p, me), self.dst(p, me)
            dst[...] = src[...]

        def arrive(self, p):
            for c in self.copies[p]:
                c.wait_recv()

    ins = (in_send, in_recv)
    outs = (out_send, out_recv)

    def plane(p, k):
        return (k, slice(None)) if p == 2 else (slice(None), k)

    in1 = Exchange(0, 0, lambda p, q: x0.at[p, q], lambda p, q: x1.at[p, q], ins)
    in2 = Exchange(1, 1, lambda p, q: x1q.at[p, q], lambda p, q: x2.at[p, q], ins)
    in3 = Exchange(2, 2, lambda p, q: x2p.at[p, q], lambda p, q: x3.at[core, p, q], ins)
    for p in range(3):
        in1.begin(p)

    def square(k, total):
        v = x0[k // 12, k // 3 % 4, :, pl.ds(al(k % 3 * 512, 512), 512)].astype(F32)
        v = v * v
        v = (v[:, :128] + v[:, 128:256]) + (v[:, 256:384] + v[:, 384:])
        return total + ((v[:8] + v[8:16]) + (v[16:24] + v[24:]))

    for p in range(3):
        in1.keep(p)
    sq[13] = lax.fori_loop(0, K // 512, square, jnp.zeros((8, 128), F32))
    sq_core = remote(sq.at[13], sq.at[14], sq_send.at[3, 0], sq_recv.at[3, 0], partner)
    sq_core.start()
    sent.append(sq_core)

    def iota(shape, d):
        return lax.broadcasted_iota(jnp.int32, shape, d)

    def ones_where(cond):
        return jnp.where(cond, 1.0, 0.0).astype(BF)

    def spread_matrix(shape, wide, unit, narrow):
        s, r = iota(shape, wide), iota(shape, 1 - wide)
        return ones_where((s % unit < narrow) & (r == (s // unit) * narrow + s % unit))

    for p in range(3):
        in1.arrive(p)
        for a in range(4):
            for q in range(4):
                x1q[p, q, a] = x1[p, a, :, q * COL2 : (q + 1) * COL2]
        in2.begin(p)
    for p in range(3):
        in2.keep(p)
    widen = spread_matrix((COL2, 512), 1, 128, COL3)
    for p in range(3):
        in2.arrive(p)
        for a in range(4):
            rows = jnp.dot(x2[p, a].reshape(4 * PIECE, COL2), widen, preferred_element_type=F32).astype(BF)
            for q in range(4):
                x2p[(p, q) + plane(p, a)] = rows[:, q * 128 : (q + 1) * 128].reshape(4, PIECE, 128)
        in3.begin(p)
    for p in range(3):
        in3.keep(p)
    crossing = []
    for p in range(3):
        in3.arrive(p)
        here = x3.at[core, p]
        c = remote(here, here, core_send.at[p], core_recv.at[p], partner)
        c.start()
        crossing.append(c)
        sent.append(c)

    pack = spread_matrix((8 * ROWS, 8 * PIECE), 1, PIECE, ROWS)

    def pack_rows(owner):
        def body(k, carry):
            x, y0, group = k // 2, k % 2 * 2, [[], [], []]
            for y in (y0, y0 + 1):
                for z in range(4):
                    group[0].append(x3[owner, 0, z, x, y])
                    group[1].append(x3[owner, 1, x, y, z])
                    group[2].append(x3[owner, 2, y, x, z])
            rows = jnp.concatenate([jnp.concatenate(e, axis=0) for e in group], axis=1)
            at = pl.ds(al(owner * HALF_M + k * 8 * ROWS), 8 * ROWS)
            s_all[at, :] = jnp.dot(pack, rows, preferred_element_type=F32).astype(BF)
            return carry

        lax.fori_loop(0, 4, lambda k, carry: body(2 * k + 1, body(2 * k, carry)), 0)

    pack_rows(core)
    for c in crossing:
        c.wait_recv()
    pack_rows(1 - core)

    def turn_all():
        kk, ll = iota((CHIP, 384), 0), iota((CHIP, 384), 1)
        pick = ones_where((ll % 128 < COL3) & (kk == (ll // 128) * COL3 + ll % 128))

        def turn(j, carry):
            at = pl.ds(al(j * BLK, BLK), BLK)
            st[:, at] = lax.dot_general(pick, s_all[at, :], NT, preferred_element_type=F32).astype(BF)
            return carry

        lax.fori_loop(0, NB // 2, lambda k, carry: turn(2 * k + 1, turn(2 * k, carry)), 0)

    def block_of(chunk, m):
        if chunk == 0:
            i = jnp.where(m < 28, m % NB, 4 * core + m - 28)
            d = jnp.where(m < 28, 2 * core + m // NB, 7)
            return i, d, jnp.where(d == 0, 0.5, 1.0)
        i = jnp.where(m < 14, m, jnp.where(m < 21, 7 * core + m - 14, (4 * core + m - 19) % NB))
        d = jnp.where(m < 14, 4 + 2 * core, jnp.where(m < 21, 5, 7))
        return i, d, jnp.where((d == 7) & ((i >= 7) | (m == 23)), 0.0, 1.0)

    def gram_block(chunk, m, t):
        i, d, scale = block_of(chunk, m)
        j = (i + d) % NB
        ri = pl.ds(al(i * BLK, BLK), BLK)
        rj = pl.ds(al(j * BLK, BLK), BLK)
        acc = lax.dot_general(s_all[ri, :], s_all[rj, :], NT, preferred_element_type=F32)
        acc = (scale * acc).astype(BF)
        t[pl.ds(al(m * 512, 512), 256), :] = acc[:, :128]
        t[pl.ds(al(m * 512 + 256, 256), 256), :] = acc[:, 128:]

    def square_begin(s):
        group = [
            remote(sq.at[4 * s], sq.at[4 * s + 1 + k], sq_send.at[s, k], sq_recv.at[s, k], dev)
            for k, dev in enumerate((right[s], left[s], across[s]))
        ]
        for c in group:
            c.start()
        sent.extend(group)
        return group

    def square_end(s, group):
        for c in group:
            c.wait_recv()
        sq[4 * s + 4] = (sq[4 * s] + sq[4 * s + 3]) + (sq[4 * s + 1] + sq[4 * s + 2])

    class Chunk:
        def __init__(self, no, t, bufs, rs, ag):
            self.no, self.t, self.bufs, self.rs, self.ag = no, t, bufs, rs, ag
            self.blocks = PER_PART[no]
            self.sizes = SIZES[no]
            base = [p * self.blocks * 512 for p in range(3)]
            self.bases = [base]
            for k in range(3):
                base = [base[p] + pos[AXES[p][k]] * self.sizes[k] for p in range(3)]
                self.bases.append(base)
            self.mine = no * SECOND * 512
            self.copies = {}

        def quarter(self, k, p, by):
            return self.bases[k][p] + ((pos[AXES[p][k]] + by) % 4) * self.sizes[k]

        def gram(self, p, start, count):
            for m in range(count):
                gram_block(self.no, p * self.blocks + start + m, self.t)

        def gram_far(self):
            for p in range(3):
                q = (pos[AXES[p][0]] + 2) % 4
                self.gram(p, self.blocks * q // 4, 2 + self.blocks % 4 // 2)

        def gram_near(self):
            for p in range(3):
                me = pos[AXES[p][0]]
                if self.blocks % 4:
                    self.gram(p, self.blocks // 4 + self.blocks // 2 * (me // 2), 1)
                for by in (1, 3):
                    self.gram(p, (self.blocks * ((me + by) % 4) + 2) // 4, 2)

        def gram_own(self):
            for p in range(3):
                self.gram(p, (self.blocks * pos[AXES[p][0]] + 2) // 4, 2)

        def push(self, k, p, no, off, rows):
            a = AXES[p][k]
            c = remote(
                self.t.at[pl.ds(al(off), rows), :],
                self.bufs[k].at[p, no],
                self.rs[0].at[k, p, no],
                self.rs[1].at[k, p, no],
                right[a] if no < 3 else left[a],
            )
            c.start()
            self.copies[k, p, no] = c
            sent.append(c)

        def add_rows(self, off, rows, srcs):
            step = rows // 2 if rows > 200 else rows
            t = self.t

            def body(m, carry):
                at = pl.ds(al(off + m * step), step)
                total = t[at, :]
                for src in srcs:
                    total = total + src[pl.ds(al(m * step), step), :]
                t[at, :] = total
                return carry

            lax.fori_loop(0, rows // step, body, 0)

        def scatter_far(self, k):
            half = self.sizes[k] // 2
            for p in range(3):
                self.push(k, p, 0, self.quarter(k, p, 2), half)
                self.push(k, p, 3, self.quarter(k, p, 2) + half, half)

        def scatter_near(self, k):
            half = self.sizes[k] // 2
            for p in range(3):
                self.push(k, p, 1, self.quarter(k, p, 1) + half, half)
                self.push(k, p, 4, self.quarter(k, p, 3), half)

        def scatter_mid(self, k):
            half = self.sizes[k] // 2
            for p in range(3):
                self.copies[k, p, 0].wait_recv()
                self.add_rows(self.quarter(k, p, 1), half, [self.bufs[k].at[p, 0]])
                self.push(k, p, 2, self.quarter(k, p, 1), half)
                self.copies[k, p, 3].wait_recv()
                self.add_rows(self.quarter(k, p, 3) + half, half, [self.bufs[k].at[p, 3]])
                self.push(k, p, 5, self.quarter(k, p, 3) + half, half)

        def scatter_end(self, k):
            half = self.sizes[k] // 2
            for p in range(3):
                for h, one, two in ((0, 4, 2), (1, 1, 5)):
                    self.copies[k, p, one].wait_recv()
                    self.copies[k, p, two].wait_recv()
                    self.add_rows(
                        self.quarter(k, p, 0) + h * half, half, [self.bufs[k].at[p, one], self.bufs[k].at[p, two]]
                    )

        def ring_begin(self, s):
            size = self.sizes[s]
            for p in range(3):
                a = AXES[p][s]
                for k, dev in ((2, across[a]), (1, right[a]), (3, left[a])):
                    c = remote(
                        self.t.at[pl.ds(al(self.quarter(s, p, k)), size), :],
                        self.bufs[s].at[p, k - 1],
                        self.rs[0].at[s, p, k - 1],
                        self.rs[1].at[s, p, k - 1],
                        dev,
                    )
                    c.start()
                    self.copies[s, p, k] = c
                    sent.append(c)

        def ring_end(self, s):
            size = self.sizes[s]
            for p in range(3):
                for k in (1, 2, 3):
                    self.copies[s, p, k].wait_recv()
                off = self.bases[s + 1][p]
                step = 80 if size % 80 == 0 else 64

                def body(m, carry):
                    at = pl.ds(al(off + m * step), step)
                    total = self.t[at, :].astype(F32)
                    for k in range(3):
                        total = total + self.bufs[s][p, k, pl.ds(al(m * step), step)].astype(F32)
                    if s == 2:
                        g[pl.ds(al(self.mine + off), size), :] = total.astype(BF)
                    else:
                        self.t[at, :] = total.astype(BF)
                    return carry

                lax.fori_loop(0, size // step, body, 0)
            if s == 2:
                self.rounds(2)

        def rounds(self, s):
            for p in range(3):
                a = AXES[p][s]
                off = self.bases[s + 1][p]
                for k, dev in ((2, across[a]), (1, right[a]), (3, left[a])):
                    self.spread(s, p, k - 1, off, self.sizes[s], dev)

        def rounds_end(self, s):
            for p in range(3):
                self.got(s, p, 0, 1, 2)

        def spread(self, k, p, no, off, rows, dev):
            here = g.at[pl.ds(al(self.mine + off), rows), :]
            c = remote(here, here, self.ag[0].at[k, p, no], self.ag[1].at[k, p, no], dev)
            c.start()
            self.copies["g", k, p, no] = c
            sent.append(c)

        def got(self, k, p, *nos):
            for no in nos:
                self.copies["g", k, p, no].wait_recv()

        def gather_begin(self, k):
            half = self.sizes[k] // 2
            for p in range(3):
                own = self.quarter(k, p, 0)
                a = AXES[p][k]
                self.spread(k, p, 0, own, half, right[a])
                self.spread(k, p, 1, own + half, half, left[a])
            for p in range(3):
                own = self.quarter(k, p, 0)
                a = AXES[p][k]
                self.spread(k, p, 2, own + half, half, right[a])
                self.spread(k, p, 3, own, half, left[a])

        def gather_mid(self, k):
            half = self.sizes[k] // 2
            for p in range(3):
                a = AXES[p][k]
                self.got(k, p, 0)
                self.spread(k, p, 4, self.quarter(k, p, 3), half, right[a])
                self.got(k, p, 1)
                self.spread(k, p, 5, self.quarter(k, p, 1) + half, half, left[a])

        def gather_end(self, k):
            for p in range(3):
                self.got(k, p, 2, 3, 4, 5)

    one = Chunk(0, ta, (r1a, r2a, r3a), (rsa_send, rsa_recv), (aga_send, aga_recv))
    two = Chunk(1, tb, (r1b, r2b, r3b), (rsb_send, rsb_recv), (agb_send, agb_recv))

    early = list(sent)
    sent.clear()
    one.gram_far()
    one.scatter_far(0)
    one.gram_near()
    one.scatter_near(0)
    two.gram_far()
    one.gram_own()
    one.scatter_mid(0)
    two.scatter_far(0)
    two.gram_near()
    two.scatter_near(0)
    two.gram_own()
    sq_core.wait_recv()
    sq[0] = sq[13] + sq[14]
    squares = square_begin(0)
    turn_all()
    flush(early)
    one.scatter_end(0)
    one.ring_begin(1)
    square_end(0, squares)
    squares = square_begin(1)
    two.scatter_mid(0)
    one.ring_end(1)
    one.ring_begin(2)
    square_end(1, squares)
    squares = square_begin(2)
    two.scatter_end(0)
    two.ring_begin(1)
    one.ring_end(2)
    square_end(2, squares)
    two.ring_end(1)
    two.ring_begin(2)
    one.rounds_end(2)
    one.rounds(1)
    two.ring_end(2)
    one.rounds_end(1)
    early.extend(sent)
    sent.clear()
    one.gather_begin(0)
    two.rounds_end(2)
    two.rounds(1)
    one.gather_mid(0)
    two.rounds_end(1)
    two.gather_begin(0)
    flush(early)
    one.gather_end(0)

    def cols(a_ref, i):
        return a_ref[:, pl.ds(al(i * BLK, BLK), BLK)]

    def block(slot):
        o = slot * 512
        return jnp.concatenate([g[pl.ds(al(o, 512), 256), :], g[pl.ds(al(o + 256, 256), 256), :]], axis=1)

    def band(a_ref, j, ds):
        def straight(d, first):
            i = (j + NB - d) % NB
            return cols(a_ref, i), block(first + i)

        def turned(d, first):
            return cols(a_ref, (j + d) % NB), block(first + j)

        a, b = zip(*[straight(*e) for e in ds])
        acc = jnp.dot(jnp.concatenate(a, axis=1), jnp.concatenate(b, axis=0), preferred_element_type=F32)
        a, b = zip(*[turned(*e) for e in ds])
        return acc + lax.dot_general(
            jnp.concatenate(a, axis=1), jnp.concatenate(b, axis=1), NT, preferred_element_type=F32
        )

    whole_one = ((2 * core, 0), (2 * core + 1, NB))
    whole_two = ((2 * core + 4, SECOND),)

    def single(acc_ref, a_ref, chunk, m):
        i, d, _ = block_of(chunk, m)
        j = (i + d) % NB
        b = block(chunk * SECOND + m)
        acc_ref[:, pl.ds(al(j * BLK, BLK), BLK)] += jnp.dot(cols(a_ref, i), b, preferred_element_type=F32)
        acc_ref[:, pl.ds(al(i * BLK, BLK), BLK)] += lax.dot_general(
            cols(a_ref, j), b, NT, preferred_element_type=F32
        )

    def loop(first_k, last_k, f):
        def body(k, carry):
            f(first_k + 2 * k)
            f(first_k + 2 * k + 1)
            return carry

        lax.fori_loop(0, (last_k - first_k) // 2, body, 0)
        if (last_k - first_k) % 2:
            f(last_k - 1)

    def band_at(j):
        return pl.ds(al(j * BLK, BLK), BLK)

    def to_partner(no, src, dst):
        c = remote(src, dst, part_send.at[no], part_recv.at[no], partner)
        c.start()
        sent.append(c)
        return c

    def y_one(j):
        yf[:, band_at(j)] = band(st, j, whole_one)

    loop(0, 6, y_one)
    two.gather_mid(0)
    loop(6, NB, y_one)
    zf[...] = jnp.zeros((CHIP, M), F32)
    for m in (28, 29):
        single(yf, st, 0, m)
    two.gather_end(0)
    def shared(k, a_ref=st, acc_ref=yf):
        single(acc_ref, a_ref, 1, 14 + k)

    loop(0, 9, shared)

    def y_two(j):
        v = yf[:, band_at(j)] + band(st, j, whole_two)
        yf[:, band_at(j)] = v
        yp[:, band_at(j)] = v.astype(BF)

    shares = []
    for h in range(2):
        loop(h * 7, h * 7 + 7, y_two)
        here = pl.ds(h * HALF_M, HALF_M)
        shares.append(to_partner(h, yp.at[:, here], yr.at[:, here]))

    factor = 0.3 * math.sqrt(M) / (jnp.sqrt(jnp.sum(sq[12], axis=(0, 1), keepdims=True)) + 1e-07)
    factor2 = factor * factor

    def y_sum(j):
        v = factor2 * (yf[:, band_at(j)] + yr[:, band_at(j)].astype(F32))
        yf[:, band_at(j)] = v
        ybf[:, band_at(j)] = v.astype(BF)

    for h in range(2):
        shares[h].wait_recv()
        loop(h * 7, h * 7 + 7, y_sum)

    for m in (28, 29):
        single(zf, ybf, 0, m)
    def shared(k, a_ref=ybf, acc_ref=zf):
        single(acc_ref, a_ref, 1, 14 + k)

    loop(0, 9, shared)

    def z_band(j):
        return factor2 * (zf[:, band_at(j)] + band(ybf, j, whole_one + whole_two))

    def z_theirs(k):
        zp[:, band_at(k)] = z_band((1 - core) * 7 + k).astype(BF)

    loop(0, 7, z_theirs)
    share = to_partner(2, zp, zr)

    def z_mine(k):
        zf[:, band_at(core * 7 + k)] = z_band(core * 7 + k)

    loop(0, 7, z_mine)
    share.wait_recv()
    for p in range(3):
        ut[pl.ds(p * 128 + COL3, 128 - COL3), :] = jnp.zeros((128 - COL3, HALF_M), BF)

    def finish(k):
        at = band_at(core * 7 + k)
        scaled = (factor * st[:, at].astype(F32)).astype(BF).astype(F32)
        product = factor * (COEFF_B * yf[:, at] + COEFF_C * (zf[:, at] + zr[:, band_at(k)].astype(F32)))
        u = (math.sqrt(K) * (COEFF_A * scaled + product)).astype(BF)
        for p in range(3):
            ut[pl.ds(p * 128, COL3), band_at(k)] = u[p * COL3 : (p + 1) * COL3]

    loop(0, 7, finish)

    early.extend(sent)
    sent.clear()
    y3, y2, y1q = x2p, x1q, x0
    unpack = spread_matrix((8 * PIECE, 8 * ROWS), 0, PIECE, ROWS)
    for m in range(8):
        o = m * 8 * ROWS
        first_lane = o // 128 * 128
        skip = o - first_lane
        width = -(-(skip + 8 * ROWS) // 128) * 128
        v = ut[:, pl.ds(first_lane, width)][:, skip : skip + 8 * ROWS]
        rows = lax.dot_general(unpack, v, NT, preferred_element_type=F32).astype(BF)
        for r in range(8):
            x, y, z = m // 2, m % 2 * 2 + r // 4, r % 4
            for p, at in enumerate(((z, x, y), (x, y, z), (y, x, z))):
                y3[(p,) + at] = rows[r * PIECE : (r + 1) * PIECE, p * 128 : (p + 1) * 128]

    out1 = Exchange(0, 2, lambda p, q: y3.at[p, q], lambda p, q: y2p.at[p, q], outs)
    out2 = Exchange(1, 1, lambda p, q: y2.at[p, q], lambda p, q: y1.at[p, q], outs)
    out3 = Exchange(2, 0, lambda p, q: y1q.at[p, q], lambda p, q: y0.at[p, q], outs)
    for p in range(3):
        out1.begin(p)
    for p in range(3):
        out1.keep(p)
    flush(early)
    early.extend(sent)
    sent.clear()
    narrow = spread_matrix((512, COL2), 0, 128, COL3)
    for p in range(3):
        out1.arrive(p)
        for a in range(4):
            rows = [y2p[(p, q) + plane(p, a)].reshape(4 * PIECE, 128) for q in range(4)]
            rows = jnp.dot(jnp.concatenate(rows, axis=1), narrow, preferred_element_type=F32)
            y2[p, a] = rows.astype(BF).reshape(4, PIECE, COL2)
        out2.begin(p)
    for p in range(3):
        out2.keep(p)
    flush(early)
    early.extend(sent)
    sent.clear()
    for p in range(3):
        out2.arrive(p)
        for a in range(4):
            for q in range(4):
                y1q[p, a, :, q * COL2 : (q + 1) * COL2] = y1[p, q, a]
        out3.begin(p)
    for p in range(3):
        out3.keep(p)
    flush(early)
    for p in range(3):
        out3.arrive(p)
        for q in range(4):
            o = p * THIRD + q * COL1
            out_ref[:, o : o + COL1] = y0[p, q][:ROWS]

    flush(sent)


def local(gradient):
    vmem = pl.BlockSpec(memory_space=pltpu.VMEM)
    dma = pltpu.SemaphoreType.DMA
    return pl.pallas_call(
        kernel,
        out_shape=jax.ShapeDtypeStruct((ROWS, K), BF),
        in_specs=[vmem],
        out_specs=vmem,
        scratch_shapes=[
            pltpu.VMEM((3, 4, PIECE, COL1), BF),
            pltpu.VMEM((3, 4, PIECE, COL1), BF),
            pltpu.VMEM((3, 4, 4, PIECE, COL2), BF),
            pltpu.VMEM((3, 4, 4, PIECE, COL2), BF),
            pltpu.VMEM((3, 4, 4, 4, PIECE, 128), BF),
            pltpu.VMEM((2, 3, 4, 4, 4, PIECE, 128), BF),
            pltpu.VMEM((M, 384), BF),
            pltpu.VMEM((CHIP, M), BF),
            pltpu.VMEM((384, HALF_M), BF),
            pltpu.VMEM((3, 4, 4, 4, PIECE, 128), BF),
            pltpu.VMEM((3, 4, 4, PIECE, COL2), BF),
            pltpu.VMEM((3, 4, PIECE, COL1), BF),
            pltpu.VMEM((3 * 10 * 512, 128), BF),
            pltpu.VMEM((3 * 8 * 512, 128), BF),
            pltpu.VMEM((SLOTS * 512, 128), BF),
            pltpu.VMEM((3, 6, 640, 128), BF),
            pltpu.VMEM((3, 3, 320, 128), BF),
            pltpu.VMEM((3, 3, 80, 128), BF),
            pltpu.VMEM((3, 6, 512, 128), BF),
            pltpu.VMEM((3, 3, 256, 128), BF),
            pltpu.VMEM((3, 3, 64, 128), BF),
            pltpu.VMEM((15, 8, 128), F32),
            pltpu.VMEM((CHIP, M), F32),
            pltpu.VMEM((CHIP, M), BF),
            pltpu.VMEM((CHIP, M), BF),
            pltpu.VMEM((CHIP, M), BF),
            pltpu.VMEM((CHIP, M), F32),
            pltpu.VMEM((CHIP, HALF_M), BF),
            pltpu.VMEM((CHIP, HALF_M), BF),
            dma((3, 3, 3)),
            dma((3, 3, 3)),
            dma((3,)),
            dma((3,)),
            dma((3, 3, 3)),
            dma((3, 3, 3)),
            dma((3,)),
            dma((3,)),
            dma((3, 3, 6)),
            dma((3, 3, 6)),
            dma((3, 3, 6)),
            dma((3, 3, 6)),
            dma((3, 3, 6)),
            dma((3, 3, 6)),
            dma((3, 3, 6)),
            dma((3, 3, 6)),
            dma((4, 3)),
            dma((4, 3)),
        ],
        compiler_params=pltpu.CompilerParams(
            collective_id=0, has_side_effects=True, vmem_limit_bytes=60 * 1024 * 1024
        ),
        cost_estimate=pl.CostEstimate(flops=16 * 10**9, bytes_accessed=5 * 10**6, transcendentals=0),
    )(gradient)


def solution(mesh):
    spec = P(("wide", "narrow"), None)
    return jax.shard_map(local, mesh=mesh, in_specs=(spec,), out_specs=spec, check_vma=False)
```

```python
import math

import jax
import jax.numpy as jnp
from jax import lax
from jax.experimental import pallas as pl
from jax.experimental.pallas import tpu as pltpu
from jax.sharding import PartitionSpec as P

M = 3584
K = 18432

COEFF_A = 3.4445
COEFF_B = -4.775
COEFF_C = 2.0315

MESH = pl.DeviceIdType.MESH
BF = jnp.bfloat16
F32 = jnp.float32
NT = (((1,), (1,)), ((), ()))

ROWS = 28
PIECE = 32
THIRD = K // 3
COL1 = THIRD // 4
COL2 = COL1 // 4
COL3 = COL2 // 4
CHIP = 3 * COL3
HALF_M = M // 2
AXES = ((0, 1, 2), (1, 2, 0), (2, 0, 1))

BLK = 256
NB = M // BLK
PER_PART = (10, 8)
SECOND = 3 * PER_PART[0]
SLOTS = 3 * sum(PER_PART)
SIZES = ((1280, 320, 80), (1024, 256, 64))


def al(x, m=16):
    return pl.multiple_of(x, m)


def kernel(
    in_ref, y0,
    rows_in, x0, x2, x2p, x3, s_all, st,
    ut, y2p, y2,
    ta, tb, g, r1a, r2a, r3a, r1b, r2b, r3b, sq, yf, ybf, yp, yr, zf, zp, zr,
    io_sem, in_send, in_recv, in_plane_send, in_plane_recv, core_send, core_recv,
    out_send, out_recv, out_plane_send, out_plane_recv, part_send, part_recv,
    rsa_send, rsa_recv, aga_send, aga_recv, rsb_send, rsb_recv, agb_send, agb_recv, sq_send, sq_recv,
):
    w, n_ = lax.axis_index("wide"), lax.axis_index("narrow")
    core, z_lo, y = w % 2, (w // 2) % 2, w // 4
    x, z_hi = n_ % 4, n_ // 4
    z = z_hi * 2 + z_lo
    pos = (x, y, z)

    def device(x, y, z, core):
        return ((y * 2 + z % 2) * 2 + core, (z // 2) * 4 + x)

    def shifted(axis, by):
        p = [x, y, z]
        p[axis] = (p[axis] + by) % 4
        return device(*p, core)

    right = [shifted(a, 1) for a in range(3)]
    left = [shifted(a, 3) for a in range(3)]
    across = [shifted(a, 2) for a in range(3)]
    partner = device(x, y, z, 1 - core)

    def in_plane(p, d, e):
        a, b, _ = AXES[p]
        if e == 0:
            return (right, across, left)[d - 1][a]
        if d == 0:
            return (right, across, left)[e - 1][b]
        v = [x, y, z]
        v[a] = (v[a] + d) % 4
        v[b] = (v[b] + e) % 4
        return device(*v, core)

    steps = [(d, e) for d in range(4) for e in range(4) if d or e]
    plane_devices = [[in_plane(p, d, e) for d, e in steps] for p in range(3)]
    diagonal = [plane_devices[p][k] for p in range(3) for k, (d, e) in enumerate(steps) if d and e]

    barrier = pltpu.get_barrier_semaphore()
    for d in right + left + across + diagonal + [partner]:
        pl.semaphore_signal(barrier, inc=1, device_id=d, device_id_type=MESH)

    fetch = pltpu.make_async_copy(in_ref, rows_in, io_sem.at[0])
    fetch.start()
    fetch.wait()

    def load(k, carry):
        p, q = k // 4, k % 4
        v = rows_in[:, pl.ds(al(k * COL1, COL1), COL1)]
        for e in range(4):
            x0[p, q * 4 + e, pl.ds(0, ROWS), :] = v[:, e * COL2 : (e + 1) * COL2]
            x0[p, q * 4 + e, pl.ds(ROWS, PIECE - ROWS), :] = jnp.zeros((PIECE - ROWS, COL2), BF)
        return carry

    lax.fori_loop(0, 12, load, 0)
    pl.semaphore_wait(barrier, 37)

    def remote(src, dst, send, recv, dev):
        return pltpu.make_async_remote_copy(
            src_ref=src, dst_ref=dst, send_sem=send, recv_sem=recv, device_id=dev, device_id_type=MESH
        )

    sent = []

    def flush(group):
        for c in group:
            c.wait_send()
        group.clear()

    class Exchange:
        def __init__(self, stage, axis_no, src, dst, sems):
            self.stage, self.axis_no, self.src, self.dst, self.sems = stage, axis_no, src, dst, sems
            self.copies = {}

        def begin(self, p):
            a = AXES[p][self.axis_no]
            me = pos[a]
            send, recv = self.sems
            group = []
            for k, dev in ((2, across[a]), (1, right[a]), (3, left[a])):
                c = remote(
                    self.src(p, (me + k) % 4), self.dst(p, me),
                    send.at[self.stage, p, k - 1], recv.at[self.stage, p, k - 1], dev,
                )
                c.start()
                group.append(c)
                sent.append(c)
            self.copies[p] = group

        def keep(self, p):
            me = pos[AXES[p][self.axis_no]]
            src, dst = self.src(p, me), self.dst(p, me)
            dst[...] = src[...]

        def arrive(self, p):
            for c in self.copies[p]:
                c.wait_recv()

    def spot(p, a, b):
        return b * 4 + a if p == 2 else a * 4 + b

    class PlaneExchange:
        def __init__(self, src, dst, src_spot, dst_spot, send, recv):
            self.src, self.dst, self.src_spot, self.dst_spot = src, dst, src_spot, dst_spot
            self.send, self.recv = send, recv

        def begin(self, p):
            a, b, _ = AXES[p]
            here = self.dst.at[p, self.dst_spot(p, pos[a], pos[b])]
            for (d, e), dev in zip(steps, plane_devices[p]):
                there = self.src_spot(p, (pos[a] + d) % 4, (pos[b] + e) % 4)
                remote(self.src.at[p, there], here, self.send.at[p], self.recv.at[p], dev).start()

        def keep(self, p):
            a, b, _ = AXES[p]
            self.dst[p, self.dst_spot(p, pos[a], pos[b])] = self.src[p, self.src_spot(p, pos[a], pos[b])]

        def arrive(self, p):
            all_of = self.dst.at[p, pl.ds(0, 15)]
            pltpu.make_async_copy(all_of, all_of, self.recv.at[p]).wait()

        def left(self, p):
            all_of = self.src.at[p, pl.ds(0, 15)]
            pltpu.make_async_copy(all_of, all_of, self.send.at[p]).wait()

    ins = (in_send, in_recv)
    outs = (out_send, out_recv)
    columns = lambda p, a, b: a * 4 + b
    in1 = PlaneExchange(x0, x2, columns, spot, in_plane_send, in_plane_recv)
    in3 = Exchange(0, 2, lambda p, q: x2p.at[p, q], lambda p, q: x3.at[core, p, q], ins)
    for p in range(3):
        in1.begin(p)

    def square(k, total):
        for e in range(4):
            v = x0[k // 4, k % 4 * 4 + e].astype(F32)
            v = v * v
            v = (v[:, :128] + v[:, 128:256]) + v[:, 256:]
            total = total + ((v[:8] + v[8:16]) + (v[16:24] + v[24:]))
        return total

    for p in range(3):
        in1.keep(p)
    sq[13] = lax.fori_loop(0, 12, square, jnp.zeros((8, 128), F32))
    sq_core = remote(sq.at[13], sq.at[14], sq_send.at[3, 0], sq_recv.at[3, 0], partner)
    sq_core.start()
    sent.append(sq_core)

    def iota(shape, d):
        return lax.broadcasted_iota(jnp.int32, shape, d)

    def ones_where(cond):
        return jnp.where(cond, 1.0, 0.0).astype(BF)

    def spread_matrix(shape, wide, unit, narrow):
        s, r = iota(shape, wide), iota(shape, 1 - wide)
        return ones_where((s % unit < narrow) & (r == (s // unit) * narrow + s % unit))

    widen = spread_matrix((COL2, 512), 1, 128, COL3)
    for p in range(3):
        in1.arrive(p)
        for u in range(4):
            rows = x2[p, pl.ds(4 * u, 4)].reshape(4 * PIECE, COL2)
            rows = jnp.dot(rows, widen, preferred_element_type=F32).astype(BF)
            for q in range(4):
                x2p[p, q, u] = rows[:, q * 128 : (q + 1) * 128].reshape(4, PIECE, 128)
        in3.begin(p)
    for p in range(3):
        in3.keep(p)
    crossing = []
    for p in range(3):
        in3.arrive(p)
        here = x3.at[core, p]
        c = remote(here, here, core_send.at[p], core_recv.at[p], partner)
        c.start()
        crossing.append(c)
        sent.append(c)

    pack = spread_matrix((8 * ROWS, 8 * PIECE), 1, PIECE, ROWS)

    def pack_rows(owner):
        def body(k, carry):
            x, y0, group = k // 2, k % 2 * 2, [[], [], []]
            for y in (y0, y0 + 1):
                for z in range(4):
                    group[0].append(x3[owner, 0, z, x, y])
                    group[1].append(x3[owner, 1, x, y, z])
                    group[2].append(x3[owner, 2, y, x, z])
            rows = jnp.concatenate([jnp.concatenate(e, axis=0) for e in group], axis=1)
            at = pl.ds(al(owner * HALF_M + k * 8 * ROWS), 8 * ROWS)
            s_all[at, :] = jnp.dot(pack, rows, preferred_element_type=F32).astype(BF)
            return carry

        lax.fori_loop(0, 4, lambda k, carry: body(2 * k + 1, body(2 * k, carry)), 0)

    pack_rows(core)
    for c in crossing:
        c.wait_recv()
    pack_rows(1 - core)

    def turn_all():
        kk, ll = iota((CHIP, 384), 0), iota((CHIP, 384), 1)
        pick = ones_where((ll % 128 < COL3) & (kk == (ll // 128) * COL3 + ll % 128))

        def turn(j, carry):
            at = pl.ds(al(j * BLK, BLK), BLK)
            st[:, at] = lax.dot_general(pick, s_all[at, :], NT, preferred_element_type=F32).astype(BF)
            return carry

        lax.fori_loop(0, NB // 2, lambda k, carry: turn(2 * k + 1, turn(2 * k, carry)), 0)

    def block_of(chunk, m):
        if chunk == 0:
            i = jnp.where(m < 28, m % NB, 4 * core + m - 28)
            d = jnp.where(m < 28, 2 * core + m // NB, 7)
            return i, d, jnp.where(d == 0, 0.5, 1.0)
        i = jnp.where(m < 14, m, jnp.where(m < 21, 7 * core + m - 14, (4 * core + m - 19) % NB))
        d = jnp.where(m < 14, 4 + 2 * core, jnp.where(m < 21, 5, 7))
        return i, d, jnp.where((d == 7) & ((i >= 7) | (m == 23)), 0.0, 1.0)

    def gram_block(chunk, m, t):
        i, d, scale = block_of(chunk, m)
        j = (i + d) % NB
        ri = pl.ds(al(i * BLK, BLK), BLK)
        rj = pl.ds(al(j * BLK, BLK), BLK)
        acc = lax.dot_general(s_all[ri, :], s_all[rj, :], NT, preferred_element_type=F32)
        acc = (scale * acc).astype(BF)
        t[pl.ds(al(m * 512, 512), 256), :] = acc[:, :128]
        t[pl.ds(al(m * 512 + 256, 256), 256), :] = acc[:, 128:]

    def square_begin(s):
        group = [
            remote(sq.at[4 * s], sq.at[4 * s + 1 + k], sq_send.at[s, k], sq_recv.at[s, k], dev)
            for k, dev in enumerate((right[s], left[s], across[s]))
        ]
        for c in group:
            c.start()
        sent.extend(group)
        return group

    def square_end(s, group):
        for c in group:
            c.wait_recv()
        sq[4 * s + 4] = (sq[4 * s] + sq[4 * s + 3]) + (sq[4 * s + 1] + sq[4 * s + 2])

    class Chunk:
        def __init__(self, no, t, bufs, rs, ag):
            self.no, self.t, self.bufs, self.rs, self.ag = no, t, bufs, rs, ag
            self.blocks = PER_PART[no]
            self.sizes = SIZES[no]
            base = [p * self.blocks * 512 for p in range(3)]
            self.bases = [base]
            for k in range(3):
                base = [base[p] + pos[AXES[p][k]] * self.sizes[k] for p in range(3)]
                self.bases.append(base)
            self.mine = no * SECOND * 512
            self.copies = {}

        def quarter(self, k, p, by):
            return self.bases[k][p] + ((pos[AXES[p][k]] + by) % 4) * self.sizes[k]

        def gram(self, p, start, count):
            for m in range(count):
                gram_block(self.no, p * self.blocks + start + m, self.t)

        def gram_far(self):
            for p in range(3):
                q = (pos[AXES[p][0]] + 2) % 4
                self.gram(p, self.blocks * q // 4, 2 + self.blocks % 4 // 2)

        def gram_near(self):
            for p in range(3):
                me = pos[AXES[p][0]]
                if self.blocks % 4:
                    self.gram(p, self.blocks // 4 + self.blocks // 2 * (me // 2), 1)
                for by in (1, 3):
                    self.gram(p, (self.blocks * ((me + by) % 4) + 2) // 4, 2)

        def gram_own(self):
            for p in range(3):
                self.gram(p, (self.blocks * pos[AXES[p][0]] + 2) // 4, 2)

        def push(self, k, p, no, off, rows):
            a = AXES[p][k]
            c = remote(
                self.t.at[pl.ds(al(off), rows), :],
                self.bufs[k].at[p, no],
                self.rs[0].at[k, p, no],
                self.rs[1].at[k, p, no],
                right[a] if no < 3 else left[a],
            )
            c.start()
            self.copies[k, p, no] = c
            sent.append(c)

        def add_rows(self, off, rows, srcs):
            step = rows // 2 if rows > 200 else rows
            t = self.t

            def body(m, carry):
                at = pl.ds(al(off + m * step), step)
                total = t[at, :]
                for src in srcs:
                    total = total + src[pl.ds(al(m * step), step), :]
                t[at, :] = total
                return carry

            lax.fori_loop(0, rows // step, body, 0)

        def scatter_far(self, k):
            half = self.sizes[k] // 2
            for p in range(3):
                self.push(k, p, 0, self.quarter(k, p, 2), half)
                self.push(k, p, 3, self.quarter(k, p, 2) + half, half)

        def scatter_near(self, k):
            half = self.sizes[k] // 2
            for p in range(3):
                self.push(k, p, 1, self.quarter(k, p, 1) + half, half)
                self.push(k, p, 4, self.quarter(k, p, 3), half)

        def scatter_mid(self, k):
            half = self.sizes[k] // 2
            for p in range(3):
                self.copies[k, p, 0].wait_recv()
                self.add_rows(self.quarter(k, p, 1), half, [self.bufs[k].at[p, 0]])
                self.push(k, p, 2, self.quarter(k, p, 1), half)
                self.copies[k, p, 3].wait_recv()
                self.add_rows(self.quarter(k, p, 3) + half, half, [self.bufs[k].at[p, 3]])
                self.push(k, p, 5, self.quarter(k, p, 3) + half, half)

        def scatter_end(self, k):
            half = self.sizes[k] // 2
            for p in range(3):
                for h, one, two in ((0, 4, 2), (1, 1, 5)):
                    self.copies[k, p, one].wait_recv()
                    self.copies[k, p, two].wait_recv()
                    self.add_rows(
                        self.quarter(k, p, 0) + h * half, half, [self.bufs[k].at[p, one], self.bufs[k].at[p, two]]
                    )

        def ring_begin(self, s):
            size = self.sizes[s]
            for p in range(3):
                a = AXES[p][s]
                for k, dev in ((2, across[a]), (1, right[a]), (3, left[a])):
                    c = remote(
                        self.t.at[pl.ds(al(self.quarter(s, p, k)), size), :],
                        self.bufs[s].at[p, k - 1],
                        self.rs[0].at[s, p, k - 1],
                        self.rs[1].at[s, p, k - 1],
                        dev,
                    )
                    c.start()
                    self.copies[s, p, k] = c
                    sent.append(c)

        def ring_end(self, s):
            size = self.sizes[s]
            for p in range(3):
                for k in (1, 2, 3):
                    self.copies[s, p, k].wait_recv()
                off = self.bases[s + 1][p]
                step = 80 if size % 80 == 0 else 64

                def body(m, carry):
                    at = pl.ds(al(off + m * step), step)
                    total = self.t[at, :].astype(F32)
                    for k in range(3):
                        total = total + self.bufs[s][p, k, pl.ds(al(m * step), step)].astype(F32)
                    if s == 2:
                        g[pl.ds(al(self.mine + off), size), :] = total.astype(BF)
                    else:
                        self.t[at, :] = total.astype(BF)
                    return carry

                lax.fori_loop(0, size // step, body, 0)
            if s == 2:
                self.rounds(2)

        def rounds(self, s):
            for p in range(3):
                a = AXES[p][s]
                off = self.bases[s + 1][p]
                for k, dev in ((2, across[a]), (1, right[a]), (3, left[a])):
                    self.spread(s, p, k - 1, off, self.sizes[s], dev)

        def rounds_end(self, s):
            for p in range(3):
                self.got(s, p, 0, 1, 2)

        def spread(self, k, p, no, off, rows, dev):
            here = g.at[pl.ds(al(self.mine + off), rows), :]
            c = remote(here, here, self.ag[0].at[k, p, no], self.ag[1].at[k, p, no], dev)
            c.start()
            self.copies["g", k, p, no] = c
            sent.append(c)

        def got(self, k, p, *nos):
            for no in nos:
                self.copies["g", k, p, no].wait_recv()

        def gather_begin(self, k):
            half = self.sizes[k] // 2
            for p in range(3):
                own = self.quarter(k, p, 0)
                a = AXES[p][k]
                self.spread(k, p, 0, own, half, right[a])
                self.spread(k, p, 1, own + half, half, left[a])
            for p in range(3):
                own = self.quarter(k, p, 0)
                a = AXES[p][k]
                self.spread(k, p, 2, own + half, half, right[a])
                self.spread(k, p, 3, own, half, left[a])

        def gather_mid(self, k):
            half = self.sizes[k] // 2
            for p in range(3):
                a = AXES[p][k]
                self.got(k, p, 0)
                self.spread(k, p, 4, self.quarter(k, p, 3), half, right[a])
                self.got(k, p, 1)
                self.spread(k, p, 5, self.quarter(k, p, 1) + half, half, left[a])

        def gather_end(self, k):
            for p in range(3):
                self.got(k, p, 2, 3, 4, 5)

    one = Chunk(0, ta, (r1a, r2a, r3a), (rsa_send, rsa_recv), (aga_send, aga_recv))
    two = Chunk(1, tb, (r1b, r2b, r3b), (rsb_send, rsb_recv), (agb_send, agb_recv))

    early = list(sent)
    sent.clear()
    one.gram_far()
    one.scatter_far(0)
    one.gram_near()
    one.scatter_near(0)
    two.gram_far()
    one.gram_own()
    one.scatter_mid(0)
    two.scatter_far(0)
    two.gram_near()
    two.scatter_near(0)
    two.gram_own()
    sq_core.wait_recv()
    sq[0] = sq[13] + sq[14]
    squares = square_begin(0)
    turn_all()
    flush(early)
    for p in range(3):
        in1.left(p)
    one.scatter_end(0)
    one.ring_begin(1)
    square_end(0, squares)
    squares = square_begin(1)
    two.scatter_mid(0)
    one.ring_end(1)
    one.ring_begin(2)
    square_end(1, squares)
    squares = square_begin(2)
    two.scatter_end(0)
    two.ring_begin(1)
    one.ring_end(2)
    square_end(2, squares)
    two.ring_end(1)
    two.ring_begin(2)
    one.rounds_end(2)
    one.rounds(1)
    two.ring_end(2)
    one.rounds_end(1)
    early.extend(sent)
    sent.clear()
    one.gather_begin(0)
    two.rounds_end(2)
    two.rounds(1)
    one.gather_mid(0)
    two.rounds_end(1)
    two.gather_begin(0)
    flush(early)
    one.gather_end(0)

    def cols(a_ref, i):
        return a_ref[:, pl.ds(al(i * BLK, BLK), BLK)]

    def block(slot):
        o = slot * 512
        return jnp.concatenate([g[pl.ds(al(o, 512), 256), :], g[pl.ds(al(o + 256, 256), 256), :]], axis=1)

    def band(a_ref, j, ds):
        def straight(d, first):
            i = (j + NB - d) % NB
            return cols(a_ref, i), block(first + i)

        def turned(d, first):
            return cols(a_ref, (j + d) % NB), block(first + j)

        a, b = zip(*[straight(*e) for e in ds])
        acc = jnp.dot(jnp.concatenate(a, axis=1), jnp.concatenate(b, axis=0), preferred_element_type=F32)
        a, b = zip(*[turned(*e) for e in ds])
        return acc + lax.dot_general(
            jnp.concatenate(a, axis=1), jnp.concatenate(b, axis=1), NT, preferred_element_type=F32
        )

    whole_one = ((2 * core, 0), (2 * core + 1, NB))
    whole_two = ((2 * core + 4, SECOND),)

    def single(acc_ref, a_ref, chunk, m):
        i, d, _ = block_of(chunk, m)
        j = (i + d) % NB
        b = block(chunk * SECOND + m)
        acc_ref[:, pl.ds(al(j * BLK, BLK), BLK)] += jnp.dot(cols(a_ref, i), b, preferred_element_type=F32)
        acc_ref[:, pl.ds(al(i * BLK, BLK), BLK)] += lax.dot_general(
            cols(a_ref, j), b, NT, preferred_element_type=F32
        )

    def loop(first_k, last_k, f):
        def body(k, carry):
            f(first_k + 2 * k)
            f(first_k + 2 * k + 1)
            return carry

        lax.fori_loop(0, (last_k - first_k) // 2, body, 0)
        if (last_k - first_k) % 2:
            f(last_k - 1)

    def band_at(j):
        return pl.ds(al(j * BLK, BLK), BLK)

    def to_partner(no, src, dst):
        c = remote(src, dst, part_send.at[no], part_recv.at[no], partner)
        c.start()
        sent.append(c)
        return c

    def y_one(j):
        yf[:, band_at(j)] = band(st, j, whole_one)

    loop(0, 6, y_one)
    two.gather_mid(0)
    loop(6, NB, y_one)
    zf[...] = jnp.zeros((CHIP, M), F32)
    for m in (28, 29):
        single(yf, st, 0, m)
    two.gather_end(0)
    def shared(k, a_ref=st, acc_ref=yf):
        single(acc_ref, a_ref, 1, 14 + k)

    loop(0, 9, shared)

    def y_two(j):
        v = yf[:, band_at(j)] + band(st, j, whole_two)
        yf[:, band_at(j)] = v
        yp[:, band_at(j)] = v.astype(BF)

    shares = []
    for h in range(2):
        loop(h * 7, h * 7 + 7, y_two)
        here = pl.ds(h * HALF_M, HALF_M)
        shares.append(to_partner(h, yp.at[:, here], yr.at[:, here]))

    factor = 0.3 * math.sqrt(M) / (jnp.sqrt(jnp.sum(sq[12], axis=(0, 1), keepdims=True)) + 1e-07)
    factor2 = factor * factor

    def y_sum(j):
        v = factor2 * (yf[:, band_at(j)] + yr[:, band_at(j)].astype(F32))
        yf[:, band_at(j)] = v
        ybf[:, band_at(j)] = v.astype(BF)

    for h in range(2):
        shares[h].wait_recv()
        loop(h * 7, h * 7 + 7, y_sum)

    for m in (28, 29):
        single(zf, ybf, 0, m)
    def shared(k, a_ref=ybf, acc_ref=zf):
        single(acc_ref, a_ref, 1, 14 + k)

    loop(0, 9, shared)

    def z_band(j):
        return factor2 * (zf[:, band_at(j)] + band(ybf, j, whole_one + whole_two))

    def z_theirs(k):
        zp[:, band_at(k)] = z_band((1 - core) * 7 + k).astype(BF)

    loop(0, 7, z_theirs)
    share = to_partner(2, zp, zr)

    def z_mine(k):
        zf[:, band_at(core * 7 + k)] = z_band(core * 7 + k)

    loop(0, 7, z_mine)
    share.wait_recv()
    for p in range(3):
        ut[pl.ds(p * 128 + COL3, 128 - COL3), :] = jnp.zeros((128 - COL3, HALF_M), BF)

    def finish(k):
        at = band_at(core * 7 + k)
        scaled = (factor * st[:, at].astype(F32)).astype(BF).astype(F32)
        product = factor * (COEFF_B * yf[:, at] + COEFF_C * (zf[:, at] + zr[:, band_at(k)].astype(F32)))
        u = (math.sqrt(K) * (COEFF_A * scaled + product)).astype(BF)
        for p in range(3):
            ut[pl.ds(p * 128, COL3), band_at(k)] = u[p * COL3 : (p + 1) * COL3]

    loop(0, 7, finish)

    early.extend(sent)
    sent.clear()
    y3 = x2p
    unpack = spread_matrix((8 * PIECE, 8 * ROWS), 0, PIECE, ROWS)
    for m in range(8):
        o = m * 8 * ROWS
        first_lane = o // 128 * 128
        skip = o - first_lane
        width = -(-(skip + 8 * ROWS) // 128) * 128
        v = ut[:, pl.ds(first_lane, width)][:, skip : skip + 8 * ROWS]
        rows = lax.dot_general(unpack, v, NT, preferred_element_type=F32).astype(BF)
        for r in range(8):
            x, y, z = m // 2, m % 2 * 2 + r // 4, r % 4
            for p, at in enumerate(((z, x, y), (x, y, z), (y, x, z))):
                y3[(p,) + at] = rows[r * PIECE : (r + 1) * PIECE, p * 128 : (p + 1) * 128]

    out1 = Exchange(0, 2, lambda p, q: y3.at[p, q], lambda p, q: y2p.at[p, q], outs)
    out2 = PlaneExchange(y2, y0, spot, columns, out_plane_send, out_plane_recv)
    for p in range(3):
        out1.begin(p)
    for p in range(3):
        out1.keep(p)
    flush(early)
    early.extend(sent)
    sent.clear()
    narrow = spread_matrix((512, COL2), 0, 128, COL3)
    for p in range(3):
        out1.arrive(p)
        for u in range(4):
            rows = [y2p[p, q, u].reshape(4 * PIECE, 128) for q in range(4)]
            rows = jnp.dot(jnp.concatenate(rows, axis=1), narrow, preferred_element_type=F32)
            y2[p, pl.ds(4 * u, 4)] = rows.astype(BF).reshape(4, PIECE, COL2)
        out2.begin(p)
    own = []
    for p in range(3):
        a, b, _ = AXES[p]
        at = (pos[a], pos[b])
        own.append(pltpu.make_async_copy(y2.at[p, spot(p, *at)], y0.at[p, columns(p, *at)], io_sem.at[1 + p]))
        own[p].start()
    flush(early)
    for p in range(3):
        out2.arrive(p)
        own[p].wait()
    for p in range(3):
        out2.left(p)
    flush(sent)


def lay_out(pieces_ref, out_ref):
    for e in range(4):
        out_ref[:, e * COL2 : (e + 1) * COL2] = pieces_ref[0, e][:ROWS]


def local(gradient):
    dma = pltpu.SemaphoreType.DMA
    hbm = pl.BlockSpec(memory_space=pl.ANY)
    pieces = pl.pallas_call(
        kernel,
        out_shape=jax.ShapeDtypeStruct((3, 16, PIECE, COL2), BF),
        in_specs=[hbm],
        out_specs=hbm,
        scratch_shapes=[
            pltpu.VMEM((ROWS, K), BF),
            pltpu.VMEM((3, 16, PIECE, COL2), BF),
            pltpu.VMEM((3, 16, PIECE, COL2), BF),
            pltpu.VMEM((3, 4, 4, 4, PIECE, 128), BF),
            pltpu.VMEM((2, 3, 4, 4, 4, PIECE, 128), BF),
            pltpu.VMEM((M, 384), BF),
            pltpu.VMEM((CHIP, M), BF),
            pltpu.VMEM((384, HALF_M), BF),
            pltpu.VMEM((3, 4, 4, 4, PIECE, 128), BF),
            pltpu.VMEM((3, 16, PIECE, COL2), BF),
            pltpu.VMEM((3 * 10 * 512, 128), BF),
            pltpu.VMEM((3 * 8 * 512, 128), BF),
            pltpu.VMEM((SLOTS * 512, 128), BF),
            pltpu.VMEM((3, 6, 640, 128), BF),
            pltpu.VMEM((3, 3, 320, 128), BF),
            pltpu.VMEM((3, 3, 80, 128), BF),
            pltpu.VMEM((3, 6, 512, 128), BF),
            pltpu.VMEM((3, 3, 256, 128), BF),
            pltpu.VMEM((3, 3, 64, 128), BF),
            pltpu.VMEM((15, 8, 128), F32),
            pltpu.VMEM((CHIP, M), F32),
            pltpu.VMEM((CHIP, M), BF),
            pltpu.VMEM((CHIP, M), BF),
            pltpu.VMEM((CHIP, M), BF),
            pltpu.VMEM((CHIP, M), F32),
            pltpu.VMEM((CHIP, HALF_M), BF),
            pltpu.VMEM((CHIP, HALF_M), BF),
            dma((4,)),
            dma((1, 3, 3)),
            dma((1, 3, 3)),
            dma((3,)),
            dma((3,)),
            dma((3,)),
            dma((3,)),
            dma((1, 3, 3)),
            dma((1, 3, 3)),
            dma((3,)),
            dma((3,)),
            dma((3,)),
            dma((3,)),
            dma((3, 3, 6)),
            dma((3, 3, 6)),
            dma((3, 3, 6)),
            dma((3, 3, 6)),
            dma((3, 3, 6)),
            dma((3, 3, 6)),
            dma((3, 3, 6)),
            dma((3, 3, 6)),
            dma((4, 3)),
            dma((4, 3)),
        ],
        compiler_params=pltpu.CompilerParams(
            collective_id=0, has_side_effects=True, vmem_limit_bytes=60 * 1024 * 1024
        ),
        cost_estimate=pl.CostEstimate(flops=16 * 10**9, bytes_accessed=5 * 10**6, transcendentals=0),
    )(gradient)
    return pl.pallas_call(
        lay_out,
        grid=(12,),
        out_shape=jax.ShapeDtypeStruct((ROWS, K), BF),
        in_specs=[pl.BlockSpec((1, 4, PIECE, COL2), lambda k: (k // 4, k % 4, 0, 0))],
        out_specs=pl.BlockSpec((ROWS, COL1), lambda k: (0, k)),
    )(pieces)


def solution(mesh):
    spec = P(("wide", "narrow"), None)
    return jax.shard_map(local, mesh=mesh, in_specs=(spec,), out_specs=spec, check_vma=False)
```

```python
import math

import jax
import jax.numpy as jnp
from jax import lax
from jax.experimental import pallas as pl
from jax.experimental.pallas import tpu as pltpu
from jax.sharding import PartitionSpec as P

M = 3584
K = 18432

COEFF_A = 3.4445
COEFF_B = -4.775
COEFF_C = 2.0315

MESH = pl.DeviceIdType.MESH
BF = jnp.bfloat16
F32 = jnp.float32
NT = (((1,), (1,)), ((), ()))

ROWS = 28
PIECE = 32
THIRD = K // 3
COL1 = THIRD // 4
COL2 = COL1 // 4
COL3 = COL2 // 4
CHIP = 3 * COL3
HALF_M = M // 2
AXES = ((0, 1, 2), (1, 2, 0), (2, 0, 1))

BLK = 256
NB = M // BLK
PER_PART = (10, 8)
SECOND = 3 * PER_PART[0]
SLOTS = 3 * sum(PER_PART)
SIZES = ((1280, 320, 80), (1024, 256, 64))


def al(x, m=16):
    return pl.multiple_of(x, m)


def kernel(
    in_ref, y0,
    rows_in, x0, x2, x2p, x3, s_all, st,
    ut, y2p, y2,
    ta, tb, g, r1a, r2a, r3a, r1b, r2b, r3b, sq, yf, ybf, yp, yr, zf, zp, zr,
    io_sem, in_send, in_recv, in_plane_send, in_plane_recv, core_send, core_recv,
    out_send, out_recv, out_plane_send, out_plane_recv, part_send, part_recv,
    rsa_send, rsa_recv, aga_send, aga_recv, rsb_send, rsb_recv, agb_send, agb_recv, sq_send, sq_recv,
):
    w, n_ = lax.axis_index("wide"), lax.axis_index("narrow")
    core, z_lo, y = w % 2, (w // 2) % 2, w // 4
    x, z_hi = n_ % 4, n_ // 4
    z = z_hi * 2 + z_lo
    pos = (x, y, z)

    def device(x, y, z, core):
        return ((y * 2 + z % 2) * 2 + core, (z // 2) * 4 + x)

    def shifted(axis, by):
        p = [x, y, z]
        p[axis] = (p[axis] + by) % 4
        return device(*p, core)

    right = [shifted(a, 1) for a in range(3)]
    left = [shifted(a, 3) for a in range(3)]
    across = [shifted(a, 2) for a in range(3)]
    partner = device(x, y, z, 1 - core)

    def in_plane(p, d, e):
        a, b, _ = AXES[p]
        if e == 0:
            return (right, across, left)[d - 1][a]
        if d == 0:
            return (right, across, left)[e - 1][b]
        v = [x, y, z]
        v[a] = (v[a] + d) % 4
        v[b] = (v[b] + e) % 4
        return device(*v, core)

    steps = [(d, e) for d in range(4) for e in range(4) if d or e]
    plane_devices = [[in_plane(p, d, e) for d, e in steps] for p in range(3)]
    diagonal = [plane_devices[p][k] for p in range(3) for k, (d, e) in enumerate(steps) if d and e]

    barrier = pltpu.get_barrier_semaphore()
    for d in right + left + across + diagonal + [partner]:
        pl.semaphore_signal(barrier, inc=1, device_id=d, device_id_type=MESH)

    fetch = pltpu.make_async_copy(in_ref, rows_in, io_sem.at[0])
    fetch.start()
    fetch.wait()

    def load(k, carry):
        p, q = k // 4, k % 4
        v = rows_in[:, pl.ds(al(k * COL1, COL1), COL1)]
        for e in range(4):
            x0[p, q * 4 + e, pl.ds(0, ROWS), :] = v[:, e * COL2 : (e + 1) * COL2]
            x0[p, q * 4 + e, pl.ds(ROWS, PIECE - ROWS), :] = jnp.zeros((PIECE - ROWS, COL2), BF)
        return carry

    lax.fori_loop(0, 12, load, 0)
    pl.semaphore_wait(barrier, 37)

    def remote(src, dst, send, recv, dev):
        return pltpu.make_async_remote_copy(
            src_ref=src, dst_ref=dst, send_sem=send, recv_sem=recv, device_id=dev, device_id_type=MESH
        )

    sent = []

    def flush(group):
        for c in group:
            c.wait_send()
        group.clear()

    class Exchange:
        def __init__(self, stage, axis_no, src, dst, sems):
            self.stage, self.axis_no, self.src, self.dst, self.sems = stage, axis_no, src, dst, sems
            self.copies = {}

        def begin(self, p):
            a = AXES[p][self.axis_no]
            me = pos[a]
            send, recv = self.sems
            group = []
            for k, dev in ((2, across[a]), (1, right[a]), (3, left[a])):
                c = remote(
                    self.src(p, (me + k) % 4), self.dst(p, me),
                    send.at[self.stage, p, k - 1], recv.at[self.stage, p, k - 1], dev,
                )
                c.start()
                group.append(c)
                sent.append(c)
            self.copies[p] = group

        def keep(self, p):
            me = pos[AXES[p][self.axis_no]]
            src, dst = self.src(p, me), self.dst(p, me)
            dst[...] = src[...]

        def arrive(self, p):
            for c in self.copies[p]:
                c.wait_recv()

    def spot(p, a, b):
        return b * 4 + a if p == 2 else a * 4 + b

    class PlaneExchange:
        def __init__(self, src, dst, src_spot, dst_spot, send, recv):
            self.src, self.dst, self.src_spot, self.dst_spot = src, dst, src_spot, dst_spot
            self.send, self.recv = send, recv

        def begin(self, p):
            a, b, _ = AXES[p]
            here = self.dst(p, self.dst_spot(p, pos[a], pos[b]))
            for (d, e), dev in zip(steps, plane_devices[p]):
                there = self.src_spot(p, (pos[a] + d) % 4, (pos[b] + e) % 4)
                remote(self.src.at[p, there], here, self.send.at[p], self.recv.at[p], dev).start()

        def keep(self, p):
            a, b, _ = AXES[p]
            self.dst(p, self.dst_spot(p, pos[a], pos[b]))[...] = self.src[p, self.src_spot(p, pos[a], pos[b])]

        def arrive(self, p):
            all_of = self.src.at[p, pl.ds(0, 15)]
            pltpu.make_async_copy(all_of, all_of, self.recv.at[p]).wait()

        def left(self, p):
            all_of = self.src.at[p, pl.ds(0, 15)]
            pltpu.make_async_copy(all_of, all_of, self.send.at[p]).wait()

    ins = (in_send, in_recv)
    outs = (out_send, out_recv)
    columns = lambda p, a, b: a * 4 + b
    in1 = PlaneExchange(x0, lambda p, s: x2.at[p, s], columns, spot, in_plane_send, in_plane_recv)
    in3 = Exchange(0, 2, lambda p, q: x2p.at[p, q], lambda p, q: x3.at[core, p, q], ins)
    for p in range(3):
        in1.begin(p)

    def square(k, total):
        for e in range(4):
            v = x0[k // 4, k % 4 * 4 + e].astype(F32)
            v = v * v
            v = (v[:, :128] + v[:, 128:256]) + v[:, 256:]
            total = total + ((v[:8] + v[8:16]) + (v[16:24] + v[24:]))
        return total

    for p in range(3):
        in1.keep(p)
    sq[13] = lax.fori_loop(0, 12, square, jnp.zeros((8, 128), F32))
    sq_core = remote(sq.at[13], sq.at[14], sq_send.at[3, 0], sq_recv.at[3, 0], partner)
    sq_core.start()
    sent.append(sq_core)

    def iota(shape, d):
        return lax.broadcasted_iota(jnp.int32, shape, d)

    def ones_where(cond):
        return jnp.where(cond, 1.0, 0.0).astype(BF)

    def spread_matrix(shape, wide, unit, narrow):
        s, r = iota(shape, wide), iota(shape, 1 - wide)
        return ones_where((s % unit < narrow) & (r == (s // unit) * narrow + s % unit))

    widen = spread_matrix((COL2, 512), 1, 128, COL3)
    for p in range(3):
        in1.arrive(p)
        for u in range(4):
            rows = x2[p, pl.ds(4 * u, 4)].reshape(4 * PIECE, COL2)
            rows = jnp.dot(rows, widen, preferred_element_type=F32).astype(BF)
            for q in range(4):
                x2p[p, q, u] = rows[:, q * 128 : (q + 1) * 128].reshape(4, PIECE, 128)
        in3.begin(p)
    for p in range(3):
        in3.keep(p)
    crossing = []
    for p in range(3):
        in3.arrive(p)
        here = x3.at[core, p]
        c = remote(here, here, core_send.at[p], core_recv.at[p], partner)
        c.start()
        crossing.append(c)
        sent.append(c)

    pack = spread_matrix((8 * ROWS, 8 * PIECE), 1, PIECE, ROWS)

    def pack_rows(owner):
        def body(k, carry):
            x, y0, group = k // 2, k % 2 * 2, [[], [], []]
            for y in (y0, y0 + 1):
                for z in range(4):
                    group[0].append(x3[owner, 0, z, x, y])
                    group[1].append(x3[owner, 1, x, y, z])
                    group[2].append(x3[owner, 2, y, x, z])
            rows = jnp.concatenate([jnp.concatenate(e, axis=0) for e in group], axis=1)
            at = pl.ds(al(owner * HALF_M + k * 8 * ROWS), 8 * ROWS)
            s_all[at, :] = jnp.dot(pack, rows, preferred_element_type=F32).astype(BF)
            return carry

        lax.fori_loop(0, 4, lambda k, carry: body(2 * k + 1, body(2 * k, carry)), 0)

    pack_rows(core)
    for c in crossing:
        c.wait_recv()
    pack_rows(1 - core)

    def turn_all():
        kk, ll = iota((CHIP, 384), 0), iota((CHIP, 384), 1)
        pick = ones_where((ll % 128 < COL3) & (kk == (ll // 128) * COL3 + ll % 128))

        def turn(j, carry):
            at = pl.ds(al(j * BLK, BLK), BLK)
            st[:, at] = lax.dot_general(pick, s_all[at, :], NT, preferred_element_type=F32).astype(BF)
            return carry

        lax.fori_loop(0, NB // 2, lambda k, carry: turn(2 * k + 1, turn(2 * k, carry)), 0)

    def block_of(chunk, m):
        if chunk == 0:
            i = jnp.where(m < 28, m % NB, 4 * core + m - 28)
            d = jnp.where(m < 28, 2 * core + m // NB, 7)
            return i, d, jnp.where(d == 0, 0.5, 1.0)
        i = jnp.where(m < 14, m, jnp.where(m < 21, 7 * core + m - 14, (4 * core + m - 19) % NB))
        d = jnp.where(m < 14, 4 + 2 * core, jnp.where(m < 21, 5, 7))
        return i, d, jnp.where((d == 7) & ((i >= 7) | (m == 23)), 0.0, 1.0)

    def gram_block(chunk, m, t):
        i, d, scale = block_of(chunk, m)
        j = (i + d) % NB
        ri = pl.ds(al(i * BLK, BLK), BLK)
        rj = pl.ds(al(j * BLK, BLK), BLK)
        acc = lax.dot_general(s_all[ri, :], s_all[rj, :], NT, preferred_element_type=F32)
        acc = (scale * acc).astype(BF)
        t[pl.ds(al(m * 512, 512), 256), :] = acc[:, :128]
        t[pl.ds(al(m * 512 + 256, 256), 256), :] = acc[:, 128:]

    def square_begin(s):
        group = [
            remote(sq.at[4 * s], sq.at[4 * s + 1 + k], sq_send.at[s, k], sq_recv.at[s, k], dev)
            for k, dev in enumerate((right[s], left[s], across[s]))
        ]
        for c in group:
            c.start()
        sent.extend(group)
        return group

    def square_end(s, group):
        for c in group:
            c.wait_recv()
        sq[4 * s + 4] = (sq[4 * s] + sq[4 * s + 3]) + (sq[4 * s + 1] + sq[4 * s + 2])

    class Chunk:
        def __init__(self, no, t, bufs, rs, ag):
            self.no, self.t, self.bufs, self.rs, self.ag = no, t, bufs, rs, ag
            self.blocks = PER_PART[no]
            self.sizes = SIZES[no]
            base = [p * self.blocks * 512 for p in range(3)]
            self.bases = [base]
            for k in range(3):
                base = [base[p] + pos[AXES[p][k]] * self.sizes[k] for p in range(3)]
                self.bases.append(base)
            self.mine = no * SECOND * 512
            self.copies = {}

        def quarter(self, k, p, by):
            return self.bases[k][p] + ((pos[AXES[p][k]] + by) % 4) * self.sizes[k]

        def gram(self, p, start, count):
            for m in range(count):
                gram_block(self.no, p * self.blocks + start + m, self.t)

        def gram_far(self):
            for p in range(3):
                q = (pos[AXES[p][0]] + 2) % 4
                self.gram(p, self.blocks * q // 4, 2 + self.blocks % 4 // 2)

        def gram_near(self):
            for p in range(3):
                me = pos[AXES[p][0]]
                if self.blocks % 4:
                    self.gram(p, self.blocks // 4 + self.blocks // 2 * (me // 2), 1)
                for by in (1, 3):
                    self.gram(p, (self.blocks * ((me + by) % 4) + 2) // 4, 2)

        def gram_own(self):
            for p in range(3):
                self.gram(p, (self.blocks * pos[AXES[p][0]] + 2) // 4, 2)

        def push(self, k, p, no, off, rows):
            a = AXES[p][k]
            c = remote(
                self.t.at[pl.ds(al(off), rows), :],
                self.bufs[k].at[p, no],
                self.rs[0].at[k, p, no],
                self.rs[1].at[k, p, no],
                right[a] if no < 3 else left[a],
            )
            c.start()
            self.copies[k, p, no] = c
            sent.append(c)

        def add_rows(self, off, rows, srcs):
            step = rows // 2 if rows > 200 else rows
            t = self.t

            def body(m, carry):
                at = pl.ds(al(off + m * step), step)
                total = t[at, :]
                for src in srcs:
                    total = total + src[pl.ds(al(m * step), step), :]
                t[at, :] = total
                return carry

            lax.fori_loop(0, rows // step, body, 0)

        def scatter_far(self, k):
            half = self.sizes[k] // 2
            for p in range(3):
                self.push(k, p, 0, self.quarter(k, p, 2), half)
                self.push(k, p, 3, self.quarter(k, p, 2) + half, half)

        def scatter_near(self, k):
            half = self.sizes[k] // 2
            for p in range(3):
                self.push(k, p, 1, self.quarter(k, p, 1) + half, half)
                self.push(k, p, 4, self.quarter(k, p, 3), half)

        def scatter_mid(self, k):
            half = self.sizes[k] // 2
            for p in range(3):
                self.copies[k, p, 0].wait_recv()
                self.add_rows(self.quarter(k, p, 1), half, [self.bufs[k].at[p, 0]])
                self.push(k, p, 2, self.quarter(k, p, 1), half)
                self.copies[k, p, 3].wait_recv()
                self.add_rows(self.quarter(k, p, 3) + half, half, [self.bufs[k].at[p, 3]])
                self.push(k, p, 5, self.quarter(k, p, 3) + half, half)

        def scatter_end(self, k):
            half = self.sizes[k] // 2
            for p in range(3):
                for h, one, two in ((0, 4, 2), (1, 1, 5)):
                    self.copies[k, p, one].wait_recv()
                    self.copies[k, p, two].wait_recv()
                    self.add_rows(
                        self.quarter(k, p, 0) + h * half, half, [self.bufs[k].at[p, one], self.bufs[k].at[p, two]]
                    )

        def ring_begin(self, s):
            size = self.sizes[s]
            for p in range(3):
                a = AXES[p][s]
                for k, dev in ((2, across[a]), (1, right[a]), (3, left[a])):
                    c = remote(
                        self.t.at[pl.ds(al(self.quarter(s, p, k)), size), :],
                        self.bufs[s].at[p, k - 1],
                        self.rs[0].at[s, p, k - 1],
                        self.rs[1].at[s, p, k - 1],
                        dev,
                    )
                    c.start()
                    self.copies[s, p, k] = c
                    sent.append(c)

        def ring_end(self, s):
            size = self.sizes[s]
            for p in range(3):
                for k in (1, 2, 3):
                    self.copies[s, p, k].wait_recv()
                off = self.bases[s + 1][p]
                step = 80 if size % 80 == 0 else 64

                def body(m, carry):
                    at = pl.ds(al(off + m * step), step)
                    total = self.t[at, :].astype(F32)
                    for k in range(3):
                        total = total + self.bufs[s][p, k, pl.ds(al(m * step), step)].astype(F32)
                    if s == 2:
                        g[pl.ds(al(self.mine + off), size), :] = total.astype(BF)
                    else:
                        self.t[at, :] = total.astype(BF)
                    return carry

                lax.fori_loop(0, size // step, body, 0)
            if s == 2:
                self.rounds(2)

        def rounds(self, s):
            for p in range(3):
                a = AXES[p][s]
                off = self.bases[s + 1][p]
                for k, dev in ((2, across[a]), (1, right[a]), (3, left[a])):
                    self.spread(s, p, k - 1, off, self.sizes[s], dev)

        def rounds_end(self, s):
            for p in range(3):
                self.got(s, p, 0, 1, 2)

        def spread(self, k, p, no, off, rows, dev):
            here = g.at[pl.ds(al(self.mine + off), rows), :]
            c = remote(here, here, self.ag[0].at[k, p, no], self.ag[1].at[k, p, no], dev)
            c.start()
            self.copies["g", k, p, no] = c
            sent.append(c)

        def got(self, k, p, *nos):
            for no in nos:
                self.copies["g", k, p, no].wait_recv()

        def gather_begin(self, k):
            half = self.sizes[k] // 2
            for p in range(3):
                own = self.quarter(k, p, 0)
                a = AXES[p][k]
                self.spread(k, p, 0, own, half, right[a])
                self.spread(k, p, 1, own + half, half, left[a])
            for p in range(3):
                own = self.quarter(k, p, 0)
                a = AXES[p][k]
                self.spread(k, p, 2, own + half, half, right[a])
                self.spread(k, p, 3, own, half, left[a])

        def gather_mid(self, k):
            half = self.sizes[k] // 2
            for p in range(3):
                a = AXES[p][k]
                self.got(k, p, 0)
                self.spread(k, p, 4, self.quarter(k, p, 3), half, right[a])
                self.got(k, p, 1)
                self.spread(k, p, 5, self.quarter(k, p, 1) + half, half, left[a])

        def gather_end(self, k):
            for p in range(3):
                self.got(k, p, 2, 3, 4, 5)

    one = Chunk(0, ta, (r1a, r2a, r3a), (rsa_send, rsa_recv), (aga_send, aga_recv))
    two = Chunk(1, tb, (r1b, r2b, r3b), (rsb_send, rsb_recv), (agb_send, agb_recv))

    early = list(sent)
    sent.clear()
    one.gram_far()
    one.scatter_far(0)
    one.gram_near()
    one.scatter_near(0)
    two.gram_far()
    one.gram_own()
    one.scatter_mid(0)
    two.scatter_far(0)
    two.gram_near()
    two.scatter_near(0)
    two.gram_own()
    sq_core.wait_recv()
    sq[0] = sq[13] + sq[14]
    squares = square_begin(0)
    turn_all()
    flush(early)
    for p in range(3):
        in1.left(p)
    one.scatter_end(0)
    one.ring_begin(1)
    square_end(0, squares)
    squares = square_begin(1)
    two.scatter_mid(0)
    one.ring_end(1)
    one.ring_begin(2)
    square_end(1, squares)
    squares = square_begin(2)
    two.scatter_end(0)
    two.ring_begin(1)
    one.ring_end(2)
    square_end(2, squares)
    two.ring_end(1)
    two.ring_begin(2)
    one.rounds_end(2)
    one.rounds(1)
    two.ring_end(2)
    one.rounds_end(1)
    early.extend(sent)
    sent.clear()
    one.gather_begin(0)
    two.rounds_end(2)
    two.rounds(1)
    one.gather_mid(0)
    two.rounds_end(1)
    two.gather_begin(0)
    flush(early)
    one.gather_end(0)

    def cols(a_ref, i):
        return a_ref[:, pl.ds(al(i * BLK, BLK), BLK)]

    def block(slot):
        o = slot * 512
        return jnp.concatenate([g[pl.ds(al(o, 512), 256), :], g[pl.ds(al(o + 256, 256), 256), :]], axis=1)

    def band(a_ref, j, ds):
        def straight(d, first):
            i = (j + NB - d) % NB
            return cols(a_ref, i), block(first + i)

        def turned(d, first):
            return cols(a_ref, (j + d) % NB), block(first + j)

        a, b = zip(*[straight(*e) for e in ds])
        acc = jnp.dot(jnp.concatenate(a, axis=1), jnp.concatenate(b, axis=0), preferred_element_type=F32)
        a, b = zip(*[turned(*e) for e in ds])
        return acc + lax.dot_general(
            jnp.concatenate(a, axis=1), jnp.concatenate(b, axis=1), NT, preferred_element_type=F32
        )

    whole_one = ((2 * core, 0), (2 * core + 1, NB))
    whole_two = ((2 * core + 4, SECOND),)

    def single(acc_ref, a_ref, chunk, m):
        i, d, _ = block_of(chunk, m)
        j = (i + d) % NB
        b = block(chunk * SECOND + m)
        acc_ref[:, pl.ds(al(j * BLK, BLK), BLK)] += jnp.dot(cols(a_ref, i), b, preferred_element_type=F32)
        acc_ref[:, pl.ds(al(i * BLK, BLK), BLK)] += lax.dot_general(
            cols(a_ref, j), b, NT, preferred_element_type=F32
        )

    def loop(first_k, last_k, f):
        def body(k, carry):
            f(first_k + 2 * k)
            f(first_k + 2 * k + 1)
            return carry

        lax.fori_loop(0, (last_k - first_k) // 2, body, 0)
        if (last_k - first_k) % 2:
            f(last_k - 1)

    def band_at(j):
        return pl.ds(al(j * BLK, BLK), BLK)

    def to_partner(no, src, dst):
        c = remote(src, dst, part_send.at[no], part_recv.at[no], partner)
        c.start()
        sent.append(c)
        return c

    def y_one(j):
        yf[:, band_at(j)] = band(st, j, whole_one)

    loop(0, 6, y_one)
    two.gather_mid(0)
    loop(6, NB, y_one)
    zf[...] = jnp.zeros((CHIP, M), F32)
    for m in (28, 29):
        single(yf, st, 0, m)
    two.gather_end(0)
    def shared(k, a_ref=st, acc_ref=yf):
        single(acc_ref, a_ref, 1, 14 + k)

    loop(0, 9, shared)

    def y_two(j):
        v = yf[:, band_at(j)] + band(st, j, whole_two)
        yf[:, band_at(j)] = v
        yp[:, band_at(j)] = v.astype(BF)

    shares = []
    for h in range(2):
        loop(h * 7, h * 7 + 7, y_two)
        here = pl.ds(h * HALF_M, HALF_M)
        shares.append(to_partner(h, yp.at[:, here], yr.at[:, here]))

    factor = 0.3 * math.sqrt(M) / (jnp.sqrt(jnp.sum(sq[12], axis=(0, 1), keepdims=True)) + 1e-07)
    factor2 = factor * factor

    def y_sum(j):
        v = factor2 * (yf[:, band_at(j)] + yr[:, band_at(j)].astype(F32))
        yf[:, band_at(j)] = v
        ybf[:, band_at(j)] = v.astype(BF)

    for h in range(2):
        shares[h].wait_recv()
        loop(h * 7, h * 7 + 7, y_sum)

    for m in (28, 29):
        single(zf, ybf, 0, m)
    def shared(k, a_ref=ybf, acc_ref=zf):
        single(acc_ref, a_ref, 1, 14 + k)

    loop(0, 9, shared)

    def z_band(j):
        return factor2 * (zf[:, band_at(j)] + band(ybf, j, whole_one + whole_two))

    def z_theirs(k):
        zp[:, band_at(k)] = z_band((1 - core) * 7 + k).astype(BF)

    loop(0, 7, z_theirs)
    share = to_partner(2, zp, zr)

    def z_mine(k):
        zf[:, band_at(core * 7 + k)] = z_band(core * 7 + k)

    loop(0, 7, z_mine)
    share.wait_recv()
    for p in range(3):
        ut[pl.ds(p * 128 + COL3, 128 - COL3), :] = jnp.zeros((128 - COL3, HALF_M), BF)

    def finish(k):
        at = band_at(core * 7 + k)
        scaled = (factor * st[:, at].astype(F32)).astype(BF).astype(F32)
        product = factor * (COEFF_B * yf[:, at] + COEFF_C * (zf[:, at] + zr[:, band_at(k)].astype(F32)))
        u = (math.sqrt(K) * (COEFF_A * scaled + product)).astype(BF)
        for p in range(3):
            ut[pl.ds(p * 128, COL3), band_at(k)] = u[p * COL3 : (p + 1) * COL3]

    loop(0, 7, finish)

    early.extend(sent)
    sent.clear()
    y3 = x2p
    unpack = spread_matrix((8 * PIECE, 8 * ROWS), 0, PIECE, ROWS)
    for m in range(8):
        o = m * 8 * ROWS
        first_lane = o // 128 * 128
        skip = o - first_lane
        width = -(-(skip + 8 * ROWS) // 128) * 128
        v = ut[:, pl.ds(first_lane, width)][:, skip : skip + 8 * ROWS]
        rows = lax.dot_general(unpack, v, NT, preferred_element_type=F32).astype(BF)
        for r in range(8):
            x, y, z = m // 2, m % 2 * 2 + r // 4, r % 4
            for p, at in enumerate(((z, x, y), (x, y, z), (y, x, z))):
                y3[(p,) + at] = rows[r * PIECE : (r + 1) * PIECE, p * 128 : (p + 1) * 128]

    out1 = Exchange(0, 2, lambda p, q: y3.at[p, q], lambda p, q: y2p.at[p, q], outs)
    out2 = PlaneExchange(
        y2, lambda p, s: y0.at[:, pl.ds(al(p * THIRD + s * COL2, 128), COL2)], spot, columns, out_plane_send, out_plane_recv,
    )
    for p in range(3):
        out1.begin(p)
    for p in range(3):
        out1.keep(p)
    flush(early)
    early.extend(sent)
    sent.clear()
    narrow = spread_matrix((512, COL2), 0, 128, COL3)
    for p in range(3):
        out1.arrive(p)
        for u in range(4):
            rows = [y2p[p, q, u].reshape(4 * PIECE, 128) for q in range(4)]
            rows = jnp.dot(jnp.concatenate(rows, axis=1), narrow, preferred_element_type=F32)
            y2[p, pl.ds(4 * u, 4)] = rows.astype(BF).reshape(4, PIECE, COL2)
        out2.begin(p)
    own = []
    for p in range(3):
        a, b, _ = AXES[p]
        at = (pos[a], pos[b])
        own.append(pltpu.make_async_copy(y2.at[p, spot(p, *at)], out2.dst(p, columns(p, *at)), io_sem.at[1 + p]))
        own[p].start()
    flush(early)
    for p in range(3):
        out2.arrive(p)
        own[p].wait()
    for p in range(3):
        out2.left(p)
    flush(sent)


def local(gradient):
    dma = pltpu.SemaphoreType.DMA
    hbm = pl.BlockSpec(memory_space=pl.ANY)
    padded = pl.pallas_call(
        kernel,
        out_shape=jax.ShapeDtypeStruct((PIECE, K), BF),
        in_specs=[hbm],
        out_specs=hbm,
        scratch_shapes=[
            pltpu.VMEM((ROWS, K), BF),
            pltpu.VMEM((3, 16, PIECE, COL2), BF),
            pltpu.VMEM((3, 16, PIECE, COL2), BF),
            pltpu.VMEM((3, 4, 4, 4, PIECE, 128), BF),
            pltpu.VMEM((2, 3, 4, 4, 4, PIECE, 128), BF),
            pltpu.VMEM((M, 384), BF),
            pltpu.VMEM((CHIP, M), BF),
            pltpu.VMEM((384, HALF_M), BF),
            pltpu.VMEM((3, 4, 4, 4, PIECE, 128), BF),
            pltpu.VMEM((3, 16, PIECE, COL2), BF),
            pltpu.VMEM((3 * 10 * 512, 128), BF),
            pltpu.VMEM((3 * 8 * 512, 128), BF),
            pltpu.VMEM((SLOTS * 512, 128), BF),
            pltpu.VMEM((3, 6, 640, 128), BF),
            pltpu.VMEM((3, 3, 320, 128), BF),
            pltpu.VMEM((3, 3, 80, 128), BF),
            pltpu.VMEM((3, 6, 512, 128), BF),
            pltpu.VMEM((3, 3, 256, 128), BF),
            pltpu.VMEM((3, 3, 64, 128), BF),
            pltpu.VMEM((15, 8, 128), F32),
            pltpu.VMEM((CHIP, M), F32),
            pltpu.VMEM((CHIP, M), BF),
            pltpu.VMEM((CHIP, M), BF),
            pltpu.VMEM((CHIP, M), BF),
            pltpu.VMEM((CHIP, M), F32),
            pltpu.VMEM((CHIP, HALF_M), BF),
            pltpu.VMEM((CHIP, HALF_M), BF),
            dma((4,)),
            dma((1, 3, 3)),
            dma((1, 3, 3)),
            dma((3,)),
            dma((3,)),
            dma((3,)),
            dma((3,)),
            dma((1, 3, 3)),
            dma((1, 3, 3)),
            dma((3,)),
            dma((3,)),
            dma((3,)),
            dma((3,)),
            dma((3, 3, 6)),
            dma((3, 3, 6)),
            dma((3, 3, 6)),
            dma((3, 3, 6)),
            dma((3, 3, 6)),
            dma((3, 3, 6)),
            dma((3, 3, 6)),
            dma((3, 3, 6)),
            dma((4, 3)),
            dma((4, 3)),
        ],
        compiler_params=pltpu.CompilerParams(
            collective_id=0, has_side_effects=True, vmem_limit_bytes=60 * 1024 * 1024
        ),
        cost_estimate=pl.CostEstimate(flops=16 * 10**9, bytes_accessed=5 * 10**6, transcendentals=0),
    )(gradient)
    return padded[:ROWS]


def solution(mesh):
    spec = P(("wide", "narrow"), None)
    return jax.shard_map(local, mesh=mesh, in_specs=(spec,), out_specs=spec, check_vma=False)
```

```python
import math

import jax
import jax.numpy as jnp
from jax import lax
from jax.experimental import pallas as pl
from jax.experimental.pallas import tpu as pltpu
from jax.sharding import PartitionSpec as P

M = 3584
K = 18432

COEFF_A = 3.4445
COEFF_B = -4.775
COEFF_C = 2.0315

MESH = pl.DeviceIdType.MESH
BF = jnp.bfloat16
F32 = jnp.float32
NT = (((1,), (1,)), ((), ()))

ROWS = 28
PIECE = 32
THIRD = K // 3
COL1 = THIRD // 4
COL2 = COL1 // 4
COL3 = COL2 // 4
CHIP = 3 * COL3
HALF_M = M // 2
AXES = ((0, 1, 2), (1, 2, 0), (2, 0, 1))

BLK = 256
NB = M // BLK
PER_PART = (10, 8)
SECOND = 3 * PER_PART[0]
SLOTS = 3 * sum(PER_PART)
SIZES = ((1280, 320, 80), (1024, 256, 64))


def al(x, m=16):
    return pl.multiple_of(x, m)


def kernel(
    in_ref, y0,
    rows_in, x0, x2, x2p, x3, s_all, st,
    ut, y2p, y2,
    ta, tb, g, r1a, r2a, r3a, r1b, r2b, r3b, sq, yf, ybf, yp, yr, zf, zp, zr,
    io_sem, in_send, in_recv, in_plane_send, in_plane_recv, core_send, core_recv,
    out_send, out_recv, out_plane_send, out_plane_recv, part_send, part_recv,
    rsa_send, rsa_recv, aga_send, aga_recv, rsb_send, rsb_recv, agb_send, agb_recv, sq_send, sq_recv,
):
    w, n_ = lax.axis_index("wide"), lax.axis_index("narrow")
    core, z_lo, y = w % 2, (w // 2) % 2, w // 4
    x, z_hi = n_ % 4, n_ // 4
    z = z_hi * 2 + z_lo
    pos = (x, y, z)

    def device(x, y, z, core):
        return ((y * 2 + z % 2) * 2 + core, (z // 2) * 4 + x)

    def shifted(axis, by):
        p = [x, y, z]
        p[axis] = (p[axis] + by) % 4
        return device(*p, core)

    right = [shifted(a, 1) for a in range(3)]
    left = [shifted(a, 3) for a in range(3)]
    across = [shifted(a, 2) for a in range(3)]
    partner = device(x, y, z, 1 - core)

    def in_plane(p, d, e):
        a, b, _ = AXES[p]
        if e == 0:
            return (right, across, left)[d - 1][a]
        if d == 0:
            return (right, across, left)[e - 1][b]
        v = [x, y, z]
        v[a] = (v[a] + d) % 4
        v[b] = (v[b] + e) % 4
        return device(*v, core)

    steps = [(d, e) for d in range(4) for e in range(4) if d or e]
    plane_devices = [[in_plane(p, d, e) for d, e in steps] for p in range(3)]
    diagonal = [plane_devices[p][k] for p in range(3) for k, (d, e) in enumerate(steps) if d and e]

    barrier = pltpu.get_barrier_semaphore()
    for d in right + left + across + diagonal + [partner]:
        pl.semaphore_signal(barrier, inc=1, device_id=d, device_id_type=MESH)

    fetch = pltpu.make_async_copy(in_ref, rows_in, io_sem.at[0])
    fetch.start()
    fetch.wait()

    def load(k, carry):
        p, q = k // 4, k % 4
        v = rows_in[:, pl.ds(al(k * COL1, COL1), COL1)]
        for e in range(4):
            x0[p, q * 4 + e, pl.ds(0, ROWS), :] = v[:, e * COL2 : (e + 1) * COL2]
            x0[p, q * 4 + e, pl.ds(ROWS, PIECE - ROWS), :] = jnp.zeros((PIECE - ROWS, COL2), BF)
        return carry

    lax.fori_loop(0, 12, load, 0)
    pl.semaphore_wait(barrier, 37)

    def remote(src, dst, send, recv, dev):
        return pltpu.make_async_remote_copy(
            src_ref=src, dst_ref=dst, send_sem=send, recv_sem=recv, device_id=dev, device_id_type=MESH
        )

    sent = []

    def flush(group):
        for c in group:
            c.wait_send()
        group.clear()

    class Exchange:
        def __init__(self, stage, axis_no, src, dst, sems):
            self.stage, self.axis_no, self.src, self.dst, self.sems = stage, axis_no, src, dst, sems
            self.copies = {}

        def begin(self, p):
            a = AXES[p][self.axis_no]
            me = pos[a]
            send, recv = self.sems
            group = []
            for k, dev in ((2, across[a]), (1, right[a]), (3, left[a])):
                c = remote(
                    self.src(p, (me + k) % 4), self.dst(p, me),
                    send.at[self.stage, p, k - 1], recv.at[self.stage, p, k - 1], dev,
                )
                c.start()
                group.append(c)
                sent.append(c)
            self.copies[p] = group

        def keep(self, p):
            me = pos[AXES[p][self.axis_no]]
            src, dst = self.src(p, me), self.dst(p, me)
            dst[...] = src[...]

        def arrive(self, p):
            for c in self.copies[p]:
                c.wait_recv()

    def spot(p, a, b):
        return b * 4 + a if p == 2 else a * 4 + b

    class PlaneExchange:
        def __init__(self, src, dst, src_spot, dst_spot, send, recv):
            self.src, self.dst, self.src_spot, self.dst_spot = src, dst, src_spot, dst_spot
            self.send, self.recv = send, recv

        def begin(self, p):
            a, b, _ = AXES[p]
            here = self.dst(p, self.dst_spot(p, pos[a], pos[b]))
            for (d, e), dev in zip(steps, plane_devices[p]):
                there = self.src_spot(p, (pos[a] + d) % 4, (pos[b] + e) % 4)
                remote(self.src.at[p, there], here, self.send.at[p], self.recv.at[p], dev).start()

        def keep(self, p):
            a, b, _ = AXES[p]
            self.dst(p, self.dst_spot(p, pos[a], pos[b]))[...] = self.src[p, self.src_spot(p, pos[a], pos[b])]

        def arrive(self, p):
            all_of = self.src.at[p, pl.ds(0, 15)]
            pltpu.make_async_copy(all_of, all_of, self.recv.at[p]).wait()

        def left(self, p):
            all_of = self.src.at[p, pl.ds(0, 15)]
            pltpu.make_async_copy(all_of, all_of, self.send.at[p]).wait()

    ins = (in_send, in_recv)
    outs = (out_send, out_recv)
    columns = lambda p, a, b: a * 4 + b
    in1 = PlaneExchange(x0, lambda p, s: x2.at[p, s], columns, spot, in_plane_send, in_plane_recv)
    in3 = Exchange(0, 2, lambda p, q: x2p.at[p, q], lambda p, q: x3.at[core, p, q], ins)
    for p in range(3):
        in1.begin(p)

    def square(k, total):
        for e in range(4):
            v = x0[k // 4, k % 4 * 4 + e].astype(F32)
            v = v * v
            v = (v[:, :128] + v[:, 128:256]) + v[:, 256:]
            total = total + ((v[:8] + v[8:16]) + (v[16:24] + v[24:]))
        return total

    for p in range(3):
        in1.keep(p)
    sq[13] = lax.fori_loop(0, 12, square, jnp.zeros((8, 128), F32))
    sq_core = remote(sq.at[13], sq.at[14], sq_send.at[3, 0], sq_recv.at[3, 0], partner)
    sq_core.start()
    sent.append(sq_core)

    def iota(shape, d):
        return lax.broadcasted_iota(jnp.int32, shape, d)

    def ones_where(cond):
        return jnp.where(cond, 1.0, 0.0).astype(BF)

    def spread_matrix(shape, wide, unit, narrow):
        s, r = iota(shape, wide), iota(shape, 1 - wide)
        return ones_where((s % unit < narrow) & (r == (s // unit) * narrow + s % unit))

    widen = spread_matrix((COL2, 512), 1, 128, COL3)
    for p in range(3):
        in1.arrive(p)
        for u in range(4):
            rows = x2[p, pl.ds(4 * u, 4)].reshape(4 * PIECE, COL2)
            rows = jnp.dot(rows, widen, preferred_element_type=F32).astype(BF)
            for q in range(4):
                x2p[p, q, u] = rows[:, q * 128 : (q + 1) * 128].reshape(4, PIECE, 128)
        in3.begin(p)
    for p in range(3):
        in3.keep(p)
    crossing = []
    for p in range(3):
        in3.arrive(p)
        here = x3.at[core, p]
        c = remote(here, here, core_send.at[p], core_recv.at[p], partner)
        c.start()
        crossing.append(c)
        sent.append(c)

    pack = spread_matrix((8 * ROWS, 8 * PIECE), 1, PIECE, ROWS)

    def pack_rows(owner):
        def body(k, carry):
            x, y0, group = k // 2, k % 2 * 2, [[], [], []]
            for y in (y0, y0 + 1):
                for z in range(4):
                    group[0].append(x3[owner, 0, z, x, y])
                    group[1].append(x3[owner, 1, x, y, z])
                    group[2].append(x3[owner, 2, y, x, z])
            rows = jnp.concatenate([jnp.concatenate(e, axis=0) for e in group], axis=1)
            at = pl.ds(al(owner * HALF_M + k * 8 * ROWS), 8 * ROWS)
            s_all[at, :] = jnp.dot(pack, rows, preferred_element_type=F32).astype(BF)
            return carry

        lax.fori_loop(0, 4, lambda k, carry: body(2 * k + 1, body(2 * k, carry)), 0)

    pack_rows(core)
    for c in crossing:
        c.wait_recv()
    pack_rows(1 - core)

    def turn_all():
        kk, ll = iota((CHIP, 384), 0), iota((CHIP, 384), 1)
        pick = ones_where((ll % 128 < COL3) & (kk == (ll // 128) * COL3 + ll % 128))

        def turn(j, carry):
            at = pl.ds(al(j * BLK, BLK), BLK)
            st[:, at] = lax.dot_general(pick, s_all[at, :], NT, preferred_element_type=F32).astype(BF)
            return carry

        lax.fori_loop(0, NB // 2, lambda k, carry: turn(2 * k + 1, turn(2 * k, carry)), 0)

    def block_of(chunk, m):
        if chunk == 0:
            i = jnp.where(m < 28, m % NB, 4 * core + m - 28)
            d = jnp.where(m < 28, 2 * core + m // NB, 7)
            return i, d, jnp.where(d == 0, 0.5, 1.0)
        i = jnp.where(m < 14, m, jnp.where(m < 21, 7 * core + m - 14, (4 * core + m - 19) % NB))
        d = jnp.where(m < 14, 4 + 2 * core, jnp.where(m < 21, 5, 7))
        return i, d, jnp.where((d == 7) & ((i >= 7) | (m == 23)), 0.0, 1.0)

    def gram_block(chunk, m, t):
        i, d, scale = block_of(chunk, m)
        j = (i + d) % NB
        ri = pl.ds(al(i * BLK, BLK), BLK)
        rj = pl.ds(al(j * BLK, BLK), BLK)
        acc = lax.dot_general(s_all[ri, :], s_all[rj, :], NT, preferred_element_type=F32)
        acc = (scale * acc).astype(BF)
        t[pl.ds(al(m * 512, 512), 256), :] = acc[:, :128]
        t[pl.ds(al(m * 512 + 256, 256), 256), :] = acc[:, 128:]

    def square_begin(s):
        group = [
            remote(sq.at[4 * s], sq.at[4 * s + 1 + k], sq_send.at[s, k], sq_recv.at[s, k], dev)
            for k, dev in enumerate((right[s], left[s], across[s]))
        ]
        for c in group:
            c.start()
        sent.extend(group)
        return group

    def square_end(s, group):
        for c in group:
            c.wait_recv()
        sq[4 * s + 4] = (sq[4 * s] + sq[4 * s + 3]) + (sq[4 * s + 1] + sq[4 * s + 2])

    class Chunk:
        def __init__(self, no, t, bufs, rs, ag):
            self.no, self.t, self.bufs, self.rs, self.ag = no, t, bufs, rs, ag
            self.blocks = PER_PART[no]
            self.sizes = SIZES[no]
            base = [p * self.blocks * 512 for p in range(3)]
            self.bases = [base]
            for k in range(3):
                base = [base[p] + pos[AXES[p][k]] * self.sizes[k] for p in range(3)]
                self.bases.append(base)
            self.mine = no * SECOND * 512
            self.copies = {}

        def quarter(self, k, p, by):
            return self.bases[k][p] + ((pos[AXES[p][k]] + by) % 4) * self.sizes[k]

        def gram(self, p, start, count):
            for m in range(count):
                gram_block(self.no, p * self.blocks + start + m, self.t)

        def gram_far(self):
            for p in range(3):
                q = (pos[AXES[p][0]] + 2) % 4
                self.gram(p, self.blocks * q // 4, 2 + self.blocks % 4 // 2)

        def gram_near(self):
            for p in range(3):
                me = pos[AXES[p][0]]
                if self.blocks % 4:
                    self.gram(p, self.blocks // 4 + self.blocks // 2 * (me // 2), 1)
                for by in (1, 3):
                    self.gram(p, (self.blocks * ((me + by) % 4) + 2) // 4, 2)

        def gram_own(self):
            for p in range(3):
                self.gram(p, (self.blocks * pos[AXES[p][0]] + 2) // 4, 2)

        def push(self, k, p, no, off, rows):
            a = AXES[p][k]
            c = remote(
                self.t.at[pl.ds(al(off), rows), :],
                self.bufs[k].at[p, no],
                self.rs[0].at[k, p, no],
                self.rs[1].at[k, p, no],
                right[a] if no < 3 else left[a],
            )
            c.start()
            self.copies[k, p, no] = c
            sent.append(c)

        def add_rows(self, off, rows, srcs):
            step = rows // 2 if rows > 200 else rows
            t = self.t

            def body(m, carry):
                at = pl.ds(al(off + m * step), step)
                total = t[at, :]
                for src in srcs:
                    total = total + src[pl.ds(al(m * step), step), :]
                t[at, :] = total
                return carry

            lax.fori_loop(0, rows // step, body, 0)

        def scatter_far(self, k):
            half = self.sizes[k] // 2
            for p in range(3):
                self.push(k, p, 0, self.quarter(k, p, 2), half)
                self.push(k, p, 3, self.quarter(k, p, 2) + half, half)

        def scatter_near(self, k):
            half = self.sizes[k] // 2
            for p in range(3):
                self.push(k, p, 1, self.quarter(k, p, 1) + half, half)
                self.push(k, p, 4, self.quarter(k, p, 3), half)

        def scatter_mid(self, k):
            half = self.sizes[k] // 2
            for p in range(3):
                self.copies[k, p, 0].wait_recv()
                self.add_rows(self.quarter(k, p, 1), half, [self.bufs[k].at[p, 0]])
                self.push(k, p, 2, self.quarter(k, p, 1), half)
                self.copies[k, p, 3].wait_recv()
                self.add_rows(self.quarter(k, p, 3) + half, half, [self.bufs[k].at[p, 3]])
                self.push(k, p, 5, self.quarter(k, p, 3) + half, half)

        def scatter_end(self, k):
            half = self.sizes[k] // 2
            for p in range(3):
                for h, one, two in ((0, 4, 2), (1, 1, 5)):
                    self.copies[k, p, one].wait_recv()
                    self.copies[k, p, two].wait_recv()
                    self.add_rows(
                        self.quarter(k, p, 0) + h * half, half, [self.bufs[k].at[p, one], self.bufs[k].at[p, two]]
                    )

        def ring_begin(self, s):
            size = self.sizes[s]
            for p in range(3):
                a = AXES[p][s]
                for k, dev in ((2, across[a]), (1, right[a]), (3, left[a])):
                    c = remote(
                        self.t.at[pl.ds(al(self.quarter(s, p, k)), size), :],
                        self.bufs[s].at[p, k - 1],
                        self.rs[0].at[s, p, k - 1],
                        self.rs[1].at[s, p, k - 1],
                        dev,
                    )
                    c.start()
                    self.copies[s, p, k] = c
                    sent.append(c)

        def ring_end(self, s):
            size = self.sizes[s]
            for p in range(3):
                for k in (1, 2, 3):
                    self.copies[s, p, k].wait_recv()
                off = self.bases[s + 1][p]
                step = 80 if size % 80 == 0 else 64

                def body(m, carry):
                    at = pl.ds(al(off + m * step), step)
                    total = self.t[at, :].astype(F32)
                    for k in range(3):
                        total = total + self.bufs[s][p, k, pl.ds(al(m * step), step)].astype(F32)
                    if s == 2:
                        g[pl.ds(al(self.mine + off), size), :] = total.astype(BF)
                    else:
                        self.t[at, :] = total.astype(BF)
                    return carry

                lax.fori_loop(0, size // step, body, 0)
            if s == 2:
                self.rounds(2)

        def rounds(self, s):
            for p in range(3):
                a = AXES[p][s]
                off = self.bases[s + 1][p]
                for k, dev in ((2, across[a]), (1, right[a]), (3, left[a])):
                    self.spread(s, p, k - 1, off, self.sizes[s], dev)

        def rounds_end(self, s):
            for p in range(3):
                self.got(s, p, 0, 1, 2)

        def spread(self, k, p, no, off, rows, dev):
            here = g.at[pl.ds(al(self.mine + off), rows), :]
            c = remote(here, here, self.ag[0].at[k, p, no], self.ag[1].at[k, p, no], dev)
            c.start()
            self.copies["g", k, p, no] = c
            sent.append(c)

        def got(self, k, p, *nos):
            for no in nos:
                self.copies["g", k, p, no].wait_recv()

        def gather_begin(self, k):
            half = self.sizes[k] // 2
            for p in range(3):
                own = self.quarter(k, p, 0)
                a = AXES[p][k]
                self.spread(k, p, 0, own, half, right[a])
                self.spread(k, p, 1, own + half, half, left[a])
            for p in range(3):
                own = self.quarter(k, p, 0)
                a = AXES[p][k]
                self.spread(k, p, 2, own + half, half, right[a])
                self.spread(k, p, 3, own, half, left[a])

        def gather_mid(self, k):
            half = self.sizes[k] // 2
            for p in range(3):
                a = AXES[p][k]
                self.got(k, p, 0)
                self.spread(k, p, 4, self.quarter(k, p, 3), half, right[a])
                self.got(k, p, 1)
                self.spread(k, p, 5, self.quarter(k, p, 1) + half, half, left[a])

        def gather_end(self, k):
            for p in range(3):
                self.got(k, p, 2, 3, 4, 5)

    one = Chunk(0, ta, (r1a, r2a, r3a), (rsa_send, rsa_recv), (aga_send, aga_recv))
    two = Chunk(1, tb, (r1b, r2b, r3b), (rsb_send, rsb_recv), (agb_send, agb_recv))

    early = list(sent)
    sent.clear()
    one.gram_far()
    one.scatter_far(0)
    one.gram_near()
    one.scatter_near(0)
    two.gram_far()
    one.gram_own()
    one.scatter_mid(0)
    two.scatter_far(0)
    two.gram_near()
    two.scatter_near(0)
    two.gram_own()
    sq_core.wait_recv()
    sq[0] = sq[13] + sq[14]
    squares = square_begin(0)
    turn_all()
    flush(early)
    for p in range(3):
        in1.left(p)
    one.scatter_end(0)
    one.ring_begin(1)
    two.scatter_mid(0)
    square_end(0, squares)
    squares = square_begin(1)
    one.ring_end(1)
    one.ring_begin(2)
    square_end(1, squares)
    squares = square_begin(2)
    one.ring_end(2)
    one.rounds_end(2)
    one.rounds(1)
    two.scatter_end(0)
    two.ring_begin(1)
    square_end(2, squares)
    one.rounds_end(1)
    early.extend(sent)
    sent.clear()
    one.gather_begin(0)
    two.ring_end(1)
    two.ring_begin(2)
    two.ring_end(2)
    one.gather_mid(0)
    two.rounds_end(2)
    two.rounds(1)
    two.rounds_end(1)
    two.gather_begin(0)
    flush(early)
    one.gather_end(0)

    def cols(a_ref, i):
        return a_ref[:, pl.ds(al(i * BLK, BLK), BLK)]

    def block(slot):
        o = slot * 512
        return jnp.concatenate([g[pl.ds(al(o, 512), 256), :], g[pl.ds(al(o + 256, 256), 256), :]], axis=1)

    def band(a_ref, j, ds):
        def straight(d, first):
            i = (j + NB - d) % NB
            return cols(a_ref, i), block(first + i)

        def turned(d, first):
            return cols(a_ref, (j + d) % NB), block(first + j)

        a, b = zip(*[straight(*e) for e in ds])
        acc = jnp.dot(jnp.concatenate(a, axis=1), jnp.concatenate(b, axis=0), preferred_element_type=F32)
        a, b = zip(*[turned(*e) for e in ds])
        return acc + lax.dot_general(
            jnp.concatenate(a, axis=1), jnp.concatenate(b, axis=1), NT, preferred_element_type=F32
        )

    whole_one = ((2 * core, 0), (2 * core + 1, NB))
    whole_two = ((2 * core + 4, SECOND),)

    def single(acc_ref, a_ref, chunk, m):
        i, d, _ = block_of(chunk, m)
        j = (i + d) % NB
        b = block(chunk * SECOND + m)
        acc_ref[:, pl.ds(al(j * BLK, BLK), BLK)] += jnp.dot(cols(a_ref, i), b, preferred_element_type=F32)
        acc_ref[:, pl.ds(al(i * BLK, BLK), BLK)] += lax.dot_general(
            cols(a_ref, j), b, NT, preferred_element_type=F32
        )

    def loop(first_k, last_k, f):
        def body(k, carry):
            f(first_k + 2 * k)
            f(first_k + 2 * k + 1)
            return carry

        lax.fori_loop(0, (last_k - first_k) // 2, body, 0)
        if (last_k - first_k) % 2:
            f(last_k - 1)

    def band_at(j):
        return pl.ds(al(j * BLK, BLK), BLK)

    def to_partner(no, src, dst):
        c = remote(src, dst, part_send.at[no], part_recv.at[no], partner)
        c.start()
        sent.append(c)
        return c

    def y_one(j):
        yf[:, band_at(j)] = band(st, j, whole_one)

    loop(0, 6, y_one)
    two.gather_mid(0)
    loop(6, NB, y_one)
    zf[...] = jnp.zeros((CHIP, M), F32)
    for m in (28, 29):
        single(yf, st, 0, m)
    two.gather_end(0)
    def shared(k, a_ref=st, acc_ref=yf):
        single(acc_ref, a_ref, 1, 14 + k)

    loop(0, 9, shared)

    def y_two(j):
        v = yf[:, band_at(j)] + band(st, j, whole_two)
        yf[:, band_at(j)] = v
        yp[:, band_at(j)] = v.astype(BF)

    shares = []
    for lo, hi in ((0, 4), (4, 8), (8, 12), (12, 14)):
        loop(lo, hi, y_two)
        here = pl.ds(lo * BLK, (hi - lo) * BLK)
        shares.append((lo, hi, to_partner(len(shares), yp.at[:, here], yr.at[:, here])))

    factor = 0.3 * math.sqrt(M) / (jnp.sqrt(jnp.sum(sq[12], axis=(0, 1), keepdims=True)) + 1e-07)
    factor2 = factor * factor

    def y_sum(j):
        v = factor2 * (yf[:, band_at(j)] + yr[:, band_at(j)].astype(F32))
        yf[:, band_at(j)] = v
        ybf[:, band_at(j)] = v.astype(BF)

    for lo, hi, arriving in shares:
        arriving.wait_recv()
        loop(lo, hi, y_sum)

    for m in (28, 29):
        single(zf, ybf, 0, m)
    def shared(k, a_ref=ybf, acc_ref=zf):
        single(acc_ref, a_ref, 1, 14 + k)

    loop(0, 9, shared)

    def z_band(j):
        return factor2 * (zf[:, band_at(j)] + band(ybf, j, whole_one + whole_two))

    def z_theirs(k):
        zp[:, band_at(k)] = z_band((1 - core) * 7 + k).astype(BF)

    loop(0, 7, z_theirs)
    share = to_partner(4, zp, zr)

    def z_mine(k):
        zf[:, band_at(core * 7 + k)] = z_band(core * 7 + k)

    loop(0, 7, z_mine)
    share.wait_recv()
    for p in range(3):
        ut[pl.ds(p * 128 + COL3, 128 - COL3), :] = jnp.zeros((128 - COL3, HALF_M), BF)

    def finish(k):
        at = band_at(core * 7 + k)
        scaled = (factor * st[:, at].astype(F32)).astype(BF).astype(F32)
        product = factor * (COEFF_B * yf[:, at] + COEFF_C * (zf[:, at] + zr[:, band_at(k)].astype(F32)))
        u = (math.sqrt(K) * (COEFF_A * scaled + product)).astype(BF)
        for p in range(3):
            ut[pl.ds(p * 128, COL3), band_at(k)] = u[p * COL3 : (p + 1) * COL3]

    loop(0, 7, finish)

    early.extend(sent)
    sent.clear()
    y3 = x2p
    unpack = spread_matrix((8 * PIECE, 8 * ROWS), 0, PIECE, ROWS)
    for m in range(8):
        o = m * 8 * ROWS
        first_lane = o // 128 * 128
        skip = o - first_lane
        width = -(-(skip + 8 * ROWS) // 128) * 128
        v = ut[:, pl.ds(first_lane, width)][:, skip : skip + 8 * ROWS]
        rows = lax.dot_general(unpack, v, NT, preferred_element_type=F32).astype(BF)
        for r in range(8):
            x, y, z = m // 2, m % 2 * 2 + r // 4, r % 4
            for p, at in enumerate(((z, x, y), (x, y, z), (y, x, z))):
                y3[(p,) + at] = rows[r * PIECE : (r + 1) * PIECE, p * 128 : (p + 1) * 128]

    out1 = Exchange(0, 2, lambda p, q: y3.at[p, q], lambda p, q: y2p.at[p, q], outs)
    out2 = PlaneExchange(
        y2, lambda p, s: y0.at[:, pl.ds(al(p * THIRD + s * COL2, 128), COL2)], spot, columns, out_plane_send, out_plane_recv,
    )
    for p in range(3):
        out1.begin(p)
    for p in range(3):
        out1.keep(p)
    flush(early)
    early.extend(sent)
    sent.clear()
    narrow = spread_matrix((512, COL2), 0, 128, COL3)
    for p in range(3):
        out1.arrive(p)
        for u in range(4):
            rows = [y2p[p, q, u].reshape(4 * PIECE, 128) for q in range(4)]
            rows = jnp.dot(jnp.concatenate(rows, axis=1), narrow, preferred_element_type=F32)
            y2[p, pl.ds(4 * u, 4)] = rows.astype(BF).reshape(4, PIECE, COL2)
        out2.begin(p)
    own = []
    for p in range(3):
        a, b, _ = AXES[p]
        at = (pos[a], pos[b])
        own.append(pltpu.make_async_copy(y2.at[p, spot(p, *at)], out2.dst(p, columns(p, *at)), io_sem.at[1 + p]))
        own[p].start()
    flush(early)
    for p in range(3):
        out2.arrive(p)
        own[p].wait()
    for p in range(3):
        out2.left(p)
    flush(sent)


def local(gradient):
    dma = pltpu.SemaphoreType.DMA
    hbm = pl.BlockSpec(memory_space=pl.ANY)
    padded = pl.pallas_call(
        kernel,
        out_shape=jax.ShapeDtypeStruct((PIECE, K), BF),
        in_specs=[hbm],
        out_specs=hbm,
        scratch_shapes=[
            pltpu.VMEM((ROWS, K), BF),
            pltpu.VMEM((3, 16, PIECE, COL2), BF),
            pltpu.VMEM((3, 16, PIECE, COL2), BF),
            pltpu.VMEM((3, 4, 4, 4, PIECE, 128), BF),
            pltpu.VMEM((2, 3, 4, 4, 4, PIECE, 128), BF),
            pltpu.VMEM((M, 384), BF),
            pltpu.VMEM((CHIP, M), BF),
            pltpu.VMEM((384, HALF_M), BF),
            pltpu.VMEM((3, 4, 4, 4, PIECE, 128), BF),
            pltpu.VMEM((3, 16, PIECE, COL2), BF),
            pltpu.VMEM((3 * 10 * 512, 128), BF),
            pltpu.VMEM((3 * 8 * 512, 128), BF),
            pltpu.VMEM((SLOTS * 512, 128), BF),
            pltpu.VMEM((3, 6, 640, 128), BF),
            pltpu.VMEM((3, 3, 320, 128), BF),
            pltpu.VMEM((3, 3, 80, 128), BF),
            pltpu.VMEM((3, 6, 512, 128), BF),
            pltpu.VMEM((3, 3, 256, 128), BF),
            pltpu.VMEM((3, 3, 64, 128), BF),
            pltpu.VMEM((15, 8, 128), F32),
            pltpu.VMEM((CHIP, M), F32),
            pltpu.VMEM((CHIP, M), BF),
            pltpu.VMEM((CHIP, M), BF),
            pltpu.VMEM((CHIP, M), BF),
            pltpu.VMEM((CHIP, M), F32),
            pltpu.VMEM((CHIP, HALF_M), BF),
            pltpu.VMEM((CHIP, HALF_M), BF),
            dma((4,)),
            dma((1, 3, 3)),
            dma((1, 3, 3)),
            dma((3,)),
            dma((3,)),
            dma((3,)),
            dma((3,)),
            dma((1, 3, 3)),
            dma((1, 3, 3)),
            dma((3,)),
            dma((3,)),
            dma((5,)),
            dma((5,)),
            dma((3, 3, 6)),
            dma((3, 3, 6)),
            dma((3, 3, 6)),
            dma((3, 3, 6)),
            dma((3, 3, 6)),
            dma((3, 3, 6)),
            dma((3, 3, 6)),
            dma((3, 3, 6)),
            dma((4, 3)),
            dma((4, 3)),
        ],
        compiler_params=pltpu.CompilerParams(
            collective_id=0, has_side_effects=True, vmem_limit_bytes=60 * 1024 * 1024
        ),
        cost_estimate=pl.CostEstimate(flops=16 * 10**9, bytes_accessed=5 * 10**6, transcendentals=0),
    )(gradient)
    return padded[:ROWS]


def solution(mesh):
    spec = P(("wide", "narrow"), None)
    return jax.shard_map(local, mesh=mesh, in_specs=(spec,), out_specs=spec, check_vma=False)
```

```python
import math

import jax
import jax.numpy as jnp
from jax import lax
from jax.experimental import pallas as pl
from jax.experimental.pallas import tpu as pltpu
from jax.sharding import PartitionSpec as P

M = 3584
K = 18432

COEFF_A = 3.4445
COEFF_B = -4.775
COEFF_C = 2.0315

MESH = pl.DeviceIdType.MESH
BF = jnp.bfloat16
F32 = jnp.float32
NT = (((1,), (1,)), ((), ()))

ROWS = 28
PIECE = 32
THIRD = K // 3
COL1 = THIRD // 4
COL2 = COL1 // 4
COL3 = COL2 // 4
CHIP = 3 * COL3
HALF_M = M // 2
AXES = ((0, 1, 2), (1, 2, 0), (2, 0, 1))

BLK = 256
NB = M // BLK
PER_PART = (12, 6)
SECOND = 3 * PER_PART[0]
SLOTS = 3 * sum(PER_PART)
SIZES = ((1536, 384, 96), (768, 192, 48))


def al(x, m=16):
    return pl.multiple_of(x, m)


def kernel(
    in_ref, y0,
    rows_in, x0, x2, x2p, x3, s_all, st,
    ut, y2p, y2,
    ta, tb, g, r1a, r2a, r3a, r1b, r2b, r3b, sq, yf, ybf, yp, yr, zf, zp, zr,
    io_sem, in_send, in_recv, in_plane_send, in_plane_recv, core_send, core_recv,
    out_send, out_recv, out_plane_send, out_plane_recv, part_send, part_recv,
    rsa_send, rsa_recv, aga_send, aga_recv, rsb_send, rsb_recv, agb_send, agb_recv, sq_send, sq_recv,
):
    w, n_ = lax.axis_index("wide"), lax.axis_index("narrow")
    core, z_lo, y = w % 2, (w // 2) % 2, w // 4
    x, z_hi = n_ % 4, n_ // 4
    z = z_hi * 2 + z_lo
    pos = (x, y, z)

    def device(x, y, z, core):
        return ((y * 2 + z % 2) * 2 + core, (z // 2) * 4 + x)

    def shifted(axis, by):
        p = [x, y, z]
        p[axis] = (p[axis] + by) % 4
        return device(*p, core)

    right = [shifted(a, 1) for a in range(3)]
    left = [shifted(a, 3) for a in range(3)]
    across = [shifted(a, 2) for a in range(3)]
    partner = device(x, y, z, 1 - core)

    def in_plane(p, d, e):
        a, b, _ = AXES[p]
        if e == 0:
            return (right, across, left)[d - 1][a]
        if d == 0:
            return (right, across, left)[e - 1][b]
        v = [x, y, z]
        v[a] = (v[a] + d) % 4
        v[b] = (v[b] + e) % 4
        return device(*v, core)

    steps = [(d, e) for d in range(4) for e in range(4) if d or e]
    plane_devices = [[in_plane(p, d, e) for d, e in steps] for p in range(3)]
    diagonal = [plane_devices[p][k] for p in range(3) for k, (d, e) in enumerate(steps) if d and e]

    barrier = pltpu.get_barrier_semaphore()
    for d in right + left + across + diagonal + [partner]:
        pl.semaphore_signal(barrier, inc=1, device_id=d, device_id_type=MESH)

    fetch = pltpu.make_async_copy(in_ref, rows_in, io_sem.at[0])
    fetch.start()
    fetch.wait()

    def load(k, carry):
        p, q = k // 4, k % 4
        v = rows_in[:, pl.ds(al(k * COL1, COL1), COL1)]
        for e in range(4):
            x0[p, q * 4 + e, pl.ds(0, ROWS), :] = v[:, e * COL2 : (e + 1) * COL2]
            x0[p, q * 4 + e, pl.ds(ROWS, PIECE - ROWS), :] = jnp.zeros((PIECE - ROWS, COL2), BF)
        return carry

    lax.fori_loop(0, 12, load, 0)
    pl.semaphore_wait(barrier, 37)

    def remote(src, dst, send, recv, dev):
        return pltpu.make_async_remote_copy(
            src_ref=src, dst_ref=dst, send_sem=send, recv_sem=recv, device_id=dev, device_id_type=MESH
        )

    sent = []

    def flush(group):
        for c in group:
            c.wait_send()
        group.clear()

    class Exchange:
        def __init__(self, stage, axis_no, src, dst, sems):
            self.stage, self.axis_no, self.src, self.dst, self.sems = stage, axis_no, src, dst, sems
            self.copies = {}

        def begin(self, p):
            a = AXES[p][self.axis_no]
            me = pos[a]
            send, recv = self.sems
            group = []
            for k, dev in ((2, across[a]), (1, right[a]), (3, left[a])):
                c = remote(
                    self.src(p, (me + k) % 4), self.dst(p, me),
                    send.at[self.stage, p, k - 1], recv.at[self.stage, p, k - 1], dev,
                )
                c.start()
                group.append(c)
                sent.append(c)
            self.copies[p] = group

        def keep(self, p):
            me = pos[AXES[p][self.axis_no]]
            src, dst = self.src(p, me), self.dst(p, me)
            dst[...] = src[...]

        def arrive(self, p):
            for c in self.copies[p]:
                c.wait_recv()

    def spot(p, a, b):
        return b * 4 + a if p == 2 else a * 4 + b

    class PlaneExchange:
        def __init__(self, src, dst, src_spot, dst_spot, send, recv):
            self.src, self.dst, self.src_spot, self.dst_spot = src, dst, src_spot, dst_spot
            self.send, self.recv = send, recv

        def begin(self, p):
            a, b, _ = AXES[p]
            here = self.dst(p, self.dst_spot(p, pos[a], pos[b]))
            for (d, e), dev in zip(steps, plane_devices[p]):
                there = self.src_spot(p, (pos[a] + d) % 4, (pos[b] + e) % 4)
                remote(self.src.at[p, there], here, self.send.at[p], self.recv.at[p], dev).start()

        def keep(self, p):
            a, b, _ = AXES[p]
            self.dst(p, self.dst_spot(p, pos[a], pos[b]))[...] = self.src[p, self.src_spot(p, pos[a], pos[b])]

        def arrive(self, p):
            all_of = self.src.at[p, pl.ds(0, 15)]
            pltpu.make_async_copy(all_of, all_of, self.recv.at[p]).wait()

        def left(self, p):
            all_of = self.src.at[p, pl.ds(0, 15)]
            pltpu.make_async_copy(all_of, all_of, self.send.at[p]).wait()

    ins = (in_send, in_recv)
    outs = (out_send, out_recv)
    columns = lambda p, a, b: a * 4 + b
    in1 = PlaneExchange(x0, lambda p, s: x2.at[p, s], columns, spot, in_plane_send, in_plane_recv)
    in3 = Exchange(0, 2, lambda p, q: x2p.at[p, q], lambda p, q: x3.at[core, p, q], ins)
    for p in range(3):
        in1.begin(p)

    def square(k, total):
        for e in range(4):
            v = x0[k // 4, k % 4 * 4 + e].astype(F32)
            v = v * v
            v = (v[:, :128] + v[:, 128:256]) + v[:, 256:]
            total = total + ((v[:8] + v[8:16]) + (v[16:24] + v[24:]))
        return total

    for p in range(3):
        in1.keep(p)
    sq[13] = lax.fori_loop(0, 12, square, jnp.zeros((8, 128), F32))
    sq_core = remote(sq.at[13], sq.at[14], sq_send.at[3, 0], sq_recv.at[3, 0], partner)
    sq_core.start()
    sent.append(sq_core)

    def iota(shape, d):
        return lax.broadcasted_iota(jnp.int32, shape, d)

    def ones_where(cond):
        return jnp.where(cond, 1.0, 0.0).astype(BF)

    def spread_matrix(shape, wide, unit, narrow):
        s, r = iota(shape, wide), iota(shape, 1 - wide)
        return ones_where((s % unit < narrow) & (r == (s // unit) * narrow + s % unit))

    widen = spread_matrix((COL2, 512), 1, 128, COL3)
    for p in range(3):
        in1.arrive(p)
        for u in range(4):
            rows = x2[p, pl.ds(4 * u, 4)].reshape(4 * PIECE, COL2)
            rows = jnp.dot(rows, widen, preferred_element_type=F32).astype(BF)
            for q in range(4):
                x2p[p, q, u] = rows[:, q * 128 : (q + 1) * 128].reshape(4, PIECE, 128)
        in3.begin(p)
    for p in range(3):
        in3.keep(p)
    crossing = []
    for p in range(3):
        in3.arrive(p)
        here = x3.at[core, p]
        c = remote(here, here, core_send.at[p], core_recv.at[p], partner)
        c.start()
        crossing.append(c)
        sent.append(c)

    pack = spread_matrix((8 * ROWS, 8 * PIECE), 1, PIECE, ROWS)

    def pack_rows(owner):
        def body(k, carry):
            x, y0, group = k // 2, k % 2 * 2, [[], [], []]
            for y in (y0, y0 + 1):
                for z in range(4):
                    group[0].append(x3[owner, 0, z, x, y])
                    group[1].append(x3[owner, 1, x, y, z])
                    group[2].append(x3[owner, 2, y, x, z])
            rows = jnp.concatenate([jnp.concatenate(e, axis=0) for e in group], axis=1)
            at = pl.ds(al(owner * HALF_M + k * 8 * ROWS), 8 * ROWS)
            s_all[at, :] = jnp.dot(pack, rows, preferred_element_type=F32).astype(BF)
            return carry

        lax.fori_loop(0, 4, lambda k, carry: body(2 * k + 1, body(2 * k, carry)), 0)

    pack_rows(core)
    for c in crossing:
        c.wait_recv()
    pack_rows(1 - core)

    def turn_all():
        kk, ll = iota((CHIP, 384), 0), iota((CHIP, 384), 1)
        pick = ones_where((ll % 128 < COL3) & (kk == (ll // 128) * COL3 + ll % 128))

        def turn(j, carry):
            at = pl.ds(al(j * BLK, BLK), BLK)
            st[:, at] = lax.dot_general(pick, s_all[at, :], NT, preferred_element_type=F32).astype(BF)
            return carry

        lax.fori_loop(0, NB // 2, lambda k, carry: turn(2 * k + 1, turn(2 * k, carry)), 0)

    def block_of(chunk, m):
        if chunk == 0:
            i = jnp.where(m < 28, m % NB, jnp.where(m < 35, 7 * core + m - 28, 4 * core))
            d = jnp.where(m < 28, 2 * core + m // NB, jnp.where(m < 35, 5, 7))
            return i, d, jnp.where(d == 0, 0.5, 1.0)
        i = jnp.where(m < 14, m, 4 * core + jnp.minimum(m, 16) - 13)
        d = jnp.where(m < 14, 4 + 2 * core, 7)
        return i, d, jnp.where((d == 7) & ((i >= 7) | (m == 17)), 0.0, 1.0)

    def gram_block(chunk, m, t):
        i, d, scale = block_of(chunk, m)
        j = (i + d) % NB
        ri = pl.ds(al(i * BLK, BLK), BLK)
        rj = pl.ds(al(j * BLK, BLK), BLK)
        acc = lax.dot_general(s_all[ri, :], s_all[rj, :], NT, preferred_element_type=F32)
        acc = (scale * acc).astype(BF)
        t[pl.ds(al(m * 512, 512), 256), :] = acc[:, :128]
        t[pl.ds(al(m * 512 + 256, 256), 256), :] = acc[:, 128:]

    def square_begin(s):
        group = [
            remote(sq.at[4 * s], sq.at[4 * s + 1 + k], sq_send.at[s, k], sq_recv.at[s, k], dev)
            for k, dev in enumerate((right[s], left[s], across[s]))
        ]
        for c in group:
            c.start()
        sent.extend(group)
        return group

    def square_end(s, group):
        for c in group:
            c.wait_recv()
        sq[4 * s + 4] = (sq[4 * s] + sq[4 * s + 3]) + (sq[4 * s + 1] + sq[4 * s + 2])

    class Chunk:
        def __init__(self, no, t, bufs, rs, ag):
            self.no, self.t, self.bufs, self.rs, self.ag = no, t, bufs, rs, ag
            self.blocks = PER_PART[no]
            self.sizes = SIZES[no]
            base = [p * self.blocks * 512 for p in range(3)]
            self.bases = [base]
            for k in range(3):
                base = [base[p] + pos[AXES[p][k]] * self.sizes[k] for p in range(3)]
                self.bases.append(base)
            self.mine = no * SECOND * 512
            self.copies = {}

        def quarter(self, k, p, by):
            return self.bases[k][p] + ((pos[AXES[p][k]] + by) % 4) * self.sizes[k]

        def gram(self, p, start, count):
            for m in range(count):
                gram_block(self.no, p * self.blocks + start + m, self.t)

        def gram_far(self):
            for p in range(3):
                q = (pos[AXES[p][0]] + 2) % 4
                self.gram(p, self.blocks * q // 4, -(-self.blocks // 4))

        def gram_near(self):
            for p in range(3):
                me = pos[AXES[p][0]]
                if self.blocks % 4:
                    self.gram(p, self.blocks // 4 + self.blocks // 2 * (me // 2), 1)
                for by in (1, 3):
                    self.gram(p, (self.blocks * ((me + by) % 4) + 2) // 4, self.blocks // 4)

        def gram_own(self):
            for p in range(3):
                self.gram(p, (self.blocks * pos[AXES[p][0]] + 2) // 4, self.blocks // 4)

        def push(self, k, p, no, off, rows):
            a = AXES[p][k]
            c = remote(
                self.t.at[pl.ds(al(off), rows), :],
                self.bufs[k].at[p, no],
                self.rs[0].at[k, p, no],
                self.rs[1].at[k, p, no],
                right[a] if no < 3 else left[a],
            )
            c.start()
            self.copies[k, p, no] = c
            sent.append(c)

        def add_rows(self, off, rows, srcs):
            step = rows // 2 if rows > 200 else rows
            t = self.t

            def body(m, carry):
                at = pl.ds(al(off + m * step), step)
                total = t[at, :]
                for src in srcs:
                    total = total + src[pl.ds(al(m * step), step), :]
                t[at, :] = total
                return carry

            lax.fori_loop(0, rows // step, body, 0)

        def scatter_far(self, k):
            half = self.sizes[k] // 2
            for p in range(3):
                self.push(k, p, 0, self.quarter(k, p, 2), half)
                self.push(k, p, 3, self.quarter(k, p, 2) + half, half)

        def scatter_near(self, k):
            half = self.sizes[k] // 2
            for p in range(3):
                self.push(k, p, 1, self.quarter(k, p, 1) + half, half)
                self.push(k, p, 4, self.quarter(k, p, 3), half)

        def scatter_mid(self, k):
            half = self.sizes[k] // 2
            for p in range(3):
                self.copies[k, p, 0].wait_recv()
                self.add_rows(self.quarter(k, p, 1), half, [self.bufs[k].at[p, 0]])
                self.push(k, p, 2, self.quarter(k, p, 1), half)
                self.copies[k, p, 3].wait_recv()
                self.add_rows(self.quarter(k, p, 3) + half, half, [self.bufs[k].at[p, 3]])
                self.push(k, p, 5, self.quarter(k, p, 3) + half, half)

        def scatter_end(self, k):
            half = self.sizes[k] // 2
            for p in range(3):
                for h, one, two in ((0, 4, 2), (1, 1, 5)):
                    self.copies[k, p, one].wait_recv()
                    self.copies[k, p, two].wait_recv()
                    self.add_rows(
                        self.quarter(k, p, 0) + h * half, half, [self.bufs[k].at[p, one], self.bufs[k].at[p, two]]
                    )

        def ring_begin(self, s):
            size = self.sizes[s]
            for p in range(3):
                a = AXES[p][s]
                for k, dev in ((2, across[a]), (1, right[a]), (3, left[a])):
                    c = remote(
                        self.t.at[pl.ds(al(self.quarter(s, p, k)), size), :],
                        self.bufs[s].at[p, k - 1],
                        self.rs[0].at[s, p, k - 1],
                        self.rs[1].at[s, p, k - 1],
                        dev,
                    )
                    c.start()
                    self.copies[s, p, k] = c
                    sent.append(c)

        def ring_end(self, s):
            size = self.sizes[s]
            for p in range(3):
                for k in (1, 2, 3):
                    self.copies[s, p, k].wait_recv()
                off = self.bases[s + 1][p]
                step = min(size, 96)

                def body(m, carry):
                    at = pl.ds(al(off + m * step), step)
                    total = self.t[at, :].astype(F32)
                    for k in range(3):
                        total = total + self.bufs[s][p, k, pl.ds(al(m * step), step)].astype(F32)
                    if s == 2:
                        g[pl.ds(al(self.mine + off), size), :] = total.astype(BF)
                    else:
                        self.t[at, :] = total.astype(BF)
                    return carry

                lax.fori_loop(0, size // step, body, 0)
            if s == 2:
                self.rounds(2)

        def rounds(self, s):
            for p in range(3):
                a = AXES[p][s]
                off = self.bases[s + 1][p]
                for k, dev in ((2, across[a]), (1, right[a]), (3, left[a])):
                    self.spread(s, p, k - 1, off, self.sizes[s], dev)

        def rounds_end(self, s):
            for p in range(3):
                self.got(s, p, 0, 1, 2)

        def spread(self, k, p, no, off, rows, dev):
            here = g.at[pl.ds(al(self.mine + off), rows), :]
            c = remote(here, here, self.ag[0].at[k, p, no], self.ag[1].at[k, p, no], dev)
            c.start()
            self.copies["g", k, p, no] = c
            sent.append(c)

        def got(self, k, p, *nos):
            for no in nos:
                self.copies["g", k, p, no].wait_recv()

        def gather_begin(self, k):
            half = self.sizes[k] // 2
            for p in range(3):
                own = self.quarter(k, p, 0)
                a = AXES[p][k]
                self.spread(k, p, 0, own, half, right[a])
                self.spread(k, p, 1, own + half, half, left[a])
            for p in range(3):
                own = self.quarter(k, p, 0)
                a = AXES[p][k]
                self.spread(k, p, 2, own + half, half, right[a])
                self.spread(k, p, 3, own, half, left[a])

        def gather_mid(self, k):
            half = self.sizes[k] // 2
            for p in range(3):
                a = AXES[p][k]
                self.got(k, p, 0)
                self.spread(k, p, 4, self.quarter(k, p, 3), half, right[a])
                self.got(k, p, 1)
                self.spread(k, p, 5, self.quarter(k, p, 1) + half, half, left[a])

        def gather_end(self, k):
            for p in range(3):
                self.got(k, p, 2, 3, 4, 5)

    one = Chunk(0, ta, (r1a, r2a, r3a), (rsa_send, rsa_recv), (aga_send, aga_recv))
    two = Chunk(1, tb, (r1b, r2b, r3b), (rsb_send, rsb_recv), (agb_send, agb_recv))

    early = list(sent)
    sent.clear()
    one.gram_far()
    one.scatter_far(0)
    one.gram_near()
    one.scatter_near(0)
    two.gram_far()
    one.gram_own()
    one.scatter_mid(0)
    two.scatter_far(0)
    two.gram_near()
    two.scatter_near(0)
    two.gram_own()
    sq_core.wait_recv()
    sq[0] = sq[13] + sq[14]
    squares = square_begin(0)
    turn_all()
    flush(early)
    for p in range(3):
        in1.left(p)
    one.scatter_end(0)
    one.ring_begin(1)
    square_end(0, squares)
    squares = square_begin(1)
    two.scatter_mid(0)
    one.ring_end(1)
    one.ring_begin(2)
    square_end(1, squares)
    squares = square_begin(2)
    two.scatter_end(0)
    two.ring_begin(1)
    one.ring_end(2)
    square_end(2, squares)
    two.ring_end(1)
    two.ring_begin(2)
    one.rounds_end(2)
    one.rounds(1)
    two.ring_end(2)
    one.rounds_end(1)
    early.extend(sent)
    sent.clear()
    one.gather_begin(0)
    two.rounds_end(2)
    two.rounds(1)
    one.gather_mid(0)
    two.rounds_end(1)
    two.gather_begin(0)
    flush(early)
    one.gather_end(0)

    def cols(a_ref, i):
        return a_ref[:, pl.ds(al(i * BLK, BLK), BLK)]

    def block(slot):
        o = slot * 512
        return jnp.concatenate([g[pl.ds(al(o, 512), 256), :], g[pl.ds(al(o + 256, 256), 256), :]], axis=1)

    def band(a_ref, j, ds):
        def straight(d, first):
            i = (j + NB - d) % NB
            return cols(a_ref, i), block(first + i)

        def turned(d, first):
            return cols(a_ref, (j + d) % NB), block(first + j)

        a, b = zip(*[straight(*e) for e in ds])
        acc = jnp.dot(jnp.concatenate(a, axis=1), jnp.concatenate(b, axis=0), preferred_element_type=F32)
        a, b = zip(*[turned(*e) for e in ds])
        return acc + lax.dot_general(
            jnp.concatenate(a, axis=1), jnp.concatenate(b, axis=1), NT, preferred_element_type=F32
        )

    whole_one = ((2 * core, 0), (2 * core + 1, NB))
    whole_two = ((2 * core + 4, SECOND),)

    def single(acc_ref, a_ref, chunk, m):
        i, d, _ = block_of(chunk, m)
        j = (i + d) % NB
        b = block(chunk * SECOND + m)
        acc_ref[:, pl.ds(al(j * BLK, BLK), BLK)] += jnp.dot(cols(a_ref, i), b, preferred_element_type=F32)
        acc_ref[:, pl.ds(al(i * BLK, BLK), BLK)] += lax.dot_general(
            cols(a_ref, j), b, NT, preferred_element_type=F32
        )

    def loop(first_k, last_k, f):
        def body(k, carry):
            f(first_k + 2 * k)
            f(first_k + 2 * k + 1)
            return carry

        lax.fori_loop(0, (last_k - first_k) // 2, body, 0)
        if (last_k - first_k) % 2:
            f(last_k - 1)

    def band_at(j):
        return pl.ds(al(j * BLK, BLK), BLK)

    def to_partner(no, src, dst):
        c = remote(src, dst, part_send.at[no], part_recv.at[no], partner)
        c.start()
        sent.append(c)
        return c

    def y_one(j):
        yf[:, band_at(j)] = band(st, j, whole_one)

    def shared(acc_ref, a_ref):
        return lambda m: single(acc_ref, a_ref, 0, 28 + m), lambda m: single(acc_ref, a_ref, 1, 14 + m)

    y_first, y_rest = shared(yf, st)
    loop(0, 6, y_one)
    two.gather_mid(0)
    loop(6, NB, y_one)
    zf[...] = jnp.zeros((CHIP, M), F32)
    loop(0, 8, y_first)
    two.gather_end(0)
    loop(0, 3, y_rest)

    def y_two(j):
        v = yf[:, band_at(j)] + band(st, j, whole_two)
        yf[:, band_at(j)] = v
        yp[:, band_at(j)] = v.astype(BF)

    shares = []
    for h in range(2):
        loop(h * 7, h * 7 + 7, y_two)
        here = pl.ds(h * HALF_M, HALF_M)
        shares.append(to_partner(h, yp.at[:, here], yr.at[:, here]))

    factor = 0.3 * math.sqrt(M) / (jnp.sqrt(jnp.sum(sq[12], axis=(0, 1), keepdims=True)) + 1e-07)
    factor2 = factor * factor

    def y_sum(j):
        v = factor2 * (yf[:, band_at(j)] + yr[:, band_at(j)].astype(F32))
        yf[:, band_at(j)] = v
        ybf[:, band_at(j)] = v.astype(BF)

    for h in range(2):
        shares[h].wait_recv()
        loop(h * 7, h * 7 + 7, y_sum)

    z_first, z_rest = shared(zf, ybf)
    loop(0, 8, z_first)
    loop(0, 3, z_rest)

    def z_band(j):
        return factor2 * (zf[:, band_at(j)] + band(ybf, j, whole_one + whole_two))

    def z_theirs(k):
        zp[:, band_at(k)] = z_band((1 - core) * 7 + k).astype(BF)

    loop(0, 7, z_theirs)
    share = to_partner(2, zp, zr)

    def z_mine(k):
        zf[:, band_at(core * 7 + k)] = z_band(core * 7 + k)

    loop(0, 7, z_mine)
    share.wait_recv()
    for p in range(3):
        ut[pl.ds(p * 128 + COL3, 128 - COL3), :] = jnp.zeros((128 - COL3, HALF_M), BF)

    def finish(k):
        at = band_at(core * 7 + k)
        scaled = (factor * st[:, at].astype(F32)).astype(BF).astype(F32)
        product = factor * (COEFF_B * yf[:, at] + COEFF_C * (zf[:, at] + zr[:, band_at(k)].astype(F32)))
        u = (math.sqrt(K) * (COEFF_A * scaled + product)).astype(BF)
        for p in range(3):
            ut[pl.ds(p * 128, COL3), band_at(k)] = u[p * COL3 : (p + 1) * COL3]

    loop(0, 7, finish)

    early.extend(sent)
    sent.clear()
    y3 = x2p
    unpack = spread_matrix((8 * PIECE, 8 * ROWS), 0, PIECE, ROWS)
    for m in range(8):
        o = m * 8 * ROWS
        first_lane = o // 128 * 128
        skip = o - first_lane
        width = -(-(skip + 8 * ROWS) // 128) * 128
        v = ut[:, pl.ds(first_lane, width)][:, skip : skip + 8 * ROWS]
        rows = lax.dot_general(unpack, v, NT, preferred_element_type=F32).astype(BF)
        for r in range(8):
            x, y, z = m // 2, m % 2 * 2 + r // 4, r % 4
            for p, at in enumerate(((z, x, y), (x, y, z), (y, x, z))):
                y3[(p,) + at] = rows[r * PIECE : (r + 1) * PIECE, p * 128 : (p + 1) * 128]

    out1 = Exchange(0, 2, lambda p, q: y3.at[p, q], lambda p, q: y2p.at[p, q], outs)
    out2 = PlaneExchange(
        y2, lambda p, s: y0.at[:, pl.ds(al(p * THIRD + s * COL2, 128), COL2)], spot, columns, out_plane_send, out_plane_recv,
    )
    for p in range(3):
        out1.begin(p)
    for p in range(3):
        out1.keep(p)
    flush(early)
    early.extend(sent)
    sent.clear()
    narrow = spread_matrix((512, COL2), 0, 128, COL3)
    for p in range(3):
        out1.arrive(p)
        for u in range(4):
            rows = [y2p[p, q, u].reshape(4 * PIECE, 128) for q in range(4)]
            rows = jnp.dot(jnp.concatenate(rows, axis=1), narrow, preferred_element_type=F32)
            y2[p, pl.ds(4 * u, 4)] = rows.astype(BF).reshape(4, PIECE, COL2)
        out2.begin(p)
    own = []
    for p in range(3):
        a, b, _ = AXES[p]
        at = (pos[a], pos[b])
        own.append(pltpu.make_async_copy(y2.at[p, spot(p, *at)], out2.dst(p, columns(p, *at)), io_sem.at[1 + p]))
        own[p].start()
    flush(early)
    for p in range(3):
        out2.arrive(p)
        own[p].wait()
    for p in range(3):
        out2.left(p)
    flush(sent)


def local(gradient):
    dma = pltpu.SemaphoreType.DMA
    hbm = pl.BlockSpec(memory_space=pl.ANY)
    padded = pl.pallas_call(
        kernel,
        out_shape=jax.ShapeDtypeStruct((PIECE, K), BF),
        in_specs=[hbm],
        out_specs=hbm,
        scratch_shapes=[
            pltpu.VMEM((ROWS, K), BF),
            pltpu.VMEM((3, 16, PIECE, COL2), BF),
            pltpu.VMEM((3, 16, PIECE, COL2), BF),
            pltpu.VMEM((3, 4, 4, 4, PIECE, 128), BF),
            pltpu.VMEM((2, 3, 4, 4, 4, PIECE, 128), BF),
            pltpu.VMEM((M, 384), BF),
            pltpu.VMEM((CHIP, M), BF),
            pltpu.VMEM((384, HALF_M), BF),
            pltpu.VMEM((3, 4, 4, 4, PIECE, 128), BF),
            pltpu.VMEM((3, 16, PIECE, COL2), BF),
            pltpu.VMEM((3 * 12 * 512, 128), BF),
            pltpu.VMEM((3 * 6 * 512, 128), BF),
            pltpu.VMEM((SLOTS * 512, 128), BF),
            pltpu.VMEM((3, 6, 768, 128), BF),
            pltpu.VMEM((3, 3, 384, 128), BF),
            pltpu.VMEM((3, 3, 96, 128), BF),
            pltpu.VMEM((3, 6, 384, 128), BF),
            pltpu.VMEM((3, 3, 192, 128), BF),
            pltpu.VMEM((3, 3, 48, 128), BF),
            pltpu.VMEM((15, 8, 128), F32),
            pltpu.VMEM((CHIP, M), F32),
            pltpu.VMEM((CHIP, M), BF),
            pltpu.VMEM((CHIP, M), BF),
            pltpu.VMEM((CHIP, M), BF),
            pltpu.VMEM((CHIP, M), F32),
            pltpu.VMEM((CHIP, HALF_M), BF),
            pltpu.VMEM((CHIP, HALF_M), BF),
            dma((4,)),
            dma((1, 3, 3)),
            dma((1, 3, 3)),
            dma((3,)),
            dma((3,)),
            dma((3,)),
            dma((3,)),
            dma((1, 3, 3)),
            dma((1, 3, 3)),
            dma((3,)),
            dma((3,)),
            dma((3,)),
            dma((3,)),
            dma((3, 3, 6)),
            dma((3, 3, 6)),
            dma((3, 3, 6)),
            dma((3, 3, 6)),
            dma((3, 3, 6)),
            dma((3, 3, 6)),
            dma((3, 3, 6)),
            dma((3, 3, 6)),
            dma((4, 3)),
            dma((4, 3)),
        ],
        compiler_params=pltpu.CompilerParams(
            collective_id=0, has_side_effects=True, vmem_limit_bytes=60 * 1024 * 1024
        ),
        cost_estimate=pl.CostEstimate(flops=16 * 10**9, bytes_accessed=5 * 10**6, transcendentals=0),
    )(gradient)
    return padded[:ROWS]


def solution(mesh):
    spec = P(("wide", "narrow"), None)
    return jax.shard_map(local, mesh=mesh, in_specs=(spec,), out_specs=spec, check_vma=False)
```

```python
import math

import jax
import jax.numpy as jnp
from jax import lax
from jax.experimental import pallas as pl
from jax.experimental.pallas import tpu as pltpu
from jax.sharding import PartitionSpec as P

M = 3584
K = 18432

COEFF_A = 3.4445
COEFF_B = -4.775
COEFF_C = 2.0315

MESH = pl.DeviceIdType.MESH
BF = jnp.bfloat16
F32 = jnp.float32
NT = (((1,), (1,)), ((), ()))

ROWS = 28
PIECE = 32
THIRD = K // 3
COL1 = THIRD // 4
COL2 = COL1 // 4
COL3 = COL2 // 4
CHIP = 3 * COL3
HALF_M = M // 2
AXES = ((0, 1, 2), (1, 2, 0), (2, 0, 1))

BLK = 256
NB = M // BLK
PER_PART = (12, 6)
SECOND = 3 * PER_PART[0]
SLOTS = 3 * sum(PER_PART)
SIZES = ((1536, 384, 96), (768, 192, 48))


def al(x, m=16):
    return pl.multiple_of(x, m)


def kernel(
    in_ref, y0,
    rows_in, x0, x2, x2p, x3, s_all, st,
    ut, y2p, y2,
    ta, tb, g, r1a, r2a, r3a, r1b, r2b, r3b, sq, yf, ybf, yp, yr, zf, zp, zr,
    io_sem, in_send, in_recv, in_plane_send, in_plane_recv, core_send, core_recv,
    out_send, out_recv, out_plane_send, out_plane_recv, part_send, part_recv,
    rsa_send, rsa_recv, aga_send, aga_recv, rsb_send, rsb_recv, agb_send, agb_recv, sq_send, sq_recv,
):
    w, n_ = lax.axis_index("wide"), lax.axis_index("narrow")
    core, z_lo, y = w % 2, (w // 2) % 2, w // 4
    x, z_hi = n_ % 4, n_ // 4
    z = z_hi * 2 + z_lo
    pos = (x, y, z)

    def device(x, y, z, core):
        return ((y * 2 + z % 2) * 2 + core, (z // 2) * 4 + x)

    def shifted(axis, by):
        p = [x, y, z]
        p[axis] = (p[axis] + by) % 4
        return device(*p, core)

    right = [shifted(a, 1) for a in range(3)]
    left = [shifted(a, 3) for a in range(3)]
    across = [shifted(a, 2) for a in range(3)]
    partner = device(x, y, z, 1 - core)

    def in_plane(p, d, e):
        a, b, _ = AXES[p]
        if e == 0:
            return (right, across, left)[d - 1][a]
        if d == 0:
            return (right, across, left)[e - 1][b]
        v = [x, y, z]
        v[a] = (v[a] + d) % 4
        v[b] = (v[b] + e) % 4
        return device(*v, core)

    steps = [(d, e) for d in range(4) for e in range(4) if d or e]
    plane_devices = [[in_plane(p, d, e) for d, e in steps] for p in range(3)]
    diagonal = [plane_devices[p][k] for p in range(3) for k, (d, e) in enumerate(steps) if d and e]

    barrier = pltpu.get_barrier_semaphore()
    for d in right + left + across + diagonal + [partner]:
        pl.semaphore_signal(barrier, inc=1, device_id=d, device_id_type=MESH)

    fetch = pltpu.make_async_copy(in_ref, rows_in, io_sem.at[0])
    fetch.start()
    fetch.wait()

    def load(k, carry):
        p, q = k // 4, k % 4
        v = rows_in[:, pl.ds(al(k * COL1, COL1), COL1)]
        for e in range(4):
            x0[p, q * 4 + e, pl.ds(0, ROWS), :] = v[:, e * COL2 : (e + 1) * COL2]
            x0[p, q * 4 + e, pl.ds(ROWS, PIECE - ROWS), :] = jnp.zeros((PIECE - ROWS, COL2), BF)
        return carry

    lax.fori_loop(0, 12, load, 0)
    pl.semaphore_wait(barrier, 37)

    def remote(src, dst, send, recv, dev):
        return pltpu.make_async_remote_copy(
            src_ref=src, dst_ref=dst, send_sem=send, recv_sem=recv, device_id=dev, device_id_type=MESH
        )

    sent = []

    def flush(group):
        for c in group:
            c.wait_send()
        group.clear()

    class Exchange:
        def __init__(self, stage, axis_no, src, dst, sems):
            self.stage, self.axis_no, self.src, self.dst, self.sems = stage, axis_no, src, dst, sems
            self.copies = {}

        def begin(self, p):
            a = AXES[p][self.axis_no]
            me = pos[a]
            send, recv = self.sems
            group = []
            for k, dev in ((2, across[a]), (1, right[a]), (3, left[a])):
                c = remote(
                    self.src(p, (me + k) % 4), self.dst(p, me),
                    send.at[self.stage, p, k - 1], recv.at[self.stage, p, k - 1], dev,
                )
                c.start()
                group.append(c)
                sent.append(c)
            self.copies[p] = group

        def keep(self, p):
            me = pos[AXES[p][self.axis_no]]
            src, dst = self.src(p, me), self.dst(p, me)
            dst[...] = src[...]

        def arrive(self, p):
            for c in self.copies[p]:
                c.wait_recv()

    def spot(p, a, b):
        return b * 4 + a if p == 2 else a * 4 + b

    class PlaneExchange:
        def __init__(self, src, dst, src_spot, dst_spot, send, recv):
            self.src, self.dst, self.src_spot, self.dst_spot = src, dst, src_spot, dst_spot
            self.send, self.recv = send, recv

        def begin(self, p):
            a, b, _ = AXES[p]
            here = self.dst(p, self.dst_spot(p, pos[a], pos[b]))
            for (d, e), dev in zip(steps, plane_devices[p]):
                there = self.src_spot(p, (pos[a] + d) % 4, (pos[b] + e) % 4)
                remote(self.src.at[p, there], here, self.send.at[p], self.recv.at[p], dev).start()

        def keep(self, p):
            a, b, _ = AXES[p]
            self.dst(p, self.dst_spot(p, pos[a], pos[b]))[...] = self.src[p, self.src_spot(p, pos[a], pos[b])]

        def arrive(self, p):
            all_of = self.src.at[p, pl.ds(0, 15)]
            pltpu.make_async_copy(all_of, all_of, self.recv.at[p]).wait()

        def left(self, p):
            all_of = self.src.at[p, pl.ds(0, 15)]
            pltpu.make_async_copy(all_of, all_of, self.send.at[p]).wait()

    ins = (in_send, in_recv)
    outs = (out_send, out_recv)
    columns = lambda p, a, b: a * 4 + b
    in1 = PlaneExchange(x0, lambda p, s: x2.at[p, s], columns, spot, in_plane_send, in_plane_recv)
    in3 = Exchange(0, 2, lambda p, q: x2p.at[p, q], lambda p, q: x3.at[core, p, q], ins)
    for p in range(3):
        in1.begin(p)

    def square(k, total):
        for e in range(4):
            v = x0[k // 4, k % 4 * 4 + e].astype(F32)
            v = v * v
            v = (v[:, :128] + v[:, 128:256]) + v[:, 256:]
            total = total + ((v[:8] + v[8:16]) + (v[16:24] + v[24:]))
        return total

    for p in range(3):
        in1.keep(p)
    sq[13] = lax.fori_loop(0, 12, square, jnp.zeros((8, 128), F32))
    sq_core = remote(sq.at[13], sq.at[14], sq_send.at[3, 0], sq_recv.at[3, 0], partner)
    sq_core.start()
    sent.append(sq_core)

    def iota(shape, d):
        return lax.broadcasted_iota(jnp.int32, shape, d)

    def ones_where(cond):
        return jnp.where(cond, 1.0, 0.0).astype(BF)

    def spread_matrix(shape, wide, unit, narrow):
        s, r = iota(shape, wide), iota(shape, 1 - wide)
        return ones_where((s % unit < narrow) & (r == (s // unit) * narrow + s % unit))

    widen = spread_matrix((COL2, 512), 1, 128, COL3)
    for p in range(3):
        in1.arrive(p)
        for u in range(4):
            rows = x2[p, pl.ds(4 * u, 4)].reshape(4 * PIECE, COL2)
            rows = jnp.dot(rows, widen, preferred_element_type=F32).astype(BF)
            for q in range(4):
                x2p[p, q, u] = rows[:, q * 128 : (q + 1) * 128].reshape(4, PIECE, 128)
        in3.begin(p)
    for p in range(3):
        in3.keep(p)
    crossing = []
    for p in range(3):
        in3.arrive(p)
        here = x3.at[core, p]
        c = remote(here, here, core_send.at[p], core_recv.at[p], partner)
        c.start()
        crossing.append(c)
        sent.append(c)

    pack = spread_matrix((8 * ROWS, 8 * PIECE), 1, PIECE, ROWS)

    def pack_rows(owner):
        def body(k, carry):
            x, y0, group = k // 2, k % 2 * 2, [[], [], []]
            for y in (y0, y0 + 1):
                for z in range(4):
                    group[0].append(x3[owner, 0, z, x, y])
                    group[1].append(x3[owner, 1, x, y, z])
                    group[2].append(x3[owner, 2, y, x, z])
            rows = jnp.concatenate([jnp.concatenate(e, axis=0) for e in group], axis=1)
            at = pl.ds(al(owner * HALF_M + k * 8 * ROWS), 8 * ROWS)
            s_all[at, :] = jnp.dot(pack, rows, preferred_element_type=F32).astype(BF)
            return carry

        lax.fori_loop(0, 4, lambda k, carry: body(2 * k + 1, body(2 * k, carry)), 0)

    pack_rows(core)
    for c in crossing:
        c.wait_recv()
    pack_rows(1 - core)

    def turn_all():
        kk, ll = iota((CHIP, 384), 0), iota((CHIP, 384), 1)
        pick = ones_where((ll % 128 < COL3) & (kk == (ll // 128) * COL3 + ll % 128))

        def turn(j, carry):
            at = pl.ds(al(j * BLK, BLK), BLK)
            st[:, at] = lax.dot_general(pick, s_all[at, :], NT, preferred_element_type=F32).astype(BF)
            return carry

        lax.fori_loop(0, NB // 2, lambda k, carry: turn(2 * k + 1, turn(2 * k, carry)), 0)

    def block_of(chunk, m):
        if chunk == 0:
            i = jnp.where(m < 28, m % NB, jnp.where(m < 35, 7 * core + m - 28, 4 * core))
            d = jnp.where(m < 28, 2 * core + m // NB, jnp.where(m < 35, 5, 7))
            return i, d, jnp.where(d == 0, 0.5, 1.0)
        i = jnp.where(m < 14, m, 4 * core + jnp.minimum(m, 16) - 13)
        d = jnp.where(m < 14, 4 + 2 * core, 7)
        return i, d, jnp.where((d == 7) & ((i >= 7) | (m == 17)), 0.0, 1.0)

    def gram_block(chunk, m, t):
        i, d, scale = block_of(chunk, m)
        j = (i + d) % NB
        ri = pl.ds(al(i * BLK, BLK), BLK)
        rj = pl.ds(al(j * BLK, BLK), BLK)
        acc = lax.dot_general(s_all[ri, :], s_all[rj, :], NT, preferred_element_type=F32)
        acc = (scale * acc).astype(BF)
        t[pl.ds(al(m * 512, 512), 256), :] = acc[:, :128]
        t[pl.ds(al(m * 512 + 256, 256), 256), :] = acc[:, 128:]

    def square_begin(s):
        group = [
            remote(sq.at[4 * s], sq.at[4 * s + 1 + k], sq_send.at[s, k], sq_recv.at[s, k], dev)
            for k, dev in enumerate((right[s], left[s], across[s]))
        ]
        for c in group:
            c.start()
        sent.extend(group)
        return group

    def square_end(s, group):
        for c in group:
            c.wait_recv()
        sq[4 * s + 4] = (sq[4 * s] + sq[4 * s + 3]) + (sq[4 * s + 1] + sq[4 * s + 2])

    class Chunk:
        def __init__(self, no, t, bufs, rs, ag):
            self.no, self.t, self.bufs, self.rs, self.ag = no, t, bufs, rs, ag
            self.blocks = PER_PART[no]
            self.sizes = SIZES[no]
            self.size0 = self.sizes[0]
            base = [p * self.blocks * 512 for p in range(3)]
            self.bases = [base]
            for k in range(3):
                base = [base[p] + pos[AXES[p][k]] * self.sizes[k] for p in range(3)]
                self.bases.append(base)
            self.mine = no * SECOND * 512
            self.copies = {}

        def quarter(self, k, p, by):
            return self.bases[k][p] + ((pos[AXES[p][k]] + by) % 4) * self.sizes[k]

        def gram(self, p, start, count):
            for m in range(count):
                gram_block(self.no, p * self.blocks + start + m, self.t)

        def gram_far(self):
            for p in range(3):
                q = (pos[AXES[p][0]] + 2) % 4
                self.gram(p, self.blocks * q // 4, -(-self.blocks // 4))

        def gram_near(self):
            for p in range(3):
                me = pos[AXES[p][0]]
                if self.blocks % 4:
                    self.gram(p, self.blocks // 4 + self.blocks // 2 * (me // 2), 1)
                for by in (1, 3):
                    self.gram(p, (self.blocks * ((me + by) % 4) + 2) // 4, self.blocks // 4)

        def gram_own(self):
            for p in range(3):
                self.gram(p, (self.blocks * pos[AXES[p][0]] + 2) // 4, self.blocks // 4)

        def push(self, k, p, no, off, rows):
            a = AXES[p][k]
            c = remote(
                self.t.at[pl.ds(al(off), rows), :],
                self.bufs[k].at[p, no],
                self.rs[0].at[k, p, no],
                self.rs[1].at[k, p, no],
                right[a] if no < 3 else left[a],
            )
            c.start()
            self.copies[k, p, no] = c
            sent.append(c)

        def add_rows(self, off, rows, srcs):
            step = rows // 2 if rows > 200 else rows
            t = self.t

            def body(m, carry):
                at = pl.ds(al(off + m * step), step)
                total = t[at, :]
                for src in srcs:
                    total = total + src[pl.ds(al(m * step), step), :]
                t[at, :] = total
                return carry

            lax.fori_loop(0, rows // step, body, 0)

        def scatter_far(self, k):
            half = self.sizes[k] // 2
            for p in range(3):
                self.push(k, p, 0, self.quarter(k, p, 2), half)
                self.push(k, p, 3, self.quarter(k, p, 2) + half, half)

        def scatter_near(self, k):
            half = self.sizes[k] // 2
            for p in range(3):
                self.push(k, p, 1, self.quarter(k, p, 1) + half, half)
                self.push(k, p, 4, self.quarter(k, p, 3), half)

        def scatter_mid(self, k):
            half = self.sizes[k] // 2
            for p in range(3):
                self.copies[k, p, 0].wait_recv()
                self.add_rows(self.quarter(k, p, 1), half, [self.bufs[k].at[p, 0]])
                self.push(k, p, 2, self.quarter(k, p, 1), half)
                self.copies[k, p, 3].wait_recv()
                self.add_rows(self.quarter(k, p, 3) + half, half, [self.bufs[k].at[p, 3]])
                self.push(k, p, 5, self.quarter(k, p, 3) + half, half)

        def scatter_end(self, k):
            half = self.sizes[k] // 2
            for p in range(3):
                for h, one, two in ((0, 4, 2), (1, 1, 5)):
                    self.copies[k, p, one].wait_recv()
                    self.copies[k, p, two].wait_recv()
                    self.add_rows(
                        self.quarter(k, p, 0) + h * half, half, [self.bufs[k].at[p, one], self.bufs[k].at[p, two]]
                    )

        def ring_begin(self, s):
            size = self.sizes[s]
            for p in range(3):
                a = AXES[p][s]
                for k, dev in ((2, across[a]), (1, right[a]), (3, left[a])):
                    c = remote(
                        self.t.at[pl.ds(al(self.quarter(s, p, k)), size), :],
                        self.bufs[s].at[p, k - 1],
                        self.rs[0].at[s, p, k - 1],
                        self.rs[1].at[s, p, k - 1],
                        dev,
                    )
                    c.start()
                    self.copies[s, p, k] = c
                    sent.append(c)

        def ring_end(self, s):
            size = self.sizes[s]
            for p in range(3):
                for k in (1, 2, 3):
                    self.copies[s, p, k].wait_recv()
                off = self.bases[s + 1][p]
                step = min(size, 96)

                def body(m, carry):
                    at = pl.ds(al(off + m * step), step)
                    total = self.t[at, :].astype(F32)
                    for k in range(3):
                        total = total + self.bufs[s][p, k, pl.ds(al(m * step), step)].astype(F32)
                    if s == 2:
                        g[pl.ds(al(self.mine + off), size), :] = total.astype(BF)
                    else:
                        self.t[at, :] = total.astype(BF)
                    return carry

                lax.fori_loop(0, size // step, body, 0)
            if s == 2:
                self.rounds(2)

        def rounds(self, s):
            for p in range(3):
                a = AXES[p][s]
                off = self.bases[s + 1][p]
                for k, dev in ((2, across[a]), (1, right[a]), (3, left[a])):
                    self.spread(s, p, k - 1, off, self.sizes[s], dev)

        def rounds_end(self, s):
            for p in range(3):
                self.got(s, p, 0, 1, 2)

        def spread(self, k, p, no, off, rows, dev):
            here = g.at[pl.ds(al(self.mine + off), rows), :]
            c = remote(here, here, self.ag[0].at[k, p, no], self.ag[1].at[k, p, no], dev)
            c.start()
            self.copies["g", k, p, no] = c
            sent.append(c)

        def got(self, k, p, *nos):
            for no in nos:
                self.copies["g", k, p, no].wait_recv()

        def gather_begin(self, k):
            half = self.sizes[k] // 2
            for p in range(3):
                own = self.quarter(k, p, 0)
                a = AXES[p][k]
                self.spread(k, p, 0, own, half, right[a])
                self.spread(k, p, 1, own + half, half, left[a])
            for p in range(3):
                own = self.quarter(k, p, 0)
                a = AXES[p][k]
                self.spread(k, p, 2, own + half, half, right[a])
                self.spread(k, p, 3, own, half, left[a])

        def piece(self, i):
            rows = self.size0 // 4
            for p in range(3):
                own = self.quarter(0, p, 0)
                self.spread(0, p, i, own + i * rows, rows, right[p])
                self.spread(0, p, 4 + i, own + (i + 2) % 4 * rows, rows, left[p])

        def hand_on(self, i):
            rows = self.size0 // 4
            for p in range(3):
                self.got(0, p, i)
                self.spread(0, p, 8 + i, self.quarter(0, p, 3) + i * rows, rows, right[p])
                self.got(0, p, 4 + i)
                self.spread(0, p, 10 + i, self.quarter(0, p, 1) + (i + 2) * rows, rows, left[p])

        def pieces_end(self):
            for p in range(3):
                self.got(0, p, 2, 3, 6, 7, 8, 9, 10, 11)

        def gather_mid(self, k):
            half = self.sizes[k] // 2
            for p in range(3):
                a = AXES[p][k]
                self.got(k, p, 0)
                self.spread(k, p, 4, self.quarter(k, p, 3), half, right[a])
                self.got(k, p, 1)
                self.spread(k, p, 5, self.quarter(k, p, 1) + half, half, left[a])

        def gather_end(self, k):
            for p in range(3):
                self.got(k, p, 2, 3, 4, 5)

    one = Chunk(0, ta, (r1a, r2a, r3a), (rsa_send, rsa_recv), (aga_send, aga_recv))
    two = Chunk(1, tb, (r1b, r2b, r3b), (rsb_send, rsb_recv), (agb_send, agb_recv))

    early = list(sent)
    sent.clear()
    one.gram_far()
    one.scatter_far(0)
    one.gram_near()
    one.scatter_near(0)
    two.gram_far()
    one.gram_own()
    one.scatter_mid(0)
    two.scatter_far(0)
    two.gram_near()
    two.gram_own()
    sq_core.wait_recv()
    sq[0] = sq[13] + sq[14]
    squares = square_begin(0)
    turn_all()
    flush(early)
    for p in range(3):
        in1.left(p)
    one.scatter_end(0)
    one.ring_begin(1)
    two.scatter_near(0)
    square_end(0, squares)
    squares = square_begin(1)
    one.ring_end(1)
    one.ring_begin(2)
    two.scatter_mid(0)
    square_end(1, squares)
    squares = square_begin(2)
    one.ring_end(2)
    two.scatter_end(0)
    two.ring_begin(1)
    square_end(2, squares)
    one.rounds_end(2)
    one.rounds(1)
    two.ring_end(1)
    two.ring_begin(2)
    one.rounds_end(1)
    early.extend(sent)
    sent.clear()
    one.piece(0)
    two.ring_end(2)
    one.piece(1)
    two.rounds_end(2)
    two.rounds(1)
    one.piece(2)
    one.hand_on(0)
    two.rounds_end(1)
    one.piece(3)
    one.hand_on(1)
    two.gather_begin(0)
    flush(early)
    one.pieces_end()

    def cols(a_ref, i):
        return a_ref[:, pl.ds(al(i * BLK, BLK), BLK)]

    def block(slot):
        o = slot * 512
        return jnp.concatenate([g[pl.ds(al(o, 512), 256), :], g[pl.ds(al(o + 256, 256), 256), :]], axis=1)

    def band(a_ref, j, ds):
        def straight(d, first):
            i = (j + NB - d) % NB
            return cols(a_ref, i), block(first + i)

        def turned(d, first):
            return cols(a_ref, (j + d) % NB), block(first + j)

        a, b = zip(*[straight(*e) for e in ds])
        acc = jnp.dot(jnp.concatenate(a, axis=1), jnp.concatenate(b, axis=0), preferred_element_type=F32)
        a, b = zip(*[turned(*e) for e in ds])
        return acc + lax.dot_general(
            jnp.concatenate(a, axis=1), jnp.concatenate(b, axis=1), NT, preferred_element_type=F32
        )

    whole_one = ((2 * core, 0), (2 * core + 1, NB))
    whole_two = ((2 * core + 4, SECOND),)

    def single(acc_ref, a_ref, chunk, m):
        i, d, _ = block_of(chunk, m)
        j = (i + d) % NB
        b = block(chunk * SECOND + m)
        acc_ref[:, pl.ds(al(j * BLK, BLK), BLK)] += jnp.dot(cols(a_ref, i), b, preferred_element_type=F32)
        acc_ref[:, pl.ds(al(i * BLK, BLK), BLK)] += lax.dot_general(
            cols(a_ref, j), b, NT, preferred_element_type=F32
        )

    def loop(first_k, last_k, f):
        def body(k, carry):
            f(first_k + 2 * k)
            f(first_k + 2 * k + 1)
            return carry

        lax.fori_loop(0, (last_k - first_k) // 2, body, 0)
        if (last_k - first_k) % 2:
            f(last_k - 1)

    def band_at(j):
        return pl.ds(al(j * BLK, BLK), BLK)

    def to_partner(no, src, dst):
        c = remote(src, dst, part_send.at[no], part_recv.at[no], partner)
        c.start()
        sent.append(c)
        return c

    def y_one(j):
        yf[:, band_at(j)] = band(st, j, whole_one)

    def shared(acc_ref, a_ref):
        return lambda m: single(acc_ref, a_ref, 0, 28 + m), lambda m: single(acc_ref, a_ref, 1, 14 + m)

    y_first, y_rest = shared(yf, st)
    loop(0, 6, y_one)
    two.gather_mid(0)
    loop(6, NB, y_one)
    zf[...] = jnp.zeros((CHIP, M), F32)
    loop(0, 8, y_first)
    two.gather_end(0)
    loop(0, 3, y_rest)

    def y_two(j):
        v = yf[:, band_at(j)] + band(st, j, whole_two)
        yf[:, band_at(j)] = v
        yp[:, band_at(j)] = v.astype(BF)

    shares = []
    for h in range(2):
        loop(h * 7, h * 7 + 7, y_two)
        here = pl.ds(h * HALF_M, HALF_M)
        shares.append(to_partner(h, yp.at[:, here], yr.at[:, here]))

    factor = 0.3 * math.sqrt(M) / (jnp.sqrt(jnp.sum(sq[12], axis=(0, 1), keepdims=True)) + 1e-07)
    factor2 = factor * factor

    def y_sum(j):
        v = factor2 * (yf[:, band_at(j)] + yr[:, band_at(j)].astype(F32))
        yf[:, band_at(j)] = v
        ybf[:, band_at(j)] = v.astype(BF)

    for h in range(2):
        shares[h].wait_recv()
        loop(h * 7, h * 7 + 7, y_sum)

    z_first, z_rest = shared(zf, ybf)
    loop(0, 8, z_first)
    loop(0, 3, z_rest)

    def z_band(j):
        return factor2 * (zf[:, band_at(j)] + band(ybf, j, whole_one + whole_two))

    def z_theirs(k):
        zp[:, band_at(k)] = z_band((1 - core) * 7 + k).astype(BF)

    loop(0, 7, z_theirs)
    share = to_partner(2, zp, zr)

    def z_mine(k):
        zf[:, band_at(core * 7 + k)] = z_band(core * 7 + k)

    loop(0, 7, z_mine)
    share.wait_recv()
    for p in range(3):
        ut[pl.ds(p * 128 + COL3, 128 - COL3), :] = jnp.zeros((128 - COL3, HALF_M), BF)

    def finish(k):
        at = band_at(core * 7 + k)
        scaled = (factor * st[:, at].astype(F32)).astype(BF).astype(F32)
        product = factor * (COEFF_B * yf[:, at] + COEFF_C * (zf[:, at] + zr[:, band_at(k)].astype(F32)))
        u = (math.sqrt(K) * (COEFF_A * scaled + product)).astype(BF)
        for p in range(3):
            ut[pl.ds(p * 128, COL3), band_at(k)] = u[p * COL3 : (p + 1) * COL3]

    loop(0, 7, finish)

    early.extend(sent)
    sent.clear()
    y3 = x2p
    unpack = spread_matrix((8 * PIECE, 8 * ROWS), 0, PIECE, ROWS)
    for m in range(8):
        o = m * 8 * ROWS
        first_lane = o // 128 * 128
        skip = o - first_lane
        width = -(-(skip + 8 * ROWS) // 128) * 128
        v = ut[:, pl.ds(first_lane, width)][:, skip : skip + 8 * ROWS]
        rows = lax.dot_general(unpack, v, NT, preferred_element_type=F32).astype(BF)
        for r in range(8):
            x, y, z = m // 2, m % 2 * 2 + r // 4, r % 4
            for p, at in enumerate(((z, x, y), (x, y, z), (y, x, z))):
                y3[(p,) + at] = rows[r * PIECE : (r + 1) * PIECE, p * 128 : (p + 1) * 128]

    out1 = Exchange(0, 2, lambda p, q: y3.at[p, q], lambda p, q: y2p.at[p, q], outs)
    out2 = PlaneExchange(
        y2, lambda p, s: y0.at[:, pl.ds(al(p * THIRD + s * COL2, 128), COL2)], spot, columns, out_plane_send, out_plane_recv,
    )
    for p in range(3):
        out1.begin(p)
    for p in range(3):
        out1.keep(p)
    flush(early)
    early.extend(sent)
    sent.clear()
    narrow = spread_matrix((512, COL2), 0, 128, COL3)
    for p in range(3):
        out1.arrive(p)
        for u in range(4):
            rows = [y2p[p, q, u].reshape(4 * PIECE, 128) for q in range(4)]
            rows = jnp.dot(jnp.concatenate(rows, axis=1), narrow, preferred_element_type=F32)
            y2[p, pl.ds(4 * u, 4)] = rows.astype(BF).reshape(4, PIECE, COL2)
        out2.begin(p)
    own = []
    for p in range(3):
        a, b, _ = AXES[p]
        at = (pos[a], pos[b])
        own.append(pltpu.make_async_copy(y2.at[p, spot(p, *at)], out2.dst(p, columns(p, *at)), io_sem.at[1 + p]))
        own[p].start()
    flush(early)
    for p in range(3):
        out2.arrive(p)
        own[p].wait()
    for p in range(3):
        out2.left(p)
    flush(sent)


def local(gradient):
    dma = pltpu.SemaphoreType.DMA
    hbm = pl.BlockSpec(memory_space=pl.ANY)
    padded = pl.pallas_call(
        kernel,
        out_shape=jax.ShapeDtypeStruct((PIECE, K), BF),
        in_specs=[hbm],
        out_specs=hbm,
        scratch_shapes=[
            pltpu.VMEM((ROWS, K), BF),
            pltpu.VMEM((3, 16, PIECE, COL2), BF),
            pltpu.VMEM((3, 16, PIECE, COL2), BF),
            pltpu.VMEM((3, 4, 4, 4, PIECE, 128), BF),
            pltpu.VMEM((2, 3, 4, 4, 4, PIECE, 128), BF),
            pltpu.VMEM((M, 384), BF),
            pltpu.VMEM((CHIP, M), BF),
            pltpu.VMEM((384, HALF_M), BF),
            pltpu.VMEM((3, 4, 4, 4, PIECE, 128), BF),
            pltpu.VMEM((3, 16, PIECE, COL2), BF),
            pltpu.VMEM((3 * 12 * 512, 128), BF),
            pltpu.VMEM((3 * 6 * 512, 128), BF),
            pltpu.VMEM((SLOTS * 512, 128), BF),
            pltpu.VMEM((3, 6, 768, 128), BF),
            pltpu.VMEM((3, 3, 384, 128), BF),
            pltpu.VMEM((3, 3, 96, 128), BF),
            pltpu.VMEM((3, 6, 384, 128), BF),
            pltpu.VMEM((3, 3, 192, 128), BF),
            pltpu.VMEM((3, 3, 48, 128), BF),
            pltpu.VMEM((15, 8, 128), F32),
            pltpu.VMEM((CHIP, M), F32),
            pltpu.VMEM((CHIP, M), BF),
            pltpu.VMEM((CHIP, M), BF),
            pltpu.VMEM((CHIP, M), BF),
            pltpu.VMEM((CHIP, M), F32),
            pltpu.VMEM((CHIP, HALF_M), BF),
            pltpu.VMEM((CHIP, HALF_M), BF),
            dma((4,)),
            dma((1, 3, 3)),
            dma((1, 3, 3)),
            dma((3,)),
            dma((3,)),
            dma((3,)),
            dma((3,)),
            dma((1, 3, 3)),
            dma((1, 3, 3)),
            dma((3,)),
            dma((3,)),
            dma((3,)),
            dma((3,)),
            dma((3, 3, 6)),
            dma((3, 3, 6)),
            dma((3, 3, 12)),
            dma((3, 3, 12)),
            dma((3, 3, 6)),
            dma((3, 3, 6)),
            dma((3, 3, 6)),
            dma((3, 3, 6)),
            dma((4, 3)),
            dma((4, 3)),
        ],
        compiler_params=pltpu.CompilerParams(
            collective_id=0, has_side_effects=True, vmem_limit_bytes=60 * 1024 * 1024
        ),
        cost_estimate=pl.CostEstimate(flops=16 * 10**9, bytes_accessed=5 * 10**6, transcendentals=0),
    )(gradient)
    return padded[:ROWS]


def solution(mesh):
    spec = P(("wide", "narrow"), None)
    return jax.shard_map(local, mesh=mesh, in_specs=(spec,), out_specs=spec, check_vma=False)
```

```python
import math

import jax
import jax.numpy as jnp
from jax import lax
from jax.experimental import pallas as pl
from jax.experimental.pallas import tpu as pltpu
from jax.sharding import PartitionSpec as P

M = 3584
K = 18432

COEFF_A = 3.4445
COEFF_B = -4.775
COEFF_C = 2.0315

MESH = pl.DeviceIdType.MESH
BF = jnp.bfloat16
F32 = jnp.float32
NT = (((1,), (1,)), ((), ()))

ROWS = 28
PIECE = 32
THIRD = K // 3
COL1 = THIRD // 4
COL2 = COL1 // 4
COL3 = COL2 // 4
CHIP = 3 * COL3
HALF_M = M // 2
AXES = ((0, 1, 2), (1, 2, 0), (2, 0, 1))

BLK = 256
NB = M // BLK
PER_PART = (12, 6)
SECOND = 3 * PER_PART[0]
SLOTS = 3 * sum(PER_PART)
SIZES = ((1536, 384, 96), (768, 192, 48))


def al(x, m=16):
    return pl.multiple_of(x, m)


def kernel(
    in_ref, y0,
    rows_in, x0, x2, x2p, x3, s_all, st,
    ut, y2p, y2,
    ta, tb, g, r1a, r2a, r3a, r1b, r2b, r3b, sq, yf, ybf, yp, yr, zf, zp, zr,
    io_sem, in_send, in_recv, in_plane_send, in_plane_recv, core_send, core_recv,
    out_send, out_recv, out_plane_send, out_plane_recv, part_send, part_recv,
    rsa_send, rsa_recv, aga_send, aga_recv, rsb_send, rsb_recv, agb_send, agb_recv, sq_send, sq_recv,
):
    w, n_ = lax.axis_index("wide"), lax.axis_index("narrow")
    core, z_lo, y = w % 2, (w // 2) % 2, w // 4
    x, z_hi = n_ % 4, n_ // 4
    z = z_hi * 2 + z_lo
    pos = (x, y, z)

    def device(x, y, z, core):
        return ((y * 2 + z % 2) * 2 + core, (z // 2) * 4 + x)

    def shifted(axis, by):
        p = [x, y, z]
        p[axis] = (p[axis] + by) % 4
        return device(*p, core)

    right = [shifted(a, 1) for a in range(3)]
    left = [shifted(a, 3) for a in range(3)]
    across = [shifted(a, 2) for a in range(3)]
    partner = device(x, y, z, 1 - core)

    def in_plane(p, d, e):
        a, b, _ = AXES[p]
        if e == 0:
            return (right, across, left)[d - 1][a]
        if d == 0:
            return (right, across, left)[e - 1][b]
        v = [x, y, z]
        v[a] = (v[a] + d) % 4
        v[b] = (v[b] + e) % 4
        return device(*v, core)

    steps = [(d, e) for d in range(4) for e in range(4) if d or e]
    plane_devices = [[in_plane(p, d, e) for d, e in steps] for p in range(3)]
    diagonal = [plane_devices[p][k] for p in range(3) for k, (d, e) in enumerate(steps) if d and e]

    barrier = pltpu.get_barrier_semaphore()
    for d in right + left + across + diagonal + [partner]:
        pl.semaphore_signal(barrier, inc=1, device_id=d, device_id_type=MESH)

    fetch = pltpu.make_async_copy(in_ref, rows_in, io_sem.at[0])
    fetch.start()
    fetch.wait()

    def load(k, carry):
        p, q = k // 4, k % 4
        v = rows_in[:, pl.ds(al(k * COL1, COL1), COL1)]
        for e in range(4):
            x0[p, q * 4 + e, pl.ds(0, ROWS), :] = v[:, e * COL2 : (e + 1) * COL2]
            x0[p, q * 4 + e, pl.ds(ROWS, PIECE - ROWS), :] = jnp.zeros((PIECE - ROWS, COL2), BF)
        return carry

    lax.fori_loop(0, 12, load, 0)
    pl.semaphore_wait(barrier, 37)

    def remote(src, dst, send, recv, dev):
        return pltpu.make_async_remote_copy(
            src_ref=src, dst_ref=dst, send_sem=send, recv_sem=recv, device_id=dev, device_id_type=MESH
        )

    sent = []

    def flush(group):
        for c in group:
            c.wait_send()
        group.clear()

    class Exchange:
        def __init__(self, stage, axis_no, src, dst, sems):
            self.stage, self.axis_no, self.src, self.dst, self.sems = stage, axis_no, src, dst, sems
            self.copies = {}

        def begin(self, p):
            a = AXES[p][self.axis_no]
            me = pos[a]
            send, recv = self.sems
            group = []
            for k, dev in ((2, across[a]), (1, right[a]), (3, left[a])):
                c = remote(
                    self.src(p, (me + k) % 4), self.dst(p, me),
                    send.at[self.stage, p, k - 1], recv.at[self.stage, p, k - 1], dev,
                )
                c.start()
                group.append(c)
                sent.append(c)
            self.copies[p] = group

        def keep(self, p):
            me = pos[AXES[p][self.axis_no]]
            src, dst = self.src(p, me), self.dst(p, me)
            dst[...] = src[...]

        def arrive(self, p):
            for c in self.copies[p]:
                c.wait_recv()

    def spot(p, a, b):
        return b * 4 + a if p == 2 else a * 4 + b

    class PlaneExchange:
        def __init__(self, src, dst, src_spot, dst_spot, send, recv):
            self.src, self.dst, self.src_spot, self.dst_spot = src, dst, src_spot, dst_spot
            self.send, self.recv = send, recv

        def start(self, p, k):
            a, b, _ = AXES[p]
            d, e = steps[k]
            here = self.dst(p, self.dst_spot(p, pos[a], pos[b]))
            there = self.src_spot(p, (pos[a] + d) % 4, (pos[b] + e) % 4)
            remote(self.src.at[p, there], here, self.send.at[p], self.recv.at[p], plane_devices[p][k]).start()

        def begin(self, p):
            for k in range(15):
                self.start(p, k)

        def keep(self, p):
            a, b, _ = AXES[p]
            self.dst(p, self.dst_spot(p, pos[a], pos[b]))[...] = self.src[p, self.src_spot(p, pos[a], pos[b])]

        def arrive(self, p):
            all_of = self.src.at[p, pl.ds(0, 15)]
            pltpu.make_async_copy(all_of, all_of, self.recv.at[p]).wait()

        def left(self, p):
            all_of = self.src.at[p, pl.ds(0, 15)]
            pltpu.make_async_copy(all_of, all_of, self.send.at[p]).wait()

    ins = (in_send, in_recv)
    outs = (out_send, out_recv)
    columns = lambda p, a, b: a * 4 + b
    in1 = PlaneExchange(x0, lambda p, s: x2.at[p, s], columns, spot, in_plane_send, in_plane_recv)
    in3 = Exchange(0, 2, lambda p, q: x2p.at[p, q], lambda p, q: x3.at[core, p, q], ins)
    for k in range(15):
        for p in range(3):
            in1.start(p, k)

    def square(k, total):
        for e in range(4):
            v = x0[k // 4, k % 4 * 4 + e].astype(F32)
            v = v * v
            v = (v[:, :128] + v[:, 128:256]) + v[:, 256:]
            total = total + ((v[:8] + v[8:16]) + (v[16:24] + v[24:]))
        return total

    for p in range(3):
        in1.keep(p)
    sq[13] = lax.fori_loop(0, 12, square, jnp.zeros((8, 128), F32))
    sq_core = remote(sq.at[13], sq.at[14], sq_send.at[3, 0], sq_recv.at[3, 0], partner)
    sq_core.start()
    sent.append(sq_core)

    def iota(shape, d):
        return lax.broadcasted_iota(jnp.int32, shape, d)

    def ones_where(cond):
        return jnp.where(cond, 1.0, 0.0).astype(BF)

    def spread_matrix(shape, wide, unit, narrow):
        s, r = iota(shape, wide), iota(shape, 1 - wide)
        return ones_where((s % unit < narrow) & (r == (s // unit) * narrow + s % unit))

    widen = spread_matrix((COL2, 512), 1, 128, COL3)
    for p in range(3):
        in1.arrive(p)
        for u in range(4):
            rows = x2[p, pl.ds(4 * u, 4)].reshape(4 * PIECE, COL2)
            rows = jnp.dot(rows, widen, preferred_element_type=F32).astype(BF)
            for q in range(4):
                x2p[p, q, u] = rows[:, q * 128 : (q + 1) * 128].reshape(4, PIECE, 128)
        in3.begin(p)
    for p in range(3):
        in3.keep(p)
    crossing = []
    for p in range(3):
        in3.arrive(p)
        here = x3.at[core, p]
        c = remote(here, here, core_send.at[p], core_recv.at[p], partner)
        c.start()
        crossing.append(c)
        sent.append(c)

    pack = spread_matrix((8 * ROWS, 8 * PIECE), 1, PIECE, ROWS)

    def pack_rows(owner):
        def body(k, carry):
            x, y0, group = k // 2, k % 2 * 2, [[], [], []]
            for y in (y0, y0 + 1):
                for z in range(4):
                    group[0].append(x3[owner, 0, z, x, y])
                    group[1].append(x3[owner, 1, x, y, z])
                    group[2].append(x3[owner, 2, y, x, z])
            rows = jnp.concatenate([jnp.concatenate(e, axis=0) for e in group], axis=1)
            at = pl.ds(al(owner * HALF_M + k * 8 * ROWS), 8 * ROWS)
            s_all[at, :] = jnp.dot(pack, rows, preferred_element_type=F32).astype(BF)
            return carry

        lax.fori_loop(0, 4, lambda k, carry: body(2 * k + 1, body(2 * k, carry)), 0)

    pack_rows(core)
    for c in crossing:
        c.wait_recv()
    pack_rows(1 - core)

    def turn_all():
        kk, ll = iota((CHIP, 384), 0), iota((CHIP, 384), 1)
        pick = ones_where((ll % 128 < COL3) & (kk == (ll // 128) * COL3 + ll % 128))

        def turn(j, carry):
            at = pl.ds(al(j * BLK, BLK), BLK)
            st[:, at] = lax.dot_general(pick, s_all[at, :], NT, preferred_element_type=F32).astype(BF)
            return carry

        lax.fori_loop(0, NB // 2, lambda k, carry: turn(2 * k + 1, turn(2 * k, carry)), 0)

    def block_of(chunk, m):
        if chunk == 0:
            i = jnp.where(m < 28, m % NB, jnp.where(m < 35, 7 * core + m - 28, 4 * core))
            d = jnp.where(m < 28, 2 * core + m // NB, jnp.where(m < 35, 5, 7))
            return i, d, jnp.where(d == 0, 0.5, 1.0)
        i = jnp.where(m < 14, m, 4 * core + jnp.minimum(m, 16) - 13)
        d = jnp.where(m < 14, 4 + 2 * core, 7)
        return i, d, jnp.where((d == 7) & ((i >= 7) | (m == 17)), 0.0, 1.0)

    def gram_block(chunk, m, t):
        i, d, scale = block_of(chunk, m)
        j = (i + d) % NB
        ri = pl.ds(al(i * BLK, BLK), BLK)
        rj = pl.ds(al(j * BLK, BLK), BLK)
        acc = lax.dot_general(s_all[ri, :], s_all[rj, :], NT, preferred_element_type=F32)
        acc = (scale * acc).astype(BF)
        t[pl.ds(al(m * 512, 512), 256), :] = acc[:, :128]
        t[pl.ds(al(m * 512 + 256, 256), 256), :] = acc[:, 128:]

    def square_begin(s):
        group = [
            remote(sq.at[4 * s], sq.at[4 * s + 1 + k], sq_send.at[s, k], sq_recv.at[s, k], dev)
            for k, dev in enumerate((right[s], left[s], across[s]))
        ]
        for c in group:
            c.start()
        sent.extend(group)
        return group

    def square_end(s, group):
        for c in group:
            c.wait_recv()
        sq[4 * s + 4] = (sq[4 * s] + sq[4 * s + 3]) + (sq[4 * s + 1] + sq[4 * s + 2])

    class Chunk:
        def __init__(self, no, t, bufs, rs, ag):
            self.no, self.t, self.bufs, self.rs, self.ag = no, t, bufs, rs, ag
            self.blocks = PER_PART[no]
            self.sizes = SIZES[no]
            base = [p * self.blocks * 512 for p in range(3)]
            self.bases = [base]
            for k in range(3):
                base = [base[p] + pos[AXES[p][k]] * self.sizes[k] for p in range(3)]
                self.bases.append(base)
            self.mine = no * SECOND * 512
            self.copies = {}

        def quarter(self, k, p, by):
            return self.bases[k][p] + ((pos[AXES[p][k]] + by) % 4) * self.sizes[k]

        def gram(self, p, start, count):
            for m in range(count):
                gram_block(self.no, p * self.blocks + start + m, self.t)

        def gram_far(self):
            for p in range(3):
                q = (pos[AXES[p][0]] + 2) % 4
                self.gram(p, self.blocks * q // 4, -(-self.blocks // 4))

        def gram_near(self):
            for p in range(3):
                me = pos[AXES[p][0]]
                if self.blocks % 4:
                    self.gram(p, self.blocks // 4 + self.blocks // 2 * (me // 2), 1)
                for by in (1, 3):
                    self.gram(p, (self.blocks * ((me + by) % 4) + 2) // 4, self.blocks // 4)

        def gram_own(self):
            for p in range(3):
                self.gram(p, (self.blocks * pos[AXES[p][0]] + 2) // 4, self.blocks // 4)

        def push(self, k, p, no, off, rows):
            a = AXES[p][k]
            c = remote(
                self.t.at[pl.ds(al(off), rows), :],
                self.bufs[k].at[p, no],
                self.rs[0].at[k, p, no],
                self.rs[1].at[k, p, no],
                right[a] if no < 3 else left[a],
            )
            c.start()
            self.copies[k, p, no] = c
            sent.append(c)

        def add_rows(self, off, rows, srcs):
            step = rows // 2 if rows > 200 else rows
            t = self.t

            def body(m, carry):
                at = pl.ds(al(off + m * step), step)
                total = t[at, :]
                for src in srcs:
                    total = total + src[pl.ds(al(m * step), step), :]
                t[at, :] = total
                return carry

            lax.fori_loop(0, rows // step, body, 0)

        def scatter_far(self, k):
            half = self.sizes[k] // 2
            for p in range(3):
                self.push(k, p, 0, self.quarter(k, p, 2), half)
                self.push(k, p, 3, self.quarter(k, p, 2) + half, half)

        def scatter_near(self, k):
            half = self.sizes[k] // 2
            for p in range(3):
                self.push(k, p, 1, self.quarter(k, p, 1) + half, half)
                self.push(k, p, 4, self.quarter(k, p, 3), half)

        def scatter_mid(self, k):
            half = self.sizes[k] // 2
            for p in range(3):
                self.copies[k, p, 0].wait_recv()
                self.add_rows(self.quarter(k, p, 1), half, [self.bufs[k].at[p, 0]])
                self.push(k, p, 2, self.quarter(k, p, 1), half)
                self.copies[k, p, 3].wait_recv()
                self.add_rows(self.quarter(k, p, 3) + half, half, [self.bufs[k].at[p, 3]])
                self.push(k, p, 5, self.quarter(k, p, 3) + half, half)

        def scatter_end(self, k):
            half = self.sizes[k] // 2
            for p in range(3):
                for h, one, two in ((0, 4, 2), (1, 1, 5)):
                    self.copies[k, p, one].wait_recv()
                    self.copies[k, p, two].wait_recv()
                    self.add_rows(
                        self.quarter(k, p, 0) + h * half, half, [self.bufs[k].at[p, one], self.bufs[k].at[p, two]]
                    )

        def ring_begin(self, s):
            size = self.sizes[s]
            for k, dev in ((2, across), (1, right), (3, left)):
                for p in range(3):
                    c = remote(
                        self.t.at[pl.ds(al(self.quarter(s, p, k)), size), :],
                        self.bufs[s].at[p, k - 1],
                        self.rs[0].at[s, p, k - 1],
                        self.rs[1].at[s, p, k - 1],
                        dev[AXES[p][s]],
                    )
                    c.start()
                    self.copies[s, p, k] = c
                    sent.append(c)

        def ring_end(self, s):
            size = self.sizes[s]
            for p in range(3):
                for k in (1, 2, 3):
                    self.copies[s, p, k].wait_recv()
                off = self.bases[s + 1][p]
                step = min(size, 96)

                def body(m, carry):
                    at = pl.ds(al(off + m * step), step)
                    total = self.t[at, :].astype(F32)
                    for k in range(3):
                        total = total + self.bufs[s][p, k, pl.ds(al(m * step), step)].astype(F32)
                    if s == 2:
                        g[pl.ds(al(self.mine + off), size), :] = total.astype(BF)
                    else:
                        self.t[at, :] = total.astype(BF)
                    return carry

                lax.fori_loop(0, size // step, body, 0)
            if s == 2:
                self.rounds(2)

        def rounds(self, s):
            for k, dev in ((2, across), (1, right), (3, left)):
                for p in range(3):
                    self.spread(s, p, k - 1, self.bases[s + 1][p], self.sizes[s], dev[AXES[p][s]])

        def rounds_end(self, s):
            for p in range(3):
                self.got(s, p, 0, 1, 2)

        def spread(self, k, p, no, off, rows, dev):
            here = g.at[pl.ds(al(self.mine + off), rows), :]
            c = remote(here, here, self.ag[0].at[k, p, no], self.ag[1].at[k, p, no], dev)
            c.start()
            self.copies["g", k, p, no] = c
            sent.append(c)

        def got(self, k, p, *nos):
            for no in nos:
                self.copies["g", k, p, no].wait_recv()

        def gather_begin(self, k):
            half = self.sizes[k] // 2
            for p in range(3):
                own = self.quarter(k, p, 0)
                a = AXES[p][k]
                self.spread(k, p, 0, own, half, right[a])
                self.spread(k, p, 1, own + half, half, left[a])
            for p in range(3):
                own = self.quarter(k, p, 0)
                a = AXES[p][k]
                self.spread(k, p, 2, own + half, half, right[a])
                self.spread(k, p, 3, own, half, left[a])

        def gather_mid(self, k):
            half = self.sizes[k] // 2
            for p in range(3):
                a = AXES[p][k]
                self.got(k, p, 0)
                self.spread(k, p, 4, self.quarter(k, p, 3), half, right[a])
                self.got(k, p, 1)
                self.spread(k, p, 5, self.quarter(k, p, 1) + half, half, left[a])

        def gather_end(self, k):
            for p in range(3):
                self.got(k, p, 2, 3, 4, 5)

    one = Chunk(0, ta, (r1a, r2a, r3a), (rsa_send, rsa_recv), (aga_send, aga_recv))
    two = Chunk(1, tb, (r1b, r2b, r3b), (rsb_send, rsb_recv), (agb_send, agb_recv))

    early = list(sent)
    sent.clear()
    one.gram_far()
    one.scatter_far(0)
    one.gram_near()
    one.scatter_near(0)
    two.gram_far()
    one.gram_own()
    one.scatter_mid(0)
    two.scatter_far(0)
    two.gram_near()
    two.scatter_near(0)
    two.gram_own()
    sq_core.wait_recv()
    sq[0] = sq[13] + sq[14]
    squares = square_begin(0)
    turn_all()
    flush(early)
    for p in range(3):
        in1.left(p)
    one.scatter_end(0)
    one.ring_begin(1)
    square_end(0, squares)
    squares = square_begin(1)
    two.scatter_mid(0)
    one.ring_end(1)
    one.ring_begin(2)
    square_end(1, squares)
    squares = square_begin(2)
    two.scatter_end(0)
    two.ring_begin(1)
    one.ring_end(2)
    square_end(2, squares)
    two.ring_end(1)
    two.ring_begin(2)
    one.rounds_end(2)
    one.rounds(1)
    two.ring_end(2)
    one.rounds_end(1)
    early.extend(sent)
    sent.clear()
    one.gather_begin(0)
    two.rounds_end(2)
    two.rounds(1)
    one.gather_mid(0)
    two.rounds_end(1)
    two.gather_begin(0)
    flush(early)
    one.gather_end(0)

    def cols(a_ref, i):
        return a_ref[:, pl.ds(al(i * BLK, BLK), BLK)]

    def block(slot):
        o = slot * 512
        return jnp.concatenate([g[pl.ds(al(o, 512), 256), :], g[pl.ds(al(o + 256, 256), 256), :]], axis=1)

    def band(a_ref, j, ds):
        def straight(d, first):
            i = (j + NB - d) % NB
            return cols(a_ref, i), block(first + i)

        def turned(d, first):
            return cols(a_ref, (j + d) % NB), block(first + j)

        a, b = zip(*[straight(*e) for e in ds])
        acc = jnp.dot(jnp.concatenate(a, axis=1), jnp.concatenate(b, axis=0), preferred_element_type=F32)
        a, b = zip(*[turned(*e) for e in ds])
        return acc + lax.dot_general(
            jnp.concatenate(a, axis=1), jnp.concatenate(b, axis=1), NT, preferred_element_type=F32
        )

    whole_one = ((2 * core, 0), (2 * core + 1, NB))
    whole_two = ((2 * core + 4, SECOND),)

    def single(acc_ref, a_ref, chunk, m):
        i, d, _ = block_of(chunk, m)
        j = (i + d) % NB
        b = block(chunk * SECOND + m)
        acc_ref[:, pl.ds(al(j * BLK, BLK), BLK)] += jnp.dot(cols(a_ref, i), b, preferred_element_type=F32)
        acc_ref[:, pl.ds(al(i * BLK, BLK), BLK)] += lax.dot_general(
            cols(a_ref, j), b, NT, preferred_element_type=F32
        )

    def loop(first_k, last_k, f):
        def body(k, carry):
            f(first_k + 2 * k)
            f(first_k + 2 * k + 1)
            return carry

        lax.fori_loop(0, (last_k - first_k) // 2, body, 0)
        if (last_k - first_k) % 2:
            f(last_k - 1)

    def band_at(j):
        return pl.ds(al(j * BLK, BLK), BLK)

    def to_partner(no, src, dst):
        c = remote(src, dst, part_send.at[no], part_recv.at[no], partner)
        c.start()
        sent.append(c)
        return c

    def y_one(j):
        yf[:, band_at(j)] = band(st, j, whole_one)

    def shared(acc_ref, a_ref):
        return lambda m: single(acc_ref, a_ref, 0, 28 + m), lambda m: single(acc_ref, a_ref, 1, 14 + m)

    y_first, y_rest = shared(yf, st)
    loop(0, 6, y_one)
    two.gather_mid(0)
    loop(6, NB, y_one)
    zf[...] = jnp.zeros((CHIP, M), F32)
    loop(0, 8, y_first)
    two.gather_end(0)
    loop(0, 3, y_rest)

    def y_two(j):
        v = yf[:, band_at(j)] + band(st, j, whole_two)
        yf[:, band_at(j)] = v
        yp[:, band_at(j)] = v.astype(BF)

    shares = []
    for lo, hi in ((0, 4), (4, 8), (8, 12), (12, 14)):
        loop(lo, hi, y_two)
        here = pl.ds(lo * BLK, (hi - lo) * BLK)
        shares.append((lo, hi, to_partner(len(shares), yp.at[:, here], yr.at[:, here])))

    factor = 0.3 * math.sqrt(M) / (jnp.sqrt(jnp.sum(sq[12], axis=(0, 1), keepdims=True)) + 1e-07)
    factor2 = factor * factor

    def y_sum(j):
        v = factor2 * (yf[:, band_at(j)] + yr[:, band_at(j)].astype(F32))
        yf[:, band_at(j)] = v
        ybf[:, band_at(j)] = v.astype(BF)

    for lo, hi, arriving in shares:
        arriving.wait_recv()
        loop(lo, hi, y_sum)

    z_first, z_rest = shared(zf, ybf)
    loop(0, 8, z_first)
    loop(0, 3, z_rest)

    def z_band(j):
        return factor2 * (zf[:, band_at(j)] + band(ybf, j, whole_one + whole_two))

    def z_theirs(k):
        zp[:, band_at(k)] = z_band((1 - core) * 7 + k).astype(BF)

    loop(0, 7, z_theirs)
    share = to_partner(4, zp, zr)

    def z_mine(k):
        zf[:, band_at(core * 7 + k)] = z_band(core * 7 + k)

    loop(0, 7, z_mine)
    share.wait_recv()
    for p in range(3):
        ut[pl.ds(p * 128 + COL3, 128 - COL3), :] = jnp.zeros((128 - COL3, HALF_M), BF)

    def finish(k):
        at = band_at(core * 7 + k)
        scaled = (factor * st[:, at].astype(F32)).astype(BF).astype(F32)
        product = factor * (COEFF_B * yf[:, at] + COEFF_C * (zf[:, at] + zr[:, band_at(k)].astype(F32)))
        u = (math.sqrt(K) * (COEFF_A * scaled + product)).astype(BF)
        for p in range(3):
            ut[pl.ds(p * 128, COL3), band_at(k)] = u[p * COL3 : (p + 1) * COL3]

    loop(0, 7, finish)

    early.extend(sent)
    sent.clear()
    y3 = x2p
    unpack = spread_matrix((8 * PIECE, 8 * ROWS), 0, PIECE, ROWS)
    for m in range(8):
        o = m * 8 * ROWS
        first_lane = o // 128 * 128
        skip = o - first_lane
        width = -(-(skip + 8 * ROWS) // 128) * 128
        v = ut[:, pl.ds(first_lane, width)][:, skip : skip + 8 * ROWS]
        rows = lax.dot_general(unpack, v, NT, preferred_element_type=F32).astype(BF)
        for r in range(8):
            x, y, z = m // 2, m % 2 * 2 + r // 4, r % 4
            for p, at in enumerate(((z, x, y), (x, y, z), (y, x, z))):
                y3[(p,) + at] = rows[r * PIECE : (r + 1) * PIECE, p * 128 : (p + 1) * 128]

    out1 = Exchange(0, 2, lambda p, q: y3.at[p, q], lambda p, q: y2p.at[p, q], outs)
    out2 = PlaneExchange(
        y2, lambda p, s: y0.at[:, pl.ds(al(p * THIRD + s * COL2, 128), COL2)], spot, columns, out_plane_send, out_plane_recv,
    )
    for p in range(3):
        out1.begin(p)
    for p in range(3):
        out1.keep(p)
    flush(early)
    early.extend(sent)
    sent.clear()
    narrow = spread_matrix((512, COL2), 0, 128, COL3)
    for p in range(3):
        out1.arrive(p)
        for u in range(4):
            rows = [y2p[p, q, u].reshape(4 * PIECE, 128) for q in range(4)]
            rows = jnp.dot(jnp.concatenate(rows, axis=1), narrow, preferred_element_type=F32)
            y2[p, pl.ds(4 * u, 4)] = rows.astype(BF).reshape(4, PIECE, COL2)
        out2.begin(p)
    own = []
    for p in range(3):
        a, b, _ = AXES[p]
        at = (pos[a], pos[b])
        own.append(pltpu.make_async_copy(y2.at[p, spot(p, *at)], out2.dst(p, columns(p, *at)), io_sem.at[1 + p]))
        own[p].start()
    flush(early)
    for p in range(3):
        out2.arrive(p)
        own[p].wait()
    for p in range(3):
        out2.left(p)
    flush(sent)


def local(gradient):
    dma = pltpu.SemaphoreType.DMA
    hbm = pl.BlockSpec(memory_space=pl.ANY)
    padded = pl.pallas_call(
        kernel,
        out_shape=jax.ShapeDtypeStruct((PIECE, K), BF),
        in_specs=[hbm],
        out_specs=hbm,
        scratch_shapes=[
            pltpu.VMEM((ROWS, K), BF),
            pltpu.VMEM((3, 16, PIECE, COL2), BF),
            pltpu.VMEM((3, 16, PIECE, COL2), BF),
            pltpu.VMEM((3, 4, 4, 4, PIECE, 128), BF),
            pltpu.VMEM((2, 3, 4, 4, 4, PIECE, 128), BF),
            pltpu.VMEM((M, 384), BF),
            pltpu.VMEM((CHIP, M), BF),
            pltpu.VMEM((384, HALF_M), BF),
            pltpu.VMEM((3, 4, 4, 4, PIECE, 128), BF),
            pltpu.VMEM((3, 16, PIECE, COL2), BF),
            pltpu.VMEM((3 * 12 * 512, 128), BF),
            pltpu.VMEM((3 * 6 * 512, 128), BF),
            pltpu.VMEM((SLOTS * 512, 128), BF),
            pltpu.VMEM((3, 6, 768, 128), BF),
            pltpu.VMEM((3, 3, 384, 128), BF),
            pltpu.VMEM((3, 3, 96, 128), BF),
            pltpu.VMEM((3, 6, 384, 128), BF),
            pltpu.VMEM((3, 3, 192, 128), BF),
            pltpu.VMEM((3, 3, 48, 128), BF),
            pltpu.VMEM((15, 8, 128), F32),
            pltpu.VMEM((CHIP, M), F32),
            pltpu.VMEM((CHIP, M), BF),
            pltpu.VMEM((CHIP, M), BF),
            pltpu.VMEM((CHIP, M), BF),
            pltpu.VMEM((CHIP, M), F32),
            pltpu.VMEM((CHIP, HALF_M), BF),
            pltpu.VMEM((CHIP, HALF_M), BF),
            dma((4,)),
            dma((1, 3, 3)),
            dma((1, 3, 3)),
            dma((3,)),
            dma((3,)),
            dma((3,)),
            dma((3,)),
            dma((1, 3, 3)),
            dma((1, 3, 3)),
            dma((3,)),
            dma((3,)),
            dma((5,)),
            dma((5,)),
            dma((3, 3, 6)),
            dma((3, 3, 6)),
            dma((3, 3, 6)),
            dma((3, 3, 6)),
            dma((3, 3, 6)),
            dma((3, 3, 6)),
            dma((3, 3, 6)),
            dma((3, 3, 6)),
            dma((4, 3)),
            dma((4, 3)),
        ],
        compiler_params=pltpu.CompilerParams(
            collective_id=0, has_side_effects=True, vmem_limit_bytes=60 * 1024 * 1024
        ),
        cost_estimate=pl.CostEstimate(flops=16 * 10**9, bytes_accessed=5 * 10**6, transcendentals=0),
    )(gradient)
    return padded[:ROWS]


def solution(mesh):
    spec = P(("wide", "narrow"), None)
    return jax.shard_map(local, mesh=mesh, in_specs=(spec,), out_specs=spec, check_vma=False)
```

```python
import math

import jax
import jax.numpy as jnp
from jax import lax
from jax.experimental import pallas as pl
from jax.experimental.pallas import tpu as pltpu
from jax.sharding import PartitionSpec as P

M = 3584
K = 18432

COEFF_A = 3.4445
COEFF_B = -4.775
COEFF_C = 2.0315

MESH = pl.DeviceIdType.MESH
BF = jnp.bfloat16
F32 = jnp.float32
NT = (((1,), (1,)), ((), ()))

ROWS = 28
PIECE = 32
THIRD = K // 3
COL1 = THIRD // 4
COL2 = COL1 // 4
COL3 = COL2 // 4
CHIP = 3 * COL3
HALF_M = M // 2
AXES = ((0, 1, 2), (1, 2, 0), (2, 0, 1))

BLK = 256
NB = M // BLK
PER_PART = (12, 6)
SECOND = 3 * PER_PART[0]
SLOTS = 3 * sum(PER_PART)
SIZES = ((1536, 384, 96), (768, 192, 48))


def al(x, m=16):
    return pl.multiple_of(x, m)


def kernel(
    in_ref, y0,
    rows_in, x0, x2, x2p, x3, s_all, st,
    ut, y2p, y2,
    ta, tb, g, r1a, r2a, r3a, r1b, r2b, r3b, sq, yf, ybf, yp, yr, zf, zp, zr,
    io_sem, in_send, in_recv, in_plane_send, in_plane_recv, core_send, core_recv,
    out_send, out_recv, out_plane_send, out_plane_recv, part_send, part_recv,
    rsa_send, rsa_recv, aga_send, aga_recv, rsb_send, rsb_recv, agb_send, agb_recv, sq_send, sq_recv,
):
    w, n_ = lax.axis_index("wide"), lax.axis_index("narrow")
    core, z_lo, y = w % 2, (w // 2) % 2, w // 4
    x, z_hi = n_ % 4, n_ // 4
    z = z_hi * 2 + z_lo
    pos = (x, y, z)

    def device(x, y, z, core):
        return ((y * 2 + z % 2) * 2 + core, (z // 2) * 4 + x)

    def shifted(axis, by):
        p = [x, y, z]
        p[axis] = (p[axis] + by) % 4
        return device(*p, core)

    right = [shifted(a, 1) for a in range(3)]
    left = [shifted(a, 3) for a in range(3)]
    across = [shifted(a, 2) for a in range(3)]
    partner = device(x, y, z, 1 - core)

    def in_plane(p, d, e):
        a, b, _ = AXES[p]
        if e == 0:
            return (right, across, left)[d - 1][a]
        if d == 0:
            return (right, across, left)[e - 1][b]
        v = [x, y, z]
        v[a] = (v[a] + d) % 4
        v[b] = (v[b] + e) % 4
        return device(*v, core)

    steps = [(d, e) for d in range(4) for e in range(4) if d or e]
    plane_devices = [[in_plane(p, d, e) for d, e in steps] for p in range(3)]
    diagonal = [plane_devices[p][k] for p in range(3) for k, (d, e) in enumerate(steps) if d and e]

    barrier = pltpu.get_barrier_semaphore()
    for d in right + left + across + diagonal + [partner]:
        pl.semaphore_signal(barrier, inc=1, device_id=d, device_id_type=MESH)

    fetch = pltpu.make_async_copy(in_ref, rows_in, io_sem.at[0])
    fetch.start()
    fetch.wait()

    def load(k, carry):
        p, q = k // 4, k % 4
        v = rows_in[:, pl.ds(al(k * COL1, COL1), COL1)]
        for e in range(4):
            x0[p, q * 4 + e, pl.ds(0, ROWS), :] = v[:, e * COL2 : (e + 1) * COL2]
            x0[p, q * 4 + e, pl.ds(ROWS, PIECE - ROWS), :] = jnp.zeros((PIECE - ROWS, COL2), BF)
        return carry

    lax.fori_loop(0, 12, load, 0)
    pl.semaphore_wait(barrier, 37)

    def remote(src, dst, send, recv, dev):
        return pltpu.make_async_remote_copy(
            src_ref=src, dst_ref=dst, send_sem=send, recv_sem=recv, device_id=dev, device_id_type=MESH
        )

    def wait_bytes(ref, sem):
        pltpu.make_async_copy(ref, ref, sem).wait()

    sent = []

    def flush(group):
        for c in group:
            c.wait_send()
        group.clear()

    class Exchange:
        def __init__(self, axis_no, src, dst, sems):
            self.axis_no, self.src, self.dst = axis_no, src, dst
            self.send, self.recv = sems

        def begin(self, p):
            a = AXES[p][self.axis_no]
            me = pos[a]
            for k, dev in ((2, across[a]), (1, right[a]), (3, left[a])):
                remote(self.src(p, (me + k) % 4), self.dst(p, me), self.send.at[p], self.recv.at[p], dev).start()

        def keep(self, p):
            me = pos[AXES[p][self.axis_no]]
            src, dst = self.src(p, me), self.dst(p, me)
            dst[...] = src[...]

        def arrive(self, p):
            wait_bytes(self.src(p, pl.ds(0, 3)), self.recv.at[p])

        def left(self, p):
            wait_bytes(self.src(p, pl.ds(0, 3)), self.send.at[p])

    def spot(p, a, b):
        return b * 4 + a if p == 2 else a * 4 + b

    class PlaneExchange:
        def __init__(self, src, dst, src_spot, dst_spot, send, recv):
            self.src, self.dst, self.src_spot, self.dst_spot = src, dst, src_spot, dst_spot
            self.send, self.recv = send, recv

        def start(self, p, k):
            a, b, _ = AXES[p]
            d, e = steps[k]
            here = self.dst(p, self.dst_spot(p, pos[a], pos[b]))
            there = self.src_spot(p, (pos[a] + d) % 4, (pos[b] + e) % 4)
            remote(self.src.at[p, there], here, self.send.at[p], self.recv.at[p], plane_devices[p][k]).start()

        def begin(self, p):
            for k in range(15):
                self.start(p, k)

        def keep(self, p):
            a, b, _ = AXES[p]
            self.dst(p, self.dst_spot(p, pos[a], pos[b]))[...] = self.src[p, self.src_spot(p, pos[a], pos[b])]

        def arrive(self, p):
            wait_bytes(self.src.at[p, pl.ds(0, 15)], self.recv.at[p])

        def left(self, p):
            wait_bytes(self.src.at[p, pl.ds(0, 15)], self.send.at[p])

    ins = (in_send, in_recv)
    outs = (out_send, out_recv)
    columns = lambda p, a, b: a * 4 + b
    in1 = PlaneExchange(x0, lambda p, s: x2.at[p, s], columns, spot, in_plane_send, in_plane_recv)
    in3 = Exchange(2, lambda p, q: x2p.at[p, q], lambda p, q: x3.at[core, p, q], ins)
    for k in range(15):
        for p in range(3):
            in1.start(p, k)

    def square(k, total):
        for e in range(4):
            v = x0[k // 4, k % 4 * 4 + e].astype(F32)
            v = v * v
            v = (v[:, :128] + v[:, 128:256]) + v[:, 256:]
            total = total + ((v[:8] + v[8:16]) + (v[16:24] + v[24:]))
        return total

    for p in range(3):
        in1.keep(p)
    sq[13] = lax.fori_loop(0, 12, square, jnp.zeros((8, 128), F32))
    sq_core = remote(sq.at[13], sq.at[14], sq_send.at[3, 0], sq_recv.at[3, 0], partner)
    sq_core.start()
    sent.append(sq_core)

    def iota(shape, d):
        return lax.broadcasted_iota(jnp.int32, shape, d)

    def ones_where(cond):
        return jnp.where(cond, 1.0, 0.0).astype(BF)

    def spread_matrix(shape, wide, unit, narrow):
        s, r = iota(shape, wide), iota(shape, 1 - wide)
        return ones_where((s % unit < narrow) & (r == (s // unit) * narrow + s % unit))

    widen = spread_matrix((COL2, 512), 1, 128, COL3)
    for p in range(3):
        in1.arrive(p)
        for u in range(4):
            rows = x2[p, pl.ds(4 * u, 4)].reshape(4 * PIECE, COL2)
            rows = jnp.dot(rows, widen, preferred_element_type=F32).astype(BF)
            for q in range(4):
                x2p[p, q, u] = rows[:, q * 128 : (q + 1) * 128].reshape(4, PIECE, 128)
        in3.begin(p)
    for p in range(3):
        in3.keep(p)
    crossing = []
    for p in range(3):
        in3.arrive(p)
        here = x3.at[core, p]
        c = remote(here, here, core_send.at[p], core_recv.at[p], partner)
        c.start()
        crossing.append(c)
        sent.append(c)

    pack = spread_matrix((8 * ROWS, 8 * PIECE), 1, PIECE, ROWS)

    def pack_rows(owner):
        def body(k, carry):
            x, y0, group = k // 2, k % 2 * 2, [[], [], []]
            for y in (y0, y0 + 1):
                for z in range(4):
                    group[0].append(x3[owner, 0, z, x, y])
                    group[1].append(x3[owner, 1, x, y, z])
                    group[2].append(x3[owner, 2, y, x, z])
            rows = jnp.concatenate([jnp.concatenate(e, axis=0) for e in group], axis=1)
            at = pl.ds(al(owner * HALF_M + k * 8 * ROWS), 8 * ROWS)
            s_all[at, :] = jnp.dot(pack, rows, preferred_element_type=F32).astype(BF)
            return carry

        lax.fori_loop(0, 4, lambda k, carry: body(2 * k + 1, body(2 * k, carry)), 0)

    pack_rows(core)
    for c in crossing:
        c.wait_recv()
    pack_rows(1 - core)

    def turn_all():
        kk, ll = iota((CHIP, 384), 0), iota((CHIP, 384), 1)
        pick = ones_where((ll % 128 < COL3) & (kk == (ll // 128) * COL3 + ll % 128))

        def turn(j, carry):
            at = pl.ds(al(j * BLK, BLK), BLK)
            st[:, at] = lax.dot_general(pick, s_all[at, :], NT, preferred_element_type=F32).astype(BF)
            return carry

        lax.fori_loop(0, NB // 2, lambda k, carry: turn(2 * k + 1, turn(2 * k, carry)), 0)

    def block_of(chunk, m):
        if chunk == 0:
            i = jnp.where(m < 28, m % NB, jnp.where(m < 35, 7 * core + m - 28, 4 * core))
            d = jnp.where(m < 28, 2 * core + m // NB, jnp.where(m < 35, 5, 7))
            return i, d, jnp.where(d == 0, 0.5, 1.0)
        i = jnp.where(m < 14, m, 4 * core + jnp.minimum(m, 16) - 13)
        d = jnp.where(m < 14, 4 + 2 * core, 7)
        return i, d, jnp.where((d == 7) & ((i >= 7) | (m == 17)), 0.0, 1.0)

    def gram_block(chunk, m, t):
        i, d, scale = block_of(chunk, m)
        j = (i + d) % NB
        ri = pl.ds(al(i * BLK, BLK), BLK)
        rj = pl.ds(al(j * BLK, BLK), BLK)
        acc = lax.dot_general(s_all[ri, :], s_all[rj, :], NT, preferred_element_type=F32)
        acc = (scale * acc).astype(BF)
        t[pl.ds(al(m * 512, 512), 256), :] = acc[:, :128]
        t[pl.ds(al(m * 512 + 256, 256), 256), :] = acc[:, 128:]

    def square_begin(s):
        group = [
            remote(sq.at[4 * s], sq.at[4 * s + 1 + k], sq_send.at[s, k], sq_recv.at[s, k], dev)
            for k, dev in enumerate((right[s], left[s], across[s]))
        ]
        for c in group:
            c.start()
        sent.extend(group)
        return group

    def square_end(s, group):
        for c in group:
            c.wait_recv()
        sq[4 * s + 4] = (sq[4 * s] + sq[4 * s + 3]) + (sq[4 * s + 1] + sq[4 * s + 2])

    class Chunk:
        def __init__(self, no, t, bufs, rs, ag):
            self.no, self.t, self.bufs, self.rs, self.ag = no, t, bufs, rs, ag
            self.blocks = PER_PART[no]
            self.sizes = SIZES[no]
            base = [p * self.blocks * 512 for p in range(3)]
            self.bases = [base]
            for k in range(3):
                base = [base[p] + pos[AXES[p][k]] * self.sizes[k] for p in range(3)]
                self.bases.append(base)
            self.mine = no * SECOND * 512
            self.copies = {}

        def quarter(self, k, p, by):
            return self.bases[k][p] + ((pos[AXES[p][k]] + by) % 4) * self.sizes[k]

        def gram(self, p, start, count):
            for m in range(count):
                gram_block(self.no, p * self.blocks + start + m, self.t)

        def gram_far(self):
            for p in range(3):
                q = (pos[AXES[p][0]] + 2) % 4
                self.gram(p, self.blocks * q // 4, -(-self.blocks // 4))

        def gram_near(self):
            for p in range(3):
                me = pos[AXES[p][0]]
                if self.blocks % 4:
                    self.gram(p, self.blocks // 4 + self.blocks // 2 * (me // 2), 1)
                for by in (1, 3):
                    self.gram(p, (self.blocks * ((me + by) % 4) + 2) // 4, self.blocks // 4)

        def gram_own(self):
            for p in range(3):
                self.gram(p, (self.blocks * pos[AXES[p][0]] + 2) // 4, self.blocks // 4)

        def push(self, k, p, no, off, rows):
            a = AXES[p][k]
            c = remote(
                self.t.at[pl.ds(al(off), rows), :],
                self.bufs[k].at[p, no],
                self.rs[0].at[k],
                self.rs[1].at[k, p, no],
                right[a] if no < 3 else left[a],
            )
            c.start()
            self.copies[k, p, no] = c

        def add_rows(self, off, rows, srcs):
            step = rows // 2 if rows > 200 else rows
            t = self.t

            def body(m, carry):
                at = pl.ds(al(off + m * step), step)
                total = t[at, :]
                for src in srcs:
                    total = total + src[pl.ds(al(m * step), step), :]
                t[at, :] = total
                return carry

            lax.fori_loop(0, rows // step, body, 0)

        def scatter_far(self, k):
            half = self.sizes[k] // 2
            for p in range(3):
                self.push(k, p, 0, self.quarter(k, p, 2), half)
                self.push(k, p, 3, self.quarter(k, p, 2) + half, half)

        def scatter_near(self, k):
            half = self.sizes[k] // 2
            for p in range(3):
                self.push(k, p, 1, self.quarter(k, p, 1) + half, half)
                self.push(k, p, 4, self.quarter(k, p, 3), half)

        def scatter_mid(self, k):
            half = self.sizes[k] // 2
            for p in range(3):
                self.copies[k, p, 0].wait_recv()
                self.add_rows(self.quarter(k, p, 1), half, [self.bufs[k].at[p, 0]])
                self.push(k, p, 2, self.quarter(k, p, 1), half)
                self.copies[k, p, 3].wait_recv()
                self.add_rows(self.quarter(k, p, 3) + half, half, [self.bufs[k].at[p, 3]])
                self.push(k, p, 5, self.quarter(k, p, 3) + half, half)

        def scatter_end(self, k):
            half = self.sizes[k] // 2
            for p in range(3):
                for h, one, two in ((0, 4, 2), (1, 1, 5)):
                    self.copies[k, p, one].wait_recv()
                    self.copies[k, p, two].wait_recv()
                    self.add_rows(
                        self.quarter(k, p, 0) + h * half, half, [self.bufs[k].at[p, one], self.bufs[k].at[p, two]]
                    )

        def ring_begin(self, s):
            size = self.sizes[s]
            for k, dev in ((2, across), (1, right), (3, left)):
                for p in range(3):
                    remote(
                        self.t.at[pl.ds(al(self.quarter(s, p, k)), size), :],
                        self.bufs[s].at[p, k - 1],
                        self.rs[0].at[s],
                        self.rs[1].at[s, p, 0],
                        dev[AXES[p][s]],
                    ).start()

        def ring_end(self, s):
            size = self.sizes[s]
            for p in range(3):
                wait_bytes(self.t.at[pl.ds(0, 3 * size), :], self.rs[1].at[s, p, 0])
                off = self.bases[s + 1][p]
                step = min(size, 96)

                def body(m, carry):
                    at = pl.ds(al(off + m * step), step)
                    total = self.t[at, :].astype(F32)
                    for k in range(3):
                        total = total + self.bufs[s][p, k, pl.ds(al(m * step), step)].astype(F32)
                    if s == 2:
                        g[pl.ds(al(self.mine + off), size), :] = total.astype(BF)
                    else:
                        self.t[at, :] = total.astype(BF)
                    return carry

                lax.fori_loop(0, size // step, body, 0)
            if s == 2:
                self.rounds(2)

        def rounds(self, s):
            for k, dev in ((2, across), (1, right), (3, left)):
                for p in range(3):
                    self.spread(s, p, 0, self.bases[s + 1][p], self.sizes[s], dev[AXES[p][s]])

        def rounds_end(self, s):
            for p in range(3):
                wait_bytes(self.t.at[pl.ds(0, 3 * self.sizes[s]), :], self.ag[1].at[s, p, 0])

        def all_sent(self):
            for s in range(3):
                for sems in (self.rs, self.ag):
                    wait_bytes(self.t.at[pl.ds(0, 9 * self.sizes[s]), :], sems[0].at[s])

        def spread(self, k, p, no, off, rows, dev):
            here = g.at[pl.ds(al(self.mine + off), rows), :]
            c = remote(here, here, self.ag[0].at[k], self.ag[1].at[k, p, no], dev)
            c.start()
            self.copies["g", k, p, no] = c

        def got(self, k, p, *nos):
            for no in nos:
                self.copies["g", k, p, no].wait_recv()

        def gather_begin(self, k):
            half = self.sizes[k] // 2
            for p in range(3):
                own = self.quarter(k, p, 0)
                a = AXES[p][k]
                self.spread(k, p, 0, own, half, right[a])
                self.spread(k, p, 1, own + half, half, left[a])
            for p in range(3):
                own = self.quarter(k, p, 0)
                a = AXES[p][k]
                self.spread(k, p, 2, own + half, half, right[a])
                self.spread(k, p, 3, own, half, left[a])

        def gather_mid(self, k):
            half = self.sizes[k] // 2
            for p in range(3):
                a = AXES[p][k]
                self.got(k, p, 0)
                self.spread(k, p, 4, self.quarter(k, p, 3), half, right[a])
                self.got(k, p, 1)
                self.spread(k, p, 5, self.quarter(k, p, 1) + half, half, left[a])

        def gather_end(self, k):
            for p in range(3):
                self.got(k, p, 2, 3, 4, 5)

    one = Chunk(0, ta, (r1a, r2a, r3a), (rsa_send, rsa_recv), (aga_send, aga_recv))
    two = Chunk(1, tb, (r1b, r2b, r3b), (rsb_send, rsb_recv), (agb_send, agb_recv))

    one.gram_far()
    one.scatter_far(0)
    one.gram_near()
    one.scatter_near(0)
    two.gram_far()
    one.gram_own()
    one.scatter_mid(0)
    two.scatter_far(0)
    two.gram_near()
    two.scatter_near(0)
    two.gram_own()
    sq_core.wait_recv()
    sq[0] = sq[13] + sq[14]
    squares = square_begin(0)
    turn_all()
    for p in range(3):
        in1.left(p)
        in3.left(p)
    one.scatter_end(0)
    one.ring_begin(1)
    square_end(0, squares)
    squares = square_begin(1)
    two.scatter_mid(0)
    one.ring_end(1)
    one.ring_begin(2)
    square_end(1, squares)
    squares = square_begin(2)
    two.scatter_end(0)
    two.ring_begin(1)
    one.ring_end(2)
    square_end(2, squares)
    two.ring_end(1)
    two.ring_begin(2)
    one.rounds_end(2)
    one.rounds(1)
    two.ring_end(2)
    one.rounds_end(1)
    one.gather_begin(0)
    two.rounds_end(2)
    two.rounds(1)
    one.gather_mid(0)
    two.rounds_end(1)
    two.gather_begin(0)
    one.gather_end(0)

    def cols(a_ref, i):
        return a_ref[:, pl.ds(al(i * BLK, BLK), BLK)]

    def block(slot):
        o = slot * 512
        return jnp.concatenate([g[pl.ds(al(o, 512), 256), :], g[pl.ds(al(o + 256, 256), 256), :]], axis=1)

    def band(a_ref, j, ds):
        def straight(d, first):
            i = (j + NB - d) % NB
            return cols(a_ref, i), block(first + i)

        def turned(d, first):
            return cols(a_ref, (j + d) % NB), block(first + j)

        a, b = zip(*[straight(*e) for e in ds])
        acc = jnp.dot(jnp.concatenate(a, axis=1), jnp.concatenate(b, axis=0), preferred_element_type=F32)
        a, b = zip(*[turned(*e) for e in ds])
        return acc + lax.dot_general(
            jnp.concatenate(a, axis=1), jnp.concatenate(b, axis=1), NT, preferred_element_type=F32
        )

    whole_one = ((2 * core, 0), (2 * core + 1, NB))
    whole_two = ((2 * core + 4, SECOND),)

    def single(acc_ref, a_ref, chunk, m):
        i, d, _ = block_of(chunk, m)
        j = (i + d) % NB
        b = block(chunk * SECOND + m)
        acc_ref[:, pl.ds(al(j * BLK, BLK), BLK)] += jnp.dot(cols(a_ref, i), b, preferred_element_type=F32)
        acc_ref[:, pl.ds(al(i * BLK, BLK), BLK)] += lax.dot_general(
            cols(a_ref, j), b, NT, preferred_element_type=F32
        )

    def loop(first_k, last_k, f):
        def body(k, carry):
            f(first_k + 2 * k)
            f(first_k + 2 * k + 1)
            return carry

        lax.fori_loop(0, (last_k - first_k) // 2, body, 0)
        if (last_k - first_k) % 2:
            f(last_k - 1)

    def band_at(j):
        return pl.ds(al(j * BLK, BLK), BLK)

    def to_partner(no, src, dst):
        c = remote(src, dst, part_send.at[no], part_recv.at[no], partner)
        c.start()
        sent.append(c)
        return c

    def y_one(j):
        yf[:, band_at(j)] = band(st, j, whole_one)

    def shared(acc_ref, a_ref):
        return lambda m: single(acc_ref, a_ref, 0, 28 + m), lambda m: single(acc_ref, a_ref, 1, 14 + m)

    y_first, y_rest = shared(yf, st)
    loop(0, 6, y_one)
    two.gather_mid(0)
    loop(6, NB, y_one)
    zf[...] = jnp.zeros((CHIP, M), F32)
    loop(0, 8, y_first)
    two.gather_end(0)
    loop(0, 3, y_rest)

    def y_two(j):
        v = yf[:, band_at(j)] + band(st, j, whole_two)
        yf[:, band_at(j)] = v
        yp[:, band_at(j)] = v.astype(BF)

    shares = []
    for lo, hi in ((0, 4), (4, 8), (8, 12), (12, 14)):
        loop(lo, hi, y_two)
        here = pl.ds(lo * BLK, (hi - lo) * BLK)
        shares.append((lo, hi, to_partner(len(shares), yp.at[:, here], yr.at[:, here])))

    factor = 0.3 * math.sqrt(M) / (jnp.sqrt(jnp.sum(sq[12], axis=(0, 1), keepdims=True)) + 1e-07)
    factor2 = factor * factor

    def y_sum(j):
        v = factor2 * (yf[:, band_at(j)] + yr[:, band_at(j)].astype(F32))
        yf[:, band_at(j)] = v
        ybf[:, band_at(j)] = v.astype(BF)

    for lo, hi, arriving in shares:
        arriving.wait_recv()
        loop(lo, hi, y_sum)

    z_first, z_rest = shared(zf, ybf)
    loop(0, 8, z_first)
    loop(0, 3, z_rest)

    def z_band(j):
        return factor2 * (zf[:, band_at(j)] + band(ybf, j, whole_one + whole_two))

    def z_theirs(k):
        zp[:, band_at(k)] = z_band((1 - core) * 7 + k).astype(BF)

    loop(0, 7, z_theirs)
    share = to_partner(4, zp, zr)

    def z_mine(k):
        zf[:, band_at(core * 7 + k)] = z_band(core * 7 + k)

    loop(0, 7, z_mine)
    share.wait_recv()
    for p in range(3):
        ut[pl.ds(p * 128 + COL3, 128 - COL3), :] = jnp.zeros((128 - COL3, HALF_M), BF)

    def finish(k):
        at = band_at(core * 7 + k)
        scaled = (factor * st[:, at].astype(F32)).astype(BF).astype(F32)
        product = factor * (COEFF_B * yf[:, at] + COEFF_C * (zf[:, at] + zr[:, band_at(k)].astype(F32)))
        u = (math.sqrt(K) * (COEFF_A * scaled + product)).astype(BF)
        for p in range(3):
            ut[pl.ds(p * 128, COL3), band_at(k)] = u[p * COL3 : (p + 1) * COL3]

    loop(0, 7, finish)

    y3 = x2p
    unpack = spread_matrix((8 * PIECE, 8 * ROWS), 0, PIECE, ROWS)
    for m in range(8):
        o = m * 8 * ROWS
        first_lane = o // 128 * 128
        skip = o - first_lane
        width = -(-(skip + 8 * ROWS) // 128) * 128
        v = ut[:, pl.ds(first_lane, width)][:, skip : skip + 8 * ROWS]
        rows = lax.dot_general(unpack, v, NT, preferred_element_type=F32).astype(BF)
        for r in range(8):
            x, y, z = m // 2, m % 2 * 2 + r // 4, r % 4
            for p, at in enumerate(((z, x, y), (x, y, z), (y, x, z))):
                y3[(p,) + at] = rows[r * PIECE : (r + 1) * PIECE, p * 128 : (p + 1) * 128]

    out1 = Exchange(2, lambda p, q: y3.at[p, q], lambda p, q: y2p.at[p, q], outs)
    out2 = PlaneExchange(
        y2, lambda p, s: y0.at[:, pl.ds(al(p * THIRD + s * COL2, 128), COL2)], spot, columns, out_plane_send, out_plane_recv,
    )
    for p in range(3):
        out1.begin(p)
    for p in range(3):
        out1.keep(p)
    flush(sent)
    one.all_sent()
    two.all_sent()
    narrow = spread_matrix((512, COL2), 0, 128, COL3)
    for p in range(3):
        out1.arrive(p)
        for u in range(4):
            rows = [y2p[p, q, u].reshape(4 * PIECE, 128) for q in range(4)]
            rows = jnp.dot(jnp.concatenate(rows, axis=1), narrow, preferred_element_type=F32)
            y2[p, pl.ds(4 * u, 4)] = rows.astype(BF).reshape(4, PIECE, COL2)
        out2.begin(p)
    own = []
    for p in range(3):
        a, b, _ = AXES[p]
        at = (pos[a], pos[b])
        own.append(pltpu.make_async_copy(y2.at[p, spot(p, *at)], out2.dst(p, columns(p, *at)), io_sem.at[1 + p]))
        own[p].start()
        out1.left(p)
    for p in range(3):
        out2.arrive(p)
        own[p].wait()
    for p in range(3):
        out2.left(p)


def local(gradient):
    dma = pltpu.SemaphoreType.DMA
    hbm = pl.BlockSpec(memory_space=pl.ANY)
    padded = pl.pallas_call(
        kernel,
        out_shape=jax.ShapeDtypeStruct((PIECE, K), BF),
        in_specs=[hbm],
        out_specs=hbm,
        scratch_shapes=[
            pltpu.VMEM((ROWS, K), BF),
            pltpu.VMEM((3, 16, PIECE, COL2), BF),
            pltpu.VMEM((3, 16, PIECE, COL2), BF),
            pltpu.VMEM((3, 4, 4, 4, PIECE, 128), BF),
            pltpu.VMEM((2, 3, 4, 4, 4, PIECE, 128), BF),
            pltpu.VMEM((M, 384), BF),
            pltpu.VMEM((CHIP, M), BF),
            pltpu.VMEM((384, HALF_M), BF),
            pltpu.VMEM((3, 4, 4, 4, PIECE, 128), BF),
            pltpu.VMEM((3, 16, PIECE, COL2), BF),
            pltpu.VMEM((3 * 12 * 512, 128), BF),
            pltpu.VMEM((3 * 6 * 512, 128), BF),
            pltpu.VMEM((SLOTS * 512, 128), BF),
            pltpu.VMEM((3, 6, 768, 128), BF),
            pltpu.VMEM((3, 3, 384, 128), BF),
            pltpu.VMEM((3, 3, 96, 128), BF),
            pltpu.VMEM((3, 6, 384, 128), BF),
            pltpu.VMEM((3, 3, 192, 128), BF),
            pltpu.VMEM((3, 3, 48, 128), BF),
            pltpu.VMEM((15, 8, 128), F32),
            pltpu.VMEM((CHIP, M), F32),
            pltpu.VMEM((CHIP, M), BF),
            pltpu.VMEM((CHIP, M), BF),
            pltpu.VMEM((CHIP, M), BF),
            pltpu.VMEM((CHIP, M), F32),
            pltpu.VMEM((CHIP, HALF_M), BF),
            pltpu.VMEM((CHIP, HALF_M), BF),
            dma((4,)),
            dma((3,)),
            dma((3,)),
            dma((3,)),
            dma((3,)),
            dma((3,)),
            dma((3,)),
            dma((3,)),
            dma((3,)),
            dma((3,)),
            dma((3,)),
            dma((5,)),
            dma((5,)),
            dma((3,)),
            dma((3, 3, 6)),
            dma((3,)),
            dma((3, 3, 6)),
            dma((3,)),
            dma((3, 3, 6)),
            dma((3,)),
            dma((3, 3, 6)),
            dma((4, 3)),
            dma((4, 3)),
        ],
        compiler_params=pltpu.CompilerParams(
            collective_id=0, has_side_effects=True, vmem_limit_bytes=60 * 1024 * 1024
        ),
        cost_estimate=pl.CostEstimate(flops=16 * 10**9, bytes_accessed=5 * 10**6, transcendentals=0),
    )(gradient)
    return padded[:ROWS]


def solution(mesh):
    spec = P(("wide", "narrow"), None)
    return jax.shard_map(local, mesh=mesh, in_specs=(spec,), out_specs=spec, check_vma=False)
```

```python
import math

import jax
import jax.numpy as jnp
from jax import lax
from jax.experimental import pallas as pl
from jax.experimental.pallas import tpu as pltpu
from jax.sharding import PartitionSpec as P

M = 3584
K = 18432

COEFF_A = 3.4445
COEFF_B = -4.775
COEFF_C = 2.0315

MESH = pl.DeviceIdType.MESH
BF = jnp.bfloat16
F32 = jnp.float32
NT = (((1,), (1,)), ((), ()))

ROWS = 28
PIECE = 32
THIRD = K // 3
COL1 = THIRD // 4
COL2 = COL1 // 4
COL3 = COL2 // 4
CHIP = 3 * COL3
HALF_M = M // 2
AXES = ((0, 1, 2), (1, 2, 0), (2, 0, 1))

BLK = 256
NB = M // BLK
PER_PART = (12, 6)
SECOND = 3 * PER_PART[0]
SLOTS = 3 * sum(PER_PART)
SIZES = ((1536, 384, 96), (768, 192, 48))


def al(x, m=16):
    return pl.multiple_of(x, m)


def kernel(
    in_ref, y0,
    rows_in, x0, x2, x2p, x3, s_all, st,
    ut, y2p, y2,
    ta, tb, g, r1a, r2a, r3a, r1b, r2b, r3b, sq, yf, ybf, yp, yr, zf, zp, zr,
    io_sem, in_send, in_recv, in_plane_send, in_plane_recv, core_send, core_recv,
    out_send, out_recv, out_plane_send, out_plane_recv, part_send, part_recv,
    rsa_send, rsa_recv, aga_send, aga_recv, rsb_send, rsb_recv, agb_send, agb_recv, sq_send, sq_recv,
):
    w, n_ = lax.axis_index("wide"), lax.axis_index("narrow")
    core, z_lo, y = w % 2, (w // 2) % 2, w // 4
    x, z_hi = n_ % 4, n_ // 4
    z = z_hi * 2 + z_lo
    pos = (x, y, z)

    def device(x, y, z, core):
        return ((y * 2 + z % 2) * 2 + core, (z // 2) * 4 + x)

    def shifted(axis, by):
        p = [x, y, z]
        p[axis] = (p[axis] + by) % 4
        return device(*p, core)

    right = [shifted(a, 1) for a in range(3)]
    left = [shifted(a, 3) for a in range(3)]
    across = [shifted(a, 2) for a in range(3)]
    partner = device(x, y, z, 1 - core)

    def in_plane(p, d, e):
        a, b, _ = AXES[p]
        if e == 0:
            return (right, across, left)[d - 1][a]
        if d == 0:
            return (right, across, left)[e - 1][b]
        v = [x, y, z]
        v[a] = (v[a] + d) % 4
        v[b] = (v[b] + e) % 4
        return device(*v, core)

    steps = [(d, e) for d in range(4) for e in range(4) if d or e]
    plane_devices = [[in_plane(p, d, e) for d, e in steps] for p in range(3)]
    diagonal = [plane_devices[p][k] for p in range(3) for k, (d, e) in enumerate(steps) if d and e]

    barrier = pltpu.get_barrier_semaphore()
    for d in right + left + across + diagonal + [partner]:
        pl.semaphore_signal(barrier, inc=1, device_id=d, device_id_type=MESH)

    fetch = pltpu.make_async_copy(in_ref, rows_in, io_sem.at[0])
    fetch.start()
    fetch.wait()

    def load(k, carry):
        p, q = k // 4, k % 4
        v = rows_in[:, pl.ds(al(k * COL1, COL1), COL1)]
        for e in range(4):
            x0[p, q * 4 + e, pl.ds(0, ROWS), :] = v[:, e * COL2 : (e + 1) * COL2]
            x0[p, q * 4 + e, pl.ds(ROWS, PIECE - ROWS), :] = jnp.zeros((PIECE - ROWS, COL2), BF)
        return carry

    lax.fori_loop(0, 12, load, 0)
    pl.semaphore_wait(barrier, 37)

    def remote(src, dst, send, recv, dev):
        return pltpu.make_async_remote_copy(
            src_ref=src, dst_ref=dst, send_sem=send, recv_sem=recv, device_id=dev, device_id_type=MESH
        )

    def wait_bytes(ref, sem):
        pltpu.make_async_copy(ref, ref, sem).wait()

    sent = []

    def flush(group):
        for c in group:
            c.wait_send()
        group.clear()

    class Exchange:
        def __init__(self, axis_no, src, dst, sems):
            self.axis_no, self.src, self.dst = axis_no, src, dst
            self.send, self.recv = sems

        def start(self, p, k):
            a = AXES[p][self.axis_no]
            dev = (right, across, left)[k - 1][a]
            remote(self.src(p, (pos[a] + k) % 4), self.dst(p, pos[a]), self.send.at[p], self.recv.at[p], dev).start()

        def begin(self, p):
            for k in (2, 1, 3):
                self.start(p, k)

        def keep(self, p):
            me = pos[AXES[p][self.axis_no]]
            src, dst = self.src(p, me), self.dst(p, me)
            dst[...] = src[...]

        def arrive(self, p):
            wait_bytes(self.src(p, pl.ds(0, 3)), self.recv.at[p])

        def left(self, p):
            wait_bytes(self.src(p, pl.ds(0, 3)), self.send.at[p])

    def spot(p, a, b):
        return b * 4 + a if p == 2 else a * 4 + b

    class PlaneExchange:
        def __init__(self, src, dst, src_spot, dst_spot, send, recv):
            self.src, self.dst, self.src_spot, self.dst_spot = src, dst, src_spot, dst_spot
            self.send, self.recv = send, recv

        def start(self, p, k):
            a, b, _ = AXES[p]
            d, e = steps[k]
            here = self.dst(p, self.dst_spot(p, pos[a], pos[b]))
            there = self.src_spot(p, (pos[a] + d) % 4, (pos[b] + e) % 4)
            remote(self.src.at[p, there], here, self.send.at[p], self.recv.at[p], plane_devices[p][k]).start()

        def begin(self, p):
            for k in range(15):
                self.start(p, k)

        def keep(self, p):
            a, b, _ = AXES[p]
            self.dst(p, self.dst_spot(p, pos[a], pos[b]))[...] = self.src[p, self.src_spot(p, pos[a], pos[b])]

        def arrive(self, p):
            wait_bytes(self.src.at[p, pl.ds(0, 15)], self.recv.at[p])

        def left(self, p):
            wait_bytes(self.src.at[p, pl.ds(0, 15)], self.send.at[p])

    ins = (in_send, in_recv)
    outs = (out_send, out_recv)
    columns = lambda p, a, b: a * 4 + b
    in1 = PlaneExchange(x0, lambda p, s: x2.at[p, s], columns, spot, in_plane_send, in_plane_recv)
    in3 = Exchange(2, lambda p, q: x2p.at[p, q], lambda p, q: x3.at[core, p, q], ins)
    for k in range(15):
        for p in range(3):
            in1.start(p, k)

    def square(k, total):
        for e in range(4):
            v = x0[k // 4, k % 4 * 4 + e].astype(F32)
            v = v * v
            v = (v[:, :128] + v[:, 128:256]) + v[:, 256:]
            total = total + ((v[:8] + v[8:16]) + (v[16:24] + v[24:]))
        return total

    for p in range(3):
        in1.keep(p)
    sq[13] = lax.fori_loop(0, 12, square, jnp.zeros((8, 128), F32))
    sq_core = remote(sq.at[13], sq.at[14], sq_send.at[0], sq_recv.at[3], partner)
    sq_core.start()

    def iota(shape, d):
        return lax.broadcasted_iota(jnp.int32, shape, d)

    def ones_where(cond):
        return jnp.where(cond, 1.0, 0.0).astype(BF)

    def spread_matrix(shape, wide, unit, narrow):
        s, r = iota(shape, wide), iota(shape, 1 - wide)
        return ones_where((s % unit < narrow) & (r == (s // unit) * narrow + s % unit))

    widen = spread_matrix((COL2, 512), 1, 128, COL3)
    for p in range(3):
        in1.arrive(p)
        for u in range(4):
            rows = x2[p, pl.ds(4 * u, 4)].reshape(4 * PIECE, COL2)
            rows = jnp.dot(rows, widen, preferred_element_type=F32).astype(BF)
            for q in range(4):
                x2p[p, q, u] = rows[:, q * 128 : (q + 1) * 128].reshape(4, PIECE, 128)
        in3.begin(p)
    for p in range(3):
        in3.keep(p)
    crossing = []
    for p in range(3):
        in3.arrive(p)
        here = x3.at[core, p]
        c = remote(here, here, core_send.at[p], core_recv.at[p], partner)
        c.start()
        crossing.append(c)
        sent.append(c)

    pack = spread_matrix((8 * ROWS, 8 * PIECE), 1, PIECE, ROWS)

    def pack_rows(owner):
        def body(k, carry):
            x, y0, group = k // 2, k % 2 * 2, [[], [], []]
            for y in (y0, y0 + 1):
                for z in range(4):
                    group[0].append(x3[owner, 0, z, x, y])
                    group[1].append(x3[owner, 1, x, y, z])
                    group[2].append(x3[owner, 2, y, x, z])
            rows = jnp.concatenate([jnp.concatenate(e, axis=0) for e in group], axis=1)
            at = pl.ds(al(owner * HALF_M + k * 8 * ROWS), 8 * ROWS)
            s_all[at, :] = jnp.dot(pack, rows, preferred_element_type=F32).astype(BF)
            return carry

        lax.fori_loop(0, 4, lambda k, carry: body(2 * k + 1, body(2 * k, carry)), 0)

    pack_rows(core)
    for c in crossing:
        c.wait_recv()
    pack_rows(1 - core)

    def turn_all():
        kk, ll = iota((CHIP, 384), 0), iota((CHIP, 384), 1)
        pick = ones_where((ll % 128 < COL3) & (kk == (ll // 128) * COL3 + ll % 128))

        def turn(j, carry):
            at = pl.ds(al(j * BLK, BLK), BLK)
            st[:, at] = lax.dot_general(pick, s_all[at, :], NT, preferred_element_type=F32).astype(BF)
            return carry

        lax.fori_loop(0, NB // 2, lambda k, carry: turn(2 * k + 1, turn(2 * k, carry)), 0)

    def block_of(chunk, m):
        if chunk == 0:
            i = jnp.where(m < 28, m % NB, jnp.where(m < 35, 7 * core + m - 28, 4 * core))
            d = jnp.where(m < 28, 2 * core + m // NB, jnp.where(m < 35, 5, 7))
            return i, d, jnp.where(d == 0, 0.5, 1.0)
        i = jnp.where(m < 14, m, 4 * core + jnp.minimum(m, 16) - 13)
        d = jnp.where(m < 14, 4 + 2 * core, 7)
        return i, d, jnp.where((d == 7) & ((i >= 7) | (m == 17)), 0.0, 1.0)

    def gram_block(chunk, m, t):
        i, d, scale = block_of(chunk, m)
        j = (i + d) % NB
        ri = pl.ds(al(i * BLK, BLK), BLK)
        rj = pl.ds(al(j * BLK, BLK), BLK)
        acc = lax.dot_general(s_all[ri, :], s_all[rj, :], NT, preferred_element_type=F32)
        acc = (scale * acc).astype(BF)
        t[pl.ds(al(m * 512, 512), 256), :] = acc[:, :128]
        t[pl.ds(al(m * 512 + 256, 256), 256), :] = acc[:, 128:]

    def square_begin(s):
        for k, dev in enumerate((right[s], left[s], across[s])):
            remote(sq.at[4 * s], sq.at[4 * s + 1 + k], sq_send.at[0], sq_recv.at[s], dev).start()

    def square_end(s):
        wait_bytes(sq.at[pl.ds(0, 3)], sq_recv.at[s])
        sq[4 * s + 4] = (sq[4 * s] + sq[4 * s + 3]) + (sq[4 * s + 1] + sq[4 * s + 2])

    class Chunk:
        def __init__(self, no, t, bufs, rs, ag):
            self.no, self.t, self.bufs, self.rs, self.ag = no, t, bufs, rs, ag
            self.blocks = PER_PART[no]
            self.sizes = SIZES[no]
            base = [p * self.blocks * 512 for p in range(3)]
            self.bases = [base]
            for k in range(3):
                base = [base[p] + pos[AXES[p][k]] * self.sizes[k] for p in range(3)]
                self.bases.append(base)
            self.mine = no * SECOND * 512
            self.copies = {}

        def quarter(self, k, p, by):
            return self.bases[k][p] + ((pos[AXES[p][k]] + by) % 4) * self.sizes[k]

        def gram(self, p, start, count):
            for m in range(count):
                gram_block(self.no, p * self.blocks + start + m, self.t)

        def gram_far(self):
            for p in range(3):
                q = (pos[AXES[p][0]] + 2) % 4
                self.gram(p, self.blocks * q // 4, -(-self.blocks // 4))

        def gram_near(self):
            for p in range(3):
                me = pos[AXES[p][0]]
                if self.blocks % 4:
                    self.gram(p, self.blocks // 4 + self.blocks // 2 * (me // 2), 1)
                for by in (1, 3):
                    self.gram(p, (self.blocks * ((me + by) % 4) + 2) // 4, self.blocks // 4)

        def gram_own(self):
            for p in range(3):
                self.gram(p, (self.blocks * pos[AXES[p][0]] + 2) // 4, self.blocks // 4)

        def push(self, k, p, no, off, rows):
            a = AXES[p][k]
            c = remote(
                self.t.at[pl.ds(al(off), rows), :],
                self.bufs[k].at[p, no],
                self.rs[0].at[k],
                self.rs[1].at[k, p, no],
                right[a] if no < 3 else left[a],
            )
            c.start()
            self.copies[k, p, no] = c

        def add_rows(self, off, rows, srcs):
            step = rows // 2 if rows > 200 else rows
            t = self.t

            def body(m, carry):
                at = pl.ds(al(off + m * step), step)
                total = t[at, :]
                for src in srcs:
                    total = total + src[pl.ds(al(m * step), step), :]
                t[at, :] = total
                return carry

            lax.fori_loop(0, rows // step, body, 0)

        def scatter_far(self, k):
            half = self.sizes[k] // 2
            for p in range(3):
                self.push(k, p, 0, self.quarter(k, p, 2), half)
                self.push(k, p, 3, self.quarter(k, p, 2) + half, half)

        def scatter_near(self, k):
            half = self.sizes[k] // 2
            for p in range(3):
                self.push(k, p, 1, self.quarter(k, p, 1) + half, half)
                self.push(k, p, 4, self.quarter(k, p, 3), half)

        def scatter_mid(self, k):
            half = self.sizes[k] // 2
            for p in range(3):
                self.copies[k, p, 0].wait_recv()
                self.add_rows(self.quarter(k, p, 1), half, [self.bufs[k].at[p, 0]])
                self.push(k, p, 2, self.quarter(k, p, 1), half)
                self.copies[k, p, 3].wait_recv()
                self.add_rows(self.quarter(k, p, 3) + half, half, [self.bufs[k].at[p, 3]])
                self.push(k, p, 5, self.quarter(k, p, 3) + half, half)

        def scatter_end(self, k):
            half = self.sizes[k] // 2
            for p in range(3):
                for h, one, two in ((0, 4, 2), (1, 1, 5)):
                    self.copies[k, p, one].wait_recv()
                    self.copies[k, p, two].wait_recv()
                    self.add_rows(
                        self.quarter(k, p, 0) + h * half, half, [self.bufs[k].at[p, one], self.bufs[k].at[p, two]]
                    )

        def ring_begin(self, s):
            size = self.sizes[s]
            for k, dev in ((2, across), (1, right), (3, left)):
                for p in range(3):
                    remote(
                        self.t.at[pl.ds(al(self.quarter(s, p, k)), size), :],
                        self.bufs[s].at[p, k - 1],
                        self.rs[0].at[s],
                        self.rs[1].at[s, p, 0],
                        dev[AXES[p][s]],
                    ).start()

        def ring_end(self, s):
            size = self.sizes[s]
            for p in range(3):
                wait_bytes(self.t.at[pl.ds(0, 3 * size), :], self.rs[1].at[s, p, 0])
                off = self.bases[s + 1][p]
                step = min(size, 96)

                def body(m, carry):
                    at = pl.ds(al(off + m * step), step)
                    total = self.t[at, :].astype(F32)
                    for k in range(3):
                        total = total + self.bufs[s][p, k, pl.ds(al(m * step), step)].astype(F32)
                    if s == 2:
                        g[pl.ds(al(self.mine + off), size), :] = total.astype(BF)
                    else:
                        self.t[at, :] = total.astype(BF)
                    return carry

                lax.fori_loop(0, size // step, body, 0)
            if s == 2:
                self.rounds(2)

        def rounds(self, s):
            for k, dev in ((2, across), (1, right), (3, left)):
                for p in range(3):
                    self.spread(s, p, 0, self.bases[s + 1][p], self.sizes[s], dev[AXES[p][s]])

        def rounds_end(self, s):
            for p in range(3):
                wait_bytes(self.t.at[pl.ds(0, 3 * self.sizes[s]), :], self.ag[1].at[s, p, 0])

        def all_sent(self):
            for s in range(3):
                for sems in (self.rs, self.ag):
                    wait_bytes(self.t.at[pl.ds(0, 9 * self.sizes[s]), :], sems[0].at[s])

        def spread(self, k, p, no, off, rows, dev):
            here = g.at[pl.ds(al(self.mine + off), rows), :]
            c = remote(here, here, self.ag[0].at[k], self.ag[1].at[k, p, min(no, 2)], dev)
            c.start()
            self.copies["g", k, p, no] = c

        def got(self, k, p, *nos):
            for no in nos:
                self.copies["g", k, p, no].wait_recv()

        def gather_begin(self, k):
            half = self.sizes[k] // 2
            for p in range(3):
                own = self.quarter(k, p, 0)
                a = AXES[p][k]
                self.spread(k, p, 0, own, half, right[a])
                self.spread(k, p, 1, own + half, half, left[a])
            for p in range(3):
                own = self.quarter(k, p, 0)
                a = AXES[p][k]
                self.spread(k, p, 2, own + half, half, right[a])
                self.spread(k, p, 3, own, half, left[a])

        def gather_mid(self, k):
            half = self.sizes[k] // 2
            for p in range(3):
                a = AXES[p][k]
                self.got(k, p, 0)
                self.spread(k, p, 4, self.quarter(k, p, 3), half, right[a])
                self.got(k, p, 1)
                self.spread(k, p, 5, self.quarter(k, p, 1) + half, half, left[a])

        def gather_end(self, k):
            for p in range(3):
                wait_bytes(self.t.at[pl.ds(0, 2 * self.sizes[k]), :], self.ag[1].at[k, p, 2])

    one = Chunk(0, ta, (r1a, r2a, r3a), (rsa_send, rsa_recv), (aga_send, aga_recv))
    two = Chunk(1, tb, (r1b, r2b, r3b), (rsb_send, rsb_recv), (agb_send, agb_recv))

    one.gram_far()
    one.scatter_far(0)
    one.gram_near()
    one.scatter_near(0)
    two.gram_far()
    one.gram_own()
    one.scatter_mid(0)
    two.scatter_far(0)
    two.gram_near()
    two.scatter_near(0)
    two.gram_own()
    sq_core.wait_recv()
    sq[0] = sq[13] + sq[14]
    square_begin(0)
    turn_all()
    for p in range(3):
        in1.left(p)
        in3.left(p)
    one.scatter_end(0)
    one.ring_begin(1)
    square_end(0)
    square_begin(1)
    two.scatter_mid(0)
    one.ring_end(1)
    one.ring_begin(2)
    square_end(1)
    square_begin(2)
    two.scatter_end(0)
    two.ring_begin(1)
    one.ring_end(2)
    square_end(2)
    two.ring_end(1)
    two.ring_begin(2)
    one.rounds_end(2)
    one.rounds(1)
    two.ring_end(2)
    one.rounds_end(1)
    one.gather_begin(0)
    two.rounds_end(2)
    two.rounds(1)
    one.gather_mid(0)
    two.rounds_end(1)
    two.gather_begin(0)
    one.gather_end(0)

    def cols(a_ref, i):
        return a_ref[:, pl.ds(al(i * BLK, BLK), BLK)]

    def block(slot):
        o = slot * 512
        return jnp.concatenate([g[pl.ds(al(o, 512), 256), :], g[pl.ds(al(o + 256, 256), 256), :]], axis=1)

    def band(a_ref, j, ds):
        def straight(d, first):
            i = (j + NB - d) % NB
            return cols(a_ref, i), block(first + i)

        def turned(d, first):
            return cols(a_ref, (j + d) % NB), block(first + j)

        a, b = zip(*[straight(*e) for e in ds])
        acc = jnp.dot(jnp.concatenate(a, axis=1), jnp.concatenate(b, axis=0), preferred_element_type=F32)
        a, b = zip(*[turned(*e) for e in ds])
        return acc + lax.dot_general(
            jnp.concatenate(a, axis=1), jnp.concatenate(b, axis=1), NT, preferred_element_type=F32
        )

    whole_one = ((2 * core, 0), (2 * core + 1, NB))
    whole_two = ((2 * core + 4, SECOND),)

    def single(acc_ref, a_ref, chunk, m):
        i, d, _ = block_of(chunk, m)
        j = (i + d) % NB
        b = block(chunk * SECOND + m)
        acc_ref[:, pl.ds(al(j * BLK, BLK), BLK)] += jnp.dot(cols(a_ref, i), b, preferred_element_type=F32)
        acc_ref[:, pl.ds(al(i * BLK, BLK), BLK)] += lax.dot_general(
            cols(a_ref, j), b, NT, preferred_element_type=F32
        )

    def loop(first_k, last_k, f):
        def body(k, carry):
            f(first_k + 2 * k)
            f(first_k + 2 * k + 1)
            return carry

        lax.fori_loop(0, (last_k - first_k) // 2, body, 0)
        if (last_k - first_k) % 2:
            f(last_k - 1)

    def band_at(j):
        return pl.ds(al(j * BLK, BLK), BLK)

    def to_partner(no, src, dst):
        c = remote(src, dst, part_send.at[no], part_recv.at[no], partner)
        c.start()
        sent.append(c)
        return c

    def y_one(j):
        yf[:, band_at(j)] = band(st, j, whole_one)

    def shared(acc_ref, a_ref):
        return lambda m: single(acc_ref, a_ref, 0, 28 + m), lambda m: single(acc_ref, a_ref, 1, 14 + m)

    y_first, y_rest = shared(yf, st)
    loop(0, 6, y_one)
    two.gather_mid(0)
    loop(6, NB, y_one)
    zf[...] = jnp.zeros((CHIP, M), F32)
    loop(0, 8, y_first)
    two.gather_end(0)
    loop(0, 3, y_rest)

    def y_two(j):
        v = yf[:, band_at(j)] + band(st, j, whole_two)
        yf[:, band_at(j)] = v
        yp[:, band_at(j)] = v.astype(BF)

    shares = []
    for lo, hi in ((0, 4), (4, 8), (8, 12), (12, 14)):
        loop(lo, hi, y_two)
        here = pl.ds(lo * BLK, (hi - lo) * BLK)
        shares.append((lo, hi, to_partner(len(shares), yp.at[:, here], yr.at[:, here])))

    factor = 0.3 * math.sqrt(M) / (jnp.sqrt(jnp.sum(sq[12], axis=(0, 1), keepdims=True)) + 1e-07)
    factor2 = factor * factor

    def y_sum(j):
        v = factor2 * (yf[:, band_at(j)] + yr[:, band_at(j)].astype(F32))
        yf[:, band_at(j)] = v
        ybf[:, band_at(j)] = v.astype(BF)

    for lo, hi, arriving in shares:
        arriving.wait_recv()
        loop(lo, hi, y_sum)

    z_first, z_rest = shared(zf, ybf)
    loop(0, 8, z_first)
    loop(0, 3, z_rest)

    def z_band(j):
        return factor2 * (zf[:, band_at(j)] + band(ybf, j, whole_one + whole_two))

    def z_theirs(k):
        zp[:, band_at(k)] = z_band((1 - core) * 7 + k).astype(BF)

    loop(0, 7, z_theirs)
    share = to_partner(4, zp, zr)

    def z_mine(k):
        zf[:, band_at(core * 7 + k)] = z_band(core * 7 + k)

    loop(0, 7, z_mine)
    share.wait_recv()
    for p in range(3):
        ut[pl.ds(p * 128 + COL3, 128 - COL3), :] = jnp.zeros((128 - COL3, HALF_M), BF)

    def finish(k):
        at = band_at(core * 7 + k)
        scaled = (factor * st[:, at].astype(F32)).astype(BF).astype(F32)
        product = factor * (COEFF_B * yf[:, at] + COEFF_C * (zf[:, at] + zr[:, band_at(k)].astype(F32)))
        u = (math.sqrt(K) * (COEFF_A * scaled + product)).astype(BF)
        for p in range(3):
            ut[pl.ds(p * 128, COL3), band_at(k)] = u[p * COL3 : (p + 1) * COL3]

    loop(0, 7, finish)

    y3 = x2p
    unpack = spread_matrix((8 * PIECE, 8 * ROWS), 0, PIECE, ROWS)
    for m in range(8):
        o = m * 8 * ROWS
        first_lane = o // 128 * 128
        skip = o - first_lane
        width = -(-(skip + 8 * ROWS) // 128) * 128
        v = ut[:, pl.ds(first_lane, width)][:, skip : skip + 8 * ROWS]
        rows = lax.dot_general(unpack, v, NT, preferred_element_type=F32).astype(BF)
        for r in range(8):
            x, y, z = m // 2, m % 2 * 2 + r // 4, r % 4
            for p, at in enumerate(((z, x, y), (x, y, z), (y, x, z))):
                y3[(p,) + at] = rows[r * PIECE : (r + 1) * PIECE, p * 128 : (p + 1) * 128]

    out1 = Exchange(2, lambda p, q: y3.at[p, q], lambda p, q: y2p.at[p, q], outs)
    out2 = PlaneExchange(
        y2, lambda p, s: y0.at[:, pl.ds(al(p * THIRD + s * COL2, 128), COL2)], spot, columns, out_plane_send, out_plane_recv,
    )
    for k in (2, 1, 3):
        for p in range(3):
            out1.start(p, k)
    for p in range(3):
        out1.keep(p)
    flush(sent)
    wait_bytes(sq.at[pl.ds(0, 10)], sq_send.at[0])
    one.all_sent()
    two.all_sent()
    narrow = spread_matrix((512, COL2), 0, 128, COL3)
    for p in range(3):
        out1.arrive(p)
        for u in range(4):
            rows = [y2p[p, q, u].reshape(4 * PIECE, 128) for q in range(4)]
            rows = jnp.dot(jnp.concatenate(rows, axis=1), narrow, preferred_element_type=F32)
            y2[p, pl.ds(4 * u, 4)] = rows.astype(BF).reshape(4, PIECE, COL2)
        out2.begin(p)
    own = []
    for p in range(3):
        a, b, _ = AXES[p]
        at = (pos[a], pos[b])
        own.append(pltpu.make_async_copy(y2.at[p, spot(p, *at)], out2.dst(p, columns(p, *at)), io_sem.at[1 + p]))
        own[p].start()
        out1.left(p)
    for p in range(3):
        out2.arrive(p)
        own[p].wait()
    for p in range(3):
        out2.left(p)


def local(gradient):
    dma = pltpu.SemaphoreType.DMA
    hbm = pl.BlockSpec(memory_space=pl.ANY)
    padded = pl.pallas_call(
        kernel,
        out_shape=jax.ShapeDtypeStruct((PIECE, K), BF),
        in_specs=[hbm],
        out_specs=hbm,
        scratch_shapes=[
            pltpu.VMEM((ROWS, K), BF),
            pltpu.VMEM((3, 16, PIECE, COL2), BF),
            pltpu.VMEM((3, 16, PIECE, COL2), BF),
            pltpu.VMEM((3, 4, 4, 4, PIECE, 128), BF),
            pltpu.VMEM((2, 3, 4, 4, 4, PIECE, 128), BF),
            pltpu.VMEM((M, 384), BF),
            pltpu.VMEM((CHIP, M), BF),
            pltpu.VMEM((384, HALF_M), BF),
            pltpu.VMEM((3, 4, 4, 4, PIECE, 128), BF),
            pltpu.VMEM((3, 16, PIECE, COL2), BF),
            pltpu.VMEM((3 * 12 * 512, 128), BF),
            pltpu.VMEM((3 * 6 * 512, 128), BF),
            pltpu.VMEM((SLOTS * 512, 128), BF),
            pltpu.VMEM((3, 6, 768, 128), BF),
            pltpu.VMEM((3, 3, 384, 128), BF),
            pltpu.VMEM((3, 3, 96, 128), BF),
            pltpu.VMEM((3, 6, 384, 128), BF),
            pltpu.VMEM((3, 3, 192, 128), BF),
            pltpu.VMEM((3, 3, 48, 128), BF),
            pltpu.VMEM((15, 8, 128), F32),
            pltpu.VMEM((CHIP, M), F32),
            pltpu.VMEM((CHIP, M), BF),
            pltpu.VMEM((CHIP, M), BF),
            pltpu.VMEM((CHIP, M), BF),
            pltpu.VMEM((CHIP, M), F32),
            pltpu.VMEM((CHIP, HALF_M), BF),
            pltpu.VMEM((CHIP, HALF_M), BF),
            dma((4,)),
            dma((3,)),
            dma((3,)),
            dma((3,)),
            dma((3,)),
            dma((3,)),
            dma((3,)),
            dma((3,)),
            dma((3,)),
            dma((3,)),
            dma((3,)),
            dma((5,)),
            dma((5,)),
            dma((3,)),
            dma((3, 3, 6)),
            dma((3,)),
            dma((3, 3, 6)),
            dma((3,)),
            dma((3, 3, 6)),
            dma((3,)),
            dma((3, 3, 6)),
            dma((1,)),
            dma((4,)),
        ],
        compiler_params=pltpu.CompilerParams(
            collective_id=0, has_side_effects=True, vmem_limit_bytes=60 * 1024 * 1024
        ),
        cost_estimate=pl.CostEstimate(flops=16 * 10**9, bytes_accessed=5 * 10**6, transcendentals=0),
    )(gradient)
    return padded[:ROWS]


def solution(mesh):
    spec = P(("wide", "narrow"), None)
    return jax.shard_map(local, mesh=mesh, in_specs=(spec,), out_specs=spec, check_vma=False)
```

```python
import math

import jax
import jax.numpy as jnp
from jax import lax
from jax.experimental import pallas as pl
from jax.experimental.pallas import tpu as pltpu
from jax.sharding import PartitionSpec as P

M = 3584
K = 18432

COEFF_A = 3.4445
COEFF_B = -4.775
COEFF_C = 2.0315

MESH = pl.DeviceIdType.MESH
BF = jnp.bfloat16
F32 = jnp.float32
NT = (((1,), (1,)), ((), ()))

ROWS = 28
PIECE = 32
THIRD = K // 3
COL1 = THIRD // 4
COL2 = COL1 // 4
COL3 = COL2 // 4
CHIP = 3 * COL3
HALF_M = M // 2
AXES = ((0, 1, 2), (1, 2, 0), (2, 0, 1))

BLK = 256
NB = M // BLK
PER_PART = (12, 6)
SECOND = 3 * PER_PART[0]
SLOTS = 3 * sum(PER_PART)
SIZES = ((1536, 384, 96), (768, 192, 48))


def al(x, m=16):
    return pl.multiple_of(x, m)


def kernel(
    in_ref, y0,
    rows_in, x0, x2, x2p, x3, s_all, st,
    ut, y2p, y2,
    ta, tb, g, r1a, r2a, r3a, r1b, r2b, r3b, sq, yf, ybf, yp, yr, zf, zp, zr,
    io_sem, in_send, in_recv, in_plane_send, in_plane_recv, core_send, core_recv,
    out_send, out_recv, out_plane_send, out_plane_recv, part_send, part_recv,
    rsa_send, rsa_recv, aga_send, aga_recv, rsb_send, rsb_recv, agb_send, agb_recv, sq_send, sq_recv,
):
    fetch = pltpu.make_async_copy(in_ref, rows_in, io_sem.at[0])
    fetch.start()
    w, n_ = lax.axis_index("wide"), lax.axis_index("narrow")
    core, z_lo, y = w % 2, (w // 2) % 2, w // 4
    x, z_hi = n_ % 4, n_ // 4
    z = z_hi * 2 + z_lo
    pos = (x, y, z)

    def device(x, y, z, core):
        return ((y * 2 + z % 2) * 2 + core, (z // 2) * 4 + x)

    def shifted(axis, by):
        p = [x, y, z]
        p[axis] = (p[axis] + by) % 4
        return device(*p, core)

    right = [shifted(a, 1) for a in range(3)]
    left = [shifted(a, 3) for a in range(3)]
    across = [shifted(a, 2) for a in range(3)]
    partner = device(x, y, z, 1 - core)

    def in_plane(p, d, e):
        a, b, _ = AXES[p]
        if e == 0:
            return (right, across, left)[d - 1][a]
        if d == 0:
            return (right, across, left)[e - 1][b]
        v = [x, y, z]
        v[a] = (v[a] + d) % 4
        v[b] = (v[b] + e) % 4
        return device(*v, core)

    steps = [(d, e) for d in range(4) for e in range(4) if d or e]
    plane_devices = [[in_plane(p, d, e) for d, e in steps] for p in range(3)]
    diagonal = [plane_devices[p][k] for p in range(3) for k, (d, e) in enumerate(steps) if d and e]

    barrier = pltpu.get_barrier_semaphore()
    for d in right + left + across + diagonal + [partner]:
        pl.semaphore_signal(barrier, inc=1, device_id=d, device_id_type=MESH)

    for p in range(3):
        for q in range(16):
            x0[p, q, pl.ds(ROWS, PIECE - ROWS), :] = jnp.zeros((PIECE - ROWS, COL2), BF)
    fetch.wait()

    def load(k, carry):
        p, q = k // 4, k % 4
        v = rows_in[:, pl.ds(al(k * COL1, COL1), COL1)]
        for e in range(4):
            x0[p, q * 4 + e, pl.ds(0, ROWS), :] = v[:, e * COL2 : (e + 1) * COL2]
        return carry

    lax.fori_loop(0, 12, load, 0)
    pl.semaphore_wait(barrier, 37)

    def remote(src, dst, send, recv, dev):
        return pltpu.make_async_remote_copy(
            src_ref=src, dst_ref=dst, send_sem=send, recv_sem=recv, device_id=dev, device_id_type=MESH
        )

    def wait_bytes(ref, sem):
        pltpu.make_async_copy(ref, ref, sem).wait()

    sent = []

    def flush(group):
        for c in group:
            c.wait_send()
        group.clear()

    class Exchange:
        def __init__(self, axis_no, src, dst, sems):
            self.axis_no, self.src, self.dst = axis_no, src, dst
            self.send, self.recv = sems

        def start(self, p, k):
            a = AXES[p][self.axis_no]
            dev = (right, across, left)[k - 1][a]
            remote(self.src(p, (pos[a] + k) % 4), self.dst(p, pos[a]), self.send.at[p], self.recv.at[p], dev).start()

        def begin(self, p):
            for k in (2, 1, 3):
                self.start(p, k)

        def keep(self, p):
            me = pos[AXES[p][self.axis_no]]
            src, dst = self.src(p, me), self.dst(p, me)
            dst[...] = src[...]

        def arrive(self, p):
            wait_bytes(self.src(p, pl.ds(0, 3)), self.recv.at[p])

        def left(self, p):
            wait_bytes(self.src(p, pl.ds(0, 3)), self.send.at[p])

    def spot(p, a, b):
        return b * 4 + a if p == 2 else a * 4 + b

    class PlaneExchange:
        def __init__(self, src, dst, src_spot, dst_spot, send, recv):
            self.src, self.dst, self.src_spot, self.dst_spot = src, dst, src_spot, dst_spot
            self.send, self.recv = send, recv

        def start(self, p, k):
            a, b, _ = AXES[p]
            d, e = steps[k]
            here = self.dst(p, self.dst_spot(p, pos[a], pos[b]))
            there = self.src_spot(p, (pos[a] + d) % 4, (pos[b] + e) % 4)
            remote(self.src.at[p, there], here, self.send.at[p], self.recv.at[p], plane_devices[p][k]).start()

        def begin(self, p):
            for k in range(15):
                self.start(p, k)

        def keep(self, p):
            a, b, _ = AXES[p]
            self.dst(p, self.dst_spot(p, pos[a], pos[b]))[...] = self.src[p, self.src_spot(p, pos[a], pos[b])]

        def arrive(self, p):
            wait_bytes(self.src.at[p, pl.ds(0, 15)], self.recv.at[p])

        def left(self, p):
            wait_bytes(self.src.at[p, pl.ds(0, 15)], self.send.at[p])

    ins = (in_send, in_recv)
    outs = (out_send, out_recv)
    columns = lambda p, a, b: a * 4 + b
    in1 = PlaneExchange(x0, lambda p, s: x2.at[p, s], columns, spot, in_plane_send, in_plane_recv)
    in3 = Exchange(2, lambda p, q: x2p.at[p, q], lambda p, q: x3.at[core, p, q], ins)
    for k in range(15):
        for p in range(3):
            in1.start(p, k)

    def square(k, total):
        for e in range(4):
            v = x0[k // 4, k % 4 * 4 + e].astype(F32)
            v = v * v
            v = (v[:, :128] + v[:, 128:256]) + v[:, 256:]
            total = total + ((v[:8] + v[8:16]) + (v[16:24] + v[24:]))
        return total

    for p in range(3):
        in1.keep(p)
    sq[13] = lax.fori_loop(0, 12, square, jnp.zeros((8, 128), F32))
    sq_core = remote(sq.at[13], sq.at[14], sq_send.at[0], sq_recv.at[3], partner)
    sq_core.start()

    def iota(shape, d):
        return lax.broadcasted_iota(jnp.int32, shape, d)

    def ones_where(cond):
        return jnp.where(cond, 1.0, 0.0).astype(BF)

    def spread_matrix(shape, wide, unit, narrow):
        s, r = iota(shape, wide), iota(shape, 1 - wide)
        return ones_where((s % unit < narrow) & (r == (s // unit) * narrow + s % unit))

    widen = spread_matrix((COL2, 512), 1, 128, COL3)
    for p in range(3):
        in1.arrive(p)
        for u in range(4):
            rows = x2[p, pl.ds(4 * u, 4)].reshape(4 * PIECE, COL2)
            rows = jnp.dot(rows, widen, preferred_element_type=F32).astype(BF)
            for q in range(4):
                x2p[p, q, u] = rows[:, q * 128 : (q + 1) * 128].reshape(4, PIECE, 128)
        in3.begin(p)
    for p in range(3):
        in3.keep(p)
    pack = spread_matrix((8 * ROWS, 8 * PIECE), 1, PIECE, ROWS)
    crossing = []
    for p in range(3):
        in3.arrive(p)
        here = x3.at[core, p]
        c = remote(here, here, core_send.at[p], core_recv.at[p], partner)
        c.start()
        crossing.append(c)
        sent.append(c)


    def pack_rows(owner):
        def body(k, carry):
            x, y0, group = k // 2, k % 2 * 2, [[], [], []]
            for y in (y0, y0 + 1):
                for z in range(4):
                    group[0].append(x3[owner, 0, z, x, y])
                    group[1].append(x3[owner, 1, x, y, z])
                    group[2].append(x3[owner, 2, y, x, z])
            rows = jnp.concatenate([jnp.concatenate(e, axis=0) for e in group], axis=1)
            at = pl.ds(al(owner * HALF_M + k * 8 * ROWS), 8 * ROWS)
            s_all[at, :] = jnp.dot(pack, rows, preferred_element_type=F32).astype(BF)
            return carry

        lax.fori_loop(0, 4, lambda k, carry: body(2 * k + 1, body(2 * k, carry)), 0)

    pack_rows(core)
    for c in crossing:
        c.wait_recv()
    pack_rows(1 - core)

    def turn_all():
        kk, ll = iota((CHIP, 384), 0), iota((CHIP, 384), 1)
        pick = ones_where((ll % 128 < COL3) & (kk == (ll // 128) * COL3 + ll % 128))

        def turn(j, carry):
            at = pl.ds(al(j * BLK, BLK), BLK)
            st[:, at] = lax.dot_general(pick, s_all[at, :], NT, preferred_element_type=F32).astype(BF)
            return carry

        lax.fori_loop(0, NB // 2, lambda k, carry: turn(2 * k + 1, turn(2 * k, carry)), 0)

    def block_of(chunk, m):
        if chunk == 0:
            i = jnp.where(m < 28, m % NB, jnp.where(m < 35, 7 * core + m - 28, 4 * core))
            d = jnp.where(m < 28, 2 * core + m // NB, jnp.where(m < 35, 5, 7))
            return i, d, jnp.where(d == 0, 0.5, 1.0)
        i = jnp.where(m < 14, m, 4 * core + jnp.minimum(m, 16) - 13)
        d = jnp.where(m < 14, 4 + 2 * core, 7)
        return i, d, jnp.where((d == 7) & ((i >= 7) | (m == 17)), 0.0, 1.0)

    def gram_block(chunk, m, t):
        i, d, scale = block_of(chunk, m)
        j = (i + d) % NB
        ri = pl.ds(al(i * BLK, BLK), BLK)
        rj = pl.ds(al(j * BLK, BLK), BLK)
        acc = lax.dot_general(s_all[ri, :], s_all[rj, :], NT, preferred_element_type=F32)
        acc = (scale * acc).astype(BF)
        t[pl.ds(al(m * 512, 512), 256), :] = acc[:, :128]
        t[pl.ds(al(m * 512 + 256, 256), 256), :] = acc[:, 128:]

    def square_begin(s):
        for k, dev in enumerate((right[s], left[s], across[s])):
            remote(sq.at[4 * s], sq.at[4 * s + 1 + k], sq_send.at[0], sq_recv.at[s], dev).start()

    def square_end(s):
        wait_bytes(sq.at[pl.ds(0, 3)], sq_recv.at[s])
        sq[4 * s + 4] = (sq[4 * s] + sq[4 * s + 3]) + (sq[4 * s + 1] + sq[4 * s + 2])

    class Chunk:
        def __init__(self, no, t, bufs, rs, ag):
            self.no, self.t, self.bufs, self.rs, self.ag = no, t, bufs, rs, ag
            self.blocks = PER_PART[no]
            self.sizes = SIZES[no]
            base = [p * self.blocks * 512 for p in range(3)]
            self.bases = [base]
            for k in range(3):
                base = [base[p] + pos[AXES[p][k]] * self.sizes[k] for p in range(3)]
                self.bases.append(base)
            self.mine = no * SECOND * 512
            self.copies = {}

        def quarter(self, k, p, by):
            return self.bases[k][p] + ((pos[AXES[p][k]] + by) % 4) * self.sizes[k]

        def gram(self, p, start, count):
            for m in range(count):
                gram_block(self.no, p * self.blocks + start + m, self.t)

        def gram_far(self):
            for p in range(3):
                q = (pos[AXES[p][0]] + 2) % 4
                self.gram(p, self.blocks * q // 4, -(-self.blocks // 4))

        def gram_near(self):
            for p in range(3):
                me = pos[AXES[p][0]]
                if self.blocks % 4:
                    self.gram(p, self.blocks // 4 + self.blocks // 2 * (me // 2), 1)
                for by in (1, 3):
                    self.gram(p, (self.blocks * ((me + by) % 4) + 2) // 4, self.blocks // 4)

        def gram_own(self):
            for p in range(3):
                self.gram(p, (self.blocks * pos[AXES[p][0]] + 2) // 4, self.blocks // 4)

        def push(self, k, p, no, off, rows):
            a = AXES[p][k]
            c = remote(
                self.t.at[pl.ds(al(off), rows), :],
                self.bufs[k].at[p, no],
                self.rs[0].at[k],
                self.rs[1].at[k, p, no],
                right[a] if no < 3 else left[a],
            )
            c.start()
            self.copies[k, p, no] = c

        def add_rows(self, off, rows, srcs):
            step = rows // 2 if rows > 200 else rows
            t = self.t

            def body(m, carry):
                at = pl.ds(al(off + m * step), step)
                total = t[at, :]
                for src in srcs:
                    total = total + src[pl.ds(al(m * step), step), :]
                t[at, :] = total
                return carry

            lax.fori_loop(0, rows // step, body, 0)

        def scatter_far(self, k):
            half = self.sizes[k] // 2
            for p in range(3):
                self.push(k, p, 0, self.quarter(k, p, 2), half)
                self.push(k, p, 3, self.quarter(k, p, 2) + half, half)

        def scatter_near(self, k):
            half = self.sizes[k] // 2
            for p in range(3):
                self.push(k, p, 1, self.quarter(k, p, 1) + half, half)
                self.push(k, p, 4, self.quarter(k, p, 3), half)

        def scatter_mid(self, k):
            half = self.sizes[k] // 2
            for p in range(3):
                self.copies[k, p, 0].wait_recv()
                self.add_rows(self.quarter(k, p, 1), half, [self.bufs[k].at[p, 0]])
                self.push(k, p, 2, self.quarter(k, p, 1), half)
                self.copies[k, p, 3].wait_recv()
                self.add_rows(self.quarter(k, p, 3) + half, half, [self.bufs[k].at[p, 3]])
                self.push(k, p, 5, self.quarter(k, p, 3) + half, half)

        def scatter_end(self, k):
            half = self.sizes[k] // 2
            for p in range(3):
                for h, one, two in ((0, 4, 2), (1, 1, 5)):
                    self.copies[k, p, one].wait_recv()
                    self.copies[k, p, two].wait_recv()
                    self.add_rows(
                        self.quarter(k, p, 0) + h * half, half, [self.bufs[k].at[p, one], self.bufs[k].at[p, two]]
                    )

        def ring_begin(self, s):
            size = self.sizes[s]
            for k, dev in ((2, across), (1, right), (3, left)):
                for p in range(3):
                    remote(
                        self.t.at[pl.ds(al(self.quarter(s, p, k)), size), :],
                        self.bufs[s].at[p, k - 1],
                        self.rs[0].at[s],
                        self.rs[1].at[s, p, 0],
                        dev[AXES[p][s]],
                    ).start()

        def ring_end(self, s):
            size = self.sizes[s]
            for p in range(3):
                wait_bytes(self.t.at[pl.ds(0, 3 * size), :], self.rs[1].at[s, p, 0])
                off = self.bases[s + 1][p]
                step = min(size, 96)

                def body(m, carry):
                    at = pl.ds(al(off + m * step), step)
                    total = self.t[at, :].astype(F32)
                    for k in range(3):
                        total = total + self.bufs[s][p, k, pl.ds(al(m * step), step)].astype(F32)
                    if s == 2:
                        g[pl.ds(al(self.mine + off), size), :] = total.astype(BF)
                    else:
                        self.t[at, :] = total.astype(BF)
                    return carry

                lax.fori_loop(0, size // step, body, 0)
            if s == 2:
                self.rounds(2)

        def rounds(self, s):
            for k, dev in ((2, across), (1, right), (3, left)):
                for p in range(3):
                    self.spread(s, p, 0, self.bases[s + 1][p], self.sizes[s], dev[AXES[p][s]])

        def rounds_end(self, s):
            for p in range(3):
                wait_bytes(self.t.at[pl.ds(0, 3 * self.sizes[s]), :], self.ag[1].at[s, p, 0])

        def all_sent(self):
            for s in range(3):
                for sems in (self.rs, self.ag):
                    wait_bytes(self.t.at[pl.ds(0, 9 * self.sizes[s]), :], sems[0].at[s])

        def spread(self, k, p, no, off, rows, dev):
            here = g.at[pl.ds(al(self.mine + off), rows), :]
            c = remote(here, here, self.ag[0].at[k], self.ag[1].at[k, p, min(no, 2)], dev)
            c.start()
            self.copies["g", k, p, no] = c

        def got(self, k, p, *nos):
            for no in nos:
                self.copies["g", k, p, no].wait_recv()

        def gather_begin(self, k):
            half = self.sizes[k] // 2
            for p in range(3):
                own = self.quarter(k, p, 0)
                a = AXES[p][k]
                self.spread(k, p, 0, own, half, right[a])
                self.spread(k, p, 1, own + half, half, left[a])
            for p in range(3):
                own = self.quarter(k, p, 0)
                a = AXES[p][k]
                self.spread(k, p, 2, own + half, half, right[a])
                self.spread(k, p, 3, own, half, left[a])

        def gather_mid(self, k):
            half = self.sizes[k] // 2
            for p in range(3):
                a = AXES[p][k]
                self.got(k, p, 0)
                self.spread(k, p, 4, self.quarter(k, p, 3), half, right[a])
                self.got(k, p, 1)
                self.spread(k, p, 5, self.quarter(k, p, 1) + half, half, left[a])

        def gather_end(self, k):
            for p in range(3):
                wait_bytes(self.t.at[pl.ds(0, 2 * self.sizes[k]), :], self.ag[1].at[k, p, 2])

    one = Chunk(0, ta, (r1a, r2a, r3a), (rsa_send, rsa_recv), (aga_send, aga_recv))
    two = Chunk(1, tb, (r1b, r2b, r3b), (rsb_send, rsb_recv), (agb_send, agb_recv))

    one.gram_far()
    one.scatter_far(0)
    one.gram_near()
    one.scatter_near(0)
    two.gram_far()
    one.gram_own()
    one.scatter_mid(0)
    two.scatter_far(0)
    two.gram_near()
    two.scatter_near(0)
    two.gram_own()
    sq_core.wait_recv()
    sq[0] = sq[13] + sq[14]
    square_begin(0)
    turn_all()
    for p in range(3):
        in1.left(p)
        in3.left(p)
    one.scatter_end(0)
    one.ring_begin(1)
    square_end(0)
    square_begin(1)
    two.scatter_mid(0)
    one.ring_end(1)
    one.ring_begin(2)
    square_end(1)
    square_begin(2)
    two.scatter_end(0)
    two.ring_begin(1)
    one.ring_end(2)
    square_end(2)
    two.ring_end(1)
    two.ring_begin(2)
    one.rounds_end(2)
    one.rounds(1)
    two.ring_end(2)
    one.rounds_end(1)
    one.gather_begin(0)
    two.rounds_end(2)
    two.rounds(1)
    one.gather_mid(0)
    two.rounds_end(1)
    two.gather_begin(0)
    one.gather_end(0)

    def cols(a_ref, i):
        return a_ref[:, pl.ds(al(i * BLK, BLK), BLK)]

    def block(slot):
        o = slot * 512
        return jnp.concatenate([g[pl.ds(al(o, 512), 256), :], g[pl.ds(al(o + 256, 256), 256), :]], axis=1)

    def band(a_ref, j, ds):
        def straight(d, first):
            i = (j + NB - d) % NB
            return cols(a_ref, i), block(first + i)

        def turned(d, first):
            return cols(a_ref, (j + d) % NB), block(first + j)

        a, b = zip(*[straight(*e) for e in ds])
        acc = jnp.dot(jnp.concatenate(a, axis=1), jnp.concatenate(b, axis=0), preferred_element_type=F32)
        a, b = zip(*[turned(*e) for e in ds])
        return acc + lax.dot_general(
            jnp.concatenate(a, axis=1), jnp.concatenate(b, axis=1), NT, preferred_element_type=F32
        )

    whole_one = ((2 * core, 0), (2 * core + 1, NB))
    whole_two = ((2 * core + 4, SECOND),)

    def single(acc_ref, a_ref, chunk, m):
        i, d, _ = block_of(chunk, m)
        j = (i + d) % NB
        b = block(chunk * SECOND + m)
        acc_ref[:, pl.ds(al(j * BLK, BLK), BLK)] += jnp.dot(cols(a_ref, i), b, preferred_element_type=F32)
        acc_ref[:, pl.ds(al(i * BLK, BLK), BLK)] += lax.dot_general(
            cols(a_ref, j), b, NT, preferred_element_type=F32
        )

    def loop(first_k, last_k, f):
        def body(k, carry):
            f(first_k + 2 * k)
            f(first_k + 2 * k + 1)
            return carry

        lax.fori_loop(0, (last_k - first_k) // 2, body, 0)
        if (last_k - first_k) % 2:
            f(last_k - 1)

    def band_at(j):
        return pl.ds(al(j * BLK, BLK), BLK)

    def to_partner(no, src, dst):
        c = remote(src, dst, part_send.at[no], part_recv.at[no], partner)
        c.start()
        sent.append(c)
        return c

    def y_one(j):
        yf[:, band_at(j)] = band(st, j, whole_one)

    def shared(acc_ref, a_ref):
        return lambda m: single(acc_ref, a_ref, 0, 28 + m), lambda m: single(acc_ref, a_ref, 1, 14 + m)

    y_first, y_rest = shared(yf, st)
    loop(0, 4, y_one)
    two.gather_mid(0)
    loop(4, NB, y_one)
    zf[...] = jnp.zeros((CHIP, M), F32)
    loop(0, 8, y_first)
    two.gather_end(0)
    loop(0, 3, y_rest)

    def y_two(j):
        v = yf[:, band_at(j)] + band(st, j, whole_two)
        yf[:, band_at(j)] = v
        yp[:, band_at(j)] = v.astype(BF)

    shares = []
    for lo, hi in ((0, 4), (4, 8), (8, 12), (12, 14)):
        loop(lo, hi, y_two)
        here = pl.ds(lo * BLK, (hi - lo) * BLK)
        shares.append((lo, hi, to_partner(len(shares), yp.at[:, here], yr.at[:, here])))

    factor = 0.3 * math.sqrt(M) / (jnp.sqrt(jnp.sum(sq[12], axis=(0, 1), keepdims=True)) + 1e-07)
    factor2 = factor * factor

    def y_sum(j):
        v = factor2 * (yf[:, band_at(j)] + yr[:, band_at(j)].astype(F32))
        yf[:, band_at(j)] = v
        ybf[:, band_at(j)] = v.astype(BF)

    for lo, hi, arriving in shares:
        arriving.wait_recv()
        loop(lo, hi, y_sum)

    z_first, z_rest = shared(zf, ybf)
    loop(0, 8, z_first)
    loop(0, 3, z_rest)

    def z_band(j):
        return factor2 * (zf[:, band_at(j)] + band(ybf, j, whole_one + whole_two))

    def z_theirs(k):
        zp[:, band_at(k)] = z_band((1 - core) * 7 + k).astype(BF)

    loop(0, 7, z_theirs)
    share = to_partner(4, zp, zr)

    def z_mine(k):
        zf[:, band_at(core * 7 + k)] = z_band(core * 7 + k)

    loop(0, 7, z_mine)
    share.wait_recv()
    for p in range(3):
        ut[pl.ds(p * 128 + COL3, 128 - COL3), :] = jnp.zeros((128 - COL3, HALF_M), BF)

    def finish(k):
        at = band_at(core * 7 + k)
        scaled = (factor * st[:, at].astype(F32)).astype(BF).astype(F32)
        product = factor * (COEFF_B * yf[:, at] + COEFF_C * (zf[:, at] + zr[:, band_at(k)].astype(F32)))
        u = (math.sqrt(K) * (COEFF_A * scaled + product)).astype(BF)
        for p in range(3):
            ut[pl.ds(p * 128, COL3), band_at(k)] = u[p * COL3 : (p + 1) * COL3]

    loop(0, 7, finish)

    y3 = x2p
    unpack = spread_matrix((8 * PIECE, 8 * ROWS), 0, PIECE, ROWS)
    for m in range(8):
        o = m * 8 * ROWS
        first_lane = o // 128 * 128
        skip = o - first_lane
        width = -(-(skip + 8 * ROWS) // 128) * 128
        v = ut[:, pl.ds(first_lane, width)][:, skip : skip + 8 * ROWS]
        rows = lax.dot_general(unpack, v, NT, preferred_element_type=F32).astype(BF)
        for r in range(8):
            x, y, z = m // 2, m % 2 * 2 + r // 4, r % 4
            for p, at in enumerate(((z, x, y), (x, y, z), (y, x, z))):
                y3[(p,) + at] = rows[r * PIECE : (r + 1) * PIECE, p * 128 : (p + 1) * 128]

    out1 = Exchange(2, lambda p, q: y3.at[p, q], lambda p, q: y2p.at[p, q], outs)
    out2 = PlaneExchange(
        y2, lambda p, s: y0.at[:, pl.ds(al(p * THIRD + s * COL2, 128), COL2)], spot, columns, out_plane_send, out_plane_recv,
    )
    for k in (2, 1, 3):
        for p in range(3):
            out1.start(p, k)
    for p in range(3):
        out1.keep(p)
    flush(sent)
    wait_bytes(sq.at[pl.ds(0, 10)], sq_send.at[0])
    one.all_sent()
    two.all_sent()
    narrow = spread_matrix((512, COL2), 0, 128, COL3)
    for p in range(3):
        out1.arrive(p)
        for u in range(4):
            rows = [y2p[p, q, u].reshape(4 * PIECE, 128) for q in range(4)]
            rows = jnp.dot(jnp.concatenate(rows, axis=1), narrow, preferred_element_type=F32)
            y2[p, pl.ds(4 * u, 4)] = rows.astype(BF).reshape(4, PIECE, COL2)
        out2.begin(p)
    own = []
    for p in range(3):
        a, b, _ = AXES[p]
        at = (pos[a], pos[b])
        own.append(pltpu.make_async_copy(y2.at[p, spot(p, *at)], out2.dst(p, columns(p, *at)), io_sem.at[1 + p]))
        own[p].start()
        out1.left(p)
    for p in range(3):
        out2.arrive(p)
        own[p].wait()
    for p in range(3):
        out2.left(p)


def local(gradient):
    dma = pltpu.SemaphoreType.DMA
    hbm = pl.BlockSpec(memory_space=pl.ANY)
    padded = pl.pallas_call(
        kernel,
        out_shape=jax.ShapeDtypeStruct((PIECE, K), BF),
        in_specs=[hbm],
        out_specs=hbm,
        scratch_shapes=[
            pltpu.VMEM((ROWS, K), BF),
            pltpu.VMEM((3, 16, PIECE, COL2), BF),
            pltpu.VMEM((3, 16, PIECE, COL2), BF),
            pltpu.VMEM((3, 4, 4, 4, PIECE, 128), BF),
            pltpu.VMEM((2, 3, 4, 4, 4, PIECE, 128), BF),
            pltpu.VMEM((M, 384), BF),
            pltpu.VMEM((CHIP, M), BF),
            pltpu.VMEM((384, HALF_M), BF),
            pltpu.VMEM((3, 4, 4, 4, PIECE, 128), BF),
            pltpu.VMEM((3, 16, PIECE, COL2), BF),
            pltpu.VMEM((3 * 12 * 512, 128), BF),
            pltpu.VMEM((3 * 6 * 512, 128), BF),
            pltpu.VMEM((SLOTS * 512, 128), BF),
            pltpu.VMEM((3, 6, 768, 128), BF),
            pltpu.VMEM((3, 3, 384, 128), BF),
            pltpu.VMEM((3, 3, 96, 128), BF),
            pltpu.VMEM((3, 6, 384, 128), BF),
            pltpu.VMEM((3, 3, 192, 128), BF),
            pltpu.VMEM((3, 3, 48, 128), BF),
            pltpu.VMEM((15, 8, 128), F32),
            pltpu.VMEM((CHIP, M), F32),
            pltpu.VMEM((CHIP, M), BF),
            pltpu.VMEM((CHIP, M), BF),
            pltpu.VMEM((CHIP, M), BF),
            pltpu.VMEM((CHIP, M), F32),
            pltpu.VMEM((CHIP, HALF_M), BF),
            pltpu.VMEM((CHIP, HALF_M), BF),
            dma((4,)),
            dma((3,)),
            dma((3,)),
            dma((3,)),
            dma((3,)),
            dma((3,)),
            dma((3,)),
            dma((3,)),
            dma((3,)),
            dma((3,)),
            dma((3,)),
            dma((5,)),
            dma((5,)),
            dma((3,)),
            dma((3, 3, 6)),
            dma((3,)),
            dma((3, 3, 6)),
            dma((3,)),
            dma((3, 3, 6)),
            dma((3,)),
            dma((3, 3, 6)),
            dma((1,)),
            dma((4,)),
        ],
        compiler_params=pltpu.CompilerParams(
            collective_id=0, has_side_effects=True, vmem_limit_bytes=60 * 1024 * 1024
        ),
        cost_estimate=pl.CostEstimate(flops=16 * 10**9, bytes_accessed=5 * 10**6, transcendentals=0),
    )(gradient)
    return padded[:ROWS]


def solution(mesh):
    spec = P(("wide", "narrow"), None)
    return jax.shard_map(local, mesh=mesh, in_specs=(spec,), out_specs=spec, check_vma=False)
```

```python
import math

import jax
import jax.numpy as jnp
from jax import lax
from jax.experimental import pallas as pl
from jax.experimental.pallas import tpu as pltpu
from jax.sharding import PartitionSpec as P

M = 3584
K = 18432

COEFF_A = 3.4445
COEFF_B = -4.775
COEFF_C = 2.0315

MESH = pl.DeviceIdType.MESH
BF = jnp.bfloat16
F32 = jnp.float32
NT = (((1,), (1,)), ((), ()))

ROWS = 28
PIECE = 32
THIRD = K // 3
COL1 = THIRD // 4
COL2 = COL1 // 4
COL3 = COL2 // 4
CHIP = 3 * COL3
HALF_M = M // 2
AXES = ((0, 1, 2), (1, 2, 0), (2, 0, 1))

BLK = 256
NB = M // BLK
PER_PART = (12, 6)
SECOND = 3 * PER_PART[0]
SLOTS = 3 * sum(PER_PART)
SIZES = ((1536, 384, 96), (768, 192, 48))


def al(x, m=16):
    return pl.multiple_of(x, m)


def kernel(
    in_ref, y0,
    rows_in, x0, x2, x2p, x3, s_all, st,
    ut, y2p, y2,
    ta, tb, g, r1a, r2a, r3a, r1b, r2b, r3b, sq, yf, ybf, yp, yr, zf, zp, zr,
    io_sem, in_send, in_recv, in_plane_send, in_plane_recv, core_send, core_recv,
    out_send, out_recv, out_plane_send, out_plane_recv, part_send, part_recv,
    rsa_send, rsa_recv, aga_send, aga_recv, rsb_send, rsb_recv, agb_send, agb_recv, sq_send, sq_recv,
):
    fetch = pltpu.make_async_copy(in_ref, rows_in, io_sem.at[0])
    fetch.start()
    w, n_ = lax.axis_index("wide"), lax.axis_index("narrow")
    core, z_lo, y = w % 2, (w // 2) % 2, w // 4
    x, z_hi = n_ % 4, n_ // 4
    z = z_hi * 2 + z_lo
    pos = (x, y, z)

    def device(x, y, z, core):
        return ((y * 2 + z % 2) * 2 + core, (z // 2) * 4 + x)

    def shifted(axis, by):
        p = [x, y, z]
        p[axis] = (p[axis] + by) % 4
        return device(*p, core)

    right = [shifted(a, 1) for a in range(3)]
    left = [shifted(a, 3) for a in range(3)]
    across = [shifted(a, 2) for a in range(3)]
    partner = device(x, y, z, 1 - core)

    def in_plane(p, d, e):
        a, b, _ = AXES[p]
        if e == 0:
            return (right, across, left)[d - 1][a]
        if d == 0:
            return (right, across, left)[e - 1][b]
        v = [x, y, z]
        v[a] = (v[a] + d) % 4
        v[b] = (v[b] + e) % 4
        return device(*v, core)

    steps = [(d, e) for d in (2, 1, 3, 0) for e in (2, 1, 3, 0) if d or e]
    plane_devices = [[in_plane(p, d, e) for d, e in steps] for p in range(3)]
    diagonal = [plane_devices[p][k] for p in range(3) for k, (d, e) in enumerate(steps) if d and e]

    barrier = pltpu.get_barrier_semaphore()
    for d in right + left + across + diagonal + [partner]:
        pl.semaphore_signal(barrier, inc=1, device_id=d, device_id_type=MESH)

    for p in range(3):
        for q in range(16):
            x0[p, q, pl.ds(ROWS, PIECE - ROWS), :] = jnp.zeros((PIECE - ROWS, COL2), BF)
    fetch.wait()

    def load(k, carry):
        p, q = k // 4, k % 4
        v = rows_in[:, pl.ds(al(k * COL1, COL1), COL1)]
        for e in range(4):
            x0[p, q * 4 + e, pl.ds(0, ROWS), :] = v[:, e * COL2 : (e + 1) * COL2]
        return carry

    lax.fori_loop(0, 12, load, 0)
    pl.semaphore_wait(barrier, 37)

    def remote(src, dst, send, recv, dev):
        return pltpu.make_async_remote_copy(
            src_ref=src, dst_ref=dst, send_sem=send, recv_sem=recv, device_id=dev, device_id_type=MESH
        )

    def wait_bytes(ref, sem):
        pltpu.make_async_copy(ref, ref, sem).wait()

    sent = []

    def flush(group):
        for c in group:
            c.wait_send()
        group.clear()

    class Exchange:
        def __init__(self, axis_no, src, dst, sems):
            self.axis_no, self.src, self.dst = axis_no, src, dst
            self.send, self.recv = sems

        def start(self, p, k):
            a = AXES[p][self.axis_no]
            dev = (right, across, left)[k - 1][a]
            remote(self.src(p, (pos[a] + k) % 4), self.dst(p, pos[a]), self.send.at[p], self.recv.at[p], dev).start()

        def begin(self, p):
            for k in (2, 1, 3):
                self.start(p, k)

        def keep(self, p):
            me = pos[AXES[p][self.axis_no]]
            src, dst = self.src(p, me), self.dst(p, me)
            dst[...] = src[...]

        def arrive(self, p):
            wait_bytes(self.src(p, pl.ds(0, 3)), self.recv.at[p])

        def left(self, p):
            wait_bytes(self.src(p, pl.ds(0, 3)), self.send.at[p])

    def spot(p, a, b):
        return b * 4 + a if p == 2 else a * 4 + b

    class PlaneExchange:
        def __init__(self, src, dst, src_spot, dst_spot, send, recv):
            self.src, self.dst, self.src_spot, self.dst_spot = src, dst, src_spot, dst_spot
            self.send, self.recv = send, recv

        def start(self, p, k):
            a, b, _ = AXES[p]
            d, e = steps[k]
            here = self.dst(p, self.dst_spot(p, pos[a], pos[b]))
            there = self.src_spot(p, (pos[a] + d) % 4, (pos[b] + e) % 4)
            remote(self.src.at[p, there], here, self.send.at[p], self.recv.at[p], plane_devices[p][k]).start()

        def begin(self, p):
            for k in range(15):
                self.start(p, k)

        def keep(self, p):
            a, b, _ = AXES[p]
            self.dst(p, self.dst_spot(p, pos[a], pos[b]))[...] = self.src[p, self.src_spot(p, pos[a], pos[b])]

        def arrive(self, p):
            wait_bytes(self.src.at[p, pl.ds(0, 15)], self.recv.at[p])

        def left(self, p):
            wait_bytes(self.src.at[p, pl.ds(0, 15)], self.send.at[p])

    ins = (in_send, in_recv)
    outs = (out_send, out_recv)
    columns = lambda p, a, b: a * 4 + b
    in1 = PlaneExchange(x0, lambda p, s: x2.at[p, s], columns, spot, in_plane_send, in_plane_recv)
    in3 = Exchange(2, lambda p, q: x2p.at[p, q], lambda p, q: x3.at[core, p, q], ins)
    for k in range(15):
        for p in range(3):
            in1.start(p, k)

    def square(k, total):
        for e in range(4):
            v = x0[k // 4, k % 4 * 4 + e].astype(F32)
            v = v * v
            v = (v[:, :128] + v[:, 128:256]) + v[:, 256:]
            total = total + ((v[:8] + v[8:16]) + (v[16:24] + v[24:]))
        return total

    for p in range(3):
        in1.keep(p)
    sq[13] = lax.fori_loop(0, 12, square, jnp.zeros((8, 128), F32))
    sq_core = remote(sq.at[13], sq.at[14], sq_send.at[0], sq_recv.at[3], partner)
    sq_core.start()

    def iota(shape, d):
        return lax.broadcasted_iota(jnp.int32, shape, d)

    def ones_where(cond):
        return jnp.where(cond, 1.0, 0.0).astype(BF)

    def spread_matrix(shape, wide, unit, narrow):
        s, r = iota(shape, wide), iota(shape, 1 - wide)
        return ones_where((s % unit < narrow) & (r == (s // unit) * narrow + s % unit))

    widen = spread_matrix((COL2, 512), 1, 128, COL3)
    for p in range(3):
        in1.arrive(p)
        for u in range(4):
            rows = x2[p, pl.ds(4 * u, 4)].reshape(4 * PIECE, COL2)
            rows = jnp.dot(rows, widen, preferred_element_type=F32).astype(BF)
            for q in range(4):
                x2p[p, q, u] = rows[:, q * 128 : (q + 1) * 128].reshape(4, PIECE, 128)
        in3.begin(p)
    for p in range(3):
        in3.keep(p)
    pack = spread_matrix((8 * ROWS, 8 * PIECE), 1, PIECE, ROWS)
    crossing = []
    for p in range(3):
        in3.arrive(p)
        here = x3.at[core, p]
        c = remote(here, here, core_send.at[p], core_recv.at[p], partner)
        c.start()
        crossing.append(c)
        sent.append(c)


    def pack_rows(owner):
        def body(k, carry):
            x, y0, group = k // 2, k % 2 * 2, [[], [], []]
            for y in (y0, y0 + 1):
                for z in range(4):
                    group[0].append(x3[owner, 0, z, x, y])
                    group[1].append(x3[owner, 1, x, y, z])
                    group[2].append(x3[owner, 2, y, x, z])
            rows = jnp.concatenate([jnp.concatenate(e, axis=0) for e in group], axis=1)
            at = pl.ds(al(owner * HALF_M + k * 8 * ROWS), 8 * ROWS)
            s_all[at, :] = jnp.dot(pack, rows, preferred_element_type=F32).astype(BF)
            return carry

        lax.fori_loop(0, 4, lambda k, carry: body(2 * k + 1, body(2 * k, carry)), 0)

    pack_rows(core)
    for c in crossing:
        c.wait_recv()
    pack_rows(1 - core)

    def turn_all():
        kk, ll = iota((CHIP, 384), 0), iota((CHIP, 384), 1)
        pick = ones_where((ll % 128 < COL3) & (kk == (ll // 128) * COL3 + ll % 128))

        def turn(j, carry):
            at = pl.ds(al(j * BLK, BLK), BLK)
            st[:, at] = lax.dot_general(pick, s_all[at, :], NT, preferred_element_type=F32).astype(BF)
            return carry

        lax.fori_loop(0, NB // 2, lambda k, carry: turn(2 * k + 1, turn(2 * k, carry)), 0)

    def block_of(chunk, m):
        if chunk == 0:
            i = jnp.where(m < 28, m % NB, jnp.where(m < 35, 7 * core + m - 28, 4 * core))
            d = jnp.where(m < 28, 2 * core + m // NB, jnp.where(m < 35, 5, 7))
            return i, d, jnp.where(d == 0, 0.5, 1.0)
        i = jnp.where(m < 14, m, 4 * core + jnp.minimum(m, 16) - 13)
        d = jnp.where(m < 14, 4 + 2 * core, 7)
        return i, d, jnp.where((d == 7) & ((i >= 7) | (m == 17)), 0.0, 1.0)

    def gram_block(chunk, m, t):
        i, d, scale = block_of(chunk, m)
        j = (i + d) % NB
        ri = pl.ds(al(i * BLK, BLK), BLK)
        rj = pl.ds(al(j * BLK, BLK), BLK)
        acc = lax.dot_general(s_all[ri, :], s_all[rj, :], NT, preferred_element_type=F32)
        acc = (scale * acc).astype(BF)
        t[pl.ds(al(m * 512, 512), 256), :] = acc[:, :128]
        t[pl.ds(al(m * 512 + 256, 256), 256), :] = acc[:, 128:]

    def square_begin(s):
        for k, dev in enumerate((right[s], left[s], across[s])):
            remote(sq.at[4 * s], sq.at[4 * s + 1 + k], sq_send.at[0], sq_recv.at[s], dev).start()

    def square_end(s):
        wait_bytes(sq.at[pl.ds(0, 3)], sq_recv.at[s])
        sq[4 * s + 4] = (sq[4 * s] + sq[4 * s + 3]) + (sq[4 * s + 1] + sq[4 * s + 2])

    class Chunk:
        def __init__(self, no, t, bufs, rs, ag):
            self.no, self.t, self.bufs, self.rs, self.ag = no, t, bufs, rs, ag
            self.blocks = PER_PART[no]
            self.sizes = SIZES[no]
            self.size0 = self.sizes[0]
            base = [p * self.blocks * 512 for p in range(3)]
            self.bases = [base]
            for k in range(3):
                base = [base[p] + pos[AXES[p][k]] * self.sizes[k] for p in range(3)]
                self.bases.append(base)
            self.mine = no * SECOND * 512
            self.copies = {}

        def quarter(self, k, p, by):
            return self.bases[k][p] + ((pos[AXES[p][k]] + by) % 4) * self.sizes[k]

        def gram(self, p, start, count):
            for m in range(count):
                gram_block(self.no, p * self.blocks + start + m, self.t)

        def gram_far(self, p):
            q = (pos[AXES[p][0]] + 2) % 4
            self.gram(p, self.blocks * q // 4, -(-self.blocks // 4))

        def gram_near(self, p):
            me = pos[AXES[p][0]]
            if self.blocks % 4:
                self.gram(p, self.blocks // 4 + self.blocks // 2 * (me // 2), 1)
            for by in (1, 3):
                self.gram(p, (self.blocks * ((me + by) % 4) + 2) // 4, self.blocks // 4)

        def gram_own(self):
            for p in range(3):
                self.gram(p, (self.blocks * pos[AXES[p][0]] + 2) // 4, self.blocks // 4)

        def push(self, k, p, no, off, rows):
            a = AXES[p][k]
            c = remote(
                self.t.at[pl.ds(al(off), rows), :],
                self.bufs[k].at[p, no],
                self.rs[0].at[k],
                self.rs[1].at[k, p, no],
                right[a] if no < 3 else left[a],
            )
            c.start()
            self.copies[k, p, no] = c

        def add_rows(self, off, rows, srcs):
            step = rows // 2 if rows > 200 else rows
            t = self.t

            def body(m, carry):
                at = pl.ds(al(off + m * step), step)
                total = t[at, :]
                for src in srcs:
                    total = total + src[pl.ds(al(m * step), step), :]
                t[at, :] = total
                return carry

            lax.fori_loop(0, rows // step, body, 0)

        def scatter_far(self, p):
            half = self.size0 // 2
            self.push(0, p, 0, self.quarter(0, p, 2), half)
            self.push(0, p, 3, self.quarter(0, p, 2) + half, half)

        def scatter_near(self, p):
            half = self.size0 // 2
            self.push(0, p, 1, self.quarter(0, p, 1) + half, half)
            self.push(0, p, 4, self.quarter(0, p, 3), half)

        def scatter_mid(self, k):
            half = self.sizes[k] // 2
            for p in range(3):
                self.copies[k, p, 0].wait_recv()
                self.add_rows(self.quarter(k, p, 1), half, [self.bufs[k].at[p, 0]])
                self.push(k, p, 2, self.quarter(k, p, 1), half)
                self.copies[k, p, 3].wait_recv()
                self.add_rows(self.quarter(k, p, 3) + half, half, [self.bufs[k].at[p, 3]])
                self.push(k, p, 5, self.quarter(k, p, 3) + half, half)

        def scatter_end(self, k):
            half = self.sizes[k] // 2
            for p in range(3):
                for h, one, two in ((0, 4, 2), (1, 1, 5)):
                    self.copies[k, p, one].wait_recv()
                    self.copies[k, p, two].wait_recv()
                    self.add_rows(
                        self.quarter(k, p, 0) + h * half, half, [self.bufs[k].at[p, one], self.bufs[k].at[p, two]]
                    )

        def ring_begin(self, s):
            size = self.sizes[s]
            for k, dev in ((2, across), (1, right), (3, left)):
                for p in range(3):
                    remote(
                        self.t.at[pl.ds(al(self.quarter(s, p, k)), size), :],
                        self.bufs[s].at[p, k - 1],
                        self.rs[0].at[s],
                        self.rs[1].at[s, p, 0],
                        dev[AXES[p][s]],
                    ).start()

        def ring_end(self, s):
            size = self.sizes[s]
            for p in range(3):
                wait_bytes(self.t.at[pl.ds(0, 3 * size), :], self.rs[1].at[s, p, 0])
                off = self.bases[s + 1][p]
                step = min(size, 96)

                def body(m, carry):
                    at = pl.ds(al(off + m * step), step)
                    total = self.t[at, :].astype(F32)
                    for k in range(3):
                        total = total + self.bufs[s][p, k, pl.ds(al(m * step), step)].astype(F32)
                    if s == 2:
                        g[pl.ds(al(self.mine + off), size), :] = total.astype(BF)
                    else:
                        self.t[at, :] = total.astype(BF)
                    return carry

                lax.fori_loop(0, size // step, body, 0)
            if s == 2:
                self.rounds(2)

        def rounds(self, s):
            for k, dev in ((2, across), (1, right), (3, left)):
                for p in range(3):
                    self.spread(s, p, 0, self.bases[s + 1][p], self.sizes[s], dev[AXES[p][s]])

        def rounds_end(self, s):
            for p in range(3):
                wait_bytes(self.t.at[pl.ds(0, 3 * self.sizes[s]), :], self.ag[1].at[s, p, 0])

        def all_sent(self):
            for s in range(3):
                for sems in (self.rs, self.ag):
                    wait_bytes(self.t.at[pl.ds(0, 9 * self.sizes[s]), :], sems[0].at[s])

        def spread(self, k, p, no, off, rows, dev):
            here = g.at[pl.ds(al(self.mine + off), rows), :]
            c = remote(here, here, self.ag[0].at[k], self.ag[1].at[k, p, min(no, 2)], dev)
            c.start()
            self.copies["g", k, p, no] = c

        def got(self, k, p, *nos):
            for no in nos:
                self.copies["g", k, p, no].wait_recv()

        def gather_begin(self, k):
            half = self.sizes[k] // 2
            for p in range(3):
                own = self.quarter(k, p, 0)
                a = AXES[p][k]
                self.spread(k, p, 0, own, half, right[a])
                self.spread(k, p, 1, own + half, half, left[a])
            for p in range(3):
                own = self.quarter(k, p, 0)
                a = AXES[p][k]
                self.spread(k, p, 2, own + half, half, right[a])
                self.spread(k, p, 3, own, half, left[a])

        def gather_mid(self, k):
            half = self.sizes[k] // 2
            for p in range(3):
                a = AXES[p][k]
                self.got(k, p, 0)
                self.spread(k, p, 4, self.quarter(k, p, 3), half, right[a])
                self.got(k, p, 1)
                self.spread(k, p, 5, self.quarter(k, p, 1) + half, half, left[a])

        def gather_end(self, k):
            for p in range(3):
                wait_bytes(self.t.at[pl.ds(0, 2 * self.sizes[k]), :], self.ag[1].at[k, p, 2])

    one = Chunk(0, ta, (r1a, r2a, r3a), (rsa_send, rsa_recv), (aga_send, aga_recv))
    two = Chunk(1, tb, (r1b, r2b, r3b), (rsb_send, rsb_recv), (agb_send, agb_recv))

    for p in range(3):
        one.gram_far(p)
        one.scatter_far(p)
    for p in range(3):
        one.gram_near(p)
        one.scatter_near(p)
    for p in range(3):
        two.gram_far(p)
    one.gram_own()
    one.scatter_mid(0)
    for p in range(3):
        two.scatter_far(p)
    for p in range(3):
        two.gram_near(p)
        two.scatter_near(p)
    two.gram_own()
    sq_core.wait_recv()
    sq[0] = sq[13] + sq[14]
    square_begin(0)
    turn_all()
    for p in range(3):
        in1.left(p)
        in3.left(p)
    one.scatter_end(0)
    one.ring_begin(1)
    square_end(0)
    square_begin(1)
    two.scatter_mid(0)
    one.ring_end(1)
    one.ring_begin(2)
    square_end(1)
    square_begin(2)
    two.scatter_end(0)
    two.ring_begin(1)
    one.ring_end(2)
    square_end(2)
    two.ring_end(1)
    two.ring_begin(2)
    one.rounds_end(2)
    one.rounds(1)
    two.ring_end(2)
    one.rounds_end(1)
    one.gather_begin(0)
    two.rounds_end(2)
    two.rounds(1)
    one.gather_mid(0)
    two.rounds_end(1)
    two.gather_begin(0)
    one.gather_end(0)

    def cols(a_ref, i):
        return a_ref[:, pl.ds(al(i * BLK, BLK), BLK)]

    def block(slot):
        o = slot * 512
        return jnp.concatenate([g[pl.ds(al(o, 512), 256), :], g[pl.ds(al(o + 256, 256), 256), :]], axis=1)

    def band(a_ref, j, ds):
        def straight(d, first):
            i = (j + NB - d) % NB
            return cols(a_ref, i), block(first + i)

        def turned(d, first):
            return cols(a_ref, (j + d) % NB), block(first + j)

        a, b = zip(*[straight(*e) for e in ds])
        acc = jnp.dot(jnp.concatenate(a, axis=1), jnp.concatenate(b, axis=0), preferred_element_type=F32)
        a, b = zip(*[turned(*e) for e in ds])
        return acc + lax.dot_general(
            jnp.concatenate(a, axis=1), jnp.concatenate(b, axis=1), NT, preferred_element_type=F32
        )

    whole_one = ((2 * core, 0), (2 * core + 1, NB))
    whole_two = ((2 * core + 4, SECOND),)

    def single(acc_ref, a_ref, chunk, m):
        i, d, _ = block_of(chunk, m)
        j = (i + d) % NB
        b = block(chunk * SECOND + m)
        acc_ref[:, pl.ds(al(j * BLK, BLK), BLK)] += jnp.dot(cols(a_ref, i), b, preferred_element_type=F32)
        acc_ref[:, pl.ds(al(i * BLK, BLK), BLK)] += lax.dot_general(
            cols(a_ref, j), b, NT, preferred_element_type=F32
        )

    def loop(first_k, last_k, f):
        def body(k, carry):
            f(first_k + 2 * k)
            f(first_k + 2 * k + 1)
            return carry

        lax.fori_loop(0, (last_k - first_k) // 2, body, 0)
        if (last_k - first_k) % 2:
            f(last_k - 1)

    def band_at(j):
        return pl.ds(al(j * BLK, BLK), BLK)

    def to_partner(no, src, dst):
        c = remote(src, dst, part_send.at[no], part_recv.at[no], partner)
        c.start()
        sent.append(c)
        return c

    def y_one(j):
        yf[:, band_at(j)] = band(st, j, whole_one)

    def shared(acc_ref, a_ref):
        return lambda m: single(acc_ref, a_ref, 0, 28 + m), lambda m: single(acc_ref, a_ref, 1, 14 + m)

    y_first, y_rest = shared(yf, st)
    loop(0, 4, y_one)
    two.gather_mid(0)
    loop(4, NB, y_one)
    zf[...] = jnp.zeros((CHIP, M), F32)
    loop(0, 8, y_first)
    two.gather_end(0)
    loop(0, 3, y_rest)

    def y_two(j):
        v = yf[:, band_at(j)] + band(st, j, whole_two)
        yf[:, band_at(j)] = v
        yp[:, band_at(j)] = v.astype(BF)

    shares = []
    for lo, hi in ((0, 4), (4, 8), (8, 12), (12, 14)):
        loop(lo, hi, y_two)
        here = pl.ds(lo * BLK, (hi - lo) * BLK)
        shares.append((lo, hi, to_partner(len(shares), yp.at[:, here], yr.at[:, here])))

    factor = 0.3 * math.sqrt(M) / (jnp.sqrt(jnp.sum(sq[12], axis=(0, 1), keepdims=True)) + 1e-07)
    factor2 = factor * factor

    def y_sum(j):
        v = factor2 * (yf[:, band_at(j)] + yr[:, band_at(j)].astype(F32))
        yf[:, band_at(j)] = v
        ybf[:, band_at(j)] = v.astype(BF)

    for lo, hi, arriving in shares:
        arriving.wait_recv()
        loop(lo, hi, y_sum)

    z_first, z_rest = shared(zf, ybf)
    loop(0, 8, z_first)
    loop(0, 3, z_rest)

    def z_band(j):
        return factor2 * (zf[:, band_at(j)] + band(ybf, j, whole_one + whole_two))

    def z_theirs(k):
        zp[:, band_at(k)] = z_band((1 - core) * 7 + k).astype(BF)

    loop(0, 7, z_theirs)
    share = to_partner(4, zp, zr)

    def z_mine(k):
        zf[:, band_at(core * 7 + k)] = z_band(core * 7 + k)

    loop(0, 7, z_mine)
    share.wait_recv()
    for p in range(3):
        ut[pl.ds(p * 128 + COL3, 128 - COL3), :] = jnp.zeros((128 - COL3, HALF_M), BF)

    def finish(k):
        at = band_at(core * 7 + k)
        scaled = (factor * st[:, at].astype(F32)).astype(BF).astype(F32)
        product = factor * (COEFF_B * yf[:, at] + COEFF_C * (zf[:, at] + zr[:, band_at(k)].astype(F32)))
        u = (math.sqrt(K) * (COEFF_A * scaled + product)).astype(BF)
        for p in range(3):
            ut[pl.ds(p * 128, COL3), band_at(k)] = u[p * COL3 : (p + 1) * COL3]

    loop(0, 7, finish)

    y3 = x2p
    unpack = spread_matrix((8 * PIECE, 8 * ROWS), 0, PIECE, ROWS)
    for m in range(8):
        o = m * 8 * ROWS
        first_lane = o // 128 * 128
        skip = o - first_lane
        width = -(-(skip + 8 * ROWS) // 128) * 128
        v = ut[:, pl.ds(first_lane, width)][:, skip : skip + 8 * ROWS]
        rows = lax.dot_general(unpack, v, NT, preferred_element_type=F32).astype(BF)
        for r in range(8):
            x, y, z = m // 2, m % 2 * 2 + r // 4, r % 4
            for p, at in enumerate(((z, x, y), (x, y, z), (y, x, z))):
                y3[(p,) + at] = rows[r * PIECE : (r + 1) * PIECE, p * 128 : (p + 1) * 128]

    out1 = Exchange(2, lambda p, q: y3.at[p, q], lambda p, q: y2p.at[p, q], outs)
    out2 = PlaneExchange(
        y2, lambda p, s: y0.at[:, pl.ds(al(p * THIRD + s * COL2, 128), COL2)], spot, columns, out_plane_send, out_plane_recv,
    )
    for k in (2, 1, 3):
        for p in range(3):
            out1.start(p, k)
    for p in range(3):
        out1.keep(p)
    flush(sent)
    wait_bytes(sq.at[pl.ds(0, 10)], sq_send.at[0])
    one.all_sent()
    two.all_sent()
    narrow = spread_matrix((512, COL2), 0, 128, COL3)
    for p in range(3):
        out1.arrive(p)
        for u in range(4):
            rows = [y2p[p, q, u].reshape(4 * PIECE, 128) for q in range(4)]
            rows = jnp.dot(jnp.concatenate(rows, axis=1), narrow, preferred_element_type=F32)
            y2[p, pl.ds(4 * u, 4)] = rows.astype(BF).reshape(4, PIECE, COL2)
        out2.begin(p)
    own = []
    for p in range(3):
        a, b, _ = AXES[p]
        at = (pos[a], pos[b])
        own.append(pltpu.make_async_copy(y2.at[p, spot(p, *at)], out2.dst(p, columns(p, *at)), io_sem.at[1 + p]))
        own[p].start()
        out1.left(p)
    for p in range(3):
        out2.arrive(p)
        own[p].wait()
    for p in range(3):
        out2.left(p)


def local(gradient):
    dma = pltpu.SemaphoreType.DMA
    hbm = pl.BlockSpec(memory_space=pl.ANY)
    padded = pl.pallas_call(
        kernel,
        out_shape=jax.ShapeDtypeStruct((PIECE, K), BF),
        in_specs=[hbm],
        out_specs=hbm,
        scratch_shapes=[
            pltpu.VMEM((ROWS, K), BF),
            pltpu.VMEM((3, 16, PIECE, COL2), BF),
            pltpu.VMEM((3, 16, PIECE, COL2), BF),
            pltpu.VMEM((3, 4, 4, 4, PIECE, 128), BF),
            pltpu.VMEM((2, 3, 4, 4, 4, PIECE, 128), BF),
            pltpu.VMEM((M, 384), BF),
            pltpu.VMEM((CHIP, M), BF),
            pltpu.VMEM((384, HALF_M), BF),
            pltpu.VMEM((3, 4, 4, 4, PIECE, 128), BF),
            pltpu.VMEM((3, 16, PIECE, COL2), BF),
            pltpu.VMEM((3 * 12 * 512, 128), BF),
            pltpu.VMEM((3 * 6 * 512, 128), BF),
            pltpu.VMEM((SLOTS * 512, 128), BF),
            pltpu.VMEM((3, 6, 768, 128), BF),
            pltpu.VMEM((3, 3, 384, 128), BF),
            pltpu.VMEM((3, 3, 96, 128), BF),
            pltpu.VMEM((3, 6, 384, 128), BF),
            pltpu.VMEM((3, 3, 192, 128), BF),
            pltpu.VMEM((3, 3, 48, 128), BF),
            pltpu.VMEM((15, 8, 128), F32),
            pltpu.VMEM((CHIP, M), F32),
            pltpu.VMEM((CHIP, M), BF),
            pltpu.VMEM((CHIP, M), BF),
            pltpu.VMEM((CHIP, M), BF),
            pltpu.VMEM((CHIP, M), F32),
            pltpu.VMEM((CHIP, HALF_M), BF),
            pltpu.VMEM((CHIP, HALF_M), BF),
            dma((4,)),
            dma((3,)),
            dma((3,)),
            dma((3,)),
            dma((3,)),
            dma((3,)),
            dma((3,)),
            dma((3,)),
            dma((3,)),
            dma((3,)),
            dma((3,)),
            dma((5,)),
            dma((5,)),
            dma((3,)),
            dma((3, 3, 6)),
            dma((3,)),
            dma((3, 3, 6)),
            dma((3,)),
            dma((3, 3, 6)),
            dma((3,)),
            dma((3, 3, 6)),
            dma((1,)),
            dma((4,)),
        ],
        compiler_params=pltpu.CompilerParams(
            collective_id=0, has_side_effects=True, vmem_limit_bytes=60 * 1024 * 1024
        ),
        cost_estimate=pl.CostEstimate(flops=16 * 10**9, bytes_accessed=5 * 10**6, transcendentals=0),
    )(gradient)
    return padded[:ROWS]


def solution(mesh):
    spec = P(("wide", "narrow"), None)
    return jax.shard_map(local, mesh=mesh, in_specs=(spec,), out_specs=spec, check_vma=False)
```
